32 devices in a mesh: dp: 8 (over y, x, core), axial: 4 (over z).
Axes of the slice: x: 2, y: 2, z: 4, core: 2. Of those that a mesh axis runs over, the one named last changes fastest.
Arguments:
- homolog_activity: bfloat16 [64, 32, 256], P(('dp', 'axial')), parts along dimension 0, may hold values from -6 to 6
- homolog_symbol_ids: int32 [64, 32], P(('dp', 'axial')), parts along dimension 0, may hold values from 0 to 22
- residue_present_mask: int32 [256], P('dp'), parts along dimension 0, may hold values 0 or 1
- pair_state: bfloat16 [256, 32, 128], P(('dp', 'axial')), parts along dimension 0, may hold values from -6 to 6
- pair_valid_mask: int32 [256, 32], P(('dp', 'axial')), parts along dimension 0, may hold values 0 or 1
- symbol_lookup_matrix: bfloat16 [23, 256], replicated, may hold values from -3 to 3
- row_query_weight: bfloat16 [256, 256], replicated, as said below
- horizontal_attention_matrix: bfloat16 [256, 768], replicated, may hold values from -0.375 to 0.375
- pair_bias_weight: bfloat16 [128, 8], replicated, may hold values from -0.5 to 0.5
- horizontal_final_matrix: bfloat16 [256, 256], replicated, may hold values from -0.375 to 0.375
- column_query_weight: bfloat16 [256, 256], replicated, as said below
- vertical_attention_matrix: bfloat16 [256, 768], replicated, may hold values from -0.375 to 0.375
- vertical_final_matrix: bfloat16 [256, 256], replicated, may hold values from -0.375 to 0.375
- tensor_mean_lift_matrix: bfloat16 [256, 64], replicated, may hold values from -0.375 to 0.375
- outer_product_output_weight: bfloat16 [1024, 128], replicated, may hold values from -0.75 to 0.75
- triangle_projection_weight: bfloat16 [128, 256], replicated, may hold values from -0.5 to 0.5
- triangle_projection_gate: bfloat16 [128, 256], replicated, may hold values from -0.5 to 0.5
- triangle_output_gate: bfloat16 [128, 128], replicated, may hold values from -0.5 to 0.5
- triangle_output_weight: bfloat16 [128, 128], replicated, may hold values from -0.5 to 0.5
Outputs:
- alignment_output: bfloat16 [64, 32, 256], P('dp', 'axial'), parts along dimension 0
- pair_output: bfloat16 [256, 32, 128], P(('dp', 'axial')), parts along dimension 0
The draws below stay inside these ranges and needn't reach their ends.
There are 8 independent parts, one for each index of `dp`. The reference program is written for one: setup_inputs(seed, part) draws one part's arguments, and reference() takes and returns one part's arrays. A program takes and returns all parts, laid end to end along the dimension named above; an argument that names none is the same for every part. Nothing has to cross between parts.
Inputs may be any that keep to these rules, and one draw needn't show every extreme that they name: `row_query_weight`: a projection of 256 inputs. `column_query_weight`: a projection of 256 inputs.
All inputs are finite; a program needn't handle non-finite values. No bound on the sum of `pair_valid_mask` on one device may be relied on, other than what follows from the above.
Results may differ from the reference program's by a relative error of at most 0.03.
The reference program's roundings to bfloat16 on the way count: a program that leaves them out, or rounds other values in their place, can miss the bound.
Values may be sent and summed in bfloat16 or wider, within the bound.
No kernel may reach another device: no remote copies, remote signals or barrier semaphores. Data moves between devices by JAX's collectives and lax.ppermute only.
A program may use at most 64 MiB of HBM per device.

```python
import jax
import jax.numpy as jnp
from jax import lax

FEATURE_SIZE = 256
C_Z = 128
FOCUS_TOTAL = 8
FOCUS_SIZE = 32
MEAN_HIDDEN_SIZE = 32
C_TRI = 128
SYMBOL_KINDS = 23
LOCAL_SITES = 8
HOMOLOG_TOTAL = 8
SITES_IN_SAMPLE = 32
N_AXIAL = 4


def draw_row_query_weight(key, part):
    key = jax.random.fold_in(key, 11)
    attended_entries = jax.random.normal(key, (FEATURE_SIZE, FOCUS_TOTAL * FOCUS_SIZE), jnp.float32) * FEATURE_SIZE ** (-0.5)
    return attended_entries.astype(jnp.bfloat16)


def draw_column_query_weight(key, part):
    key = jax.random.fold_in(key, 23)
    attended_entries = jax.random.normal(key, (FEATURE_SIZE, FOCUS_TOTAL * FOCUS_SIZE), jnp.float32) * FEATURE_SIZE ** (-0.5)
    return attended_entries.astype(jnp.bfloat16)


def plant(result, rng, least, top_value):
    dims = result.shape
    index_at = [jax.random.randint(jax.random.fold_in(rng, axis), (), 0, dims[axis]) for axis in range(len(dims))]
    result = result.at[tuple(index_at)].set(least)
    longest = dims.index(max(dims))
    index_at[longest] = (index_at[longest] + 1) % dims[longest]
    return result.at[tuple(index_at)].set(top_value)


def levels(own_key, extent, pieces, least, high):
    def one(dim, blocks):
        draws = jax.random.uniform(jax.random.fold_in(jax.random.fold_in(own_key, 6), dim), (blocks,), jnp.float32, least / len(pieces), high / len(pieces))
        return jnp.repeat(jnp.exp(draws), extent[dim] // blocks).reshape((-1,) + (1,) * (len(extent) - dim - 1))

    factor_of = one(*pieces[0])
    for cut in pieces[1:]:
        factor_of = factor_of * one(*cut)
    return factor_of


def bell_draw(key, dims, deviation, bound, shards=(), held_as=jnp.bfloat16):
    level = levels(key, dims, shards, -0.22, 0.18) if shards else 1.0
    values = jax.random.normal(key, dims, jnp.float32) * deviation * level
    return jnp.minimum(jnp.maximum(values, -bound), bound).astype(held_as)


def setup_inputs(seed: int = 0, part: int = 0) -> dict:
    streams_of = jax.random.split(jax.random.key(seed), 20)
    own_keys = jax.random.split(jax.random.fold_in(streams_of[19], part), 20)
    homolog_activity = bell_draw(own_keys[0], (HOMOLOG_TOTAL, SITES_IN_SAMPLE, FEATURE_SIZE), 1.0, 6.0, ((0, 4),))
    homolog_symbol_ids = plant(jax.random.randint(own_keys[1], (HOMOLOG_TOTAL, SITES_IN_SAMPLE), 0, SYMBOL_KINDS), jax.random.fold_in(own_keys[1], 1), 0, SYMBOL_KINDS - 1).astype(jnp.int32)
    residue_present_mask = plant((jax.random.randint(own_keys[2], (SITES_IN_SAMPLE,), 0, 8) < 7).astype(jnp.int32), jax.random.fold_in(own_keys[2], 1), 0, 1)
    pair_state = bell_draw(own_keys[3], (SITES_IN_SAMPLE, SITES_IN_SAMPLE, C_Z), 1.0, 6.0, ((0, 4),))
    pair_valid_mask = plant((jax.random.randint(own_keys[4], (SITES_IN_SAMPLE, SITES_IN_SAMPLE), 0, 8) < 7).astype(jnp.int32), jax.random.fold_in(own_keys[4], 1), 0, 1)
    symbol_lookup_matrix = bell_draw(streams_of[5], (SYMBOL_KINDS, FEATURE_SIZE), 0.5, 3.0)
    row_query_weight = draw_row_query_weight(jax.random.fold_in(streams_of[19], 71), part)
    horizontal_attention_matrix = bell_draw(streams_of[7], (FEATURE_SIZE, 3 * FOCUS_TOTAL * FOCUS_SIZE), FEATURE_SIZE ** -0.5, 0.375)
    pair_bias_weight = bell_draw(streams_of[8], (C_Z, FOCUS_TOTAL), C_Z ** -0.5, 0.5)
    horizontal_final_matrix = bell_draw(streams_of[9], (FOCUS_TOTAL * FOCUS_SIZE, FEATURE_SIZE), (FOCUS_TOTAL * FOCUS_SIZE) ** -0.5, 0.375)
    column_query_weight = draw_column_query_weight(jax.random.fold_in(streams_of[19], 71), part)
    vertical_attention_matrix = bell_draw(streams_of[11], (FEATURE_SIZE, 3 * FOCUS_TOTAL * FOCUS_SIZE), FEATURE_SIZE ** -0.5, 0.375)
    vertical_final_matrix = bell_draw(streams_of[12], (FOCUS_TOTAL * FOCUS_SIZE, FEATURE_SIZE), (FOCUS_TOTAL * FOCUS_SIZE) ** -0.5, 0.375)
    tensor_mean_lift_matrix = bell_draw(streams_of[13], (FEATURE_SIZE, 2 * MEAN_HIDDEN_SIZE), FEATURE_SIZE ** -0.5, 0.375)
    outer_product_output_weight = bell_draw(streams_of[14], (MEAN_HIDDEN_SIZE * MEAN_HIDDEN_SIZE, C_Z), (MEAN_HIDDEN_SIZE * MEAN_HIDDEN_SIZE // 16) ** -0.5, 0.75)
    triangle_projection_weight = bell_draw(streams_of[15], (C_Z, 2 * C_TRI), C_Z ** -0.5, 0.5)
    triangle_projection_gate = bell_draw(streams_of[16], (C_Z, 2 * C_TRI), C_Z ** -0.5, 0.5)
    triangle_output_gate = bell_draw(streams_of[17], (C_Z, C_Z), C_Z ** -0.5, 0.5)
    triangle_output_weight = bell_draw(streams_of[18], (C_TRI, C_Z), C_TRI ** -0.5, 0.5)
    return dict(homolog_activity=homolog_activity, homolog_symbol_ids=homolog_symbol_ids, residue_present_mask=residue_present_mask, pair_state=pair_state, pair_valid_mask=pair_valid_mask, symbol_lookup_matrix=symbol_lookup_matrix, row_query_weight=row_query_weight, horizontal_attention_matrix=horizontal_attention_matrix, pair_bias_weight=pair_bias_weight, horizontal_final_matrix=horizontal_final_matrix, column_query_weight=column_query_weight, vertical_attention_matrix=vertical_attention_matrix, vertical_final_matrix=vertical_final_matrix, tensor_mean_lift_matrix=tensor_mean_lift_matrix, outer_product_output_weight=outer_product_output_weight, triangle_projection_weight=triangle_projection_weight, triangle_projection_gate=triangle_projection_gate, triangle_output_gate=triangle_output_gate, triangle_output_weight=triangle_output_weight)


def layer_normalize(attended_entries):
    attended_entries = attended_entries.astype(jnp.float32)
    mean = lax.optimization_barrier(jnp.mean(attended_entries, axis=-1, keepdims=True))
    centred = attended_entries - mean
    var = lax.optimization_barrier(jnp.mean(centred * centred, axis=-1, keepdims=True))
    return centred * lax.rsqrt(var + 1e-05)

def gated_attend(evoformer_block, extra_axes, w_query, w_kvg, w_out):
    lines_list, residue_length, input_width = evoformer_block.shape
    width = FOCUS_TOTAL * FOCUS_SIZE
    flat = layer_normalize(evoformer_block).astype(jnp.bfloat16).reshape(lines_list * residue_length, input_width)
    query = (jnp.dot(flat, w_query, preferred_element_type=jnp.float32) * FOCUS_SIZE ** (-0.5)).astype(jnp.bfloat16)
    query = query.reshape(lines_list, residue_length, FOCUS_TOTAL, FOCUS_SIZE)
    kvg = jnp.dot(flat, w_kvg, preferred_element_type=jnp.float32)
    keys = kvg[:, :width].astype(jnp.bfloat16).reshape(lines_list, residue_length, FOCUS_TOTAL, FOCUS_SIZE)
    attended_entries = kvg[:, width:2 * width].astype(jnp.bfloat16).reshape(lines_list, residue_length, FOCUS_TOTAL, FOCUS_SIZE)
    gate = jax.nn.sigmoid(kvg[:, 2 * width:]).reshape(lines_list, residue_length, FOCUS_TOTAL, FOCUS_SIZE)
    scores = jnp.einsum('bihd,bjhd->bhij', query.astype(jnp.float32), keys.astype(jnp.float32)) + extra_axes
    top = lax.optimization_barrier(jnp.max(scores, axis=-1, keepdims=True))
    expo = jnp.exp(scores - top)
    weights = (expo / lax.optimization_barrier(jnp.sum(expo, axis=-1, keepdims=True))).astype(jnp.bfloat16)
    mixed = jnp.einsum('bhij,bjhd->bihd', weights.astype(jnp.float32), attended_entries.astype(jnp.float32))
    mixed = (mixed * gate).astype(jnp.bfloat16).reshape(lines_list * residue_length, width)
    return evoformer_block + jnp.dot(mixed, w_out, preferred_element_type=jnp.float32).reshape(lines_list, residue_length, input_width)

def reference(homolog_activity, homolog_symbol_ids, residue_present_mask, pair_state, pair_valid_mask, symbol_lookup_matrix, row_query_weight, horizontal_attention_matrix, pair_bias_weight, horizontal_final_matrix, column_query_weight, vertical_attention_matrix, vertical_final_matrix, tensor_mean_lift_matrix, outer_product_output_weight, triangle_projection_weight, triangle_projection_gate, triangle_output_gate, triangle_output_weight):
    homolog_starting = homolog_activity.astype(jnp.float32) + symbol_lookup_matrix.astype(jnp.float32)[homolog_symbol_ids]
    pair_norm = layer_normalize(pair_state).astype(jnp.bfloat16)
    bias = jnp.dot(pair_norm.reshape(SITES_IN_SAMPLE * SITES_IN_SAMPLE, C_Z), pair_bias_weight, preferred_element_type=jnp.float32)
    bias = jnp.transpose(bias.astype(jnp.bfloat16).reshape(SITES_IN_SAMPLE, SITES_IN_SAMPLE, FOCUS_TOTAL), (2, 0, 1)).astype(jnp.float32)
    key_bias = 1000000000.0 * (residue_present_mask.astype(jnp.float32) - 1.0)
    extra_axes = bias[None] + key_bias[None, None, None, :]
    cluster_total = homolog_starting.reshape(HOMOLOG_TOTAL // 2, 2, SITES_IN_SAMPLE, FEATURE_SIZE)
    homolog_across_update = lax.map(lambda evoformer_block: gated_attend(evoformer_block, extra_axes, row_query_weight, horizontal_attention_matrix, horizontal_final_matrix), cluster_total)
    homolog_across_update = homolog_across_update.reshape(HOMOLOG_TOTAL, SITES_IN_SAMPLE, FEATURE_SIZE).astype(jnp.bfloat16)
    column_count = jnp.swapaxes(homolog_across_update, 0, 1)
    column_finished = lax.map(lambda item: gated_attend(item[None].astype(jnp.float32), 0.0, column_query_weight, vertical_attention_matrix, vertical_final_matrix)[0], column_count)
    alignment_output = jnp.swapaxes(column_finished, 0, 1).astype(jnp.bfloat16)
    tensor_mean_scaler = layer_normalize(alignment_output).astype(jnp.bfloat16)
    split_parts = jnp.dot(tensor_mean_scaler.reshape(HOMOLOG_TOTAL * SITES_IN_SAMPLE, FEATURE_SIZE), tensor_mean_lift_matrix, preferred_element_type=jnp.float32)
    split_parts = split_parts.astype(jnp.bfloat16).reshape(HOMOLOG_TOTAL, SITES_IN_SAMPLE, 2 * MEAN_HIDDEN_SIZE)
    first_factor = split_parts[..., :MEAN_HIDDEN_SIZE].astype(jnp.float32)
    second_factor = split_parts[..., MEAN_HIDDEN_SIZE:].astype(jnp.float32)
    first_factor_lines = jnp.swapaxes(first_factor, 0, 1).reshape(N_AXIAL, LOCAL_SITES, HOMOLOG_TOTAL, MEAN_HIDDEN_SIZE)

    def opm_block(lines_list):
        tensor_mean = jnp.einsum('kxh,xgo->kgho', lines_list, second_factor) / HOMOLOG_TOTAL
        tensor_mean = tensor_mean.reshape(LOCAL_SITES * SITES_IN_SAMPLE, MEAN_HIDDEN_SIZE * MEAN_HIDDEN_SIZE).astype(jnp.bfloat16)
        return jnp.dot(tensor_mean, outer_product_output_weight, preferred_element_type=jnp.float32).reshape(LOCAL_SITES, SITES_IN_SAMPLE, C_Z)
    update = lax.map(opm_block, first_factor_lines).reshape(SITES_IN_SAMPLE, SITES_IN_SAMPLE, C_Z)
    pair_one = pair_state.astype(jnp.float32) + update
    tri_norm = layer_normalize(pair_one).astype(jnp.bfloat16)
    flat = tri_norm.reshape(SITES_IN_SAMPLE * SITES_IN_SAMPLE, C_Z)
    proj = jnp.dot(flat, triangle_projection_weight, preferred_element_type=jnp.float32)
    gates = jnp.dot(flat, triangle_projection_gate, preferred_element_type=jnp.float32)
    both = (jax.nn.sigmoid(gates) * proj * pair_valid_mask.astype(jnp.float32).reshape(SITES_IN_SAMPLE * SITES_IN_SAMPLE, 1)).astype(jnp.bfloat16)
    both = both.reshape(SITES_IN_SAMPLE, SITES_IN_SAMPLE, 2 * C_TRI)
    left_tri = jnp.transpose(both[..., :C_TRI], (2, 0, 1)).astype(jnp.float32)
    right_tri = jnp.transpose(both[..., C_TRI:], (2, 0, 1)).astype(jnp.float32)
    tri_sum = jnp.einsum('cik,cjk->cij', left_tri, right_tri)
    tri_mixed = layer_normalize(jnp.transpose(tri_sum, (1, 2, 0))).astype(jnp.bfloat16)
    tri_update = jnp.dot(tri_mixed.reshape(SITES_IN_SAMPLE * SITES_IN_SAMPLE, C_TRI), triangle_output_weight, preferred_element_type=jnp.float32).reshape(SITES_IN_SAMPLE, SITES_IN_SAMPLE, C_Z)
    out_gate = jax.nn.sigmoid(jnp.dot(flat, triangle_output_gate, preferred_element_type=jnp.float32)).reshape(SITES_IN_SAMPLE, SITES_IN_SAMPLE, C_Z)
    pair_output = (pair_one + out_gate * tri_update).astype(jnp.bfloat16)
    return (alignment_output, pair_output)
```

```python
import functools

import jax
import jax.numpy as jnp
from jax import lax
from jax.experimental import pallas as pl
from jax.experimental.pallas import tpu as pltpu
from jax.sharding import PartitionSpec as P

FOCUS_TOTAL = 8
FOCUS_SIZE = 32
MEAN_HIDDEN_SIZE = 32
C_TRI = 128


def layer_normalize(attended_entries):
    attended_entries = attended_entries.astype(jnp.float32)
    mean = jnp.mean(attended_entries, axis=-1, keepdims=True)
    centred = attended_entries - mean
    var = jnp.mean(centred * centred, axis=-1, keepdims=True)
    return centred * lax.rsqrt(var + 1e-05)


def gated_attend(evoformer_block, extra_axes, w_query, w_kvg, w_out):
    lines_list, residue_length, input_width = evoformer_block.shape
    width = FOCUS_TOTAL * FOCUS_SIZE
    flat = (
        layer_normalize(evoformer_block)
        .astype(jnp.bfloat16)
        .reshape(lines_list * residue_length, input_width)
    )
    query = (
        jnp.dot(flat, w_query, preferred_element_type=jnp.float32) * FOCUS_SIZE ** (-0.5)
    ).astype(jnp.bfloat16)
    query = query.reshape(lines_list, residue_length, FOCUS_TOTAL, FOCUS_SIZE)
    kvg = jnp.dot(flat, w_kvg, preferred_element_type=jnp.float32)
    keys = (
        kvg[:, :width]
        .astype(jnp.bfloat16)
        .reshape(lines_list, residue_length, FOCUS_TOTAL, FOCUS_SIZE)
    )
    attended_entries = (
        kvg[:, width : 2 * width]
        .astype(jnp.bfloat16)
        .reshape(lines_list, residue_length, FOCUS_TOTAL, FOCUS_SIZE)
    )
    gate = jax.nn.sigmoid(kvg[:, 2 * width :]).reshape(
        lines_list, residue_length, FOCUS_TOTAL, FOCUS_SIZE
    )
    scores = (
        jnp.einsum("bihd,bjhd->bhij", query, keys, preferred_element_type=jnp.float32) + extra_axes
    )
    top = jnp.max(scores, axis=-1, keepdims=True)
    expo = jnp.exp(scores - top)
    weights = (expo / jnp.sum(expo, axis=-1, keepdims=True)).astype(jnp.bfloat16)
    mixed = jnp.einsum(
        "bhij,bjhd->bihd", weights, attended_entries, preferred_element_type=jnp.float32
    )
    mixed = (mixed * gate).astype(jnp.bfloat16).reshape(lines_list * residue_length, width)
    return evoformer_block + jnp.dot(mixed, w_out, preferred_element_type=jnp.float32).reshape(
        lines_list, residue_length, input_width
    )


def finish_sums(evoformer_block, triangle_output_weight):
    mixed = layer_normalize(jnp.transpose(evoformer_block, (1, 2, 0))).astype(jnp.bfloat16)
    return jnp.einsum(
        "ijc,cz->ijz", mixed, triangle_output_weight, preferred_element_type=jnp.float32
    )


def local_sharded(
    homolog_activity,
    homolog_symbol_ids,
    residue_present_mask,
    pair_state,
    pair_valid_mask,
    symbol_lookup_matrix,
    row_query_weight,
    horizontal_attention_matrix,
    pair_bias_weight,
    horizontal_final_matrix,
    column_query_weight,
    vertical_attention_matrix,
    vertical_final_matrix,
    tensor_mean_lift_matrix,
    outer_product_output_weight,
    triangle_projection_weight,
    triangle_projection_gate,
    triangle_output_gate,
    triangle_output_weight,
):
    sequence_per_device, residue_length, input_width = homolog_activity.shape
    res_dev = pair_state.shape[0]
    group_size = lax.axis_size("axial")
    token_classes = symbol_lookup_matrix.shape[0]
    token_one_hot = (
        homolog_symbol_ids[..., None] == jnp.arange(token_classes, dtype=jnp.int32)
    ).astype(jnp.bfloat16)
    token_embedded = jnp.einsum(
        "slt,tc->slc", token_one_hot, symbol_lookup_matrix, preferred_element_type=jnp.float32
    )
    homolog_starting = homolog_activity.astype(jnp.float32) + token_embedded
    pair_norm = layer_normalize(pair_state).astype(jnp.bfloat16)
    bias_rows = jnp.einsum(
        "ijc,ch->hij", pair_norm, pair_bias_weight, preferred_element_type=jnp.float32
    ).astype(jnp.bfloat16)
    bias_full = lax.all_gather(bias_rows, "axial", axis=1, tiled=True)
    key_bias = 1000000000.0 * (residue_present_mask.astype(jnp.float32) - 1.0)
    extra_axes = bias_full.astype(jnp.float32)[None] + key_bias[None, None, None, :]
    cluster_total = homolog_starting.reshape(
        sequence_per_device // 2, 2, residue_length, input_width
    )
    homolog_across_update = lax.map(
        lambda evoformer_block: gated_attend(
            evoformer_block,
            extra_axes,
            row_query_weight,
            horizontal_attention_matrix,
            horizontal_final_matrix,
        ),
        cluster_total,
    )
    homolog_across_update = homolog_across_update.reshape(
        sequence_per_device, group_size, res_dev, input_width
    ).astype(jnp.bfloat16)
    moved = jnp.swapaxes(
        lax.all_to_all(homolog_across_update, "axial", split_axis=1, concat_axis=0, tiled=True)[
            :, 0
        ],
        0,
        1,
    )
    finished = lax.map(
        lambda item: gated_attend(
            item[None].astype(jnp.float32),
            0.0,
            column_query_weight,
            vertical_attention_matrix,
            vertical_final_matrix,
        )[0],
        moved,
    )
    exchanged = jnp.swapaxes(finished, 0, 1).astype(jnp.bfloat16)[:, None]
    sequence_count = exchanged.shape[0]
    alignment_after_columns = exchanged.reshape(sequence_count, res_dev, input_width)
    tensor_mean_scaler = layer_normalize(alignment_after_columns).astype(jnp.bfloat16)
    split_parts = jnp.einsum(
        "src,cf->rsf",
        tensor_mean_scaler,
        tensor_mean_lift_matrix,
        preferred_element_type=jnp.float32,
    ).astype(jnp.bfloat16)
    first_factor = split_parts[..., :MEAN_HIDDEN_SIZE]
    second_factor = split_parts[..., MEAN_HIDDEN_SIZE:].reshape(
        res_dev, sequence_count * MEAN_HIDDEN_SIZE
    )
    step_rows = 8
    left_blocks = first_factor.reshape(
        res_dev // step_rows, step_rows, sequence_count, MEAN_HIDDEN_SIZE
    )
    piece = lax.all_gather(second_factor, "axial", axis=0, tiled=True)
    count = piece.shape[0]
    right_part = piece.reshape(count, sequence_count, MEAN_HIDDEN_SIZE)

    def one_block(lines_list):
        tensor_mean = (
            jnp.einsum("isc,jsd->ijcd", lines_list, right_part, preferred_element_type=jnp.float32)
            / sequence_count
        )
        tensor_mean = tensor_mean.reshape(
            step_rows, count, MEAN_HIDDEN_SIZE * MEAN_HIDDEN_SIZE
        ).astype(jnp.bfloat16)
        return jnp.einsum(
            "ijf,fz->ijz",
            tensor_mean,
            outer_product_output_weight,
            preferred_element_type=jnp.float32,
        )

    update = lax.map(one_block, left_blocks).reshape(
        res_dev, count, outer_product_output_weight.shape[1]
    )
    pair_one = pair_state.astype(jnp.float32) + update
    tri_norm = layer_normalize(pair_one).astype(jnp.bfloat16)
    proj = jnp.einsum(
        "ikc,cf->fik", tri_norm, triangle_projection_weight, preferred_element_type=jnp.float32
    )
    gates = jnp.einsum(
        "ikc,cf->fik", tri_norm, triangle_projection_gate, preferred_element_type=jnp.float32
    )
    both = (jax.nn.sigmoid(gates) * proj * pair_valid_mask.astype(jnp.float32)[None]).astype(
        jnp.bfloat16
    )
    left_tri = both[:C_TRI]
    right_tri = both[C_TRI:]
    moved_left, moved_right = (
        lax.all_to_all(left_tri, "axial", split_axis=0, concat_axis=1, tiled=True),
        lax.all_to_all(right_tri, "axial", split_axis=0, concat_axis=1, tiled=True),
    )
    partial_sum = jnp.einsum(
        "cik,cjk->cij", moved_left, moved_right, preferred_element_type=jnp.float32
    )
    tri_sum = lax.all_to_all(
        partial_sum.astype(jnp.bfloat16), "axial", split_axis=1, concat_axis=0, tiled=True
    ).astype(partial_sum.dtype)
    tri_update = finish_sums(tri_sum, triangle_output_weight)
    out_gate = jax.nn.sigmoid(
        jnp.einsum(
            "ijc,cz->ijz", tri_norm, triangle_output_gate, preferred_element_type=jnp.float32
        )
    )
    pair_output = (pair_one + out_gate * tri_update).astype(jnp.bfloat16)
    return (alignment_after_columns, pair_output)


BF16 = jnp.bfloat16
F32 = jnp.float32
VMEM_LIMIT = 40 * 1024 * 1024


def mul(lhs, rhs, over=((1,), (0,))):
    return lax.dot_general(lhs, rhs, (over, ((), ())), preferred_element_type=F32)


def iota(shape, axis):
    return lax.broadcasted_iota(jnp.int32, shape, axis)


def zero_one(condition):
    return jnp.where(condition, 1.0, 0.0).astype(BF16)


def normal(x):
    mean = jnp.mean(x, axis=-1, keepdims=True)
    centred = x - mean
    var = jnp.mean(centred * centred, axis=-1, keepdims=True)
    return centred * lax.rsqrt(var + 1e-05)


def sigmoid(x):
    return 1.0 / (1.0 + jnp.exp(-x))


def column_softmax(scores):
    expo = jnp.exp(scores - jnp.max(scores, axis=0, keepdims=True))
    return expo * (1.0 / jnp.sum(expo, axis=0, keepdims=True))


def head_masks(width):
    return [
        zero_one(iota((1, width), 1) // FOCUS_SIZE == h) for h in range(FOCUS_TOTAL)
    ]


def packet_rows(residues, res_dev):
    return residues + 16 if res_dev <= 8 else residues + 2 * res_dev


def packet_kernel(pair_ref, ids_ref, valid_ref, weight_ref, packet_ref, held):
    rows, residues, width = pair_ref.shape
    lanes = FOCUS_TOTAL * rows
    flat = normal(pair_ref[...].astype(F32).reshape(rows * residues, width)).astype(BF16)
    spread = zero_one(iota((FOCUS_TOTAL, lanes), 1) // rows == iota((FOCUS_TOTAL, lanes), 0))
    weight = mul(weight_ref[...], spread)
    row_of = iota((width, lanes), 1) % rows
    bias = jnp.zeros((residues, lanes), F32)
    for i in range(rows):
        one_row = jnp.where(row_of == i, weight, 0.0).astype(BF16)
        bias += mul(flat[i * residues : (i + 1) * residues], one_row)
    held[...] = jnp.zeros_like(held)
    held[0:residues, 0:lanes] = bias
    held[residues : residues + rows, 0:residues] = valid_ref[...].astype(F32)
    held[residues + 8 : residues + 8 + ids_ref.shape[0], 0:residues] = ids_ref[...].astype(F32)
    packet_ref[...] = held[...].astype(BF16)


def project(x, w_query, w_kvg):
    width = FOCUS_TOTAL * FOCUS_SIZE
    flat = normal(x).astype(BF16)
    query = (mul(flat, w_query[...]) * FOCUS_SIZE ** (-0.5)).astype(BF16)
    keys = mul(flat, w_kvg[:, :width]).astype(BF16)
    values = mul(flat, w_kvg[:, width : 2 * width]).astype(BF16)
    gate = sigmoid(mul(flat, w_kvg[:, 2 * width :]))
    return query, keys, values, gate


def msa_kernel(n, *refs):
    acts, packets, refs = refs[:n], refs[n : 2 * n], refs[2 * n :]
    (present, table, row_q, row_kvg, row_out, col_q, col_kvg, col_out, lift, outer_w), refs = (
        refs[:10],
        refs[10:],
    )
    align_ref, update_ref, start, lifted = refs
    per, residues, width = acts[0].shape
    count = per * n
    res_dev = residues // n
    tokens = count * residues
    lanes = FOCUS_TOTAL * residues
    me = lax.axis_index("axial")
    masks = head_masks(width)
    kinds = table.shape[0]

    place = iota((FOCUS_TOTAL * res_dev, lanes), 0)
    place = (place // res_dev) * residues + place % res_dev - iota(place.shape, 1)
    extra = jnp.zeros((residues, lanes), F32)
    for r in range(n):
        owner = lax.rem(me + r, n)
        packet = packets[r][...].astype(F32)
        bias = packet[:residues, : FOCUS_TOTAL * res_dev].astype(BF16)
        extra += mul(bias, zero_one(place == -owner * res_dev))
        for q in range(per):
            ids = packet[residues + 8 + q : residues + 9 + q, :residues]
            hot = zero_one(iota((kinds, residues), 0).astype(F32) == ids)
            start[pl.ds(pl.multiple_of((owner * per + q) * residues, residues), residues), :] = (
                acts[r][q].astype(F32) + mul(hot, table[...], ((0,), (0,)))
            )
    shown = mul(present[...].astype(F32).astype(BF16), jnp.ones((1, lanes), BF16), ((0,), (0,)))
    extra = extra + 1000000000.0 * (shown - 1.0)

    zero = start[...]
    query, keys, values, gate = project(zero, row_q, row_kvg)
    rows = []
    for s in range(count):
        here = slice(s * residues, (s + 1) * residues)
        spread = jnp.concatenate([query[here] * mask for mask in masks], axis=0)
        weights = column_softmax(mul(keys[here], spread, ((1,), (1,))) + extra).astype(BF16)
        heads = mul(weights, values[here], ((0,), (0,)))
        mixed = jnp.zeros((residues, width), F32)
        for h in range(FOCUS_TOTAL):
            part = heads[h * residues : (h + 1) * residues]
            mixed = jnp.where(iota((1, width), 1) // FOCUS_SIZE == h, part, mixed)
        rows.append(mixed)
    mixed = (jnp.concatenate(rows, axis=0) * gate).astype(BF16)
    msa_one = (zero + mul(mixed, row_out[...])).astype(BF16)

    row_at, lane_at = iota((tokens, tokens), 0), iota((tokens, tokens), 1)
    turn = zero_one(lane_at == (row_at % count) * residues + row_at // count)
    one = mul(turn, msa_one)
    query, keys, values, gate = project(one, col_q, col_kvg)
    group = min(tokens, 128)
    sites = group // count
    same = iota((sites, count, group), 2) // count == iota((sites, count, group), 0)
    groups = []
    for g in range(tokens // group):
        here = slice(g * group, (g + 1) * group)
        all_weights, all_values = [], []
        for mask in masks:
            scores = mul(keys[here], query[here] * mask, ((1,), (1,)))
            scores = jnp.sum(jnp.where(same, scores.reshape(sites, count, group), 0.0), axis=0)
            weights = column_softmax(scores)
            weights = jnp.where(same, weights[None], 0.0).reshape(group, group)
            all_weights.append(weights.astype(BF16))
            all_values.append(values[here] * mask)
        groups.append(
            mul(
                jnp.concatenate(all_weights, axis=0),
                jnp.concatenate(all_values, axis=0),
                ((0,), (0,)),
            )
        )
    mixed = (jnp.concatenate(groups, axis=0) * gate).astype(BF16)
    align = (one + mul(mixed, col_out[...])).astype(BF16)
    own = count * res_dev
    row_at, lane_at = iota((own, tokens), 0), iota((own, tokens), 1)
    pick = zero_one(
        lane_at == (row_at % res_dev + me * res_dev) * count + row_at // res_dev
    )
    align_ref[...] = mul(pick, align).reshape(count, res_dev, width).astype(BF16)

    opm = mul(normal(align.astype(F32)).astype(BF16), lift[...]).astype(BF16)
    hidden = MEAN_HIDDEN_SIZE
    deep = hidden * count
    spread = zero_one(
        iota((2 * hidden, deep), 1) // count == iota((2 * hidden, deep), 0)
    )
    left = mul(opm, spread)
    left = jnp.where(
        iota((tokens, deep), 0) % count == iota((tokens, deep), 1) % count, left, 0.0
    ).astype(BF16)
    gather = zero_one(iota((residues, tokens), 1) // count == iota((residues, tokens), 0))
    left = mul(gather, left).astype(BF16)
    right = opm[:, hidden:]
    for c in range(hidden):
        lifted[c] = mul(right, outer_w[c * hidden : (c + 1) * hidden, :])
    for j in range(residues):
        part = lifted[:, j * count : (j + 1) * count, :].reshape(deep, outer_w.shape[1])
        update_ref[j] = mul(left, part.astype(BF16)) * (1.0 / count)


def pair_kernel(n, *refs):
    pairs, packets, refs = refs[:n], refs[n : 2 * n], refs[2 * n :]
    update, proj, gates, gate_out, w_out, out_ref, state, one, right_at, left_at, valid = refs
    res_dev, residues, width = pairs[0].shape
    me = lax.axis_index("axial")
    for r in range(n):
        owner = lax.rem(me + r, n)
        size = res_dev * residues
        state[pl.ds(pl.multiple_of(owner * size, size), size), :] = (
            pairs[r][...].astype(F32).reshape(size, width)
        )
        valid[pl.ds(pl.multiple_of(owner * res_dev, res_dev), res_dev), :] = packets[r][
            ...
        ].astype(F32)[residues : residues + res_dev, :residues]
    for k in range(residues):
        one[k * residues : (k + 1) * residues, :] = (
            state[pl.ds(k, residues, stride=residues), :] + update[k]
        )

    choose = zero_one(
        iota((residues, residues * C_TRI), 1) // C_TRI == iota((residues, residues * C_TRI), 0)
    )
    shown = mul(valid[...].astype(BF16), choose)
    right_w = jnp.concatenate([proj[:, C_TRI:], gates[:, C_TRI:]], axis=1)
    step = 8
    for k in range(0, residues, step):
        here = slice(k * residues, (k + step) * residues)
        both = mul(normal(one[here, :]).astype(BF16), right_w)
        both = sigmoid(both[:, C_TRI:]) * both[:, :C_TRI]
        for p in range(step):
            part = both[p * residues : (p + 1) * residues]
            part = part * shown[:, (k + p) * C_TRI : (k + p + 1) * C_TRI]
            right_at[(k + p) * residues : (k + p + 1) * residues, :] = part.astype(BF16).astype(F32)

    own = jnp.concatenate(
        [one[pl.ds(me * res_dev + i, residues, stride=residues), :] for i in range(res_dev)],
        axis=0,
    )
    left_w = jnp.concatenate([proj[:, :C_TRI], gates[:, :C_TRI], gate_out[...]], axis=1)
    own_all = mul(normal(own).astype(BF16), left_w)
    own_gate = sigmoid(own_all[:, 2 * C_TRI :])
    left = sigmoid(own_all[:, C_TRI : 2 * C_TRI]) * own_all[:, :C_TRI]
    own_valid = packets[0][...].astype(F32)[residues : residues + res_dev, :residues].astype(BF16)
    choose = zero_one(
        iota((res_dev, res_dev * C_TRI), 1) // C_TRI == iota((res_dev, res_dev * C_TRI), 0)
    )
    shown = mul(own_valid, choose, ((0,), (0,)))
    for i in range(res_dev):
        part = left[i * residues : (i + 1) * residues] * shown[:, i * C_TRI : (i + 1) * C_TRI]
        left_at[i * residues : (i + 1) * residues, :] = part.astype(BF16).astype(F32)
    sums = [jnp.zeros((residues, C_TRI), F32) for _ in range(res_dev)]
    for k in range(residues):
        other = right_at[k * residues : (k + 1) * residues, :]
        for i in range(res_dev):
            sums[i] += left_at[i * residues + k : i * residues + k + 1, :] * other
    mixed = normal(jnp.concatenate(sums, axis=0)).astype(BF16)
    result = own + own_gate * mul(mixed, w_out[...])
    out_ref[...] = result.reshape(res_dev, residues, width).astype(BF16)


def call(kernel, out_shape, scratch, cost, *args):
    flops, moved = cost
    return pl.pallas_call(
        kernel,
        out_shape=out_shape,
        in_specs=[pl.BlockSpec(memory_space=pltpu.VMEM)] * len(args),
        out_specs=jax.tree.map(lambda _: pl.BlockSpec(memory_space=pltpu.VMEM), out_shape),
        scratch_shapes=scratch,
        compiler_params=pltpu.CompilerParams(vmem_limit_bytes=VMEM_LIMIT),
        cost_estimate=pl.CostEstimate(flops=flops, bytes_accessed=moved, transcendentals=0),
    )(*args)


def from_all(array, n):
    return [array] + [
        lax.ppermute(array, "axial", [(i, (i - r) % n) for i in range(n)]) for r in range(1, n)
    ]


def local_whole(
    homolog_activity,
    homolog_symbol_ids,
    residue_present_mask,
    pair_state,
    pair_valid_mask,
    symbol_lookup_matrix,
    row_query_weight,
    horizontal_attention_matrix,
    pair_bias_weight,
    horizontal_final_matrix,
    column_query_weight,
    vertical_attention_matrix,
    vertical_final_matrix,
    tensor_mean_lift_matrix,
    outer_product_output_weight,
    triangle_projection_weight,
    triangle_projection_gate,
    triangle_output_gate,
    triangle_output_weight,
):
    n = lax.axis_size("axial")
    per, residues, width = homolog_activity.shape
    res_dev, _, pair_width = pair_state.shape
    count = per * n
    rows = packet_rows(residues, res_dev)
    acts = from_all(homolog_activity, n)
    packet = call(
        packet_kernel,
        jax.ShapeDtypeStruct((rows, 128), BF16),
        [pltpu.VMEM((rows, 128), F32)],
        (2 * 10**7, 10**5),
        pair_state,
        homolog_symbol_ids,
        pair_valid_mask,
        pair_bias_weight,
    )
    packets = from_all(packet, n)
    pairs = from_all(pair_state, n)
    alignment, update = call(
        functools.partial(msa_kernel, n),
        (
            jax.ShapeDtypeStruct((count, res_dev, width), BF16),
            jax.ShapeDtypeStruct((residues, residues, pair_width), F32),
        ),
        [
            pltpu.VMEM((count * residues, width), F32),
            pltpu.VMEM((MEAN_HIDDEN_SIZE, count * residues, pair_width), F32),
        ],
        (10**9, 2 * 10**6),
        *acts,
        *packets,
        residue_present_mask.reshape(1, residues),
        symbol_lookup_matrix,
        row_query_weight,
        horizontal_attention_matrix,
        horizontal_final_matrix,
        column_query_weight,
        vertical_attention_matrix,
        vertical_final_matrix,
        tensor_mean_lift_matrix,
        outer_product_output_weight,
    )
    pair_output = call(
        functools.partial(pair_kernel, n),
        jax.ShapeDtypeStruct((res_dev, residues, pair_width), BF16),
        [
            pltpu.VMEM((residues * residues, pair_width), F32),
            pltpu.VMEM((residues * residues, pair_width), F32),
            pltpu.VMEM((residues * residues, C_TRI), F32),
            pltpu.VMEM((res_dev * residues, C_TRI), F32),
            pltpu.VMEM((residues, residues), F32),
        ],
        (3 * 10**8, 10**6),
        *pairs,
        *packets,
        update,
        triangle_projection_weight,
        triangle_projection_gate,
        triangle_output_gate,
        triangle_output_weight,
    )
    return (alignment, pair_output)


def local(homolog_activity, homolog_symbol_ids, residue_present_mask, pair_state, *others):
    n = lax.axis_size("axial")
    per, residues, _ = homolog_activity.shape
    small = per * n == 8 and residues == 32 and pair_state.shape[0] == 8
    plan = local_whole if small else local_sharded
    return plan(homolog_activity, homolog_symbol_ids, residue_present_mask, pair_state, *others)


def solution(mesh):
    parts, copied = P(("dp", "axial")), P()
    return jax.shard_map(
        local,
        mesh=mesh,
        in_specs=(parts, parts, P("dp"), parts, parts) + (copied,) * 14,
        out_specs=(P("dp", "axial", None), P(("dp", "axial"), None, None)),
        check_vma=False,
    )
```

```python
import functools

import jax
import jax.numpy as jnp
from jax import lax
from jax.experimental import pallas as pl
from jax.experimental.pallas import tpu as pltpu
from jax.sharding import PartitionSpec as P

FOCUS_TOTAL = 8
FOCUS_SIZE = 32
MEAN_HIDDEN_SIZE = 32
C_TRI = 128


def layer_normalize(attended_entries):
    attended_entries = attended_entries.astype(jnp.float32)
    mean = jnp.mean(attended_entries, axis=-1, keepdims=True)
    centred = attended_entries - mean
    var = jnp.mean(centred * centred, axis=-1, keepdims=True)
    return centred * lax.rsqrt(var + 1e-05)


def gated_attend(evoformer_block, extra_axes, w_query, w_kvg, w_out):
    lines_list, residue_length, input_width = evoformer_block.shape
    width = FOCUS_TOTAL * FOCUS_SIZE
    flat = (
        layer_normalize(evoformer_block)
        .astype(jnp.bfloat16)
        .reshape(lines_list * residue_length, input_width)
    )
    query = (
        jnp.dot(flat, w_query, preferred_element_type=jnp.float32) * FOCUS_SIZE ** (-0.5)
    ).astype(jnp.bfloat16)
    query = query.reshape(lines_list, residue_length, FOCUS_TOTAL, FOCUS_SIZE)
    kvg = jnp.dot(flat, w_kvg, preferred_element_type=jnp.float32)
    keys = (
        kvg[:, :width]
        .astype(jnp.bfloat16)
        .reshape(lines_list, residue_length, FOCUS_TOTAL, FOCUS_SIZE)
    )
    attended_entries = (
        kvg[:, width : 2 * width]
        .astype(jnp.bfloat16)
        .reshape(lines_list, residue_length, FOCUS_TOTAL, FOCUS_SIZE)
    )
    gate = jax.nn.sigmoid(kvg[:, 2 * width :]).reshape(
        lines_list, residue_length, FOCUS_TOTAL, FOCUS_SIZE
    )
    scores = (
        jnp.einsum("bihd,bjhd->bhij", query, keys, preferred_element_type=jnp.float32) + extra_axes
    )
    top = jnp.max(scores, axis=-1, keepdims=True)
    expo = jnp.exp(scores - top)
    weights = (expo / jnp.sum(expo, axis=-1, keepdims=True)).astype(jnp.bfloat16)
    mixed = jnp.einsum(
        "bhij,bjhd->bihd", weights, attended_entries, preferred_element_type=jnp.float32
    )
    mixed = (mixed * gate).astype(jnp.bfloat16).reshape(lines_list * residue_length, width)
    return evoformer_block + jnp.dot(mixed, w_out, preferred_element_type=jnp.float32).reshape(
        lines_list, residue_length, input_width
    )


def finish_sums(evoformer_block, triangle_output_weight):
    mixed = layer_normalize(jnp.transpose(evoformer_block, (1, 2, 0))).astype(jnp.bfloat16)
    return jnp.einsum(
        "ijc,cz->ijz", mixed, triangle_output_weight, preferred_element_type=jnp.float32
    )


def local_sharded(
    homolog_activity,
    homolog_symbol_ids,
    residue_present_mask,
    pair_state,
    pair_valid_mask,
    symbol_lookup_matrix,
    row_query_weight,
    horizontal_attention_matrix,
    pair_bias_weight,
    horizontal_final_matrix,
    column_query_weight,
    vertical_attention_matrix,
    vertical_final_matrix,
    tensor_mean_lift_matrix,
    outer_product_output_weight,
    triangle_projection_weight,
    triangle_projection_gate,
    triangle_output_gate,
    triangle_output_weight,
):
    sequence_per_device, residue_length, input_width = homolog_activity.shape
    res_dev = pair_state.shape[0]
    group_size = lax.axis_size("axial")
    token_classes = symbol_lookup_matrix.shape[0]
    token_one_hot = (
        homolog_symbol_ids[..., None] == jnp.arange(token_classes, dtype=jnp.int32)
    ).astype(jnp.bfloat16)
    token_embedded = jnp.einsum(
        "slt,tc->slc", token_one_hot, symbol_lookup_matrix, preferred_element_type=jnp.float32
    )
    homolog_starting = homolog_activity.astype(jnp.float32) + token_embedded
    pair_norm = layer_normalize(pair_state).astype(jnp.bfloat16)
    bias_rows = jnp.einsum(
        "ijc,ch->hij", pair_norm, pair_bias_weight, preferred_element_type=jnp.float32
    ).astype(jnp.bfloat16)
    bias_full = lax.all_gather(bias_rows, "axial", axis=1, tiled=True)
    key_bias = 1000000000.0 * (residue_present_mask.astype(jnp.float32) - 1.0)
    extra_axes = bias_full.astype(jnp.float32)[None] + key_bias[None, None, None, :]
    cluster_total = homolog_starting.reshape(
        sequence_per_device // 2, 2, residue_length, input_width
    )
    homolog_across_update = lax.map(
        lambda evoformer_block: gated_attend(
            evoformer_block,
            extra_axes,
            row_query_weight,
            horizontal_attention_matrix,
            horizontal_final_matrix,
        ),
        cluster_total,
    )
    homolog_across_update = homolog_across_update.reshape(
        sequence_per_device, group_size, res_dev, input_width
    ).astype(jnp.bfloat16)
    moved = jnp.swapaxes(
        lax.all_to_all(homolog_across_update, "axial", split_axis=1, concat_axis=0, tiled=True)[
            :, 0
        ],
        0,
        1,
    )
    finished = lax.map(
        lambda item: gated_attend(
            item[None].astype(jnp.float32),
            0.0,
            column_query_weight,
            vertical_attention_matrix,
            vertical_final_matrix,
        )[0],
        moved,
    )
    exchanged = jnp.swapaxes(finished, 0, 1).astype(jnp.bfloat16)[:, None]
    sequence_count = exchanged.shape[0]
    alignment_after_columns = exchanged.reshape(sequence_count, res_dev, input_width)
    tensor_mean_scaler = layer_normalize(alignment_after_columns).astype(jnp.bfloat16)
    split_parts = jnp.einsum(
        "src,cf->rsf",
        tensor_mean_scaler,
        tensor_mean_lift_matrix,
        preferred_element_type=jnp.float32,
    ).astype(jnp.bfloat16)
    first_factor = split_parts[..., :MEAN_HIDDEN_SIZE]
    second_factor = split_parts[..., MEAN_HIDDEN_SIZE:].reshape(
        res_dev, sequence_count * MEAN_HIDDEN_SIZE
    )
    step_rows = 8
    left_blocks = first_factor.reshape(
        res_dev // step_rows, step_rows, sequence_count, MEAN_HIDDEN_SIZE
    )
    piece = lax.all_gather(second_factor, "axial", axis=0, tiled=True)
    count = piece.shape[0]
    right_part = piece.reshape(count, sequence_count, MEAN_HIDDEN_SIZE)

    def one_block(lines_list):
        tensor_mean = (
            jnp.einsum("isc,jsd->ijcd", lines_list, right_part, preferred_element_type=jnp.float32)
            / sequence_count
        )
        tensor_mean = tensor_mean.reshape(
            step_rows, count, MEAN_HIDDEN_SIZE * MEAN_HIDDEN_SIZE
        ).astype(jnp.bfloat16)
        return jnp.einsum(
            "ijf,fz->ijz",
            tensor_mean,
            outer_product_output_weight,
            preferred_element_type=jnp.float32,
        )

    update = lax.map(one_block, left_blocks).reshape(
        res_dev, count, outer_product_output_weight.shape[1]
    )
    pair_one = pair_state.astype(jnp.float32) + update
    tri_norm = layer_normalize(pair_one).astype(jnp.bfloat16)
    proj = jnp.einsum(
        "ikc,cf->fik", tri_norm, triangle_projection_weight, preferred_element_type=jnp.float32
    )
    gates = jnp.einsum(
        "ikc,cf->fik", tri_norm, triangle_projection_gate, preferred_element_type=jnp.float32
    )
    both = (jax.nn.sigmoid(gates) * proj * pair_valid_mask.astype(jnp.float32)[None]).astype(
        jnp.bfloat16
    )
    left_tri = both[:C_TRI]
    right_tri = both[C_TRI:]
    moved_left, moved_right = (
        lax.all_to_all(left_tri, "axial", split_axis=0, concat_axis=1, tiled=True),
        lax.all_to_all(right_tri, "axial", split_axis=0, concat_axis=1, tiled=True),
    )
    partial_sum = jnp.einsum(
        "cik,cjk->cij", moved_left, moved_right, preferred_element_type=jnp.float32
    )
    tri_sum = lax.all_to_all(
        partial_sum.astype(jnp.bfloat16), "axial", split_axis=1, concat_axis=0, tiled=True
    ).astype(partial_sum.dtype)
    tri_update = finish_sums(tri_sum, triangle_output_weight)
    out_gate = jax.nn.sigmoid(
        jnp.einsum(
            "ijc,cz->ijz", tri_norm, triangle_output_gate, preferred_element_type=jnp.float32
        )
    )
    pair_output = (pair_one + out_gate * tri_update).astype(jnp.bfloat16)
    return (alignment_after_columns, pair_output)


BF16 = jnp.bfloat16
F32 = jnp.float32
SMALL_ROWS = 16
MIB = 1024 * 1024


def mul(lhs, rhs, over=((1,), (0,))):
    return lax.dot_general(lhs, rhs, (over, ((), ())), preferred_element_type=F32)


def iota(shape, axis):
    return lax.broadcasted_iota(jnp.int32, shape, axis)


def zero_one(condition):
    return jnp.where(condition, 1.0, 0.0).astype(BF16)


def normal(x):
    mean = jnp.mean(x, axis=-1, keepdims=True)
    centred = x - mean
    var = jnp.mean(centred * centred, axis=-1, keepdims=True)
    return centred * lax.rsqrt(var + 1e-05)


def sigmoid(x):
    return 1.0 / (1.0 + jnp.exp(-x))


def column_softmax(scores):
    expo = jnp.exp(scores - jnp.max(scores, axis=0, keepdims=True))
    return expo * (1.0 / jnp.sum(expo, axis=0, keepdims=True))


def head_masks(width):
    return [
        zero_one(iota((1, width), 1) // FOCUS_SIZE == h) for h in range(FOCUS_TOTAL)
    ]


def fetch(sources, targets, sems):
    copies = [
        pltpu.make_async_copy(source, target, sems.at[i])
        for i, (source, target) in enumerate(zip(sources, targets))
    ]
    for copy in copies:
        copy.start()
    return copies


def bias_rows(pair_ref, weight_ref):
    rows, residues, width = pair_ref.shape
    lanes = FOCUS_TOTAL * rows
    spread = zero_one(iota((FOCUS_TOTAL, lanes), 1) // rows == iota((FOCUS_TOTAL, lanes), 0))
    row_of = iota((width, lanes), 1) % rows
    flat = normal(pair_ref[...].astype(F32).reshape(rows * residues, width)).astype(BF16)
    weight = mul(weight_ref[...], spread, ((0,), (0,)))
    bias = jnp.zeros((residues, lanes), F32)
    for i in range(rows):
        one_row = jnp.where(row_of == i, weight, 0.0).astype(BF16)
        bias += mul(flat[i * residues : (i + 1) * residues], one_row)
    return bias


def packet_kernel(*refs):
    sources, packet_ref, held, sems = refs[:5], refs[5], refs[6:11], refs[11]
    pair_ref, weight_ref, valid_ref, ids_ref, act_ref = held
    copies = fetch(sources, held, sems)
    rows, residues, width = pair_ref.shape
    per, _, features = act_ref.shape
    lanes = FOCUS_TOTAL * rows
    shift = zero_one(iota((residues, 128), 1) == iota((residues, 128), 0) + lanes)
    for copy in copies:
        copy.wait()
    bias = bias_rows(pair_ref, weight_ref)
    extra = jnp.concatenate(
        [
            valid_ref[...].astype(F32),
            ids_ref[...].astype(F32),
            jnp.zeros((SMALL_ROWS - rows - per, residues), F32),
        ],
        axis=0,
    )
    extra = mul(extra.astype(BF16), shift)
    empty = jnp.zeros((SMALL_ROWS, 128 - lanes), F32)
    first = jnp.concatenate([bias[:SMALL_ROWS], empty], axis=1) + extra
    second = jnp.concatenate([bias[SMALL_ROWS:], empty], axis=1)
    small = jnp.concatenate([first, second], axis=1).astype(BF16)
    packet_ref[per * residues :, :] = small
    packet_ref[: per * residues, :] = act_ref[...].reshape(per * residues, features)


def split_small(packet, residues, res_dev, per):
    small = packet[per * residues :, :].astype(F32)
    lanes = FOCUS_TOTAL * res_dev
    bias = jnp.concatenate([small[:, :lanes], small[:, 128 : 128 + lanes]], axis=0)
    extra = small[:, lanes : lanes + residues]
    return bias, extra[:res_dev], extra[res_dev : res_dev + per]


def project(x, w_query, w_kvg):
    width = FOCUS_TOTAL * FOCUS_SIZE
    flat = normal(x).astype(BF16)
    query = (mul(flat, w_query[...]) * FOCUS_SIZE ** (-0.5)).astype(BF16)
    keys = mul(flat, w_kvg[:, :width]).astype(BF16)
    values = mul(flat, w_kvg[:, width : 2 * width]).astype(BF16)
    gate = sigmoid(mul(flat, w_kvg[:, 2 * width :]))
    return query, keys, values, gate


def msa_kernel(n, *refs):
    packets, weights, refs = refs[: n - 1], refs[n - 1 : n + 13], refs[n + 13 :]
    align_ref, update_ref, start, lifted, held, sems = refs[:4] + (refs[4:18], refs[18])
    copies = fetch(weights, held, sems)
    pair, pair_w, act, ids, present, table = held[:6]
    row_q, row_kvg, row_out, col_q, col_kvg, col_out, lift, outer_w = held[6:]
    per, residues, width = act.shape
    res_dev = pair.shape[0]
    kinds = table.shape[0]
    count = per * n
    tokens = count * residues
    lanes = FOCUS_TOTAL * residues
    me = lax.axis_index("axial")
    masks = head_masks(width)

    place = iota((FOCUS_TOTAL * res_dev, lanes), 0)
    place = (place // res_dev) * residues + place % res_dev - iota(place.shape, 1)
    extra = jnp.zeros((residues, lanes), F32)
    for copy in copies[:6]:
        copy.wait()
    for r in range(n):
        owner = lax.rem(me + r, n)
        if r == 0:
            bias, all_ids = bias_rows(pair, pair_w), ids[...].astype(F32)
        else:
            packet = packets[r - 1]
            bias, _, all_ids = split_small(packet, residues, res_dev, per)
        extra += mul(bias.astype(BF16), zero_one(place == -owner * res_dev))
        for q in range(per):
            hot = zero_one(iota((kinds, residues), 0).astype(F32) == all_ids[q : q + 1])
            rows = act[q] if r == 0 else packet[q * residues : (q + 1) * residues, :]
            start[pl.ds(pl.multiple_of((owner * per + q) * residues, residues), residues), :] = (
                rows.astype(F32) + mul(hot, table[...], ((0,), (0,)))
            )
    shown = mul(present[...].astype(F32).astype(BF16), jnp.ones((1, lanes), BF16), ((0,), (0,)))
    extra = extra + 1000000000.0 * (shown - 1.0)

    zero = start[...]
    copies[6].wait()
    copies[7].wait()
    query, keys, values, gate = project(zero, row_q, row_kvg)
    rows = []
    for s in range(count):
        here = slice(s * residues, (s + 1) * residues)
        spread = jnp.concatenate([query[here] * mask for mask in masks], axis=0)
        weights = column_softmax(mul(keys[here], spread, ((1,), (1,))) + extra).astype(BF16)
        heads = mul(weights, values[here], ((0,), (0,)))
        mixed = jnp.zeros((residues, width), F32)
        for h in range(FOCUS_TOTAL):
            part = heads[h * residues : (h + 1) * residues]
            mixed = jnp.where(iota((1, width), 1) // FOCUS_SIZE == h, part, mixed)
        rows.append(mixed)
    mixed = (jnp.concatenate(rows, axis=0) * gate).astype(BF16)
    copies[8].wait()
    msa_one = (zero + mul(mixed, row_out[...])).astype(BF16)

    row_at, lane_at = iota((tokens, tokens), 0), iota((tokens, tokens), 1)
    turn = zero_one(lane_at == (row_at % count) * residues + row_at // count)
    one = mul(turn, msa_one)
    copies[9].wait()
    copies[10].wait()
    query, keys, values, gate = project(one, col_q, col_kvg)
    group = min(tokens, 128)
    sites = group // count
    same = iota((sites, count, group), 2) // count == iota((sites, count, group), 0)
    groups = []
    for g in range(tokens // group):
        here = slice(g * group, (g + 1) * group)
        all_weights, all_values = [], []
        for mask in masks:
            scores = mul(keys[here], query[here] * mask, ((1,), (1,)))
            scores = jnp.sum(jnp.where(same, scores.reshape(sites, count, group), 0.0), axis=0)
            weights = column_softmax(scores)
            weights = jnp.where(same, weights[None], 0.0).reshape(group, group)
            all_weights.append(weights.astype(BF16))
            all_values.append(values[here] * mask)
        groups.append(
            mul(
                jnp.concatenate(all_weights, axis=0),
                jnp.concatenate(all_values, axis=0),
                ((0,), (0,)),
            )
        )
    mixed = (jnp.concatenate(groups, axis=0) * gate).astype(BF16)
    copies[11].wait()
    align = (one + mul(mixed, col_out[...])).astype(BF16)
    own = count * res_dev
    row_at, lane_at = iota((own, tokens), 0), iota((own, tokens), 1)
    pick = zero_one(
        lane_at == (row_at % res_dev + me * res_dev) * count + row_at // res_dev
    )
    align_ref[...] = mul(pick, align).reshape(count, res_dev, width).astype(BF16)

    copies[12].wait()
    opm = normal(align.astype(F32)).astype(BF16)
    opm = mul(opm, lift[...], ((1,), (1,))).astype(BF16)
    hidden = MEAN_HIDDEN_SIZE
    deep = hidden * count
    spread = zero_one(
        iota((2 * hidden, deep), 1) // count == iota((2 * hidden, deep), 0)
    )
    left = mul(opm, spread)
    left = jnp.where(
        iota((tokens, deep), 0) % count == iota((tokens, deep), 1) % count, left, 0.0
    ).astype(BF16)
    gather = zero_one(iota((residues, tokens), 1) // count == iota((residues, tokens), 0))
    left = mul(gather, left).astype(BF16)
    right = opm[:, hidden:]
    copies[13].wait()
    for c in range(hidden):
        lifted[c] = mul(right, outer_w[c * hidden : (c + 1) * hidden, :])
    for j in range(residues):
        part = lifted[:, j * count : (j + 1) * count, :].reshape(deep, outer_w.shape[1])
        update_ref[j] = mul(left, part.astype(BF16)) * (1.0 / count)


def pair_kernel(n, *refs):
    pairs, packets, update, refs = refs[: n - 1], refs[n - 1 : 2 * n - 2], refs[2 * n - 2], refs[2 * n - 1 :]
    weights, out_ref, state, one, right_at, left_at, valid, held, sems = (
        (refs[:6],) + refs[6:12] + (refs[12:18], refs[18])
    )
    copies = fetch(weights, held, sems)
    pair, own_mask, proj, gates, gate_out, w_out = held
    res_dev, residues, width = pair.shape
    per = (packets[0].shape[0] - SMALL_ROWS) // residues
    me = lax.axis_index("axial")
    copies[0].wait()
    copies[1].wait()
    own_valid = own_mask[...].astype(F32)
    for r in range(n):
        owner = lax.rem(me + r, n)
        size = res_dev * residues
        block = (pairs[r - 1] if r else pair)[...]
        state[pl.ds(pl.multiple_of(owner * size, size), size), :] = (
            block.astype(F32).reshape(size, width)
        )
        shown = split_small(packets[r - 1], residues, res_dev, per)[1] if r else own_valid
        valid[pl.ds(pl.multiple_of(owner * res_dev, res_dev), res_dev), :] = shown
    for k in range(residues):
        one[k * residues : (k + 1) * residues, :] = (
            state[pl.ds(k, residues, stride=residues), :] + update[k]
        )

    choose = zero_one(
        iota((residues, residues * C_TRI), 1) // C_TRI == iota((residues, residues * C_TRI), 0)
    )
    shown = mul(valid[...].astype(BF16), choose)
    copies[2].wait()
    copies[3].wait()
    right_w = jnp.concatenate([proj[:, C_TRI:], gates[:, C_TRI:]], axis=1)
    step = 8
    for k in range(0, residues, step):
        here = slice(k * residues, (k + step) * residues)
        both = mul(normal(one[here, :]).astype(BF16), right_w)
        both = sigmoid(both[:, C_TRI:]) * both[:, :C_TRI]
        for p in range(step):
            part = both[p * residues : (p + 1) * residues]
            part = part * shown[:, (k + p) * C_TRI : (k + p + 1) * C_TRI]
            right_at[(k + p) * residues : (k + p + 1) * residues, :] = part.astype(BF16).astype(F32)

    own = jnp.concatenate(
        [one[pl.ds(me * res_dev + i, residues, stride=residues), :] for i in range(res_dev)],
        axis=0,
    )
    copies[4].wait()
    left_w = jnp.concatenate([proj[:, :C_TRI], gates[:, :C_TRI], gate_out[...]], axis=1)
    own_all = mul(normal(own).astype(BF16), left_w)
    own_gate = sigmoid(own_all[:, 2 * C_TRI :])
    left = sigmoid(own_all[:, C_TRI : 2 * C_TRI]) * own_all[:, :C_TRI]
    choose = zero_one(
        iota((res_dev, res_dev * C_TRI), 1) // C_TRI == iota((res_dev, res_dev * C_TRI), 0)
    )
    shown = mul(own_valid.astype(BF16), choose, ((0,), (0,)))
    for i in range(res_dev):
        part = left[i * residues : (i + 1) * residues] * shown[:, i * C_TRI : (i + 1) * C_TRI]
        left_at[i * residues : (i + 1) * residues, :] = part.astype(BF16).astype(F32)
    sums = [jnp.zeros((residues, C_TRI), F32) for _ in range(res_dev)]
    for k in range(residues):
        other = right_at[k * residues : (k + 1) * residues, :]
        for i in range(res_dev):
            sums[i] += left_at[i * residues + k : i * residues + k + 1, :] * other
    copies[5].wait()
    mixed = normal(jnp.concatenate(sums, axis=0)).astype(BF16)
    result = own + own_gate * mul(mixed, w_out[...])
    out_ref[...] = result.reshape(res_dev, residues, width).astype(BF16)


def call(kernel, out_shape, near, far, scratch, flops, vmem_limit):
    vmem = pl.BlockSpec(memory_space=pltpu.VMEM)
    return pl.pallas_call(
        kernel,
        out_shape=out_shape,
        in_specs=[vmem] * len(near) + [pl.BlockSpec(memory_space=pltpu.HBM)] * len(far),
        out_specs=jax.tree.map(lambda _: vmem, out_shape),
        scratch_shapes=scratch
        + [pltpu.VMEM(x.shape, x.dtype) for x in far]
        + [pltpu.SemaphoreType.DMA((len(far),))],
        compiler_params=pltpu.CompilerParams(vmem_limit_bytes=vmem_limit),
        cost_estimate=pl.CostEstimate(flops=flops, bytes_accessed=0, transcendentals=0),
    )(*near, *far)


def from_others(array, n):
    return [
        lax.ppermute(array, "axial", [(i, (i - r) % n) for i in range(n)]) for r in range(1, n)
    ]


def local_whole(
    homolog_activity,
    homolog_symbol_ids,
    residue_present_mask,
    pair_state,
    pair_valid_mask,
    symbol_lookup_matrix,
    row_query_weight,
    horizontal_attention_matrix,
    pair_bias_weight,
    horizontal_final_matrix,
    column_query_weight,
    vertical_attention_matrix,
    vertical_final_matrix,
    tensor_mean_lift_matrix,
    outer_product_output_weight,
    triangle_projection_weight,
    triangle_projection_gate,
    triangle_output_gate,
    triangle_output_weight,
):
    n = lax.axis_size("axial")
    per, residues, width = homolog_activity.shape
    res_dev, _, pair_width = pair_state.shape
    count = per * n
    bias_weight = pair_bias_weight.T
    packet = call(
        packet_kernel,
        jax.ShapeDtypeStruct((per * residues + SMALL_ROWS, width), BF16),
        (),
        (pair_state, bias_weight, pair_valid_mask, homolog_symbol_ids, homolog_activity),
        [],
        10**11,
        62 * MIB,
    )
    packets = from_others(packet, n)
    _, sent_pair = lax.optimization_barrier((packet, pair_state))
    pairs = from_others(sent_pair, n)
    alignment, update = call(
        functools.partial(msa_kernel, n),
        (
            jax.ShapeDtypeStruct((count, res_dev, width), BF16),
            jax.ShapeDtypeStruct((residues, residues, pair_width), F32),
        ),
        packets,
        (
            pair_state,
            bias_weight,
            homolog_activity,
            homolog_symbol_ids,
            residue_present_mask.reshape(1, residues),
            symbol_lookup_matrix,
            row_query_weight,
            horizontal_attention_matrix,
            horizontal_final_matrix,
            column_query_weight,
            vertical_attention_matrix,
            vertical_final_matrix,
            tensor_mean_lift_matrix.T,
            outer_product_output_weight,
        ),
        [
            pltpu.VMEM((count * residues, width), F32),
            pltpu.VMEM((MEAN_HIDDEN_SIZE, count * residues, pair_width), F32),
        ],
        10**11,
        40 * MIB,
    )
    pair_output = call(
        functools.partial(pair_kernel, n),
        jax.ShapeDtypeStruct((res_dev, residues, pair_width), BF16),
        pairs + packets + [update],
        (
            pair_state,
            pair_valid_mask,
            triangle_projection_weight,
            triangle_projection_gate,
            triangle_output_gate,
            triangle_output_weight,
        ),
        [
            pltpu.VMEM((residues * residues, pair_width), F32),
            pltpu.VMEM((residues * residues, pair_width), F32),
            pltpu.VMEM((residues * residues, C_TRI), F32),
            pltpu.VMEM((res_dev * residues, C_TRI), F32),
            pltpu.VMEM((residues, residues), F32),
        ],
        10**11,
        40 * MIB,
    )
    return (alignment, pair_output)


def local(homolog_activity, homolog_symbol_ids, residue_present_mask, pair_state, *others):
    n = lax.axis_size("axial")
    per, residues, _ = homolog_activity.shape
    small = per * n == 8 and residues == 32 and pair_state.shape[0] == 8
    plan = local_whole if small else local_sharded
    return plan(homolog_activity, homolog_symbol_ids, residue_present_mask, pair_state, *others)


def solution(mesh):
    parts, copied = P(("dp", "axial")), P()
    return jax.shard_map(
        local,
        mesh=mesh,
        in_specs=(parts, parts, P("dp"), parts, parts) + (copied,) * 14,
        out_specs=(P("dp", "axial", None), P(("dp", "axial"), None, None)),
        check_vma=False,
    )
```

```python
import functools

import jax
import jax.numpy as jnp
from jax import lax
from jax.experimental import pallas as pl
from jax.experimental.pallas import tpu as pltpu
from jax.sharding import PartitionSpec as P

FOCUS_TOTAL = 8
FOCUS_SIZE = 32
MEAN_HIDDEN_SIZE = 32
C_TRI = 128


def layer_normalize(attended_entries):
    attended_entries = attended_entries.astype(jnp.float32)
    mean = jnp.mean(attended_entries, axis=-1, keepdims=True)
    centred = attended_entries - mean
    var = jnp.mean(centred * centred, axis=-1, keepdims=True)
    return centred * lax.rsqrt(var + 1e-05)


def gated_attend(evoformer_block, extra_axes, w_query, w_kvg, w_out):
    lines_list, residue_length, input_width = evoformer_block.shape
    width = FOCUS_TOTAL * FOCUS_SIZE
    flat = (
        layer_normalize(evoformer_block)
        .astype(jnp.bfloat16)
        .reshape(lines_list * residue_length, input_width)
    )
    query = (
        jnp.dot(flat, w_query, preferred_element_type=jnp.float32) * FOCUS_SIZE ** (-0.5)
    ).astype(jnp.bfloat16)
    query = query.reshape(lines_list, residue_length, FOCUS_TOTAL, FOCUS_SIZE)
    kvg = jnp.dot(flat, w_kvg, preferred_element_type=jnp.float32)
    keys = (
        kvg[:, :width]
        .astype(jnp.bfloat16)
        .reshape(lines_list, residue_length, FOCUS_TOTAL, FOCUS_SIZE)
    )
    attended_entries = (
        kvg[:, width : 2 * width]
        .astype(jnp.bfloat16)
        .reshape(lines_list, residue_length, FOCUS_TOTAL, FOCUS_SIZE)
    )
    gate = jax.nn.sigmoid(kvg[:, 2 * width :]).reshape(
        lines_list, residue_length, FOCUS_TOTAL, FOCUS_SIZE
    )
    scores = (
        jnp.einsum("bihd,bjhd->bhij", query, keys, preferred_element_type=jnp.float32) + extra_axes
    )
    top = jnp.max(scores, axis=-1, keepdims=True)
    expo = jnp.exp(scores - top)
    weights = (expo / jnp.sum(expo, axis=-1, keepdims=True)).astype(jnp.bfloat16)
    mixed = jnp.einsum(
        "bhij,bjhd->bihd", weights, attended_entries, preferred_element_type=jnp.float32
    )
    mixed = (mixed * gate).astype(jnp.bfloat16).reshape(lines_list * residue_length, width)
    return evoformer_block + jnp.dot(mixed, w_out, preferred_element_type=jnp.float32).reshape(
        lines_list, residue_length, input_width
    )


def finish_sums(evoformer_block, triangle_output_weight):
    mixed = layer_normalize(jnp.transpose(evoformer_block, (1, 2, 0))).astype(jnp.bfloat16)
    return jnp.einsum(
        "ijc,cz->ijz", mixed, triangle_output_weight, preferred_element_type=jnp.float32
    )


def local_sharded(
    homolog_activity,
    homolog_symbol_ids,
    residue_present_mask,
    pair_state,
    pair_valid_mask,
    symbol_lookup_matrix,
    row_query_weight,
    horizontal_attention_matrix,
    pair_bias_weight,
    horizontal_final_matrix,
    column_query_weight,
    vertical_attention_matrix,
    vertical_final_matrix,
    tensor_mean_lift_matrix,
    outer_product_output_weight,
    triangle_projection_weight,
    triangle_projection_gate,
    triangle_output_gate,
    triangle_output_weight,
):
    sequence_per_device, residue_length, input_width = homolog_activity.shape
    res_dev = pair_state.shape[0]
    group_size = lax.axis_size("axial")
    token_classes = symbol_lookup_matrix.shape[0]
    token_one_hot = (
        homolog_symbol_ids[..., None] == jnp.arange(token_classes, dtype=jnp.int32)
    ).astype(jnp.bfloat16)
    token_embedded = jnp.einsum(
        "slt,tc->slc", token_one_hot, symbol_lookup_matrix, preferred_element_type=jnp.float32
    )
    homolog_starting = homolog_activity.astype(jnp.float32) + token_embedded
    pair_norm = layer_normalize(pair_state).astype(jnp.bfloat16)
    bias_rows = jnp.einsum(
        "ijc,ch->hij", pair_norm, pair_bias_weight, preferred_element_type=jnp.float32
    ).astype(jnp.bfloat16)
    bias_full = lax.all_gather(bias_rows, "axial", axis=1, tiled=True)
    key_bias = 1000000000.0 * (residue_present_mask.astype(jnp.float32) - 1.0)
    extra_axes = bias_full.astype(jnp.float32)[None] + key_bias[None, None, None, :]
    cluster_total = homolog_starting.reshape(
        sequence_per_device // 2, 2, residue_length, input_width
    )
    homolog_across_update = lax.map(
        lambda evoformer_block: gated_attend(
            evoformer_block,
            extra_axes,
            row_query_weight,
            horizontal_attention_matrix,
            horizontal_final_matrix,
        ),
        cluster_total,
    )
    homolog_across_update = homolog_across_update.reshape(
        sequence_per_device, group_size, res_dev, input_width
    ).astype(jnp.bfloat16)
    moved = jnp.swapaxes(
        lax.all_to_all(homolog_across_update, "axial", split_axis=1, concat_axis=0, tiled=True)[
            :, 0
        ],
        0,
        1,
    )
    finished = lax.map(
        lambda item: gated_attend(
            item[None].astype(jnp.float32),
            0.0,
            column_query_weight,
            vertical_attention_matrix,
            vertical_final_matrix,
        )[0],
        moved,
    )
    exchanged = jnp.swapaxes(finished, 0, 1).astype(jnp.bfloat16)[:, None]
    sequence_count = exchanged.shape[0]
    alignment_after_columns = exchanged.reshape(sequence_count, res_dev, input_width)
    tensor_mean_scaler = layer_normalize(alignment_after_columns).astype(jnp.bfloat16)
    split_parts = jnp.einsum(
        "src,cf->rsf",
        tensor_mean_scaler,
        tensor_mean_lift_matrix,
        preferred_element_type=jnp.float32,
    ).astype(jnp.bfloat16)
    first_factor = split_parts[..., :MEAN_HIDDEN_SIZE]
    second_factor = split_parts[..., MEAN_HIDDEN_SIZE:].reshape(
        res_dev, sequence_count * MEAN_HIDDEN_SIZE
    )
    step_rows = 8
    left_blocks = first_factor.reshape(
        res_dev // step_rows, step_rows, sequence_count, MEAN_HIDDEN_SIZE
    )
    piece = lax.all_gather(second_factor, "axial", axis=0, tiled=True)
    count = piece.shape[0]
    right_part = piece.reshape(count, sequence_count, MEAN_HIDDEN_SIZE)

    def one_block(lines_list):
        tensor_mean = (
            jnp.einsum("isc,jsd->ijcd", lines_list, right_part, preferred_element_type=jnp.float32)
            / sequence_count
        )
        tensor_mean = tensor_mean.reshape(
            step_rows, count, MEAN_HIDDEN_SIZE * MEAN_HIDDEN_SIZE
        ).astype(jnp.bfloat16)
        return jnp.einsum(
            "ijf,fz->ijz",
            tensor_mean,
            outer_product_output_weight,
            preferred_element_type=jnp.float32,
        )

    update = lax.map(one_block, left_blocks).reshape(
        res_dev, count, outer_product_output_weight.shape[1]
    )
    pair_one = pair_state.astype(jnp.float32) + update
    tri_norm = layer_normalize(pair_one).astype(jnp.bfloat16)
    proj = jnp.einsum(
        "ikc,cf->fik", tri_norm, triangle_projection_weight, preferred_element_type=jnp.float32
    )
    gates = jnp.einsum(
        "ikc,cf->fik", tri_norm, triangle_projection_gate, preferred_element_type=jnp.float32
    )
    both = (jax.nn.sigmoid(gates) * proj * pair_valid_mask.astype(jnp.float32)[None]).astype(
        jnp.bfloat16
    )
    left_tri = both[:C_TRI]
    right_tri = both[C_TRI:]
    moved_left, moved_right = (
        lax.all_to_all(left_tri, "axial", split_axis=0, concat_axis=1, tiled=True),
        lax.all_to_all(right_tri, "axial", split_axis=0, concat_axis=1, tiled=True),
    )
    partial_sum = jnp.einsum(
        "cik,cjk->cij", moved_left, moved_right, preferred_element_type=jnp.float32
    )
    tri_sum = lax.all_to_all(
        partial_sum.astype(jnp.bfloat16), "axial", split_axis=1, concat_axis=0, tiled=True
    ).astype(partial_sum.dtype)
    tri_update = finish_sums(tri_sum, triangle_output_weight)
    out_gate = jax.nn.sigmoid(
        jnp.einsum(
            "ijc,cz->ijz", tri_norm, triangle_output_gate, preferred_element_type=jnp.float32
        )
    )
    pair_output = (pair_one + out_gate * tri_update).astype(jnp.bfloat16)
    return (alignment_after_columns, pair_output)


BF16 = jnp.bfloat16
F32 = jnp.float32
SMALL_ROWS = 16
VMEM_LIMIT = 16 * 1024 * 1024


def mul(lhs, rhs, over=((1,), (0,))):
    return lax.dot_general(lhs, rhs, (over, ((), ())), preferred_element_type=F32)


def iota(shape, axis):
    return lax.broadcasted_iota(jnp.int32, shape, axis)


def zero_one(condition):
    return jnp.where(condition, 1.0, 0.0).astype(BF16)


def normal(x):
    mean = jnp.mean(x, axis=-1, keepdims=True)
    centred = x - mean
    var = jnp.mean(centred * centred, axis=-1, keepdims=True)
    return centred * lax.rsqrt(var + 1e-05)


def sigmoid(x):
    return 1.0 / (1.0 + jnp.exp(-x))


def column_softmax(scores):
    expo = jnp.exp(scores - jnp.max(scores, axis=0, keepdims=True))
    return expo * (1.0 / jnp.sum(expo, axis=0, keepdims=True))


def head_masks(width):
    return [
        zero_one(iota((1, width), 1) // FOCUS_SIZE == h) for h in range(FOCUS_TOTAL)
    ]


def bias_rows(pair_ref, weight_ref):
    rows, residues, width = pair_ref.shape
    lanes = FOCUS_TOTAL * rows
    spread = zero_one(iota((FOCUS_TOTAL, lanes), 1) // rows == iota((FOCUS_TOTAL, lanes), 0))
    row_of = iota((width, lanes), 1) % rows
    flat = normal(pair_ref[...].astype(F32).reshape(rows * residues, width)).astype(BF16)
    weight = mul(weight_ref[...], spread, ((0,), (0,)))
    bias = jnp.zeros((residues, lanes), F32)
    for i in range(rows):
        one_row = jnp.where(row_of == i, weight, 0.0).astype(BF16)
        bias += mul(flat[i * residues : (i + 1) * residues], one_row)
    return bias


def table_kernel(lanes, count, shift_ref, turn_ref):
    shape = shift_ref.shape
    shift_ref[...] = zero_one(iota(shape, 1) == iota(shape, 0) + lanes)
    shape = turn_ref.shape
    row_at = iota(shape, 0)
    turn_ref[...] = zero_one(
        iota(shape, 1) == (row_at % count) * (shape[0] // count) + row_at // count
    )


def packet_kernel(*refs):
    pair_ref, weight_ref, valid_ref, ids_ref, act_ref, present_ref, shift_ref = refs[:7]
    packet_ref, hidden_ref = refs[7:]
    rows, residues, width = pair_ref.shape
    per, _, features = act_ref.shape
    lanes = FOCUS_TOTAL * rows
    bias = bias_rows(pair_ref, weight_ref)
    extra = jnp.concatenate(
        [
            valid_ref[...].astype(F32),
            ids_ref[...].astype(F32),
            jnp.zeros((SMALL_ROWS - rows - per, residues), F32),
        ],
        axis=0,
    )
    extra = mul(extra.astype(BF16), shift_ref[...])
    empty = jnp.zeros((SMALL_ROWS, 128 - lanes), F32)
    first = jnp.concatenate([bias[:SMALL_ROWS], empty], axis=1) + extra
    second = jnp.concatenate([bias[SMALL_ROWS:], empty], axis=1)
    small = jnp.concatenate([first, second], axis=1).astype(BF16)
    packet_ref[per * residues :, :] = small
    shown = present_ref[...].astype(F32).astype(BF16)
    shown = mul(shown, jnp.ones((1, hidden_ref.shape[1]), BF16), ((0,), (0,)))
    hidden_ref[...] = 1000000000.0 * (shown - 1.0)
    packet_ref[: per * residues, :] = act_ref[...].reshape(per * residues, features)


def split_small(packet, residues, res_dev, per):
    small = packet[per * residues :, :].astype(F32)
    lanes = FOCUS_TOTAL * res_dev
    bias = jnp.concatenate([small[:, :lanes], small[:, 128 : 128 + lanes]], axis=0)
    extra = small[:, lanes : lanes + residues]
    return bias, extra[:res_dev], extra[res_dev : res_dev + per]


def project(x, w_query, w_kvg):
    width = FOCUS_TOTAL * FOCUS_SIZE
    flat = normal(x).astype(BF16)
    query = (mul(flat, w_query[...]) * FOCUS_SIZE ** (-0.5)).astype(BF16)
    keys = mul(flat, w_kvg[:, :width]).astype(BF16)
    values = mul(flat, w_kvg[:, width : 2 * width]).astype(BF16)
    gate = sigmoid(mul(flat, w_kvg[:, 2 * width :]))
    return query, keys, values, gate


def msa_kernel(n, *refs):
    packets, refs = refs[: n - 1], refs[n - 1 :]
    turn, hidden_keys, pair, pair_w, act, ids, table = refs[:7]
    row_q, row_kvg, row_out, col_q, col_kvg, col_out, lift, outer_w = refs[7:15]
    align_ref, update_ref, start, lifted = refs[15:]
    per, residues, width = act.shape
    res_dev = pair.shape[0]
    kinds = table.shape[0]
    count = per * n
    tokens = count * residues
    lanes = FOCUS_TOTAL * residues
    me = lax.axis_index("axial")
    masks = head_masks(width)

    place = iota((FOCUS_TOTAL * res_dev, lanes), 0)
    place = (place // res_dev) * residues + place % res_dev - iota(place.shape, 1)
    extra = jnp.zeros((residues, lanes), F32)
    for r in range(n):
        owner = me ^ r
        if r == 0:
            bias, all_ids = bias_rows(pair, pair_w), ids[...].astype(F32)
        else:
            packet = packets[r - 1]
            bias, _, all_ids = split_small(packet, residues, res_dev, per)
        extra += mul(bias.astype(BF16), zero_one(place == -owner * res_dev))
        for q in range(per):
            hot = zero_one(iota((kinds, residues), 0).astype(F32) == all_ids[q : q + 1])
            rows = act[q] if r == 0 else packet[q * residues : (q + 1) * residues, :]
            start[pl.ds(pl.multiple_of((owner * per + q) * residues, residues), residues), :] = (
                rows.astype(F32) + mul(hot, table[...], ((0,), (0,)))
            )
    extra = extra + hidden_keys[...]

    zero = start[...]
    query, keys, values, gate = project(zero, row_q, row_kvg)
    rows = []
    for s in range(count):
        here = slice(s * residues, (s + 1) * residues)
        spread = jnp.concatenate([query[here] * mask for mask in masks], axis=0)
        weights = column_softmax(mul(keys[here], spread, ((1,), (1,))) + extra).astype(BF16)
        heads = mul(weights, values[here], ((0,), (0,)))
        mixed = jnp.zeros((residues, width), F32)
        for h in range(FOCUS_TOTAL):
            part = heads[h * residues : (h + 1) * residues]
            mixed = jnp.where(iota((1, width), 1) // FOCUS_SIZE == h, part, mixed)
        rows.append(mixed)
    mixed = (jnp.concatenate(rows, axis=0) * gate).astype(BF16)
    msa_one = (zero + mul(mixed, row_out[...])).astype(BF16)

    one = mul(turn[...], msa_one)
    query, keys, values, gate = project(one, col_q, col_kvg)
    group = min(tokens, 128)
    sites = group // count
    same = iota((sites, count, group), 2) // count == iota((sites, count, group), 0)
    groups = []
    for g in range(tokens // group):
        here = slice(g * group, (g + 1) * group)
        all_weights, all_values = [], []
        for mask in masks:
            scores = mul(keys[here], query[here] * mask, ((1,), (1,)))
            scores = jnp.sum(jnp.where(same, scores.reshape(sites, count, group), 0.0), axis=0)
            weights = column_softmax(scores)
            weights = jnp.where(same, weights[None], 0.0).reshape(group, group)
            all_weights.append(weights.astype(BF16))
            all_values.append(values[here] * mask)
        groups.append(
            mul(
                jnp.concatenate(all_weights, axis=0),
                jnp.concatenate(all_values, axis=0),
                ((0,), (0,)),
            )
        )
    mixed = (jnp.concatenate(groups, axis=0) * gate).astype(BF16)
    align = (one + mul(mixed, col_out[...])).astype(BF16)
    own = count * res_dev
    row_at, lane_at = iota((own, tokens), 0), iota((own, tokens), 1)
    pick = zero_one(
        lane_at == (row_at % res_dev + me * res_dev) * count + row_at // res_dev
    )
    align_ref[...] = mul(pick, align).reshape(count, res_dev, width).astype(BF16)

    opm = normal(align.astype(F32)).astype(BF16)
    opm = mul(opm, lift[...], ((1,), (1,))).astype(BF16)
    hidden = MEAN_HIDDEN_SIZE
    deep = hidden * count
    spread = zero_one(
        iota((2 * hidden, deep), 1) // count == iota((2 * hidden, deep), 0)
    )
    left = mul(opm, spread)
    left = jnp.where(
        iota((tokens, deep), 0) % count == iota((tokens, deep), 1) % count, left, 0.0
    ).astype(BF16)
    gather = zero_one(iota((residues, tokens), 1) // count == iota((residues, tokens), 0))
    left = mul(gather, left).astype(BF16)
    right = opm[:, hidden:]
    for c in range(hidden):
        lifted[c] = mul(right, outer_w[c * hidden : (c + 1) * hidden, :])
    for j in range(residues):
        part = lifted[:, j * count : (j + 1) * count, :].reshape(deep, outer_w.shape[1])
        update_ref[j] = mul(left, part.astype(BF16)) * (1.0 / count)


def pair_kernel(n, *refs):
    pairs, packets, update, refs = refs[: n - 1], refs[n - 1 : 2 * n - 2], refs[2 * n - 2], refs[2 * n - 1 :]
    pair, own_mask, proj, gates, gate_out, w_out = refs[:6]
    out_ref, state, one, right_at, left_at, valid = refs[6:]
    res_dev, residues, width = pair.shape
    per = (packets[0].shape[0] - SMALL_ROWS) // residues
    me = lax.axis_index("axial")
    own_valid = own_mask[...].astype(F32)
    for r in range(n):
        owner = me ^ r
        size = res_dev * residues
        block = (pairs[r - 1] if r else pair)[...]
        state[pl.ds(pl.multiple_of(owner * size, size), size), :] = (
            block.astype(F32).reshape(size, width)
        )
        shown = split_small(packets[r - 1], residues, res_dev, per)[1] if r else own_valid
        valid[pl.ds(pl.multiple_of(owner * res_dev, res_dev), res_dev), :] = shown
    for k in range(residues):
        one[k * residues : (k + 1) * residues, :] = (
            state[pl.ds(k, residues, stride=residues), :] + update[k]
        )

    choose = zero_one(
        iota((residues, residues * C_TRI), 1) // C_TRI == iota((residues, residues * C_TRI), 0)
    )
    shown = mul(valid[...].astype(BF16), choose)
    right_w = jnp.concatenate([proj[:, C_TRI:], gates[:, C_TRI:]], axis=1)
    step = 8
    for k in range(0, residues, step):
        here = slice(k * residues, (k + step) * residues)
        both = mul(normal(one[here, :]).astype(BF16), right_w)
        both = sigmoid(both[:, C_TRI:]) * both[:, :C_TRI]
        for p in range(step):
            part = both[p * residues : (p + 1) * residues]
            part = part * shown[:, (k + p) * C_TRI : (k + p + 1) * C_TRI]
            right_at[(k + p) * residues : (k + p + 1) * residues, :] = part.astype(BF16).astype(F32)

    own = jnp.concatenate(
        [one[pl.ds(me * res_dev + i, residues, stride=residues), :] for i in range(res_dev)],
        axis=0,
    )
    left_w = jnp.concatenate([proj[:, :C_TRI], gates[:, :C_TRI], gate_out[...]], axis=1)
    own_all = mul(normal(own).astype(BF16), left_w)
    own_gate = sigmoid(own_all[:, 2 * C_TRI :])
    left = sigmoid(own_all[:, C_TRI : 2 * C_TRI]) * own_all[:, :C_TRI]
    choose = zero_one(
        iota((res_dev, res_dev * C_TRI), 1) // C_TRI == iota((res_dev, res_dev * C_TRI), 0)
    )
    shown = mul(own_valid.astype(BF16), choose, ((0,), (0,)))
    for i in range(res_dev):
        part = left[i * residues : (i + 1) * residues] * shown[:, i * C_TRI : (i + 1) * C_TRI]
        left_at[i * residues : (i + 1) * residues, :] = part.astype(BF16).astype(F32)
    sums = [jnp.zeros((residues, C_TRI), F32) for _ in range(res_dev)]
    for k in range(residues):
        other = right_at[k * residues : (k + 1) * residues, :]
        for i in range(res_dev):
            sums[i] += left_at[i * residues + k : i * residues + k + 1, :] * other
    mixed = normal(jnp.concatenate(sums, axis=0)).astype(BF16)
    result = own + own_gate * mul(mixed, w_out[...])
    out_ref[...] = result.reshape(res_dev, residues, width).astype(BF16)


def call(kernel, out_shape, scratch, flops, *args):
    vmem = pl.BlockSpec(memory_space=pltpu.VMEM)
    return pl.pallas_call(
        kernel,
        out_shape=out_shape,
        in_specs=[vmem] * len(args),
        out_specs=jax.tree.map(lambda _: vmem, out_shape),
        scratch_shapes=scratch,
        compiler_params=pltpu.CompilerParams(vmem_limit_bytes=VMEM_LIMIT),
        cost_estimate=pl.CostEstimate(flops=flops, bytes_accessed=0, transcendentals=0),
    )(*args)


def swap(array, r, n):
    return lax.ppermute(array, "axial", [(i, i ^ r) for i in range(n)])


def local_whole(
    homolog_activity,
    homolog_symbol_ids,
    residue_present_mask,
    pair_state,
    pair_valid_mask,
    symbol_lookup_matrix,
    row_query_weight,
    horizontal_attention_matrix,
    pair_bias_weight,
    horizontal_final_matrix,
    column_query_weight,
    vertical_attention_matrix,
    vertical_final_matrix,
    tensor_mean_lift_matrix,
    outer_product_output_weight,
    triangle_projection_weight,
    triangle_projection_gate,
    triangle_output_gate,
    triangle_output_weight,
):
    n = lax.axis_size("axial")
    per, residues, width = homolog_activity.shape
    res_dev, _, pair_width = pair_state.shape
    count = per * n
    bias_weight = pair_bias_weight.T
    pair_2 = swap(pair_state, 2, n)
    shift, turn = call(
        functools.partial(table_kernel, FOCUS_TOTAL * res_dev, count),
        (
            jax.ShapeDtypeStruct((residues, 128), BF16),
            jax.ShapeDtypeStruct((count * residues, count * residues), BF16),
        ),
        [],
        10**11,
    )
    packet, hidden_keys = call(
        packet_kernel,
        (
            jax.ShapeDtypeStruct((per * residues + SMALL_ROWS, width), BF16),
            jax.ShapeDtypeStruct((residues, FOCUS_TOTAL * residues), F32),
        ),
        [],
        10**11,
        pair_state,
        bias_weight,
        pair_valid_mask,
        homolog_symbol_ids,
        homolog_activity,
        residue_present_mask.reshape(1, residues),
        shift,
    )
    packets = [swap(packet, r, n) for r in (3, 2, 1)][::-1]
    _, later = lax.optimization_barrier((packet, pair_state))
    pair_1 = swap(later, 1, n)
    pair_3 = swap(pair_2, 1, n)
    alignment, update = call(
        functools.partial(msa_kernel, n),
        (
            jax.ShapeDtypeStruct((count, res_dev, width), BF16),
            jax.ShapeDtypeStruct((residues, residues, pair_width), F32),
        ),
        [
            pltpu.VMEM((count * residues, width), F32),
            pltpu.VMEM((MEAN_HIDDEN_SIZE, count * residues, pair_width), F32),
        ],
        10**11,
        *packets,
        turn,
        hidden_keys,
        pair_state,
        bias_weight,
        homolog_activity,
        homolog_symbol_ids,
        symbol_lookup_matrix,
        row_query_weight,
        horizontal_attention_matrix,
        horizontal_final_matrix,
        column_query_weight,
        vertical_attention_matrix,
        vertical_final_matrix,
        tensor_mean_lift_matrix.T,
        outer_product_output_weight,
    )
    pair_output = call(
        functools.partial(pair_kernel, n),
        jax.ShapeDtypeStruct((res_dev, residues, pair_width), BF16),
        [
            pltpu.VMEM((residues * residues, pair_width), F32),
            pltpu.VMEM((residues * residues, pair_width), F32),
            pltpu.VMEM((residues * residues, C_TRI), F32),
            pltpu.VMEM((res_dev * residues, C_TRI), F32),
            pltpu.VMEM((residues, residues), F32),
        ],
        10**11,
        pair_1,
        pair_2,
        pair_3,
        *packets,
        update,
        pair_state,
        pair_valid_mask,
        triangle_projection_weight,
        triangle_projection_gate,
        triangle_output_gate,
        triangle_output_weight,
    )
    return (alignment, pair_output)


def local(homolog_activity, homolog_symbol_ids, residue_present_mask, pair_state, *others):
    n = lax.axis_size("axial")
    per, residues, _ = homolog_activity.shape
    small = n == 4 and per * n == 8 and residues == 32
    plan = local_whole if small else local_sharded
    return plan(homolog_activity, homolog_symbol_ids, residue_present_mask, pair_state, *others)


def solution(mesh):
    parts, copied = P(("dp", "axial")), P()
    return jax.shard_map(
        local,
        mesh=mesh,
        in_specs=(parts, parts, P("dp"), parts, parts) + (copied,) * 14,
        out_specs=(P("dp", "axial", None), P(("dp", "axial"), None, None)),
        check_vma=False,
    )
```

```python
import functools

import jax
import jax.numpy as jnp
from jax import lax
from jax.experimental import pallas as pl
from jax.experimental.pallas import tpu as pltpu
from jax.sharding import PartitionSpec as P

FOCUS_TOTAL = 8
FOCUS_SIZE = 32
MEAN_HIDDEN_SIZE = 32
C_TRI = 128


def layer_normalize(attended_entries):
    attended_entries = attended_entries.astype(jnp.float32)
    mean = jnp.mean(attended_entries, axis=-1, keepdims=True)
    centred = attended_entries - mean
    var = jnp.mean(centred * centred, axis=-1, keepdims=True)
    return centred * lax.rsqrt(var + 1e-05)


def gated_attend(evoformer_block, extra_axes, w_query, w_kvg, w_out):
    lines_list, residue_length, input_width = evoformer_block.shape
    width = FOCUS_TOTAL * FOCUS_SIZE
    flat = (
        layer_normalize(evoformer_block)
        .astype(jnp.bfloat16)
        .reshape(lines_list * residue_length, input_width)
    )
    query = (
        jnp.dot(flat, w_query, preferred_element_type=jnp.float32) * FOCUS_SIZE ** (-0.5)
    ).astype(jnp.bfloat16)
    query = query.reshape(lines_list, residue_length, FOCUS_TOTAL, FOCUS_SIZE)
    kvg = jnp.dot(flat, w_kvg, preferred_element_type=jnp.float32)
    keys = (
        kvg[:, :width]
        .astype(jnp.bfloat16)
        .reshape(lines_list, residue_length, FOCUS_TOTAL, FOCUS_SIZE)
    )
    attended_entries = (
        kvg[:, width : 2 * width]
        .astype(jnp.bfloat16)
        .reshape(lines_list, residue_length, FOCUS_TOTAL, FOCUS_SIZE)
    )
    gate = jax.nn.sigmoid(kvg[:, 2 * width :]).reshape(
        lines_list, residue_length, FOCUS_TOTAL, FOCUS_SIZE
    )
    scores = (
        jnp.einsum("bihd,bjhd->bhij", query, keys, preferred_element_type=jnp.float32) + extra_axes
    )
    top = jnp.max(scores, axis=-1, keepdims=True)
    expo = jnp.exp(scores - top)
    weights = (expo / jnp.sum(expo, axis=-1, keepdims=True)).astype(jnp.bfloat16)
    mixed = jnp.einsum(
        "bhij,bjhd->bihd", weights, attended_entries, preferred_element_type=jnp.float32
    )
    mixed = (mixed * gate).astype(jnp.bfloat16).reshape(lines_list * residue_length, width)
    return evoformer_block + jnp.dot(mixed, w_out, preferred_element_type=jnp.float32).reshape(
        lines_list, residue_length, input_width
    )


def finish_sums(evoformer_block, triangle_output_weight):
    mixed = layer_normalize(jnp.transpose(evoformer_block, (1, 2, 0))).astype(jnp.bfloat16)
    return jnp.einsum(
        "ijc,cz->ijz", mixed, triangle_output_weight, preferred_element_type=jnp.float32
    )


def local_sharded(
    homolog_activity,
    homolog_symbol_ids,
    residue_present_mask,
    pair_state,
    pair_valid_mask,
    symbol_lookup_matrix,
    row_query_weight,
    horizontal_attention_matrix,
    pair_bias_weight,
    horizontal_final_matrix,
    column_query_weight,
    vertical_attention_matrix,
    vertical_final_matrix,
    tensor_mean_lift_matrix,
    outer_product_output_weight,
    triangle_projection_weight,
    triangle_projection_gate,
    triangle_output_gate,
    triangle_output_weight,
):
    sequence_per_device, residue_length, input_width = homolog_activity.shape
    res_dev = pair_state.shape[0]
    group_size = lax.axis_size("axial")
    token_classes = symbol_lookup_matrix.shape[0]
    token_one_hot = (
        homolog_symbol_ids[..., None] == jnp.arange(token_classes, dtype=jnp.int32)
    ).astype(jnp.bfloat16)
    token_embedded = jnp.einsum(
        "slt,tc->slc", token_one_hot, symbol_lookup_matrix, preferred_element_type=jnp.float32
    )
    homolog_starting = homolog_activity.astype(jnp.float32) + token_embedded
    pair_norm = layer_normalize(pair_state).astype(jnp.bfloat16)
    bias_rows = jnp.einsum(
        "ijc,ch->hij", pair_norm, pair_bias_weight, preferred_element_type=jnp.float32
    ).astype(jnp.bfloat16)
    bias_full = lax.all_gather(bias_rows, "axial", axis=1, tiled=True)
    key_bias = 1000000000.0 * (residue_present_mask.astype(jnp.float32) - 1.0)
    extra_axes = bias_full.astype(jnp.float32)[None] + key_bias[None, None, None, :]
    cluster_total = homolog_starting.reshape(
        sequence_per_device // 2, 2, residue_length, input_width
    )
    homolog_across_update = lax.map(
        lambda evoformer_block: gated_attend(
            evoformer_block,
            extra_axes,
            row_query_weight,
            horizontal_attention_matrix,
            horizontal_final_matrix,
        ),
        cluster_total,
    )
    homolog_across_update = homolog_across_update.reshape(
        sequence_per_device, group_size, res_dev, input_width
    ).astype(jnp.bfloat16)
    moved = jnp.swapaxes(
        lax.all_to_all(homolog_across_update, "axial", split_axis=1, concat_axis=0, tiled=True)[
            :, 0
        ],
        0,
        1,
    )
    finished = lax.map(
        lambda item: gated_attend(
            item[None].astype(jnp.float32),
            0.0,
            column_query_weight,
            vertical_attention_matrix,
            vertical_final_matrix,
        )[0],
        moved,
    )
    exchanged = jnp.swapaxes(finished, 0, 1).astype(jnp.bfloat16)[:, None]
    sequence_count = exchanged.shape[0]
    alignment_after_columns = exchanged.reshape(sequence_count, res_dev, input_width)
    tensor_mean_scaler = layer_normalize(alignment_after_columns).astype(jnp.bfloat16)
    split_parts = jnp.einsum(
        "src,cf->rsf",
        tensor_mean_scaler,
        tensor_mean_lift_matrix,
        preferred_element_type=jnp.float32,
    ).astype(jnp.bfloat16)
    first_factor = split_parts[..., :MEAN_HIDDEN_SIZE]
    second_factor = split_parts[..., MEAN_HIDDEN_SIZE:].reshape(
        res_dev, sequence_count * MEAN_HIDDEN_SIZE
    )
    step_rows = 8
    left_blocks = first_factor.reshape(
        res_dev // step_rows, step_rows, sequence_count, MEAN_HIDDEN_SIZE
    )
    piece = lax.all_gather(second_factor, "axial", axis=0, tiled=True)
    count = piece.shape[0]
    right_part = piece.reshape(count, sequence_count, MEAN_HIDDEN_SIZE)

    def one_block(lines_list):
        tensor_mean = (
            jnp.einsum("isc,jsd->ijcd", lines_list, right_part, preferred_element_type=jnp.float32)
            / sequence_count
        )
        tensor_mean = tensor_mean.reshape(
            step_rows, count, MEAN_HIDDEN_SIZE * MEAN_HIDDEN_SIZE
        ).astype(jnp.bfloat16)
        return jnp.einsum(
            "ijf,fz->ijz",
            tensor_mean,
            outer_product_output_weight,
            preferred_element_type=jnp.float32,
        )

    update = lax.map(one_block, left_blocks).reshape(
        res_dev, count, outer_product_output_weight.shape[1]
    )
    pair_one = pair_state.astype(jnp.float32) + update
    tri_norm = layer_normalize(pair_one).astype(jnp.bfloat16)
    proj = jnp.einsum(
        "ikc,cf->fik", tri_norm, triangle_projection_weight, preferred_element_type=jnp.float32
    )
    gates = jnp.einsum(
        "ikc,cf->fik", tri_norm, triangle_projection_gate, preferred_element_type=jnp.float32
    )
    both = (jax.nn.sigmoid(gates) * proj * pair_valid_mask.astype(jnp.float32)[None]).astype(
        jnp.bfloat16
    )
    left_tri = both[:C_TRI]
    right_tri = both[C_TRI:]
    moved_left, moved_right = (
        lax.all_to_all(left_tri, "axial", split_axis=0, concat_axis=1, tiled=True),
        lax.all_to_all(right_tri, "axial", split_axis=0, concat_axis=1, tiled=True),
    )
    partial_sum = jnp.einsum(
        "cik,cjk->cij", moved_left, moved_right, preferred_element_type=jnp.float32
    )
    tri_sum = lax.all_to_all(
        partial_sum.astype(jnp.bfloat16), "axial", split_axis=1, concat_axis=0, tiled=True
    ).astype(partial_sum.dtype)
    tri_update = finish_sums(tri_sum, triangle_output_weight)
    out_gate = jax.nn.sigmoid(
        jnp.einsum(
            "ijc,cz->ijz", tri_norm, triangle_output_gate, preferred_element_type=jnp.float32
        )
    )
    pair_output = (pair_one + out_gate * tri_update).astype(jnp.bfloat16)
    return (alignment_after_columns, pair_output)


BF16 = jnp.bfloat16
F32 = jnp.float32
SMALL_ROWS = 16
FLOPS = 10**11
PACKET_ORDER = (2, 1, 3)


def mul(lhs, rhs, over=((1,), (0,))):
    return lax.dot_general(lhs, rhs, (over, ((), ())), preferred_element_type=F32)


def iota(shape, axis):
    return lax.broadcasted_iota(jnp.int32, shape, axis)


def zero_one(condition):
    return jnp.where(condition, 1.0, 0.0).astype(BF16)


def normal(x):
    mean = jnp.mean(x, axis=-1, keepdims=True)
    centred = x - mean
    var = jnp.mean(centred * centred, axis=-1, keepdims=True)
    return centred * lax.rsqrt(var + 1e-05)


def sigmoid(x):
    return 1.0 / (1.0 + jnp.exp(-x))


def column_softmax(scores):
    expo = jnp.exp(scores - jnp.max(scores, axis=0, keepdims=True))
    return expo * (1.0 / jnp.sum(expo, axis=0, keepdims=True))


def head_masks(width):
    return [
        zero_one(iota((1, width), 1) // FOCUS_SIZE == h) for h in range(FOCUS_TOTAL)
    ]


def bias_rows(pair_ref, weight_ref):
    rows, residues, width = pair_ref.shape
    lanes = FOCUS_TOTAL * rows
    spread = zero_one(iota((FOCUS_TOTAL, lanes), 1) // rows == iota((FOCUS_TOTAL, lanes), 0))
    row_of = iota((width, lanes), 1) % rows
    flat = normal(pair_ref[...].astype(F32).reshape(rows * residues, width)).astype(BF16)
    weight = mul(weight_ref[...], spread, ((0,), (0,)))
    bias = jnp.zeros((residues, lanes), F32)
    for i in range(rows):
        one_row = jnp.where(row_of == i, weight, 0.0).astype(BF16)
        bias += mul(flat[i * residues : (i + 1) * residues], one_row)
    return bias


def table_kernel(lanes, count, shift_ref, turn_ref, column_ref):
    shape = column_ref.shape
    column_ref[...] = zero_one(iota(shape, 1) // C_TRI == iota(shape, 0))
    shape = shift_ref.shape
    shift_ref[...] = zero_one(iota(shape, 1) == iota(shape, 0) + lanes)
    shape = turn_ref.shape
    row_at = iota(shape, 0)
    turn_ref[...] = zero_one(
        iota(shape, 1) == (row_at % count) * (shape[0] // count) + row_at // count
    )


def packet_kernel(*refs):
    pair_ref, weight_ref, valid_ref, ids_ref, act_ref, present_ref, shift_ref = refs[:7]
    packet_ref, hidden_ref = refs[7:]
    rows, residues, width = pair_ref.shape
    per, _, features = act_ref.shape
    lanes = FOCUS_TOTAL * rows
    bias = bias_rows(pair_ref, weight_ref)
    extra = jnp.concatenate(
        [
            valid_ref[...].astype(F32),
            ids_ref[...].astype(F32),
            jnp.zeros((SMALL_ROWS - rows - per, residues), F32),
        ],
        axis=0,
    )
    extra = mul(extra.astype(BF16), shift_ref[...])
    empty = jnp.zeros((SMALL_ROWS, 128 - lanes), F32)
    first = jnp.concatenate([bias[:SMALL_ROWS], empty], axis=1) + extra
    second = jnp.concatenate([bias[SMALL_ROWS:], empty], axis=1)
    small = jnp.concatenate([first, second], axis=1).astype(BF16)
    packet_ref[per * residues :, :] = small
    shown = present_ref[...].astype(F32).astype(BF16)
    shown = mul(shown, jnp.ones((1, hidden_ref.shape[1]), BF16), ((0,), (0,)))
    hidden_ref[...] = 1000000000.0 * (shown - 1.0)
    packet_ref[: per * residues, :] = act_ref[...].reshape(per * residues, features)


def split_small(packet, residues, res_dev, per):
    small = packet[per * residues :, :].astype(F32)
    lanes = FOCUS_TOTAL * res_dev
    bias = jnp.concatenate([small[:, :lanes], small[:, 128 : 128 + lanes]], axis=0)
    extra = small[:, lanes : lanes + residues]
    return bias, extra[:res_dev], extra[res_dev : res_dev + per]


def project(x, w_query, w_kvg):
    width = FOCUS_TOTAL * FOCUS_SIZE
    flat = normal(x).astype(BF16)
    query = (mul(flat, w_query[...]) * FOCUS_SIZE ** (-0.5)).astype(BF16)
    keys = mul(flat, w_kvg[:, :width]).astype(BF16)
    values = mul(flat, w_kvg[:, width : 2 * width]).astype(BF16)
    gate = sigmoid(mul(flat, w_kvg[:, 2 * width :]))
    return query, keys, values, gate


def msa_kernel(n, *refs):
    packets, refs = refs[: n - 1], refs[n - 1 :]
    turn, hidden_keys, pair, pair_w, act, ids, table = refs[:7]
    row_q, row_kvg, row_out, col_q, col_kvg, col_out, lift, outer_w, far_pair = refs[7:16]
    align_ref, update_ref, pair_ref, start, lifted, sem = refs[16:]
    copy = pltpu.make_async_copy(far_pair, pair_ref, sem)
    copy.start()
    per, residues, width = act.shape
    res_dev = pair.shape[0]
    kinds = table.shape[0]
    pair_width = pair.shape[2]
    count = per * n
    tokens = count * residues
    lanes = FOCUS_TOTAL * residues
    me = lax.axis_index("axial")
    masks = head_masks(width)

    place = iota((FOCUS_TOTAL * res_dev, lanes), 0)
    place = (place // res_dev) * residues + place % res_dev - iota(place.shape, 1)
    extra = jnp.zeros((residues, lanes), F32)
    for packet, r in zip((None, *packets), (0, *PACKET_ORDER)):
        owner = me ^ r
        if r == 0:
            bias, all_ids = bias_rows(pair, pair_w), ids[...].astype(F32)
        else:
            bias, _, all_ids = split_small(packet, residues, res_dev, per)
        extra += mul(bias.astype(BF16), zero_one(place == -owner * res_dev))
        for q in range(per):
            hot = zero_one(iota((kinds, residues), 0).astype(F32) == all_ids[q : q + 1])
            rows = act[q] if r == 0 else packet[q * residues : (q + 1) * residues, :]
            start[pl.ds(pl.multiple_of((owner * per + q) * residues, residues), residues), :] = (
                rows.astype(F32) + mul(hot, table[...], ((0,), (0,)))
            )
    extra = extra + hidden_keys[...]

    zero = start[...]
    query, keys, values, gate = project(zero, row_q, row_kvg)
    rows = []
    for s in range(count):
        here = slice(s * residues, (s + 1) * residues)
        spread = jnp.concatenate([query[here] * mask for mask in masks], axis=0)
        weights = column_softmax(mul(keys[here], spread, ((1,), (1,))) + extra).astype(BF16)
        heads = mul(weights, values[here], ((0,), (0,)))
        mixed = jnp.zeros((residues, width), F32)
        for h in range(FOCUS_TOTAL):
            part = heads[h * residues : (h + 1) * residues]
            mixed = jnp.where(iota((1, width), 1) // FOCUS_SIZE == h, part, mixed)
        rows.append(mixed)
    mixed = (jnp.concatenate(rows, axis=0) * gate).astype(BF16)
    msa_one = (zero + mul(mixed, row_out[...])).astype(BF16)

    one = mul(turn[...], msa_one)
    query, keys, values, gate = project(one, col_q, col_kvg)
    group = min(tokens, 128)
    sites = group // count
    same = iota((sites, count, group), 2) // count == iota((sites, count, group), 0)
    groups = []
    for g in range(tokens // group):
        here = slice(g * group, (g + 1) * group)
        all_weights, all_values = [], []
        for mask in masks:
            scores = mul(keys[here], query[here] * mask, ((1,), (1,)))
            scores = jnp.sum(jnp.where(same, scores.reshape(sites, count, group), 0.0), axis=0)
            weights = column_softmax(scores)
            weights = jnp.where(same, weights[None], 0.0).reshape(group, group)
            all_weights.append(weights.astype(BF16))
            all_values.append(values[here] * mask)
        groups.append(
            mul(
                jnp.concatenate(all_weights, axis=0),
                jnp.concatenate(all_values, axis=0),
                ((0,), (0,)),
            )
        )
    mixed = (jnp.concatenate(groups, axis=0) * gate).astype(BF16)
    align = (one + mul(mixed, col_out[...])).astype(BF16)
    own = count * res_dev
    row_at, lane_at = iota((own, tokens), 0), iota((own, tokens), 1)
    pick = zero_one(
        lane_at == (row_at % res_dev + me * res_dev) * count + row_at // res_dev
    )
    align_ref[...] = mul(pick, align).reshape(count, res_dev, width).astype(BF16)

    opm = normal(align.astype(F32)).astype(BF16)
    opm = mul(opm, lift[...], ((1,), (1,))).astype(BF16)
    hidden = MEAN_HIDDEN_SIZE
    deep = hidden * count
    spread = zero_one(
        iota((2 * hidden, deep), 1) // count == iota((2 * hidden, deep), 0)
    )
    left = mul(opm, spread)
    left = jnp.where(
        iota((tokens, deep), 0) % count == iota((tokens, deep), 1) % count, left, 0.0
    ).astype(BF16)
    gather = zero_one(iota((residues, tokens), 1) // count == iota((residues, tokens), 0))
    left = mul(gather, left).astype(BF16)
    two = 2 * count
    wide = zero_one(
        iota((deep, 2 * deep), 0)
        == (iota((deep, 2 * deep), 1) // two) * count + iota((deep, 2 * deep), 1) % count
    )
    wide = mul(left, wide)
    which = (iota(wide.shape, 1) % two) // count
    left = jnp.concatenate(
        [jnp.where(which == 0, wide, 0.0), jnp.where(which == 1, wide, 0.0)], axis=0
    ).astype(BF16)
    right = opm[:, hidden:]
    for c in range(0, hidden, 2):
        pair_w = jnp.concatenate(
            [outer_w[(c + k) * hidden : (c + k + 1) * hidden, :] for k in range(2)], axis=1
        )
        part = mul(right, pair_w).astype(BF16)
        lifted[c], lifted[c + 1] = part[:, :pair_width], part[:, pair_width:]
    for j in range(0, residues, 4):
        part = jnp.concatenate(
            [
                lifted[:, (j + k) * count : (j + k + 2) * count, :].reshape(2 * deep, pair_width)
                for k in (0, 2)
            ],
            axis=1,
        )
        part = mul(left, part) * (1.0 / count)
        for k in range(4):
            update_ref[j + k] = part[
                (k % 2) * residues : (k % 2 + 1) * residues,
                (k // 2) * pair_width : (k // 2 + 1) * pair_width,
            ]
    copy.wait()


def pair_kernel(n, *refs):
    pairs, packets, update, refs = refs[: n - 1], refs[n - 1 : 2 * n - 2], refs[2 * n - 2], refs[2 * n - 1 :]
    column, pair, own_mask, proj, gates, gate_out, w_out = refs[:7]
    out_ref, state, one, right_at, left_at, valid = refs[7:]
    res_dev, residues, width = pair.shape
    per = (packets[0].shape[0] - SMALL_ROWS) // residues
    me = lax.axis_index("axial")
    own_valid = own_mask[...].astype(F32)
    size = res_dev * residues
    for block, r in zip((pair, *pairs), range(n)):
        state[pl.ds(pl.multiple_of((me ^ r) * size, size), size), :] = (
            block[...].astype(F32).reshape(size, width)
        )
    for packet, r in zip((None, *packets), (0, *PACKET_ORDER)):
        shown = split_small(packet, residues, res_dev, per)[1] if r else own_valid
        valid[pl.ds(pl.multiple_of((me ^ r) * res_dev, res_dev), res_dev), :] = shown
    for k in range(residues):
        one[k * residues : (k + 1) * residues, :] = (
            state[pl.ds(k, residues, stride=residues), :] + update[k]
        )

    shown = mul(valid[...].astype(BF16), column[...])
    right_w = jnp.concatenate([proj[:, C_TRI:], gates[:, C_TRI:]], axis=1)
    step = 8
    for k in range(0, residues, step):
        here = slice(k * residues, (k + step) * residues)
        both = mul(normal(one[here, :]).astype(BF16), right_w)
        both = sigmoid(both[:, C_TRI:]) * both[:, :C_TRI]
        for p in range(step):
            part = both[p * residues : (p + 1) * residues]
            part = part * shown[:, (k + p) * C_TRI : (k + p + 1) * C_TRI]
            right_at[(k + p) * residues : (k + p + 1) * residues, :] = part.astype(BF16).astype(F32)

    own = jnp.concatenate(
        [one[pl.ds(me * res_dev + i, residues, stride=residues), :] for i in range(res_dev)],
        axis=0,
    )
    left_w = jnp.concatenate([proj[:, :C_TRI], gates[:, :C_TRI], gate_out[...]], axis=1)
    own_all = mul(normal(own).astype(BF16), left_w)
    own_gate = sigmoid(own_all[:, 2 * C_TRI :])
    left = sigmoid(own_all[:, C_TRI : 2 * C_TRI]) * own_all[:, :C_TRI]
    shown = mul(own_valid.astype(BF16), column[:res_dev, : res_dev * C_TRI], ((0,), (0,)))
    for i in range(res_dev):
        part = left[i * residues : (i + 1) * residues] * shown[:, i * C_TRI : (i + 1) * C_TRI]
        left_at[i * residues : (i + 1) * residues, :] = part.astype(BF16).astype(F32)
    sums = [jnp.zeros((residues, C_TRI), F32) for _ in range(res_dev)]
    for k in range(residues):
        other = right_at[k * residues : (k + 1) * residues, :]
        for i in range(res_dev):
            sums[i] += left_at[i * residues + k : i * residues + k + 1, :] * other
    mixed = normal(jnp.concatenate(sums, axis=0)).astype(BF16)
    result = own + own_gate * mul(mixed, w_out[...])
    out_ref[...] = result.reshape(res_dev, residues, width).astype(BF16)


def call(kernel, out_shape, scratch, vmem_mib, *args, far=0):
    vmem = pl.BlockSpec(memory_space=pltpu.VMEM)
    return pl.pallas_call(
        kernel,
        out_shape=out_shape,
        in_specs=[vmem] * (len(args) - far) + [pl.BlockSpec(memory_space=pl.ANY)] * far,
        out_specs=jax.tree.map(lambda _: vmem, out_shape),
        scratch_shapes=scratch,
        compiler_params=pltpu.CompilerParams(vmem_limit_bytes=vmem_mib * 1024 * 1024),
        cost_estimate=pl.CostEstimate(flops=FLOPS, bytes_accessed=0, transcendentals=0),
    )(*args)


def swap(array, r, n):
    return lax.ppermute(array, "axial", [(i, i ^ r) for i in range(n)])


def local_whole(
    homolog_activity,
    homolog_symbol_ids,
    residue_present_mask,
    pair_state,
    pair_valid_mask,
    symbol_lookup_matrix,
    row_query_weight,
    horizontal_attention_matrix,
    pair_bias_weight,
    horizontal_final_matrix,
    column_query_weight,
    vertical_attention_matrix,
    vertical_final_matrix,
    tensor_mean_lift_matrix,
    outer_product_output_weight,
    triangle_projection_weight,
    triangle_projection_gate,
    triangle_output_gate,
    triangle_output_weight,
):
    n = lax.axis_size("axial")
    per, residues, width = homolog_activity.shape
    res_dev, _, pair_width = pair_state.shape
    count = per * n
    bias_weight = pair_bias_weight.T
    pair_2 = swap(pair_state, 2, n)
    shift, turn, column = call(
        functools.partial(table_kernel, FOCUS_TOTAL * res_dev, count),
        (
            jax.ShapeDtypeStruct((residues, 128), BF16),
            jax.ShapeDtypeStruct((count * residues, count * residues), BF16),
            jax.ShapeDtypeStruct((residues, residues * C_TRI), BF16),
        ),
        [],
        2,
    )
    packet, hidden_keys = call(
        packet_kernel,
        (
            jax.ShapeDtypeStruct((per * residues + SMALL_ROWS, width), BF16),
            jax.ShapeDtypeStruct((residues, FOCUS_TOTAL * residues), F32),
        ),
        [],
        4,
        pair_state,
        bias_weight,
        pair_valid_mask,
        homolog_symbol_ids,
        homolog_activity,
        residue_present_mask.reshape(1, residues),
        shift,
    )
    packets = [swap(packet, r, n) for r in PACKET_ORDER]
    _, later = lax.optimization_barrier((packet, pair_state))
    pair_1 = swap(later, 1, n)
    pair_3 = swap(pair_2, 1, n)
    alignment, update, near_pair_2 = call(
        functools.partial(msa_kernel, n),
        (
            jax.ShapeDtypeStruct((count, res_dev, width), BF16),
            jax.ShapeDtypeStruct((residues, residues, pair_width), F32),
            jax.ShapeDtypeStruct(pair_state.shape, BF16),
        ),
        [
            pltpu.VMEM((count * residues, width), F32),
            pltpu.VMEM((MEAN_HIDDEN_SIZE, count * residues, pair_width), BF16),
            pltpu.SemaphoreType.DMA,
        ],
        16,
        *packets,
        turn,
        hidden_keys,
        pair_state,
        bias_weight,
        homolog_activity,
        homolog_symbol_ids,
        symbol_lookup_matrix,
        row_query_weight,
        horizontal_attention_matrix,
        horizontal_final_matrix,
        column_query_weight,
        vertical_attention_matrix,
        vertical_final_matrix,
        tensor_mean_lift_matrix.T,
        outer_product_output_weight,
        pair_2,
        far=1,
    )
    pair_output = call(
        functools.partial(pair_kernel, n),
        jax.ShapeDtypeStruct((res_dev, residues, pair_width), BF16),
        [
            pltpu.VMEM((residues * residues, pair_width), F32),
            pltpu.VMEM((residues * residues, pair_width), F32),
            pltpu.VMEM((residues * residues, C_TRI), F32),
            pltpu.VMEM((res_dev * residues, C_TRI), F32),
            pltpu.VMEM((residues, residues), F32),
        ],
        16,
        pair_1,
        near_pair_2,
        pair_3,
        *packets,
        update,
        column,
        pair_state,
        pair_valid_mask,
        triangle_projection_weight,
        triangle_projection_gate,
        triangle_output_gate,
        triangle_output_weight,
    )
    return (alignment, pair_output)


def local(homolog_activity, homolog_symbol_ids, residue_present_mask, pair_state, *others):
    n = lax.axis_size("axial")
    per, residues, _ = homolog_activity.shape
    small = n == 4 and per * n == 8 and residues == 32
    plan = local_whole if small else local_sharded
    return plan(homolog_activity, homolog_symbol_ids, residue_present_mask, pair_state, *others)


def solution(mesh):
    parts, copied = P(("dp", "axial")), P()
    return jax.shard_map(
        local,
        mesh=mesh,
        in_specs=(parts, parts, P("dp"), parts, parts) + (copied,) * 14,
        out_specs=(P("dp", "axial", None), P(("dp", "axial"), None, None)),
        check_vma=False,
    )
```

```python
import functools

import jax
import jax.numpy as jnp
from jax import lax
from jax.experimental import pallas as pl
from jax.experimental.pallas import tpu as pltpu
from jax.sharding import PartitionSpec as P

FOCUS_TOTAL = 8
FOCUS_SIZE = 32
MEAN_HIDDEN_SIZE = 32
C_TRI = 128


def layer_normalize(attended_entries):
    attended_entries = attended_entries.astype(jnp.float32)
    mean = jnp.mean(attended_entries, axis=-1, keepdims=True)
    centred = attended_entries - mean
    var = jnp.mean(centred * centred, axis=-1, keepdims=True)
    return centred * lax.rsqrt(var + 1e-05)


def gated_attend(evoformer_block, extra_axes, w_query, w_kvg, w_out):
    lines_list, residue_length, input_width = evoformer_block.shape
    width = FOCUS_TOTAL * FOCUS_SIZE
    flat = (
        layer_normalize(evoformer_block)
        .astype(jnp.bfloat16)
        .reshape(lines_list * residue_length, input_width)
    )
    query = (
        jnp.dot(flat, w_query, preferred_element_type=jnp.float32) * FOCUS_SIZE ** (-0.5)
    ).astype(jnp.bfloat16)
    query = query.reshape(lines_list, residue_length, FOCUS_TOTAL, FOCUS_SIZE)
    kvg = jnp.dot(flat, w_kvg, preferred_element_type=jnp.float32)
    keys = (
        kvg[:, :width]
        .astype(jnp.bfloat16)
        .reshape(lines_list, residue_length, FOCUS_TOTAL, FOCUS_SIZE)
    )
    attended_entries = (
        kvg[:, width : 2 * width]
        .astype(jnp.bfloat16)
        .reshape(lines_list, residue_length, FOCUS_TOTAL, FOCUS_SIZE)
    )
    gate = jax.nn.sigmoid(kvg[:, 2 * width :]).reshape(
        lines_list, residue_length, FOCUS_TOTAL, FOCUS_SIZE
    )
    scores = (
        jnp.einsum("bihd,bjhd->bhij", query, keys, preferred_element_type=jnp.float32) + extra_axes
    )
    top = jnp.max(scores, axis=-1, keepdims=True)
    expo = jnp.exp(scores - top)
    weights = (expo / jnp.sum(expo, axis=-1, keepdims=True)).astype(jnp.bfloat16)
    mixed = jnp.einsum(
        "bhij,bjhd->bihd", weights, attended_entries, preferred_element_type=jnp.float32
    )
    mixed = (mixed * gate).astype(jnp.bfloat16).reshape(lines_list * residue_length, width)
    return evoformer_block + jnp.dot(mixed, w_out, preferred_element_type=jnp.float32).reshape(
        lines_list, residue_length, input_width
    )


def finish_sums(evoformer_block, triangle_output_weight):
    mixed = layer_normalize(jnp.transpose(evoformer_block, (1, 2, 0))).astype(jnp.bfloat16)
    return jnp.einsum(
        "ijc,cz->ijz", mixed, triangle_output_weight, preferred_element_type=jnp.float32
    )


def local_sharded(
    homolog_activity,
    homolog_symbol_ids,
    residue_present_mask,
    pair_state,
    pair_valid_mask,
    symbol_lookup_matrix,
    row_query_weight,
    horizontal_attention_matrix,
    pair_bias_weight,
    horizontal_final_matrix,
    column_query_weight,
    vertical_attention_matrix,
    vertical_final_matrix,
    tensor_mean_lift_matrix,
    outer_product_output_weight,
    triangle_projection_weight,
    triangle_projection_gate,
    triangle_output_gate,
    triangle_output_weight,
):
    sequence_per_device, residue_length, input_width = homolog_activity.shape
    res_dev = pair_state.shape[0]
    group_size = lax.axis_size("axial")
    token_classes = symbol_lookup_matrix.shape[0]
    token_one_hot = (
        homolog_symbol_ids[..., None] == jnp.arange(token_classes, dtype=jnp.int32)
    ).astype(jnp.bfloat16)
    token_embedded = jnp.einsum(
        "slt,tc->slc", token_one_hot, symbol_lookup_matrix, preferred_element_type=jnp.float32
    )
    homolog_starting = homolog_activity.astype(jnp.float32) + token_embedded
    pair_norm = layer_normalize(pair_state).astype(jnp.bfloat16)
    bias_rows = jnp.einsum(
        "ijc,ch->hij", pair_norm, pair_bias_weight, preferred_element_type=jnp.float32
    ).astype(jnp.bfloat16)
    bias_full = lax.all_gather(bias_rows, "axial", axis=1, tiled=True)
    key_bias = 1000000000.0 * (residue_present_mask.astype(jnp.float32) - 1.0)
    extra_axes = bias_full.astype(jnp.float32)[None] + key_bias[None, None, None, :]
    cluster_total = homolog_starting.reshape(
        sequence_per_device // 2, 2, residue_length, input_width
    )
    homolog_across_update = lax.map(
        lambda evoformer_block: gated_attend(
            evoformer_block,
            extra_axes,
            row_query_weight,
            horizontal_attention_matrix,
            horizontal_final_matrix,
        ),
        cluster_total,
    )
    homolog_across_update = homolog_across_update.reshape(
        sequence_per_device, group_size, res_dev, input_width
    ).astype(jnp.bfloat16)
    moved = jnp.swapaxes(
        lax.all_to_all(homolog_across_update, "axial", split_axis=1, concat_axis=0, tiled=True)[
            :, 0
        ],
        0,
        1,
    )
    finished = lax.map(
        lambda item: gated_attend(
            item[None].astype(jnp.float32),
            0.0,
            column_query_weight,
            vertical_attention_matrix,
            vertical_final_matrix,
        )[0],
        moved,
    )
    exchanged = jnp.swapaxes(finished, 0, 1).astype(jnp.bfloat16)[:, None]
    sequence_count = exchanged.shape[0]
    alignment_after_columns = exchanged.reshape(sequence_count, res_dev, input_width)
    tensor_mean_scaler = layer_normalize(alignment_after_columns).astype(jnp.bfloat16)
    split_parts = jnp.einsum(
        "src,cf->rsf",
        tensor_mean_scaler,
        tensor_mean_lift_matrix,
        preferred_element_type=jnp.float32,
    ).astype(jnp.bfloat16)
    first_factor = split_parts[..., :MEAN_HIDDEN_SIZE]
    second_factor = split_parts[..., MEAN_HIDDEN_SIZE:].reshape(
        res_dev, sequence_count * MEAN_HIDDEN_SIZE
    )
    step_rows = 8
    left_blocks = first_factor.reshape(
        res_dev // step_rows, step_rows, sequence_count, MEAN_HIDDEN_SIZE
    )
    piece = lax.all_gather(second_factor, "axial", axis=0, tiled=True)
    count = piece.shape[0]
    right_part = piece.reshape(count, sequence_count, MEAN_HIDDEN_SIZE)

    def one_block(lines_list):
        tensor_mean = (
            jnp.einsum("isc,jsd->ijcd", lines_list, right_part, preferred_element_type=jnp.float32)
            / sequence_count
        )
        tensor_mean = tensor_mean.reshape(
            step_rows, count, MEAN_HIDDEN_SIZE * MEAN_HIDDEN_SIZE
        ).astype(jnp.bfloat16)
        return jnp.einsum(
            "ijf,fz->ijz",
            tensor_mean,
            outer_product_output_weight,
            preferred_element_type=jnp.float32,
        )

    update = lax.map(one_block, left_blocks).reshape(
        res_dev, count, outer_product_output_weight.shape[1]
    )
    pair_one = pair_state.astype(jnp.float32) + update
    tri_norm = layer_normalize(pair_one).astype(jnp.bfloat16)
    proj = jnp.einsum(
        "ikc,cf->fik", tri_norm, triangle_projection_weight, preferred_element_type=jnp.float32
    )
    gates = jnp.einsum(
        "ikc,cf->fik", tri_norm, triangle_projection_gate, preferred_element_type=jnp.float32
    )
    both = (jax.nn.sigmoid(gates) * proj * pair_valid_mask.astype(jnp.float32)[None]).astype(
        jnp.bfloat16
    )
    left_tri = both[:C_TRI]
    right_tri = both[C_TRI:]
    moved_left, moved_right = (
        lax.all_to_all(left_tri, "axial", split_axis=0, concat_axis=1, tiled=True),
        lax.all_to_all(right_tri, "axial", split_axis=0, concat_axis=1, tiled=True),
    )
    partial_sum = jnp.einsum(
        "cik,cjk->cij", moved_left, moved_right, preferred_element_type=jnp.float32
    )
    tri_sum = lax.all_to_all(
        partial_sum.astype(jnp.bfloat16), "axial", split_axis=1, concat_axis=0, tiled=True
    ).astype(partial_sum.dtype)
    tri_update = finish_sums(tri_sum, triangle_output_weight)
    out_gate = jax.nn.sigmoid(
        jnp.einsum(
            "ijc,cz->ijz", tri_norm, triangle_output_gate, preferred_element_type=jnp.float32
        )
    )
    pair_output = (pair_one + out_gate * tri_update).astype(jnp.bfloat16)
    return (alignment_after_columns, pair_output)


BF16 = jnp.bfloat16
F32 = jnp.float32
SMALL_ROWS = 16
FLOPS = 10**11
PACKET_ORDER = (2, 1, 3)


def mul(lhs, rhs, over=((1,), (0,))):
    return lax.dot_general(lhs, rhs, (over, ((), ())), preferred_element_type=F32)


def iota(shape, axis):
    return lax.broadcasted_iota(jnp.int32, shape, axis)


def zero_one(condition):
    return jnp.where(condition, 1.0, 0.0).astype(BF16)


def normal(x):
    mean = jnp.mean(x, axis=-1, keepdims=True)
    centred = x - mean
    var = jnp.mean(centred * centred, axis=-1, keepdims=True)
    return centred * lax.rsqrt(var + 1e-05)


def sigmoid(x):
    return 1.0 / (1.0 + jnp.exp(-x))


def column_softmax(scores):
    expo = jnp.exp(scores - jnp.max(scores, axis=0, keepdims=True))
    return expo * (1.0 / jnp.sum(expo, axis=0, keepdims=True))


def head_masks(width):
    return [
        zero_one(iota((1, width), 1) // FOCUS_SIZE == h) for h in range(FOCUS_TOTAL)
    ]


def bias_rows(pair_ref, weight_ref):
    rows, residues, width = pair_ref.shape
    lanes = FOCUS_TOTAL * rows
    spread = zero_one(iota((FOCUS_TOTAL, lanes), 1) // rows == iota((FOCUS_TOTAL, lanes), 0))
    row_of = iota((width, lanes), 1) % rows
    flat = normal(pair_ref[...].astype(F32).reshape(rows * residues, width)).astype(BF16)
    weight = mul(weight_ref[...], spread, ((0,), (0,)))
    bias = jnp.zeros((residues, lanes), F32)
    for i in range(rows):
        one_row = jnp.where(row_of == i, weight, 0.0).astype(BF16)
        bias += mul(flat[i * residues : (i + 1) * residues], one_row)
    return bias


def table_kernel(lanes, count, shift_ref, turn_ref, column_ref):
    shape = column_ref.shape
    column_ref[...] = zero_one(iota(shape, 1) // C_TRI == iota(shape, 0))
    shape = shift_ref.shape
    shift_ref[...] = zero_one(iota(shape, 1) == iota(shape, 0) + lanes)
    shape = turn_ref.shape
    row_at = iota(shape, 0)
    turn_ref[...] = zero_one(
        iota(shape, 1) == (row_at % count) * (shape[0] // count) + row_at // count
    )


def packet_kernel(*refs):
    pair_ref, weight_ref, valid_ref, ids_ref, act_ref, present_ref, shift_ref = refs[:7]
    packet_ref, hidden_ref = refs[7:]
    rows, residues, width = pair_ref.shape
    per, _, features = act_ref.shape
    lanes = FOCUS_TOTAL * rows
    bias = bias_rows(pair_ref, weight_ref)
    extra = jnp.concatenate(
        [
            valid_ref[...].astype(F32),
            ids_ref[...].astype(F32),
            jnp.zeros((SMALL_ROWS - rows - per, residues), F32),
        ],
        axis=0,
    )
    extra = mul(extra.astype(BF16), shift_ref[...])
    empty = jnp.zeros((SMALL_ROWS, 128 - lanes), F32)
    first = jnp.concatenate([bias[:SMALL_ROWS], empty], axis=1) + extra
    second = jnp.concatenate([bias[SMALL_ROWS:], empty], axis=1)
    small = jnp.concatenate([first, second], axis=1).astype(BF16)
    packet_ref[per * residues :, :] = small
    shown = present_ref[...].astype(F32).astype(BF16)
    shown = mul(shown, jnp.ones((1, hidden_ref.shape[1]), BF16), ((0,), (0,)))
    hidden_ref[...] = 1000000000.0 * (shown - 1.0)
    packet_ref[: per * residues, :] = act_ref[...].reshape(per * residues, features)


def split_small(packet, residues, res_dev, per):
    small = packet[per * residues :, :].astype(F32)
    lanes = FOCUS_TOTAL * res_dev
    bias = jnp.concatenate([small[:, :lanes], small[:, 128 : 128 + lanes]], axis=0)
    extra = small[:, lanes : lanes + residues]
    return bias, extra[:res_dev], extra[res_dev : res_dev + per]


def project(x, w_query, w_kvg):
    width = FOCUS_TOTAL * FOCUS_SIZE
    flat = normal(x).astype(BF16)
    query = (mul(flat, w_query[...]) * FOCUS_SIZE ** (-0.5)).astype(BF16)
    keys = mul(flat, w_kvg[:, :width]).astype(BF16)
    values = mul(flat, w_kvg[:, width : 2 * width]).astype(BF16)
    gate = sigmoid(mul(flat, w_kvg[:, 2 * width :]))
    return query, keys, values, gate


def msa_kernel(n, *refs):
    packets, refs = refs[: n - 1], refs[n - 1 :]
    turn, hidden_keys, pair, pair_w, act, ids, table = refs[:7]
    row_q, row_kvg, row_out, col_q, col_kvg, col_out, lift, outer_w, far_pair = refs[7:16]
    align_ref, update_ref, pair_ref, start, lifted, sem = refs[16:]
    copy = pltpu.make_async_copy(far_pair, pair_ref, sem)
    copy.start()
    per, residues, width = act.shape
    res_dev = pair.shape[0]
    kinds = table.shape[0]
    pair_width = pair.shape[2]
    count = per * n
    tokens = count * residues
    lanes = FOCUS_TOTAL * residues
    me = lax.axis_index("axial")
    masks = head_masks(width)

    place = iota((FOCUS_TOTAL * res_dev, lanes), 0)
    place = (place // res_dev) * residues + place % res_dev - iota(place.shape, 1)
    extra = jnp.zeros((residues, lanes), F32)
    for packet, r in zip((None, *packets), (0, *PACKET_ORDER)):
        owner = me ^ r
        if r == 0:
            bias, all_ids = bias_rows(pair, pair_w), ids[...].astype(F32)
        else:
            bias, _, all_ids = split_small(packet, residues, res_dev, per)
        extra += mul(bias.astype(BF16), zero_one(place == -owner * res_dev))
        for q in range(per):
            hot = zero_one(iota((kinds, residues), 0).astype(F32) == all_ids[q : q + 1])
            rows = act[q] if r == 0 else packet[q * residues : (q + 1) * residues, :]
            start[pl.ds(pl.multiple_of((owner * per + q) * residues, residues), residues), :] = (
                rows.astype(F32) + mul(hot, table[...], ((0,), (0,)))
            )
    extra = extra + hidden_keys[...]

    zero = start[...]
    query, keys, values, gate = project(zero, row_q, row_kvg)
    rows = []
    for s in range(count):
        here = slice(s * residues, (s + 1) * residues)
        spread = jnp.concatenate([query[here] * mask for mask in masks], axis=0)
        weights = column_softmax(mul(keys[here], spread, ((1,), (1,))) + extra).astype(BF16)
        heads = mul(weights, values[here], ((0,), (0,)))
        mixed = jnp.zeros((residues, width), F32)
        for h in range(FOCUS_TOTAL):
            part = heads[h * residues : (h + 1) * residues]
            mixed = jnp.where(iota((1, width), 1) // FOCUS_SIZE == h, part, mixed)
        rows.append(mixed)
    mixed = (jnp.concatenate(rows, axis=0) * gate).astype(BF16)
    msa_one = (zero + mul(mixed, row_out[...])).astype(BF16)

    one = mul(turn[...], msa_one)
    query, keys, values, gate = project(one, col_q, col_kvg)
    group = min(tokens, 128)
    sites = group // count
    same = iota((sites, count, group), 2) // count == iota((sites, count, group), 0)
    groups = []
    for g in range(tokens // group):
        here = slice(g * group, (g + 1) * group)
        all_weights, all_values = [], []
        for mask in masks:
            scores = mul(keys[here], query[here] * mask, ((1,), (1,)))
            scores = jnp.sum(jnp.where(same, scores.reshape(sites, count, group), 0.0), axis=0)
            weights = column_softmax(scores)
            weights = jnp.where(same, weights[None], 0.0).reshape(group, group)
            all_weights.append(weights.astype(BF16))
            all_values.append(values[here] * mask)
        groups.append(
            mul(
                jnp.concatenate(all_weights, axis=0),
                jnp.concatenate(all_values, axis=0),
                ((0,), (0,)),
            )
        )
    mixed = (jnp.concatenate(groups, axis=0) * gate).astype(BF16)
    align = (one + mul(mixed, col_out[...])).astype(BF16)
    own = count * res_dev
    row_at, lane_at = iota((own, tokens), 0), iota((own, tokens), 1)
    pick = zero_one(
        lane_at == (row_at % res_dev + me * res_dev) * count + row_at // res_dev
    )
    align_ref[...] = mul(pick, align).reshape(count, res_dev, width).astype(BF16)

    opm = normal(align.astype(F32)).astype(BF16)
    opm = mul(opm, lift[...], ((1,), (1,))).astype(BF16)
    hidden = MEAN_HIDDEN_SIZE
    deep = hidden * count
    spread = zero_one(
        iota((2 * hidden, deep), 1) // count == iota((2 * hidden, deep), 0)
    )
    left = mul(opm, spread)
    left = jnp.where(
        iota((tokens, deep), 0) % count == iota((tokens, deep), 1) % count, left, 0.0
    ).astype(BF16)
    gather = zero_one(iota((residues, tokens), 1) // count == iota((residues, tokens), 0))
    left = mul(gather, left).astype(BF16)
    right = opm[:, hidden:]
    for c in range(0, hidden, 2):
        pair_w = jnp.concatenate(
            [outer_w[(c + k) * hidden : (c + k + 1) * hidden, :] for k in range(2)], axis=1
        )
        part = mul(right, pair_w)
        lifted[c], lifted[c + 1] = part[:, :pair_width], part[:, pair_width:]
    for j in range(0, residues, 2):
        part = jnp.concatenate(
            [
                lifted[:, (j + k) * count : (j + k + 1) * count, :].reshape(deep, pair_width)
                for k in range(2)
            ],
            axis=1,
        )
        part = mul(left, part.astype(BF16)) * (1.0 / count)
        update_ref[j], update_ref[j + 1] = part[:, :pair_width], part[:, pair_width:]
    copy.wait()


def pair_kernel(n, *refs):
    pairs, packets, update, refs = refs[: n - 1], refs[n - 1 : 2 * n - 2], refs[2 * n - 2], refs[2 * n - 1 :]
    column, pair, own_mask, proj, gates, gate_out, w_out = refs[:7]
    out_ref, state, one, right_at, left_at, valid = refs[7:]
    res_dev, residues, width = pair.shape
    per = (packets[0].shape[0] - SMALL_ROWS) // residues
    me = lax.axis_index("axial")
    own_valid = own_mask[...].astype(F32)
    size = res_dev * residues
    for block, r in zip((pair, *pairs), range(n)):
        state[pl.ds(pl.multiple_of((me ^ r) * size, size), size), :] = (
            block[...].astype(F32).reshape(size, width)
        )
    for packet, r in zip((None, *packets), (0, *PACKET_ORDER)):
        shown = split_small(packet, residues, res_dev, per)[1] if r else own_valid
        valid[pl.ds(pl.multiple_of((me ^ r) * res_dev, res_dev), res_dev), :] = shown
    for k in range(residues):
        one[k * residues : (k + 1) * residues, :] = (
            state[pl.ds(k, residues, stride=residues), :] + update[k]
        )

    shown = mul(valid[...].astype(BF16), column[...])
    right_w = jnp.concatenate([proj[:, C_TRI:], gates[:, C_TRI:]], axis=1)
    step = 8
    for k in range(0, residues, step):
        here = slice(k * residues, (k + step) * residues)
        both = mul(normal(one[here, :]).astype(BF16), right_w)
        both = sigmoid(both[:, C_TRI:]) * both[:, :C_TRI]
        for p in range(step):
            part = both[p * residues : (p + 1) * residues]
            part = part * shown[:, (k + p) * C_TRI : (k + p + 1) * C_TRI]
            right_at[(k + p) * residues : (k + p + 1) * residues, :] = part.astype(BF16).astype(F32)

    own = jnp.concatenate(
        [one[pl.ds(me * res_dev + i, residues, stride=residues), :] for i in range(res_dev)],
        axis=0,
    )
    left_w = jnp.concatenate([proj[:, :C_TRI], gates[:, :C_TRI], gate_out[...]], axis=1)
    own_all = mul(normal(own).astype(BF16), left_w)
    own_gate = sigmoid(own_all[:, 2 * C_TRI :])
    left = sigmoid(own_all[:, C_TRI : 2 * C_TRI]) * own_all[:, :C_TRI]
    shown = mul(own_valid.astype(BF16), column[:res_dev, : res_dev * C_TRI], ((0,), (0,)))
    for i in range(res_dev):
        part = left[i * residues : (i + 1) * residues] * shown[:, i * C_TRI : (i + 1) * C_TRI]
        left_at[i * residues : (i + 1) * residues, :] = part.astype(BF16).astype(F32)
    sums = [jnp.zeros((residues, C_TRI), F32) for _ in range(res_dev)]
    for k in range(residues):
        other = right_at[k * residues : (k + 1) * residues, :]
        for i in range(res_dev):
            sums[i] += left_at[i * residues + k : i * residues + k + 1, :] * other
    mixed = normal(jnp.concatenate(sums, axis=0)).astype(BF16)
    result = own + own_gate * mul(mixed, w_out[...])
    out_ref[...] = result.reshape(res_dev, residues, width).astype(BF16)


def call(kernel, out_shape, scratch, vmem_mib, *args, far=0):
    vmem = pl.BlockSpec(memory_space=pltpu.VMEM)
    return pl.pallas_call(
        kernel,
        out_shape=out_shape,
        in_specs=[vmem] * (len(args) - far) + [pl.BlockSpec(memory_space=pl.ANY)] * far,
        out_specs=jax.tree.map(lambda _: vmem, out_shape),
        scratch_shapes=scratch,
        compiler_params=pltpu.CompilerParams(vmem_limit_bytes=vmem_mib * 1024 * 1024),
        cost_estimate=pl.CostEstimate(flops=FLOPS, bytes_accessed=0, transcendentals=0),
    )(*args)


def swap(array, r, n):
    return lax.ppermute(array, "axial", [(i, i ^ r) for i in range(n)])


def local_whole(
    homolog_activity,
    homolog_symbol_ids,
    residue_present_mask,
    pair_state,
    pair_valid_mask,
    symbol_lookup_matrix,
    row_query_weight,
    horizontal_attention_matrix,
    pair_bias_weight,
    horizontal_final_matrix,
    column_query_weight,
    vertical_attention_matrix,
    vertical_final_matrix,
    tensor_mean_lift_matrix,
    outer_product_output_weight,
    triangle_projection_weight,
    triangle_projection_gate,
    triangle_output_gate,
    triangle_output_weight,
):
    n = lax.axis_size("axial")
    per, residues, width = homolog_activity.shape
    res_dev, _, pair_width = pair_state.shape
    count = per * n
    bias_weight = pair_bias_weight.T
    pair_2, pair_1 = swap(pair_state, 2, n), swap(pair_state, 1, n)
    shift, turn, column = call(
        functools.partial(table_kernel, FOCUS_TOTAL * res_dev, count),
        (
            jax.ShapeDtypeStruct((residues, 128), BF16),
            jax.ShapeDtypeStruct((count * residues, count * residues), BF16),
            jax.ShapeDtypeStruct((residues, residues * C_TRI), BF16),
        ),
        [],
        2,
    )
    packet, hidden_keys = call(
        packet_kernel,
        (
            jax.ShapeDtypeStruct((per * residues + SMALL_ROWS, width), BF16),
            jax.ShapeDtypeStruct((residues, FOCUS_TOTAL * residues), F32),
        ),
        [],
        4,
        pair_state,
        bias_weight,
        pair_valid_mask,
        homolog_symbol_ids,
        homolog_activity,
        residue_present_mask.reshape(1, residues),
        shift,
    )
    packets = [swap(packet, r, n) for r in PACKET_ORDER]
    pair_3 = swap(pair_2, 1, n)
    alignment, update, near_pair_2 = call(
        functools.partial(msa_kernel, n),
        (
            jax.ShapeDtypeStruct((count, res_dev, width), BF16),
            jax.ShapeDtypeStruct((residues, residues, pair_width), F32),
            jax.ShapeDtypeStruct(pair_state.shape, BF16),
        ),
        [
            pltpu.VMEM((count * residues, width), F32),
            pltpu.VMEM((MEAN_HIDDEN_SIZE, count * residues, pair_width), F32),
            pltpu.SemaphoreType.DMA,
        ],
        16,
        *packets,
        turn,
        hidden_keys,
        pair_state,
        bias_weight,
        homolog_activity,
        homolog_symbol_ids,
        symbol_lookup_matrix,
        row_query_weight,
        horizontal_attention_matrix,
        horizontal_final_matrix,
        column_query_weight,
        vertical_attention_matrix,
        vertical_final_matrix,
        tensor_mean_lift_matrix.T,
        outer_product_output_weight,
        pair_2,
        far=1,
    )
    pair_output = call(
        functools.partial(pair_kernel, n),
        jax.ShapeDtypeStruct((res_dev, residues, pair_width), BF16),
        [
            pltpu.VMEM((residues * residues, pair_width), F32),
            pltpu.VMEM((residues * residues, pair_width), F32),
            pltpu.VMEM((residues * residues, C_TRI), F32),
            pltpu.VMEM((res_dev * residues, C_TRI), F32),
            pltpu.VMEM((residues, residues), F32),
        ],
        16,
        pair_1,
        near_pair_2,
        pair_3,
        *packets,
        update,
        column,
        pair_state,
        pair_valid_mask,
        triangle_projection_weight,
        triangle_projection_gate,
        triangle_output_gate,
        triangle_output_weight,
    )
    return (alignment, pair_output)


def local(homolog_activity, homolog_symbol_ids, residue_present_mask, pair_state, *others):
    n = lax.axis_size("axial")
    per, residues, _ = homolog_activity.shape
    small = n == 4 and per * n == 8 and residues == 32
    plan = local_whole if small else local_sharded
    return plan(homolog_activity, homolog_symbol_ids, residue_present_mask, pair_state, *others)


def solution(mesh):
    parts, copied = P(("dp", "axial")), P()
    return jax.shard_map(
        local,
        mesh=mesh,
        in_specs=(parts, parts, P("dp"), parts, parts) + (copied,) * 14,
        out_specs=(P("dp", "axial", None), P(("dp", "axial"), None, None)),
        check_vma=False,
    )
```

```python
import functools

import jax
import jax.numpy as jnp
from jax import lax
from jax.experimental import pallas as pl
from jax.experimental.pallas import tpu as pltpu
from jax.sharding import PartitionSpec as P

FOCUS_TOTAL = 8
FOCUS_SIZE = 32
MEAN_HIDDEN_SIZE = 32
C_TRI = 128


def layer_normalize(attended_entries):
    attended_entries = attended_entries.astype(jnp.float32)
    mean = jnp.mean(attended_entries, axis=-1, keepdims=True)
    centred = attended_entries - mean
    var = jnp.mean(centred * centred, axis=-1, keepdims=True)
    return centred * lax.rsqrt(var + 1e-05)


def gated_attend(evoformer_block, extra_axes, w_query, w_kvg, w_out):
    lines_list, residue_length, input_width = evoformer_block.shape
    width = FOCUS_TOTAL * FOCUS_SIZE
    flat = (
        layer_normalize(evoformer_block)
        .astype(jnp.bfloat16)
        .reshape(lines_list * residue_length, input_width)
    )
    query = (
        jnp.dot(flat, w_query, preferred_element_type=jnp.float32) * FOCUS_SIZE ** (-0.5)
    ).astype(jnp.bfloat16)
    query = query.reshape(lines_list, residue_length, FOCUS_TOTAL, FOCUS_SIZE)
    kvg = jnp.dot(flat, w_kvg, preferred_element_type=jnp.float32)
    keys = (
        kvg[:, :width]
        .astype(jnp.bfloat16)
        .reshape(lines_list, residue_length, FOCUS_TOTAL, FOCUS_SIZE)
    )
    attended_entries = (
        kvg[:, width : 2 * width]
        .astype(jnp.bfloat16)
        .reshape(lines_list, residue_length, FOCUS_TOTAL, FOCUS_SIZE)
    )
    gate = jax.nn.sigmoid(kvg[:, 2 * width :]).reshape(
        lines_list, residue_length, FOCUS_TOTAL, FOCUS_SIZE
    )
    scores = (
        jnp.einsum("bihd,bjhd->bhij", query, keys, preferred_element_type=jnp.float32) + extra_axes
    )
    top = jnp.max(scores, axis=-1, keepdims=True)
    expo = jnp.exp(scores - top)
    weights = (expo / jnp.sum(expo, axis=-1, keepdims=True)).astype(jnp.bfloat16)
    mixed = jnp.einsum(
        "bhij,bjhd->bihd", weights, attended_entries, preferred_element_type=jnp.float32
    )
    mixed = (mixed * gate).astype(jnp.bfloat16).reshape(lines_list * residue_length, width)
    return evoformer_block + jnp.dot(mixed, w_out, preferred_element_type=jnp.float32).reshape(
        lines_list, residue_length, input_width
    )


def finish_sums(evoformer_block, triangle_output_weight):
    mixed = layer_normalize(jnp.transpose(evoformer_block, (1, 2, 0))).astype(jnp.bfloat16)
    return jnp.einsum(
        "ijc,cz->ijz", mixed, triangle_output_weight, preferred_element_type=jnp.float32
    )


def local_sharded(
    homolog_activity,
    homolog_symbol_ids,
    residue_present_mask,
    pair_state,
    pair_valid_mask,
    symbol_lookup_matrix,
    row_query_weight,
    horizontal_attention_matrix,
    pair_bias_weight,
    horizontal_final_matrix,
    column_query_weight,
    vertical_attention_matrix,
    vertical_final_matrix,
    tensor_mean_lift_matrix,
    outer_product_output_weight,
    triangle_projection_weight,
    triangle_projection_gate,
    triangle_output_gate,
    triangle_output_weight,
):
    sequence_per_device, residue_length, input_width = homolog_activity.shape
    res_dev = pair_state.shape[0]
    group_size = lax.axis_size("axial")
    token_classes = symbol_lookup_matrix.shape[0]
    token_one_hot = (
        homolog_symbol_ids[..., None] == jnp.arange(token_classes, dtype=jnp.int32)
    ).astype(jnp.bfloat16)
    token_embedded = jnp.einsum(
        "slt,tc->slc", token_one_hot, symbol_lookup_matrix, preferred_element_type=jnp.float32
    )
    homolog_starting = homolog_activity.astype(jnp.float32) + token_embedded
    pair_norm = layer_normalize(pair_state).astype(jnp.bfloat16)
    bias_rows = jnp.einsum(
        "ijc,ch->hij", pair_norm, pair_bias_weight, preferred_element_type=jnp.float32
    ).astype(jnp.bfloat16)
    bias_full = lax.all_gather(bias_rows, "axial", axis=1, tiled=True)
    key_bias = 1000000000.0 * (residue_present_mask.astype(jnp.float32) - 1.0)
    extra_axes = bias_full.astype(jnp.float32)[None] + key_bias[None, None, None, :]
    cluster_total = homolog_starting.reshape(
        sequence_per_device // 2, 2, residue_length, input_width
    )
    homolog_across_update = lax.map(
        lambda evoformer_block: gated_attend(
            evoformer_block,
            extra_axes,
            row_query_weight,
            horizontal_attention_matrix,
            horizontal_final_matrix,
        ),
        cluster_total,
    )
    homolog_across_update = homolog_across_update.reshape(
        sequence_per_device, group_size, res_dev, input_width
    ).astype(jnp.bfloat16)
    moved = jnp.swapaxes(
        lax.all_to_all(homolog_across_update, "axial", split_axis=1, concat_axis=0, tiled=True)[
            :, 0
        ],
        0,
        1,
    )
    finished = lax.map(
        lambda item: gated_attend(
            item[None].astype(jnp.float32),
            0.0,
            column_query_weight,
            vertical_attention_matrix,
            vertical_final_matrix,
        )[0],
        moved,
    )
    exchanged = jnp.swapaxes(finished, 0, 1).astype(jnp.bfloat16)[:, None]
    sequence_count = exchanged.shape[0]
    alignment_after_columns = exchanged.reshape(sequence_count, res_dev, input_width)
    tensor_mean_scaler = layer_normalize(alignment_after_columns).astype(jnp.bfloat16)
    split_parts = jnp.einsum(
        "src,cf->rsf",
        tensor_mean_scaler,
        tensor_mean_lift_matrix,
        preferred_element_type=jnp.float32,
    ).astype(jnp.bfloat16)
    first_factor = split_parts[..., :MEAN_HIDDEN_SIZE]
    second_factor = split_parts[..., MEAN_HIDDEN_SIZE:].reshape(
        res_dev, sequence_count * MEAN_HIDDEN_SIZE
    )
    step_rows = 8
    left_blocks = first_factor.reshape(
        res_dev // step_rows, step_rows, sequence_count, MEAN_HIDDEN_SIZE
    )
    piece = lax.all_gather(second_factor, "axial", axis=0, tiled=True)
    count = piece.shape[0]
    right_part = piece.reshape(count, sequence_count, MEAN_HIDDEN_SIZE)

    def one_block(lines_list):
        tensor_mean = (
            jnp.einsum("isc,jsd->ijcd", lines_list, right_part, preferred_element_type=jnp.float32)
            / sequence_count
        )
        tensor_mean = tensor_mean.reshape(
            step_rows, count, MEAN_HIDDEN_SIZE * MEAN_HIDDEN_SIZE
        ).astype(jnp.bfloat16)
        return jnp.einsum(
            "ijf,fz->ijz",
            tensor_mean,
            outer_product_output_weight,
            preferred_element_type=jnp.float32,
        )

    update = lax.map(one_block, left_blocks).reshape(
        res_dev, count, outer_product_output_weight.shape[1]
    )
    pair_one = pair_state.astype(jnp.float32) + update
    tri_norm = layer_normalize(pair_one).astype(jnp.bfloat16)
    proj = jnp.einsum(
        "ikc,cf->fik", tri_norm, triangle_projection_weight, preferred_element_type=jnp.float32
    )
    gates = jnp.einsum(
        "ikc,cf->fik", tri_norm, triangle_projection_gate, preferred_element_type=jnp.float32
    )
    both = (jax.nn.sigmoid(gates) * proj * pair_valid_mask.astype(jnp.float32)[None]).astype(
        jnp.bfloat16
    )
    left_tri = both[:C_TRI]
    right_tri = both[C_TRI:]
    moved_left, moved_right = (
        lax.all_to_all(left_tri, "axial", split_axis=0, concat_axis=1, tiled=True),
        lax.all_to_all(right_tri, "axial", split_axis=0, concat_axis=1, tiled=True),
    )
    partial_sum = jnp.einsum(
        "cik,cjk->cij", moved_left, moved_right, preferred_element_type=jnp.float32
    )
    tri_sum = lax.all_to_all(
        partial_sum.astype(jnp.bfloat16), "axial", split_axis=1, concat_axis=0, tiled=True
    ).astype(partial_sum.dtype)
    tri_update = finish_sums(tri_sum, triangle_output_weight)
    out_gate = jax.nn.sigmoid(
        jnp.einsum(
            "ijc,cz->ijz", tri_norm, triangle_output_gate, preferred_element_type=jnp.float32
        )
    )
    pair_output = (pair_one + out_gate * tri_update).astype(jnp.bfloat16)
    return (alignment_after_columns, pair_output)


BF16 = jnp.bfloat16
F32 = jnp.float32
SMALL_ROWS = 16
FLOPS = 3 * 10**9
PACKET_ORDER = (2, 1, 3)


def mul(lhs, rhs, over=((1,), (0,))):
    return lax.dot_general(lhs, rhs, (over, ((), ())), preferred_element_type=F32)


def iota(shape, axis):
    return lax.broadcasted_iota(jnp.int32, shape, axis)


def zero_one(condition):
    return jnp.where(condition, 1.0, 0.0).astype(BF16)


def normal(x):
    mean = jnp.mean(x, axis=-1, keepdims=True)
    centred = x - mean
    var = jnp.mean(centred * centred, axis=-1, keepdims=True)
    return centred * lax.rsqrt(var + 1e-05)


def sigmoid(x):
    return 1.0 / (1.0 + jnp.exp(-x))


def column_softmax(scores):
    expo = jnp.exp(scores - jnp.max(scores, axis=0, keepdims=True))
    return expo * (1.0 / jnp.sum(expo, axis=0, keepdims=True))


def head_masks(width):
    return [
        zero_one(iota((1, width), 1) // FOCUS_SIZE == h) for h in range(FOCUS_TOTAL)
    ]


def bias_rows(pair_ref, weight_ref):
    rows, residues, width = pair_ref.shape
    lanes = FOCUS_TOTAL * rows
    spread = zero_one(iota((FOCUS_TOTAL, lanes), 1) // rows == iota((FOCUS_TOTAL, lanes), 0))
    row_of = iota((width, lanes), 1) % rows
    flat = normal(pair_ref[...].astype(F32).reshape(rows * residues, width)).astype(BF16)
    weight = mul(weight_ref[...], spread, ((0,), (0,)))
    bias = jnp.zeros((residues, lanes), F32)
    for i in range(rows):
        one_row = jnp.where(row_of == i, weight, 0.0).astype(BF16)
        bias += mul(flat[i * residues : (i + 1) * residues], one_row)
    return bias


def table_kernel(lanes, count, shift_ref, turn_ref, column_ref):
    shape = column_ref.shape
    column_ref[...] = zero_one(iota(shape, 1) // C_TRI == iota(shape, 0))
    shape = shift_ref.shape
    shift_ref[...] = zero_one(iota(shape, 1) == iota(shape, 0) + lanes)
    shape = turn_ref.shape
    row_at = iota(shape, 0)
    turn_ref[...] = zero_one(
        iota(shape, 1) == (row_at % count) * (shape[0] // count) + row_at // count
    )


def packet_kernel(*refs):
    pair_ref, weight_ref, valid_ref, ids_ref, act_ref, present_ref, shift_ref = refs[:7]
    packet_ref, hidden_ref = refs[7:]
    rows, residues, width = pair_ref.shape
    per, _, features = act_ref.shape
    lanes = FOCUS_TOTAL * rows
    bias = bias_rows(pair_ref, weight_ref)
    extra = jnp.concatenate(
        [
            valid_ref[...].astype(F32),
            ids_ref[...].astype(F32),
            jnp.zeros((SMALL_ROWS - rows - per, residues), F32),
        ],
        axis=0,
    )
    extra = mul(extra.astype(BF16), shift_ref[...])
    empty = jnp.zeros((SMALL_ROWS, 128 - lanes), F32)
    first = jnp.concatenate([bias[:SMALL_ROWS], empty], axis=1) + extra
    second = jnp.concatenate([bias[SMALL_ROWS:], empty], axis=1)
    small = jnp.concatenate([first, second], axis=1).astype(BF16)
    packet_ref[per * residues :, :] = small
    shown = present_ref[...].astype(F32).astype(BF16)
    shown = mul(shown, jnp.ones((1, hidden_ref.shape[1]), BF16), ((0,), (0,)))
    hidden_ref[...] = 1000000000.0 * (shown - 1.0)
    packet_ref[: per * residues, :] = act_ref[...].reshape(per * residues, features)


def split_small(packet, residues, res_dev, per):
    small = packet[per * residues :, :].astype(F32)
    lanes = FOCUS_TOTAL * res_dev
    bias = jnp.concatenate([small[:, :lanes], small[:, 128 : 128 + lanes]], axis=0)
    extra = small[:, lanes : lanes + residues]
    return bias, extra[:res_dev], extra[res_dev : res_dev + per]


def project(x, w_query, w_kvg):
    width = FOCUS_TOTAL * FOCUS_SIZE
    flat = normal(x).astype(BF16)
    query = (mul(flat, w_query[...]) * FOCUS_SIZE ** (-0.5)).astype(BF16)
    keys = mul(flat, w_kvg[:, :width]).astype(BF16)
    values = mul(flat, w_kvg[:, width : 2 * width]).astype(BF16)
    gate = sigmoid(mul(flat, w_kvg[:, 2 * width :]))
    return query, keys, values, gate


def msa_kernel(n, *refs):
    packets, refs = refs[: n - 1], refs[n - 1 :]
    turn, hidden_keys, pair, pair_w, act, ids, table = refs[:7]
    row_q, row_kvg, row_out, col_q, col_kvg, col_out, lift, outer_w, pair_1, pair_2 = refs[7:17]
    align_ref, one_ref, start, lifted, state = refs[17:]
    per, residues, width = act.shape
    res_dev = pair.shape[0]
    kinds = table.shape[0]
    pair_width = pair.shape[2]
    count = per * n
    tokens = count * residues
    lanes = FOCUS_TOTAL * residues
    me = lax.axis_index("axial")
    masks = head_masks(width)

    size = res_dev * residues
    for block, r in zip((pair, pair_1, pair_2, None), range(n)):
        rows = jnp.zeros((size, pair_width), F32)
        if r < 3:
            rows = block[...].astype(F32).reshape(size, pair_width)
        state[pl.ds(pl.multiple_of((me ^ r) * size, size), size), :] = rows

    place = iota((FOCUS_TOTAL * res_dev, lanes), 0)
    place = (place // res_dev) * residues + place % res_dev - iota(place.shape, 1)
    extra = jnp.zeros((residues, lanes), F32)
    for packet, r in zip((None, *packets), (0, *PACKET_ORDER)):
        owner = me ^ r
        if r == 0:
            bias, all_ids = bias_rows(pair, pair_w), ids[...].astype(F32)
        else:
            bias, _, all_ids = split_small(packet, residues, res_dev, per)
        extra += mul(bias.astype(BF16), zero_one(place == -owner * res_dev))
        for q in range(per):
            hot = zero_one(iota((kinds, residues), 0).astype(F32) == all_ids[q : q + 1])
            rows = act[q] if r == 0 else packet[q * residues : (q + 1) * residues, :]
            start[pl.ds(pl.multiple_of((owner * per + q) * residues, residues), residues), :] = (
                rows.astype(F32) + mul(hot, table[...], ((0,), (0,)))
            )
    extra = extra + hidden_keys[...]

    zero = start[...]
    query, keys, values, gate = project(zero, row_q, row_kvg)
    rows = []
    for s in range(count):
        here = slice(s * residues, (s + 1) * residues)
        spread = jnp.concatenate([query[here] * mask for mask in masks], axis=0)
        weights = column_softmax(mul(keys[here], spread, ((1,), (1,))) + extra).astype(BF16)
        heads = mul(weights, values[here], ((0,), (0,)))
        mixed = jnp.zeros((residues, width), F32)
        for h in range(FOCUS_TOTAL):
            part = heads[h * residues : (h + 1) * residues]
            mixed = jnp.where(iota((1, width), 1) // FOCUS_SIZE == h, part, mixed)
        rows.append(mixed)
    mixed = (jnp.concatenate(rows, axis=0) * gate).astype(BF16)
    msa_one = (zero + mul(mixed, row_out[...])).astype(BF16)

    one = mul(turn[...], msa_one)
    query, keys, values, gate = project(one, col_q, col_kvg)
    group = min(tokens, 128)
    sites = group // count
    same = iota((sites, count, group), 2) // count == iota((sites, count, group), 0)
    groups = []
    for g in range(tokens // group):
        here = slice(g * group, (g + 1) * group)
        all_weights, all_values = [], []
        for mask in masks:
            scores = mul(keys[here], query[here] * mask, ((1,), (1,)))
            scores = jnp.sum(jnp.where(same, scores.reshape(sites, count, group), 0.0), axis=0)
            weights = column_softmax(scores)
            weights = jnp.where(same, weights[None], 0.0).reshape(group, group)
            all_weights.append(weights.astype(BF16))
            all_values.append(values[here] * mask)
        groups.append(
            mul(
                jnp.concatenate(all_weights, axis=0),
                jnp.concatenate(all_values, axis=0),
                ((0,), (0,)),
            )
        )
    mixed = (jnp.concatenate(groups, axis=0) * gate).astype(BF16)
    align = (one + mul(mixed, col_out[...])).astype(BF16)
    own = count * res_dev
    row_at, lane_at = iota((own, tokens), 0), iota((own, tokens), 1)
    pick = zero_one(
        lane_at == (row_at % res_dev + me * res_dev) * count + row_at // res_dev
    )
    align_ref[...] = mul(pick, align).reshape(count, res_dev, width).astype(BF16)

    opm = normal(align.astype(F32)).astype(BF16)
    opm = mul(opm, lift[...], ((1,), (1,))).astype(BF16)
    hidden = MEAN_HIDDEN_SIZE
    deep = hidden * count
    spread = zero_one(
        iota((2 * hidden, deep), 1) // count == iota((2 * hidden, deep), 0)
    )
    left = mul(opm, spread)
    left = jnp.where(
        iota((tokens, deep), 0) % count == iota((tokens, deep), 1) % count, left, 0.0
    ).astype(BF16)
    gather = zero_one(iota((residues, tokens), 1) // count == iota((residues, tokens), 0))
    left = mul(gather, left).astype(BF16)
    right = opm[:, hidden:]
    for c in range(0, hidden, 2):
        pair_w = jnp.concatenate(
            [outer_w[(c + k) * hidden : (c + k + 1) * hidden, :] for k in range(2)], axis=1
        )
        part = mul(right, pair_w)
        lifted[c], lifted[c + 1] = part[:, :pair_width], part[:, pair_width:]
    for j in range(0, residues, 2):
        part = jnp.concatenate(
            [
                lifted[:, (j + k) * count : (j + k + 1) * count, :].reshape(deep, pair_width)
                for k in range(2)
            ],
            axis=1,
        )
        part = mul(left, part.astype(BF16)) * (1.0 / count)
        for k in range(2):
            rows = state[pl.ds(j + k, residues, stride=residues), :]
            one_ref[j + k] = rows + part[:, k * pair_width : (k + 1) * pair_width]


def pair_kernel(*refs):
    last, packets, partial, column, own_mask = refs[0], refs[1:4], refs[4], refs[5], refs[6]
    proj, gates, gate_out, w_out, out_ref, one, rest, right_at, left_at, valid = refs[7:]
    res_dev, residues, width = last.shape
    n = residues // res_dev
    per = (packets[0].shape[0] - SMALL_ROWS) // residues
    me = lax.axis_index("axial")
    own_valid = own_mask[...].astype(F32)
    for packet, r in zip((None, *packets), (0, *PACKET_ORDER)):
        shown = split_small(packet, residues, res_dev, per)[1] if r else own_valid
        valid[pl.ds(pl.multiple_of((me ^ r) * res_dev, res_dev), res_dev), :] = shown
    rest[...] = last[...].astype(F32).reshape(res_dev * residues, width)
    one[...] = partial[...].reshape(residues * residues, width)
    for k in range(residues):
        rows = pl.ds(pl.multiple_of(k * residues + (me ^ 3) * res_dev, res_dev), res_dev)
        one[rows, :] += rest[pl.ds(k, res_dev, stride=residues), :]

    shown = mul(valid[...].astype(BF16), column[...])
    right_w = jnp.concatenate([proj[:, C_TRI:], gates[:, C_TRI:]], axis=1)
    step = 8
    for k in range(0, residues, step):
        here = slice(k * residues, (k + step) * residues)
        both = mul(normal(one[here, :]).astype(BF16), right_w)
        both = sigmoid(both[:, C_TRI:]) * both[:, :C_TRI]
        for p in range(step):
            part = both[p * residues : (p + 1) * residues]
            part = part * shown[:, (k + p) * C_TRI : (k + p + 1) * C_TRI]
            right_at[(k + p) * residues : (k + p + 1) * residues, :] = part.astype(BF16).astype(F32)

    own = jnp.concatenate(
        [one[pl.ds(me * res_dev + i, residues, stride=residues), :] for i in range(res_dev)],
        axis=0,
    )
    left_w = jnp.concatenate([proj[:, :C_TRI], gates[:, :C_TRI], gate_out[...]], axis=1)
    own_all = mul(normal(own).astype(BF16), left_w)
    own_gate = sigmoid(own_all[:, 2 * C_TRI :])
    left = sigmoid(own_all[:, C_TRI : 2 * C_TRI]) * own_all[:, :C_TRI]
    shown = mul(own_valid.astype(BF16), column[:res_dev, : res_dev * C_TRI], ((0,), (0,)))
    for i in range(res_dev):
        part = left[i * residues : (i + 1) * residues] * shown[:, i * C_TRI : (i + 1) * C_TRI]
        left_at[i * residues : (i + 1) * residues, :] = part.astype(BF16).astype(F32)
    sums = [jnp.zeros((residues, C_TRI), F32) for _ in range(res_dev)]
    for k in range(residues):
        other = right_at[k * residues : (k + 1) * residues, :]
        for i in range(res_dev):
            sums[i] += left_at[i * residues + k : i * residues + k + 1, :] * other
    mixed = normal(jnp.concatenate(sums, axis=0)).astype(BF16)
    result = own + own_gate * mul(mixed, w_out[...])
    out_ref[...] = result.reshape(res_dev, residues, width).astype(BF16)


def call(kernel, out_shape, scratch, vmem_mib, *args):
    vmem = pl.BlockSpec(memory_space=pltpu.VMEM)
    return pl.pallas_call(
        kernel,
        out_shape=out_shape,
        in_specs=[vmem] * len(args),
        out_specs=jax.tree.map(lambda _: vmem, out_shape),
        scratch_shapes=scratch,
        compiler_params=pltpu.CompilerParams(vmem_limit_bytes=vmem_mib * 1024 * 1024),
        cost_estimate=pl.CostEstimate(flops=FLOPS, bytes_accessed=0, transcendentals=0),
    )(*args)


def swap(array, r, n):
    return lax.ppermute(array, "axial", [(i, i ^ r) for i in range(n)])


def local_whole(
    homolog_activity,
    homolog_symbol_ids,
    residue_present_mask,
    pair_state,
    pair_valid_mask,
    symbol_lookup_matrix,
    row_query_weight,
    horizontal_attention_matrix,
    pair_bias_weight,
    horizontal_final_matrix,
    column_query_weight,
    vertical_attention_matrix,
    vertical_final_matrix,
    tensor_mean_lift_matrix,
    outer_product_output_weight,
    triangle_projection_weight,
    triangle_projection_gate,
    triangle_output_gate,
    triangle_output_weight,
):
    n = lax.axis_size("axial")
    per, residues, width = homolog_activity.shape
    res_dev, _, pair_width = pair_state.shape
    count = per * n
    bias_weight = pair_bias_weight.T
    pair_2, pair_1 = swap(pair_state, 2, n), swap(pair_state, 1, n)
    shift, turn, column = call(
        functools.partial(table_kernel, FOCUS_TOTAL * res_dev, count),
        (
            jax.ShapeDtypeStruct((residues, 128), BF16),
            jax.ShapeDtypeStruct((count * residues, count * residues), BF16),
            jax.ShapeDtypeStruct((residues, residues * C_TRI), BF16),
        ),
        [],
        2,
    )
    packet, hidden_keys = call(
        packet_kernel,
        (
            jax.ShapeDtypeStruct((per * residues + SMALL_ROWS, width), BF16),
            jax.ShapeDtypeStruct((residues, FOCUS_TOTAL * residues), F32),
        ),
        [],
        4,
        pair_state,
        bias_weight,
        pair_valid_mask,
        homolog_symbol_ids,
        homolog_activity,
        residue_present_mask.reshape(1, residues),
        shift,
    )
    packets = [swap(packet, r, n) for r in PACKET_ORDER]
    pair_3 = swap(pair_2, 1, n)
    alignment, partial = call(
        functools.partial(msa_kernel, n),
        (
            jax.ShapeDtypeStruct((count, res_dev, width), BF16),
            jax.ShapeDtypeStruct((residues, residues, pair_width), F32),
        ),
        [
            pltpu.VMEM((count * residues, width), F32),
            pltpu.VMEM((MEAN_HIDDEN_SIZE, count * residues, pair_width), F32),
            pltpu.VMEM((residues * residues, pair_width), F32),
        ],
        16,
        *packets,
        turn,
        hidden_keys,
        pair_state,
        bias_weight,
        homolog_activity,
        homolog_symbol_ids,
        symbol_lookup_matrix,
        row_query_weight,
        horizontal_attention_matrix,
        horizontal_final_matrix,
        column_query_weight,
        vertical_attention_matrix,
        vertical_final_matrix,
        tensor_mean_lift_matrix.T,
        outer_product_output_weight,
        pair_1,
        pair_2,
    )
    pair_output = call(
        pair_kernel,
        jax.ShapeDtypeStruct((res_dev, residues, pair_width), BF16),
        [
            pltpu.VMEM((residues * residues, pair_width), F32),
            pltpu.VMEM((res_dev * residues, pair_width), F32),
            pltpu.VMEM((residues * residues, C_TRI), F32),
            pltpu.VMEM((res_dev * residues, C_TRI), F32),
            pltpu.VMEM((residues, residues), F32),
        ],
        16,
        pair_3,
        *packets,
        partial,
        column,
        pair_valid_mask,
        triangle_projection_weight,
        triangle_projection_gate,
        triangle_output_gate,
        triangle_output_weight,
    )
    return (alignment, pair_output)


def local(homolog_activity, homolog_symbol_ids, residue_present_mask, pair_state, *others):
    n = lax.axis_size("axial")
    per, residues, _ = homolog_activity.shape
    small = n == 4 and per * n == 8 and residues == 32
    plan = local_whole if small else local_sharded
    return plan(homolog_activity, homolog_symbol_ids, residue_present_mask, pair_state, *others)


def solution(mesh):
    parts, copied = P(("dp", "axial")), P()
    return jax.shard_map(
        local,
        mesh=mesh,
        in_specs=(parts, parts, P("dp"), parts, parts) + (copied,) * 14,
        out_specs=(P("dp", "axial", None), P(("dp", "axial"), None, None)),
        check_vma=False,
    )
```

```python
import functools

import jax
import jax.numpy as jnp
from jax import lax
from jax.experimental import pallas as pl
from jax.experimental.pallas import tpu as pltpu
from jax.sharding import PartitionSpec as P

FOCUS_TOTAL = 8
FOCUS_SIZE = 32
MEAN_HIDDEN_SIZE = 32
C_TRI = 128


def layer_normalize(attended_entries):
    attended_entries = attended_entries.astype(jnp.float32)
    mean = jnp.mean(attended_entries, axis=-1, keepdims=True)
    centred = attended_entries - mean
    var = jnp.mean(centred * centred, axis=-1, keepdims=True)
    return centred * lax.rsqrt(var + 1e-05)


def gated_attend(evoformer_block, extra_axes, w_query, w_kvg, w_out):
    lines_list, residue_length, input_width = evoformer_block.shape
    width = FOCUS_TOTAL * FOCUS_SIZE
    flat = (
        layer_normalize(evoformer_block)
        .astype(jnp.bfloat16)
        .reshape(lines_list * residue_length, input_width)
    )
    query = (
        jnp.dot(flat, w_query, preferred_element_type=jnp.float32) * FOCUS_SIZE ** (-0.5)
    ).astype(jnp.bfloat16)
    query = query.reshape(lines_list, residue_length, FOCUS_TOTAL, FOCUS_SIZE)
    kvg = jnp.dot(flat, w_kvg, preferred_element_type=jnp.float32)
    keys = (
        kvg[:, :width]
        .astype(jnp.bfloat16)
        .reshape(lines_list, residue_length, FOCUS_TOTAL, FOCUS_SIZE)
    )
    attended_entries = (
        kvg[:, width : 2 * width]
        .astype(jnp.bfloat16)
        .reshape(lines_list, residue_length, FOCUS_TOTAL, FOCUS_SIZE)
    )
    gate = jax.nn.sigmoid(kvg[:, 2 * width :]).reshape(
        lines_list, residue_length, FOCUS_TOTAL, FOCUS_SIZE
    )
    scores = (
        jnp.einsum("bihd,bjhd->bhij", query, keys, preferred_element_type=jnp.float32) + extra_axes
    )
    top = jnp.max(scores, axis=-1, keepdims=True)
    expo = jnp.exp(scores - top)
    weights = (expo / jnp.sum(expo, axis=-1, keepdims=True)).astype(jnp.bfloat16)
    mixed = jnp.einsum(
        "bhij,bjhd->bihd", weights, attended_entries, preferred_element_type=jnp.float32
    )
    mixed = (mixed * gate).astype(jnp.bfloat16).reshape(lines_list * residue_length, width)
    return evoformer_block + jnp.dot(mixed, w_out, preferred_element_type=jnp.float32).reshape(
        lines_list, residue_length, input_width
    )


def finish_sums(evoformer_block, triangle_output_weight):
    mixed = layer_normalize(jnp.transpose(evoformer_block, (1, 2, 0))).astype(jnp.bfloat16)
    return jnp.einsum(
        "ijc,cz->ijz", mixed, triangle_output_weight, preferred_element_type=jnp.float32
    )


def local_sharded(
    homolog_activity,
    homolog_symbol_ids,
    residue_present_mask,
    pair_state,
    pair_valid_mask,
    symbol_lookup_matrix,
    row_query_weight,
    horizontal_attention_matrix,
    pair_bias_weight,
    horizontal_final_matrix,
    column_query_weight,
    vertical_attention_matrix,
    vertical_final_matrix,
    tensor_mean_lift_matrix,
    outer_product_output_weight,
    triangle_projection_weight,
    triangle_projection_gate,
    triangle_output_gate,
    triangle_output_weight,
):
    sequence_per_device, residue_length, input_width = homolog_activity.shape
    res_dev = pair_state.shape[0]
    group_size = lax.axis_size("axial")
    token_classes = symbol_lookup_matrix.shape[0]
    token_one_hot = (
        homolog_symbol_ids[..., None] == jnp.arange(token_classes, dtype=jnp.int32)
    ).astype(jnp.bfloat16)
    token_embedded = jnp.einsum(
        "slt,tc->slc", token_one_hot, symbol_lookup_matrix, preferred_element_type=jnp.float32
    )
    homolog_starting = homolog_activity.astype(jnp.float32) + token_embedded
    pair_norm = layer_normalize(pair_state).astype(jnp.bfloat16)
    bias_rows = jnp.einsum(
        "ijc,ch->hij", pair_norm, pair_bias_weight, preferred_element_type=jnp.float32
    ).astype(jnp.bfloat16)
    bias_full = lax.all_gather(bias_rows, "axial", axis=1, tiled=True)
    key_bias = 1000000000.0 * (residue_present_mask.astype(jnp.float32) - 1.0)
    extra_axes = bias_full.astype(jnp.float32)[None] + key_bias[None, None, None, :]
    cluster_total = homolog_starting.reshape(
        sequence_per_device // 2, 2, residue_length, input_width
    )
    homolog_across_update = lax.map(
        lambda evoformer_block: gated_attend(
            evoformer_block,
            extra_axes,
            row_query_weight,
            horizontal_attention_matrix,
            horizontal_final_matrix,
        ),
        cluster_total,
    )
    homolog_across_update = homolog_across_update.reshape(
        sequence_per_device, group_size, res_dev, input_width
    ).astype(jnp.bfloat16)
    moved = jnp.swapaxes(
        lax.all_to_all(homolog_across_update, "axial", split_axis=1, concat_axis=0, tiled=True)[
            :, 0
        ],
        0,
        1,
    )
    finished = lax.map(
        lambda item: gated_attend(
            item[None].astype(jnp.float32),
            0.0,
            column_query_weight,
            vertical_attention_matrix,
            vertical_final_matrix,
        )[0],
        moved,
    )
    exchanged = jnp.swapaxes(finished, 0, 1).astype(jnp.bfloat16)[:, None]
    sequence_count = exchanged.shape[0]
    alignment_after_columns = exchanged.reshape(sequence_count, res_dev, input_width)
    tensor_mean_scaler = layer_normalize(alignment_after_columns).astype(jnp.bfloat16)
    split_parts = jnp.einsum(
        "src,cf->rsf",
        tensor_mean_scaler,
        tensor_mean_lift_matrix,
        preferred_element_type=jnp.float32,
    ).astype(jnp.bfloat16)
    first_factor = split_parts[..., :MEAN_HIDDEN_SIZE]
    second_factor = split_parts[..., MEAN_HIDDEN_SIZE:].reshape(
        res_dev, sequence_count * MEAN_HIDDEN_SIZE
    )
    step_rows = 8
    left_blocks = first_factor.reshape(
        res_dev // step_rows, step_rows, sequence_count, MEAN_HIDDEN_SIZE
    )
    piece = lax.all_gather(second_factor, "axial", axis=0, tiled=True)
    count = piece.shape[0]
    right_part = piece.reshape(count, sequence_count, MEAN_HIDDEN_SIZE)

    def one_block(lines_list):
        tensor_mean = (
            jnp.einsum("isc,jsd->ijcd", lines_list, right_part, preferred_element_type=jnp.float32)
            / sequence_count
        )
        tensor_mean = tensor_mean.reshape(
            step_rows, count, MEAN_HIDDEN_SIZE * MEAN_HIDDEN_SIZE
        ).astype(jnp.bfloat16)
        return jnp.einsum(
            "ijf,fz->ijz",
            tensor_mean,
            outer_product_output_weight,
            preferred_element_type=jnp.float32,
        )

    update = lax.map(one_block, left_blocks).reshape(
        res_dev, count, outer_product_output_weight.shape[1]
    )
    pair_one = pair_state.astype(jnp.float32) + update
    tri_norm = layer_normalize(pair_one).astype(jnp.bfloat16)
    proj = jnp.einsum(
        "ikc,cf->fik", tri_norm, triangle_projection_weight, preferred_element_type=jnp.float32
    )
    gates = jnp.einsum(
        "ikc,cf->fik", tri_norm, triangle_projection_gate, preferred_element_type=jnp.float32
    )
    both = (jax.nn.sigmoid(gates) * proj * pair_valid_mask.astype(jnp.float32)[None]).astype(
        jnp.bfloat16
    )
    left_tri = both[:C_TRI]
    right_tri = both[C_TRI:]
    moved_left, moved_right = (
        lax.all_to_all(left_tri, "axial", split_axis=0, concat_axis=1, tiled=True),
        lax.all_to_all(right_tri, "axial", split_axis=0, concat_axis=1, tiled=True),
    )
    partial_sum = jnp.einsum(
        "cik,cjk->cij", moved_left, moved_right, preferred_element_type=jnp.float32
    )
    tri_sum = lax.all_to_all(
        partial_sum.astype(jnp.bfloat16), "axial", split_axis=1, concat_axis=0, tiled=True
    ).astype(partial_sum.dtype)
    tri_update = finish_sums(tri_sum, triangle_output_weight)
    out_gate = jax.nn.sigmoid(
        jnp.einsum(
            "ijc,cz->ijz", tri_norm, triangle_output_gate, preferred_element_type=jnp.float32
        )
    )
    pair_output = (pair_one + out_gate * tri_update).astype(jnp.bfloat16)
    return (alignment_after_columns, pair_output)


BF16 = jnp.bfloat16
F32 = jnp.float32
SMALL_ROWS = 16
FLOPS = 3 * 10**9
PACKET_ORDER = (3, 2, 1)
PAIR_ORDER = (2, 1, 3)


def mul(lhs, rhs, over=((1,), (0,))):
    return lax.dot_general(lhs, rhs, (over, ((), ())), preferred_element_type=F32)


def iota(shape, axis):
    return lax.broadcasted_iota(jnp.int32, shape, axis)


def zero_one(condition):
    return jnp.where(condition, 1.0, 0.0).astype(BF16)


def normal(x):
    mean = jnp.mean(x, axis=-1, keepdims=True)
    centred = x - mean
    var = jnp.mean(centred * centred, axis=-1, keepdims=True)
    return centred * lax.rsqrt(var + 1e-05)


def sigmoid(x):
    return 1.0 / (1.0 + jnp.exp(-x))


def column_softmax(scores):
    expo = jnp.exp(scores - jnp.max(scores, axis=0, keepdims=True))
    return expo * (1.0 / jnp.sum(expo, axis=0, keepdims=True))


def head_masks(width):
    return [
        zero_one(iota((1, width), 1) // FOCUS_SIZE == h) for h in range(FOCUS_TOTAL)
    ]


def bias_rows(pair_ref, weight_ref):
    rows, residues, width = pair_ref.shape
    lanes = FOCUS_TOTAL * rows
    spread = zero_one(iota((FOCUS_TOTAL, lanes), 1) // rows == iota((FOCUS_TOTAL, lanes), 0))
    row_of = iota((width, lanes), 1) % rows
    flat = normal(pair_ref[...].astype(F32).reshape(rows * residues, width)).astype(BF16)
    weight = mul(weight_ref[...], spread, ((0,), (0,)))
    bias = jnp.zeros((residues, lanes), F32)
    for i in range(rows):
        one_row = jnp.where(row_of == i, weight, 0.0).astype(BF16)
        bias += mul(flat[i * residues : (i + 1) * residues], one_row)
    return bias


def table_kernel(lanes, count, shift_ref, turn_ref, column_ref):
    shape = column_ref.shape
    column_ref[...] = zero_one(iota(shape, 1) // C_TRI == iota(shape, 0))
    shape = shift_ref.shape
    shift_ref[...] = zero_one(iota(shape, 1) == iota(shape, 0) + lanes)
    shape = turn_ref.shape
    row_at = iota(shape, 0)
    turn_ref[...] = zero_one(
        iota(shape, 1) == (row_at % count) * (shape[0] // count) + row_at // count
    )


def packet_kernel(*refs):
    pair_ref, weight_ref, valid_ref, ids_ref, act_ref, present_ref, shift_ref = refs[:7]
    packet_ref, hidden_ref = refs[7:]
    rows, residues, width = pair_ref.shape
    per, _, features = act_ref.shape
    lanes = FOCUS_TOTAL * rows
    bias = bias_rows(pair_ref, weight_ref)
    extra = jnp.concatenate(
        [
            valid_ref[...].astype(F32),
            ids_ref[...].astype(F32),
            jnp.zeros((SMALL_ROWS - rows - per, residues), F32),
        ],
        axis=0,
    )
    extra = mul(extra.astype(BF16), shift_ref[...])
    empty = jnp.zeros((SMALL_ROWS, 128 - lanes), F32)
    first = jnp.concatenate([bias[:SMALL_ROWS], empty], axis=1) + extra
    second = jnp.concatenate([bias[SMALL_ROWS:], empty], axis=1)
    small = jnp.concatenate([first, second], axis=1).astype(BF16)
    packet_ref[per * residues :, :] = small
    shown = present_ref[...].astype(F32).astype(BF16)
    shown = mul(shown, jnp.ones((1, hidden_ref.shape[1]), BF16), ((0,), (0,)))
    hidden_ref[...] = 1000000000.0 * (shown - 1.0)
    packet_ref[: per * residues, :] = act_ref[...].reshape(per * residues, features)


def split_small(packet, residues, res_dev, per):
    small = packet[per * residues :, :].astype(F32)
    lanes = FOCUS_TOTAL * res_dev
    bias = jnp.concatenate([small[:, :lanes], small[:, 128 : 128 + lanes]], axis=0)
    extra = small[:, lanes : lanes + residues]
    return bias, extra[:res_dev], extra[res_dev : res_dev + per]


def project(x, w_query, w_kvg):
    width = FOCUS_TOTAL * FOCUS_SIZE
    flat = normal(x).astype(BF16)
    query = (mul(flat, w_query[...]) * FOCUS_SIZE ** (-0.5)).astype(BF16)
    keys = mul(flat, w_kvg[:, :width]).astype(BF16)
    values = mul(flat, w_kvg[:, width : 2 * width]).astype(BF16)
    gate = sigmoid(mul(flat, w_kvg[:, 2 * width :]))
    return query, keys, values, gate


def msa_kernel(n, *refs):
    packets, refs = refs[: n - 1], refs[n - 1 :]
    turn, hidden_keys, pair, pair_w, act, ids, table = refs[:7]
    row_q, row_kvg, row_out, col_q, col_kvg, col_out, lift, outer_w = refs[7:15]
    align_ref, update_ref, start, lifted = refs[15:]
    per, residues, width = act.shape
    res_dev = pair.shape[0]
    kinds = table.shape[0]
    pair_width = pair.shape[2]
    count = per * n
    tokens = count * residues
    lanes = FOCUS_TOTAL * residues
    me = lax.axis_index("axial")
    masks = head_masks(width)

    place = iota((FOCUS_TOTAL * res_dev, lanes), 0)
    place = (place // res_dev) * residues + place % res_dev - iota(place.shape, 1)
    extra = jnp.zeros((residues, lanes), F32)
    for packet, r in zip((None, *packets), (0, *PACKET_ORDER)):
        owner = me ^ r
        if r == 0:
            bias, all_ids = bias_rows(pair, pair_w), ids[...].astype(F32)
        else:
            bias, _, all_ids = split_small(packet, residues, res_dev, per)
        extra += mul(bias.astype(BF16), zero_one(place == -owner * res_dev))
        for q in range(per):
            hot = zero_one(iota((kinds, residues), 0).astype(F32) == all_ids[q : q + 1])
            rows = act[q] if r == 0 else packet[q * residues : (q + 1) * residues, :]
            start[pl.ds(pl.multiple_of((owner * per + q) * residues, residues), residues), :] = (
                rows.astype(F32) + mul(hot, table[...], ((0,), (0,)))
            )
    extra = extra + hidden_keys[...]

    zero = start[...]
    query, keys, values, gate = project(zero, row_q, row_kvg)
    rows = []
    for s in range(count):
        here = slice(s * residues, (s + 1) * residues)
        spread = jnp.concatenate([query[here] * mask for mask in masks], axis=0)
        weights = column_softmax(mul(keys[here], spread, ((1,), (1,))) + extra).astype(BF16)
        heads = mul(weights, values[here], ((0,), (0,)))
        mixed = jnp.zeros((residues, width), F32)
        for h in range(FOCUS_TOTAL):
            part = heads[h * residues : (h + 1) * residues]
            mixed = jnp.where(iota((1, width), 1) // FOCUS_SIZE == h, part, mixed)
        rows.append(mixed)
    mixed = (jnp.concatenate(rows, axis=0) * gate).astype(BF16)
    msa_one = (zero + mul(mixed, row_out[...])).astype(BF16)

    one = mul(turn[...], msa_one)
    query, keys, values, gate = project(one, col_q, col_kvg)
    group = min(tokens, 128)
    sites = group // count
    same = iota((sites, count, group), 2) // count == iota((sites, count, group), 0)
    groups = []
    for g in range(tokens // group):
        here = slice(g * group, (g + 1) * group)
        all_weights, all_values = [], []
        for mask in masks:
            scores = mul(keys[here], query[here] * mask, ((1,), (1,)))
            scores = jnp.sum(jnp.where(same, scores.reshape(sites, count, group), 0.0), axis=0)
            weights = column_softmax(scores)
            weights = jnp.where(same, weights[None], 0.0).reshape(group, group)
            all_weights.append(weights.astype(BF16))
            all_values.append(values[here] * mask)
        groups.append(
            mul(
                jnp.concatenate(all_weights, axis=0),
                jnp.concatenate(all_values, axis=0),
                ((0,), (0,)),
            )
        )
    mixed = (jnp.concatenate(groups, axis=0) * gate).astype(BF16)
    align = (one + mul(mixed, col_out[...])).astype(BF16)
    own = count * res_dev
    row_at, lane_at = iota((own, tokens), 0), iota((own, tokens), 1)
    pick = zero_one(
        lane_at == (row_at % res_dev + me * res_dev) * count + row_at // res_dev
    )
    align_ref[...] = mul(pick, align).reshape(count, res_dev, width).astype(BF16)

    opm = normal(align.astype(F32)).astype(BF16)
    opm = mul(opm, lift[...], ((1,), (1,))).astype(BF16)
    hidden = MEAN_HIDDEN_SIZE
    deep = hidden * count
    spread = zero_one(
        iota((2 * hidden, deep), 1) // count == iota((2 * hidden, deep), 0)
    )
    left = mul(opm, spread)
    left = jnp.where(
        iota((tokens, deep), 0) % count == iota((tokens, deep), 1) % count, left, 0.0
    ).astype(BF16)
    gather = zero_one(iota((residues, tokens), 1) // count == iota((residues, tokens), 0))
    left = mul(gather, left).astype(BF16)
    right = opm[:, hidden:]
    for c in range(0, hidden, 2):
        pair_w = jnp.concatenate(
            [outer_w[(c + k) * hidden : (c + k + 1) * hidden, :] for k in range(2)], axis=1
        )
        part = mul(right, pair_w)
        lifted[c], lifted[c + 1] = part[:, :pair_width], part[:, pair_width:]
    for j in range(0, residues, 2):
        part = jnp.concatenate(
            [
                lifted[:, (j + k) * count : (j + k + 1) * count, :].reshape(deep, pair_width)
                for k in range(2)
            ],
            axis=1,
        )
        part = mul(left, part.astype(BF16)) * (1.0 / count)
        update_ref[j], update_ref[j + 1] = part[:, :pair_width], part[:, pair_width:]


def pair_kernel(*refs):
    pairs, packets, update, column, pair, own_mask = refs[:3], refs[3:6], *refs[6:10]
    proj, gates, gate_out, w_out, out_ref, state, one, right_at, left_at, valid = refs[10:]
    res_dev, residues, width = pair.shape
    per = (packets[0].shape[0] - SMALL_ROWS) // residues
    me = lax.axis_index("axial")
    own_valid = own_mask[...].astype(F32)
    for packet, r in zip((None, *packets), (0, *PACKET_ORDER)):
        shown = split_small(packet, residues, res_dev, per)[1] if r else own_valid
        valid[pl.ds(pl.multiple_of((me ^ r) * res_dev, res_dev), res_dev), :] = shown
    size = res_dev * residues
    for block, r in zip((pair, *pairs), (0, *PAIR_ORDER)):
        state[pl.ds(pl.multiple_of((me ^ r) * size, size), size), :] = (
            block[...].astype(F32).reshape(size, width)
        )
    for k in range(residues):
        one[k * residues : (k + 1) * residues, :] = (
            state[pl.ds(k, residues, stride=residues), :] + update[k]
        )

    shown = mul(valid[...].astype(BF16), column[...])
    right_w = jnp.concatenate([proj[:, C_TRI:], gates[:, C_TRI:]], axis=1)
    step = 8
    for k in range(0, residues, step):
        here = slice(k * residues, (k + step) * residues)
        both = mul(normal(one[here, :]).astype(BF16), right_w)
        both = sigmoid(both[:, C_TRI:]) * both[:, :C_TRI]
        for p in range(step):
            part = both[p * residues : (p + 1) * residues]
            part = part * shown[:, (k + p) * C_TRI : (k + p + 1) * C_TRI]
            right_at[(k + p) * residues : (k + p + 1) * residues, :] = part.astype(BF16).astype(F32)

    own = jnp.concatenate(
        [one[pl.ds(me * res_dev + i, residues, stride=residues), :] for i in range(res_dev)],
        axis=0,
    )
    left_w = jnp.concatenate([proj[:, :C_TRI], gates[:, :C_TRI], gate_out[...]], axis=1)
    own_all = mul(normal(own).astype(BF16), left_w)
    own_gate = sigmoid(own_all[:, 2 * C_TRI :])
    left = sigmoid(own_all[:, C_TRI : 2 * C_TRI]) * own_all[:, :C_TRI]
    shown = mul(own_valid.astype(BF16), column[:res_dev, : res_dev * C_TRI], ((0,), (0,)))
    for i in range(res_dev):
        part = left[i * residues : (i + 1) * residues] * shown[:, i * C_TRI : (i + 1) * C_TRI]
        left_at[i * residues : (i + 1) * residues, :] = part.astype(BF16).astype(F32)
    sums = [jnp.zeros((residues, C_TRI), F32) for _ in range(res_dev)]
    for k in range(residues):
        other = right_at[k * residues : (k + 1) * residues, :]
        for i in range(res_dev):
            sums[i] += left_at[i * residues + k : i * residues + k + 1, :] * other
    mixed = normal(jnp.concatenate(sums, axis=0)).astype(BF16)
    result = own + own_gate * mul(mixed, w_out[...])
    out_ref[...] = result.reshape(res_dev, residues, width).astype(BF16)


def call(kernel, out_shape, scratch, vmem_mib, *args):
    vmem = pl.BlockSpec(memory_space=pltpu.VMEM)
    return pl.pallas_call(
        kernel,
        out_shape=out_shape,
        in_specs=[vmem] * len(args),
        out_specs=jax.tree.map(lambda _: vmem, out_shape),
        scratch_shapes=scratch,
        compiler_params=pltpu.CompilerParams(vmem_limit_bytes=vmem_mib * 1024 * 1024),
        cost_estimate=pl.CostEstimate(flops=FLOPS, bytes_accessed=0, transcendentals=0),
    )(*args)


def swap(array, r, n):
    return lax.ppermute(array, "axial", [(i, i ^ r) for i in range(n)])


def local_whole(
    homolog_activity,
    homolog_symbol_ids,
    residue_present_mask,
    pair_state,
    pair_valid_mask,
    symbol_lookup_matrix,
    row_query_weight,
    horizontal_attention_matrix,
    pair_bias_weight,
    horizontal_final_matrix,
    column_query_weight,
    vertical_attention_matrix,
    vertical_final_matrix,
    tensor_mean_lift_matrix,
    outer_product_output_weight,
    triangle_projection_weight,
    triangle_projection_gate,
    triangle_output_gate,
    triangle_output_weight,
):
    n = lax.axis_size("axial")
    per, residues, width = homolog_activity.shape
    res_dev, _, pair_width = pair_state.shape
    count = per * n
    bias_weight = pair_bias_weight.T
    shift, turn, column = call(
        functools.partial(table_kernel, FOCUS_TOTAL * res_dev, count),
        (
            jax.ShapeDtypeStruct((residues, 128), BF16),
            jax.ShapeDtypeStruct((count * residues, count * residues), BF16),
            jax.ShapeDtypeStruct((residues, residues * C_TRI), BF16),
        ),
        [],
        2,
    )
    packet, hidden_keys = call(
        packet_kernel,
        (
            jax.ShapeDtypeStruct((per * residues + SMALL_ROWS, width), BF16),
            jax.ShapeDtypeStruct((residues, FOCUS_TOTAL * residues), F32),
        ),
        [],
        4,
        pair_state,
        bias_weight,
        pair_valid_mask,
        homolog_symbol_ids,
        homolog_activity,
        residue_present_mask.reshape(1, residues),
        shift,
    )
    packets = [swap(packet, r, n) for r in PACKET_ORDER]
    _, later = lax.optimization_barrier((packet, pair_state))
    pairs = [swap(later, r, n) for r in PAIR_ORDER]
    alignment, update = call(
        functools.partial(msa_kernel, n),
        (
            jax.ShapeDtypeStruct((count, res_dev, width), BF16),
            jax.ShapeDtypeStruct((residues, residues, pair_width), F32),
        ),
        [
            pltpu.VMEM((count * residues, width), F32),
            pltpu.VMEM((MEAN_HIDDEN_SIZE, count * residues, pair_width), F32),
        ],
        16,
        *packets,
        turn,
        hidden_keys,
        pair_state,
        bias_weight,
        homolog_activity,
        homolog_symbol_ids,
        symbol_lookup_matrix,
        row_query_weight,
        horizontal_attention_matrix,
        horizontal_final_matrix,
        column_query_weight,
        vertical_attention_matrix,
        vertical_final_matrix,
        tensor_mean_lift_matrix.T,
        outer_product_output_weight,
    )
    pair_output = call(
        pair_kernel,
        jax.ShapeDtypeStruct((res_dev, residues, pair_width), BF16),
        [
            pltpu.VMEM((residues * residues, pair_width), F32),
            pltpu.VMEM((residues * residues, pair_width), F32),
            pltpu.VMEM((residues * residues, C_TRI), F32),
            pltpu.VMEM((res_dev * residues, C_TRI), F32),
            pltpu.VMEM((residues, residues), F32),
        ],
        16,
        *pairs,
        *packets,
        update,
        column,
        pair_state,
        pair_valid_mask,
        triangle_projection_weight,
        triangle_projection_gate,
        triangle_output_gate,
        triangle_output_weight,
    )
    return (alignment, pair_output)


def local(homolog_activity, homolog_symbol_ids, residue_present_mask, pair_state, *others):
    n = lax.axis_size("axial")
    per, residues, _ = homolog_activity.shape
    small = n == 4 and per * n == 8 and residues == 32
    plan = local_whole if small else local_sharded
    return plan(homolog_activity, homolog_symbol_ids, residue_present_mask, pair_state, *others)


def solution(mesh):
    parts, copied = P(("dp", "axial")), P()
    return jax.shard_map(
        local,
        mesh=mesh,
        in_specs=(parts, parts, P("dp"), parts, parts) + (copied,) * 14,
        out_specs=(P("dp", "axial", None), P(("dp", "axial"), None, None)),
        check_vma=False,
    )
```

```python
import functools

import jax
import jax.numpy as jnp
from jax import lax
from jax.experimental import pallas as pl
from jax.experimental.pallas import tpu as pltpu
from jax.sharding import PartitionSpec as P

FOCUS_TOTAL = 8
FOCUS_SIZE = 32
MEAN_HIDDEN_SIZE = 32
C_TRI = 128


def layer_normalize(attended_entries):
    attended_entries = attended_entries.astype(jnp.float32)
    mean = jnp.mean(attended_entries, axis=-1, keepdims=True)
    centred = attended_entries - mean
    var = jnp.mean(centred * centred, axis=-1, keepdims=True)
    return centred * lax.rsqrt(var + 1e-05)


def gated_attend(evoformer_block, extra_axes, w_query, w_kvg, w_out):
    lines_list, residue_length, input_width = evoformer_block.shape
    width = FOCUS_TOTAL * FOCUS_SIZE
    flat = (
        layer_normalize(evoformer_block)
        .astype(jnp.bfloat16)
        .reshape(lines_list * residue_length, input_width)
    )
    query = (
        jnp.dot(flat, w_query, preferred_element_type=jnp.float32) * FOCUS_SIZE ** (-0.5)
    ).astype(jnp.bfloat16)
    query = query.reshape(lines_list, residue_length, FOCUS_TOTAL, FOCUS_SIZE)
    kvg = jnp.dot(flat, w_kvg, preferred_element_type=jnp.float32)
    keys = (
        kvg[:, :width]
        .astype(jnp.bfloat16)
        .reshape(lines_list, residue_length, FOCUS_TOTAL, FOCUS_SIZE)
    )
    attended_entries = (
        kvg[:, width : 2 * width]
        .astype(jnp.bfloat16)
        .reshape(lines_list, residue_length, FOCUS_TOTAL, FOCUS_SIZE)
    )
    gate = jax.nn.sigmoid(kvg[:, 2 * width :]).reshape(
        lines_list, residue_length, FOCUS_TOTAL, FOCUS_SIZE
    )
    scores = (
        jnp.einsum("bihd,bjhd->bhij", query, keys, preferred_element_type=jnp.float32) + extra_axes
    )
    top = jnp.max(scores, axis=-1, keepdims=True)
    expo = jnp.exp(scores - top)
    weights = (expo / jnp.sum(expo, axis=-1, keepdims=True)).astype(jnp.bfloat16)
    mixed = jnp.einsum(
        "bhij,bjhd->bihd", weights, attended_entries, preferred_element_type=jnp.float32
    )
    mixed = (mixed * gate).astype(jnp.bfloat16).reshape(lines_list * residue_length, width)
    return evoformer_block + jnp.dot(mixed, w_out, preferred_element_type=jnp.float32).reshape(
        lines_list, residue_length, input_width
    )


def finish_sums(evoformer_block, triangle_output_weight):
    mixed = layer_normalize(jnp.transpose(evoformer_block, (1, 2, 0))).astype(jnp.bfloat16)
    return jnp.einsum(
        "ijc,cz->ijz", mixed, triangle_output_weight, preferred_element_type=jnp.float32
    )


def local_sharded(
    homolog_activity,
    homolog_symbol_ids,
    residue_present_mask,
    pair_state,
    pair_valid_mask,
    symbol_lookup_matrix,
    row_query_weight,
    horizontal_attention_matrix,
    pair_bias_weight,
    horizontal_final_matrix,
    column_query_weight,
    vertical_attention_matrix,
    vertical_final_matrix,
    tensor_mean_lift_matrix,
    outer_product_output_weight,
    triangle_projection_weight,
    triangle_projection_gate,
    triangle_output_gate,
    triangle_output_weight,
):
    sequence_per_device, residue_length, input_width = homolog_activity.shape
    res_dev = pair_state.shape[0]
    group_size = lax.axis_size("axial")
    token_classes = symbol_lookup_matrix.shape[0]
    token_one_hot = (
        homolog_symbol_ids[..., None] == jnp.arange(token_classes, dtype=jnp.int32)
    ).astype(jnp.bfloat16)
    token_embedded = jnp.einsum(
        "slt,tc->slc", token_one_hot, symbol_lookup_matrix, preferred_element_type=jnp.float32
    )
    homolog_starting = homolog_activity.astype(jnp.float32) + token_embedded
    pair_norm = layer_normalize(pair_state).astype(jnp.bfloat16)
    bias_rows = jnp.einsum(
        "ijc,ch->hij", pair_norm, pair_bias_weight, preferred_element_type=jnp.float32
    ).astype(jnp.bfloat16)
    bias_full = lax.all_gather(bias_rows, "axial", axis=1, tiled=True)
    key_bias = 1000000000.0 * (residue_present_mask.astype(jnp.float32) - 1.0)
    extra_axes = bias_full.astype(jnp.float32)[None] + key_bias[None, None, None, :]
    cluster_total = homolog_starting.reshape(
        sequence_per_device // 2, 2, residue_length, input_width
    )
    homolog_across_update = lax.map(
        lambda evoformer_block: gated_attend(
            evoformer_block,
            extra_axes,
            row_query_weight,
            horizontal_attention_matrix,
            horizontal_final_matrix,
        ),
        cluster_total,
    )
    homolog_across_update = homolog_across_update.reshape(
        sequence_per_device, group_size, res_dev, input_width
    ).astype(jnp.bfloat16)
    moved = jnp.swapaxes(
        lax.all_to_all(homolog_across_update, "axial", split_axis=1, concat_axis=0, tiled=True)[
            :, 0
        ],
        0,
        1,
    )
    finished = lax.map(
        lambda item: gated_attend(
            item[None].astype(jnp.float32),
            0.0,
            column_query_weight,
            vertical_attention_matrix,
            vertical_final_matrix,
        )[0],
        moved,
    )
    exchanged = jnp.swapaxes(finished, 0, 1).astype(jnp.bfloat16)[:, None]
    sequence_count = exchanged.shape[0]
    alignment_after_columns = exchanged.reshape(sequence_count, res_dev, input_width)
    tensor_mean_scaler = layer_normalize(alignment_after_columns).astype(jnp.bfloat16)
    split_parts = jnp.einsum(
        "src,cf->rsf",
        tensor_mean_scaler,
        tensor_mean_lift_matrix,
        preferred_element_type=jnp.float32,
    ).astype(jnp.bfloat16)
    first_factor = split_parts[..., :MEAN_HIDDEN_SIZE]
    second_factor = split_parts[..., MEAN_HIDDEN_SIZE:].reshape(
        res_dev, sequence_count * MEAN_HIDDEN_SIZE
    )
    step_rows = 8
    left_blocks = first_factor.reshape(
        res_dev // step_rows, step_rows, sequence_count, MEAN_HIDDEN_SIZE
    )
    piece = lax.all_gather(second_factor, "axial", axis=0, tiled=True)
    count = piece.shape[0]
    right_part = piece.reshape(count, sequence_count, MEAN_HIDDEN_SIZE)

    def one_block(lines_list):
        tensor_mean = (
            jnp.einsum("isc,jsd->ijcd", lines_list, right_part, preferred_element_type=jnp.float32)
            / sequence_count
        )
        tensor_mean = tensor_mean.reshape(
            step_rows, count, MEAN_HIDDEN_SIZE * MEAN_HIDDEN_SIZE
        ).astype(jnp.bfloat16)
        return jnp.einsum(
            "ijf,fz->ijz",
            tensor_mean,
            outer_product_output_weight,
            preferred_element_type=jnp.float32,
        )

    update = lax.map(one_block, left_blocks).reshape(
        res_dev, count, outer_product_output_weight.shape[1]
    )
    pair_one = pair_state.astype(jnp.float32) + update
    tri_norm = layer_normalize(pair_one).astype(jnp.bfloat16)
    proj = jnp.einsum(
        "ikc,cf->fik", tri_norm, triangle_projection_weight, preferred_element_type=jnp.float32
    )
    gates = jnp.einsum(
        "ikc,cf->fik", tri_norm, triangle_projection_gate, preferred_element_type=jnp.float32
    )
    both = (jax.nn.sigmoid(gates) * proj * pair_valid_mask.astype(jnp.float32)[None]).astype(
        jnp.bfloat16
    )
    left_tri = both[:C_TRI]
    right_tri = both[C_TRI:]
    moved_left, moved_right = (
        lax.all_to_all(left_tri, "axial", split_axis=0, concat_axis=1, tiled=True),
        lax.all_to_all(right_tri, "axial", split_axis=0, concat_axis=1, tiled=True),
    )
    partial_sum = jnp.einsum(
        "cik,cjk->cij", moved_left, moved_right, preferred_element_type=jnp.float32
    )
    tri_sum = lax.all_to_all(
        partial_sum.astype(jnp.bfloat16), "axial", split_axis=1, concat_axis=0, tiled=True
    ).astype(partial_sum.dtype)
    tri_update = finish_sums(tri_sum, triangle_output_weight)
    out_gate = jax.nn.sigmoid(
        jnp.einsum(
            "ijc,cz->ijz", tri_norm, triangle_output_gate, preferred_element_type=jnp.float32
        )
    )
    pair_output = (pair_one + out_gate * tri_update).astype(jnp.bfloat16)
    return (alignment_after_columns, pair_output)


BF16 = jnp.bfloat16
F32 = jnp.float32
SMALL_ROWS = 16
FLOPS = 3 * 10**9
PACKET_ORDER = (3, 2, 1)
PAIR_ORDER = (2, 1, 3)


def mul(lhs, rhs, over=((1,), (0,))):
    return lax.dot_general(lhs, rhs, (over, ((), ())), preferred_element_type=F32)


def iota(shape, axis):
    return lax.broadcasted_iota(jnp.int32, shape, axis)


def zero_one(condition):
    return jnp.where(condition, 1.0, 0.0).astype(BF16)


def normal(x):
    mean = jnp.mean(x, axis=-1, keepdims=True)
    centred = x - mean
    var = jnp.mean(centred * centred, axis=-1, keepdims=True)
    return centred * lax.rsqrt(var + 1e-05)


def sigmoid(x):
    return 1.0 / (1.0 + jnp.exp(-x))


def column_softmax(scores):
    expo = jnp.exp(scores - jnp.max(scores, axis=0, keepdims=True))
    return expo * (1.0 / jnp.sum(expo, axis=0, keepdims=True))


def bias_rows(pair_ref, weight_ref):
    rows, residues, width = pair_ref.shape
    lanes = FOCUS_TOTAL * rows
    spread = zero_one(iota((FOCUS_TOTAL, lanes), 1) // rows == iota((FOCUS_TOTAL, lanes), 0))
    row_of = iota((width, lanes), 1) % rows
    flat = normal(pair_ref[...].astype(F32).reshape(rows * residues, width)).astype(BF16)
    weight = mul(weight_ref[...], spread, ((0,), (0,)))
    bias = jnp.zeros((residues, lanes), F32)
    for i in range(rows):
        one_row = jnp.where(row_of == i, weight, 0.0).astype(BF16)
        bias += mul(flat[i * residues : (i + 1) * residues], one_row)
    return bias


def table_kernel(lanes, count, shift_ref, turn_ref, column_ref):
    shape = column_ref.shape
    column_ref[...] = zero_one(iota(shape, 1) // C_TRI == iota(shape, 0))
    shape = shift_ref.shape
    shift_ref[...] = zero_one(iota(shape, 1) == iota(shape, 0) + lanes)
    shape = turn_ref.shape
    row_at = iota(shape, 0)
    turn_ref[...] = zero_one(
        iota(shape, 1) == (row_at % count) * (shape[0] // count) + row_at // count
    )


def packet_kernel(*refs):
    pair_ref, weight_ref, valid_ref, ids_ref, act_ref, present_ref, shift_ref = refs[:7]
    packet_ref, hidden_ref = refs[7:]
    rows, residues, width = pair_ref.shape
    per, _, features = act_ref.shape
    lanes = FOCUS_TOTAL * rows
    bias = bias_rows(pair_ref, weight_ref)
    extra = jnp.concatenate(
        [
            valid_ref[...].astype(F32),
            ids_ref[...].astype(F32),
            jnp.zeros((SMALL_ROWS - rows - per, residues), F32),
        ],
        axis=0,
    )
    extra = mul(extra.astype(BF16), shift_ref[...])
    empty = jnp.zeros((SMALL_ROWS, 128 - lanes), F32)
    first = jnp.concatenate([bias[:SMALL_ROWS], empty], axis=1) + extra
    second = jnp.concatenate([bias[SMALL_ROWS:], empty], axis=1)
    small = jnp.concatenate([first, second], axis=1).astype(BF16)
    packet_ref[per * residues :, :] = small
    shown = present_ref[...].astype(F32).astype(BF16)
    shown = mul(shown, jnp.ones((1, hidden_ref.shape[1]), BF16), ((0,), (0,)))
    hidden_ref[...] = 1000000000.0 * (shown - 1.0)
    packet_ref[: per * residues, :] = act_ref[...].reshape(per * residues, features)


def split_small(packet, residues, res_dev, per):
    small = packet[per * residues :, :].astype(F32)
    lanes = FOCUS_TOTAL * res_dev
    bias = jnp.concatenate([small[:, :lanes], small[:, 128 : 128 + lanes]], axis=0)
    extra = small[:, lanes : lanes + residues]
    return bias, extra[:res_dev], extra[res_dev : res_dev + per]


def project(x, w_query, w_kvg):
    width = FOCUS_TOTAL * FOCUS_SIZE
    flat = normal(x).astype(BF16)
    turned = ((0,), (1,))
    keys = mul(flat, w_kvg[:, :width]).astype(BF16)
    query = (mul(w_query[...], flat, turned) * FOCUS_SIZE ** (-0.5)).astype(BF16)
    values = mul(w_kvg[:, width : 2 * width], flat, turned).astype(BF16)
    gate = sigmoid(mul(w_kvg[:, 2 * width :], flat, turned))
    return keys, query, values, gate


def attend(keys, query, values, size, extra=None):
    width, tokens = query.shape
    group = min(tokens, 128)
    blocks = group // size
    together = 128 // FOCUS_SIZE
    block_of = iota((1, group), 1) // size
    groups = []
    for start in range(0, tokens, group):
        here = slice(start, start + group)
        heads = []
        for tile in range(0, width, 128):
            apart = []
            for p in range(together):
                row = tile + p * FOCUS_SIZE
                parts = [
                    jnp.zeros((p * FOCUS_SIZE, group), BF16),
                    query[row : row + FOCUS_SIZE, here],
                    jnp.zeros((128 - (p + 1) * FOCUS_SIZE, group), BF16),
                ]
                apart.append(jnp.concatenate([x for x in parts if x.shape[0]], axis=0))
            scores = mul(keys[here, tile : tile + 128], jnp.concatenate(apart, axis=1))
            for p in range(together):
                row = tile + p * FOCUS_SIZE
                full = scores[:, p * group : (p + 1) * group]
                own = full[:size]
                for b in range(1, blocks):
                    own = jnp.where(block_of == b, full[b * size : (b + 1) * size], own)
                if extra is not None:
                    own = own + extra[row // FOCUS_SIZE]
                weights = column_softmax(own)
                weights = jnp.concatenate(
                    [jnp.where(block_of == b, weights, 0.0) for b in range(blocks)], axis=0
                )
                heads.append(mul(values[row : row + FOCUS_SIZE, here], weights.astype(BF16)))
        groups.append(jnp.concatenate(heads, axis=0))
    return jnp.concatenate(groups, axis=1)


def msa_kernel(n, res_dev, *refs):
    packets, turn, hidden_keys, table = refs[:n], refs[n], refs[n + 1], refs[n + 2]
    refs = refs[n + 3 :]
    row_q, row_kvg, row_out, col_q, col_kvg, col_out, lift, outer_w = refs[:8]
    align_ref, update_ref, start, lifted = refs[8:]
    kinds, width = table.shape
    residues, lanes = hidden_keys.shape
    pair_width = outer_w.shape[1]
    per = (packets[0].shape[0] - SMALL_ROWS) // residues
    count = per * n
    tokens = count * residues
    me = lax.axis_index("axial")

    place = iota((FOCUS_TOTAL * res_dev, lanes), 0)
    place = (place // res_dev) * residues + place % res_dev - iota(place.shape, 1)
    bias = jnp.zeros((residues, lanes), F32)
    rows = []
    for packet, r in zip(packets, (0, *PACKET_ORDER)):
        part, _, all_ids = split_small(packet, residues, res_dev, per)
        bias += mul(part.astype(BF16), zero_one(place == -(me ^ r) * res_dev))
        for q in range(per):
            hot = zero_one(iota((kinds, residues), 0).astype(F32) == all_ids[q : q + 1])
            act = packet[q * residues : (q + 1) * residues, :].astype(F32)
            rows.append(act + mul(hot, table[...], ((0,), (0,))))
    zero = jnp.concatenate(rows, axis=0)
    extra = []
    for h in range(FOCUS_TOTAL):
        part = bias + hidden_keys[...]
        part = part[:, h * residues : (h + 1) * residues]
        extra.append(jnp.concatenate([part] * (128 // residues), axis=1))

    halves = range(0, width, 128)
    for half in halves:
        start[half // 128] = zero[:, half : half + 128]
    keys, query, values, gate = project(zero, row_q, row_kvg)
    mixed = (attend(keys, query, values, residues, extra) * gate).astype(BF16)
    mixed = mul(turn[...], mixed, ((1,), (1,))).astype(BF16)
    zero = jnp.concatenate(
        [
            jnp.concatenate(
                [start[half // 128, pl.ds(l, count, stride=residues), :] for l in range(residues)],
                axis=0,
            )
            for half in halves
        ],
        axis=1,
    )
    one = (zero + mul(mixed, row_out[...])).astype(BF16).astype(F32)

    keys, query, values, gate = project(one, col_q, col_kvg)
    mixed = (attend(keys, query, values, count) * gate).astype(BF16)
    align = (one + mul(mixed, col_out[...], ((0,), (0,)))).astype(BF16)
    own = count * res_dev
    row_at, lane_at = iota((own, tokens), 0), iota((own, tokens), 1)
    sequence = row_at // res_dev
    owner = (sequence // per) ^ me
    where_is = jnp.zeros_like(owner)
    for k, r in enumerate(PACKET_ORDER):
        where_is = jnp.where(owner == r, k + 1, where_is)
    pick = zero_one(
        lane_at
        == (row_at % res_dev + me * res_dev) * count + where_is * per + sequence % per
    )
    align_ref[...] = mul(pick, align).reshape(count, res_dev, width).astype(BF16)

    opm = normal(align.astype(F32)).astype(BF16)
    opm = mul(opm, lift[...], ((1,), (1,))).astype(BF16)
    hidden = MEAN_HIDDEN_SIZE
    deep = hidden * count
    spread = zero_one(
        iota((2 * hidden, deep), 1) // count == iota((2 * hidden, deep), 0)
    )
    left = mul(opm, spread)
    left = jnp.where(
        iota((tokens, deep), 0) % count == iota((tokens, deep), 1) % count, left, 0.0
    ).astype(BF16)
    gather = zero_one(iota((residues, tokens), 1) // count == iota((residues, tokens), 0))
    left = mul(gather, left).astype(BF16)
    right = opm[:, hidden:]
    for c in range(0, hidden, 2):
        pair_w = jnp.concatenate(
            [outer_w[(c + k) * hidden : (c + k + 1) * hidden, :] for k in range(2)], axis=1
        )
        part = mul(right, pair_w)
        lifted[c], lifted[c + 1] = part[:, :pair_width], part[:, pair_width:]
    for j in range(0, residues, 2):
        part = jnp.concatenate(
            [
                lifted[:, (j + k) * count : (j + k + 1) * count, :].reshape(deep, pair_width)
                for k in range(2)
            ],
            axis=1,
        )
        part = mul(left, part.astype(BF16)) * (1.0 / count)
        update_ref[j], update_ref[j + 1] = part[:, :pair_width], part[:, pair_width:]


def pair_kernel(*refs):
    pairs, packets, update, column, pair, own_mask = refs[:3], refs[3:6], *refs[6:10]
    proj, gates, gate_out, w_out, out_ref, state, one, right_at, left_at, valid = refs[10:]
    res_dev, residues, width = pair.shape
    per = (packets[0].shape[0] - SMALL_ROWS) // residues
    me = lax.axis_index("axial")
    own_valid = own_mask[...].astype(F32)
    for packet, r in zip((None, *packets), (0, *PACKET_ORDER)):
        shown = split_small(packet, residues, res_dev, per)[1] if r else own_valid
        valid[pl.ds(pl.multiple_of((me ^ r) * res_dev, res_dev), res_dev), :] = shown
    size = res_dev * residues
    for block, r in zip((pair, *pairs), (0, *PAIR_ORDER)):
        state[pl.ds(pl.multiple_of((me ^ r) * size, size), size), :] = (
            block[...].astype(F32).reshape(size, width)
        )
    for k in range(residues):
        one[k * residues : (k + 1) * residues, :] = (
            state[pl.ds(k, residues, stride=residues), :] + update[k]
        )

    shown = mul(valid[...].astype(BF16), column[...])
    right_w = jnp.concatenate([proj[:, C_TRI:], gates[:, C_TRI:]], axis=1)
    step = 8
    for k in range(0, residues, step):
        here = slice(k * residues, (k + step) * residues)
        both = mul(normal(one[here, :]).astype(BF16), right_w)
        both = sigmoid(both[:, C_TRI:]) * both[:, :C_TRI]
        for p in range(step):
            part = both[p * residues : (p + 1) * residues]
            part = part * shown[:, (k + p) * C_TRI : (k + p + 1) * C_TRI]
            right_at[(k + p) * residues : (k + p + 1) * residues, :] = part.astype(BF16).astype(F32)

    own = jnp.concatenate(
        [one[pl.ds(me * res_dev + i, residues, stride=residues), :] for i in range(res_dev)],
        axis=0,
    )
    left_w = jnp.concatenate([proj[:, :C_TRI], gates[:, :C_TRI], gate_out[...]], axis=1)
    own_all = mul(normal(own).astype(BF16), left_w)
    own_gate = sigmoid(own_all[:, 2 * C_TRI :])
    left = sigmoid(own_all[:, C_TRI : 2 * C_TRI]) * own_all[:, :C_TRI]
    shown = mul(own_valid.astype(BF16), column[:res_dev, : res_dev * C_TRI], ((0,), (0,)))
    for i in range(res_dev):
        part = left[i * residues : (i + 1) * residues] * shown[:, i * C_TRI : (i + 1) * C_TRI]
        left_at[i * residues : (i + 1) * residues, :] = part.astype(BF16).astype(F32)
    sums = [jnp.zeros((residues, C_TRI), F32) for _ in range(res_dev)]
    for k in range(residues):
        other = right_at[k * residues : (k + 1) * residues, :]
        for i in range(res_dev):
            sums[i] += left_at[i * residues + k : i * residues + k + 1, :] * other
    mixed = normal(jnp.concatenate(sums, axis=0)).astype(BF16)
    result = own + own_gate * mul(mixed, w_out[...])
    out_ref[...] = result.reshape(res_dev, residues, width).astype(BF16)


def call(kernel, out_shape, scratch, vmem_mib, *args):
    vmem = pl.BlockSpec(memory_space=pltpu.VMEM)
    return pl.pallas_call(
        kernel,
        out_shape=out_shape,
        in_specs=[vmem] * len(args),
        out_specs=jax.tree.map(lambda _: vmem, out_shape),
        scratch_shapes=scratch,
        compiler_params=pltpu.CompilerParams(vmem_limit_bytes=vmem_mib * 1024 * 1024),
        cost_estimate=pl.CostEstimate(flops=FLOPS, bytes_accessed=0, transcendentals=0),
    )(*args)


def swap(array, r, n):
    return lax.ppermute(array, "axial", [(i, i ^ r) for i in range(n)])


def local_whole(
    homolog_activity,
    homolog_symbol_ids,
    residue_present_mask,
    pair_state,
    pair_valid_mask,
    symbol_lookup_matrix,
    row_query_weight,
    horizontal_attention_matrix,
    pair_bias_weight,
    horizontal_final_matrix,
    column_query_weight,
    vertical_attention_matrix,
    vertical_final_matrix,
    tensor_mean_lift_matrix,
    outer_product_output_weight,
    triangle_projection_weight,
    triangle_projection_gate,
    triangle_output_gate,
    triangle_output_weight,
):
    n = lax.axis_size("axial")
    per, residues, width = homolog_activity.shape
    res_dev, _, pair_width = pair_state.shape
    count = per * n
    shift, turn, column = call(
        functools.partial(table_kernel, FOCUS_TOTAL * res_dev, count),
        (
            jax.ShapeDtypeStruct((residues, 128), BF16),
            jax.ShapeDtypeStruct((count * residues, count * residues), BF16),
            jax.ShapeDtypeStruct((residues, residues * C_TRI), BF16),
        ),
        [],
        2,
    )
    packet, hidden_keys = call(
        packet_kernel,
        (
            jax.ShapeDtypeStruct((per * residues + SMALL_ROWS, width), BF16),
            jax.ShapeDtypeStruct((residues, FOCUS_TOTAL * residues), F32),
        ),
        [],
        4,
        pair_state,
        pair_bias_weight.T,
        pair_valid_mask,
        homolog_symbol_ids,
        homolog_activity,
        residue_present_mask.reshape(1, residues),
        shift,
    )
    packets = [swap(packet, r, n) for r in PACKET_ORDER]
    _, later = lax.optimization_barrier((packet, pair_state))
    pairs = [swap(later, r, n) for r in PAIR_ORDER]
    alignment, update = call(
        functools.partial(msa_kernel, n, res_dev),
        (
            jax.ShapeDtypeStruct((count, res_dev, width), BF16),
            jax.ShapeDtypeStruct((residues, residues, pair_width), F32),
        ),
        [
            pltpu.VMEM((width // 128, count * residues, 128), F32),
            pltpu.VMEM((MEAN_HIDDEN_SIZE, count * residues, pair_width), F32),
        ],
        16,
        packet,
        *packets,
        turn,
        hidden_keys,
        symbol_lookup_matrix,
        row_query_weight,
        horizontal_attention_matrix,
        horizontal_final_matrix,
        column_query_weight,
        vertical_attention_matrix,
        vertical_final_matrix,
        tensor_mean_lift_matrix.T,
        outer_product_output_weight,
    )
    pair_output = call(
        pair_kernel,
        jax.ShapeDtypeStruct((res_dev, residues, pair_width), BF16),
        [
            pltpu.VMEM((residues * residues, pair_width), F32),
            pltpu.VMEM((residues * residues, pair_width), F32),
            pltpu.VMEM((residues * residues, C_TRI), F32),
            pltpu.VMEM((res_dev * residues, C_TRI), F32),
            pltpu.VMEM((residues, residues), F32),
        ],
        16,
        *pairs,
        *packets,
        update,
        column,
        pair_state,
        pair_valid_mask,
        triangle_projection_weight,
        triangle_projection_gate,
        triangle_output_gate,
        triangle_output_weight,
    )
    return (alignment, pair_output)


def local(homolog_activity, homolog_symbol_ids, residue_present_mask, pair_state, *others):
    n = lax.axis_size("axial")
    per, residues, _ = homolog_activity.shape
    small = n == 4 and per * n == 8 and residues == 32
    plan = local_whole if small else local_sharded
    return plan(homolog_activity, homolog_symbol_ids, residue_present_mask, pair_state, *others)


def solution(mesh):
    parts, copied = P(("dp", "axial")), P()
    return jax.shard_map(
        local,
        mesh=mesh,
        in_specs=(parts, parts, P("dp"), parts, parts) + (copied,) * 14,
        out_specs=(P("dp", "axial", None), P(("dp", "axial"), None, None)),
        check_vma=False,
    )
```

```python
import functools

import jax
import jax.numpy as jnp
from jax import lax
from jax.experimental import pallas as pl
from jax.experimental.pallas import tpu as pltpu
from jax.sharding import PartitionSpec as P

FOCUS_TOTAL = 8
FOCUS_SIZE = 32
MEAN_HIDDEN_SIZE = 32
C_TRI = 128


def layer_normalize(attended_entries):
    attended_entries = attended_entries.astype(jnp.float32)
    mean = jnp.mean(attended_entries, axis=-1, keepdims=True)
    centred = attended_entries - mean
    var = jnp.mean(centred * centred, axis=-1, keepdims=True)
    return centred * lax.rsqrt(var + 1e-05)


def gated_attend(evoformer_block, extra_axes, w_query, w_kvg, w_out):
    lines_list, residue_length, input_width = evoformer_block.shape
    width = FOCUS_TOTAL * FOCUS_SIZE
    flat = (
        layer_normalize(evoformer_block)
        .astype(jnp.bfloat16)
        .reshape(lines_list * residue_length, input_width)
    )
    query = (
        jnp.dot(flat, w_query, preferred_element_type=jnp.float32) * FOCUS_SIZE ** (-0.5)
    ).astype(jnp.bfloat16)
    query = query.reshape(lines_list, residue_length, FOCUS_TOTAL, FOCUS_SIZE)
    kvg = jnp.dot(flat, w_kvg, preferred_element_type=jnp.float32)
    keys = (
        kvg[:, :width]
        .astype(jnp.bfloat16)
        .reshape(lines_list, residue_length, FOCUS_TOTAL, FOCUS_SIZE)
    )
    attended_entries = (
        kvg[:, width : 2 * width]
        .astype(jnp.bfloat16)
        .reshape(lines_list, residue_length, FOCUS_TOTAL, FOCUS_SIZE)
    )
    gate = jax.nn.sigmoid(kvg[:, 2 * width :]).reshape(
        lines_list, residue_length, FOCUS_TOTAL, FOCUS_SIZE
    )
    scores = (
        jnp.einsum("bihd,bjhd->bhij", query, keys, preferred_element_type=jnp.float32) + extra_axes
    )
    top = jnp.max(scores, axis=-1, keepdims=True)
    expo = jnp.exp(scores - top)
    weights = (expo / jnp.sum(expo, axis=-1, keepdims=True)).astype(jnp.bfloat16)
    mixed = jnp.einsum(
        "bhij,bjhd->bihd", weights, attended_entries, preferred_element_type=jnp.float32
    )
    mixed = (mixed * gate).astype(jnp.bfloat16).reshape(lines_list * residue_length, width)
    return evoformer_block + jnp.dot(mixed, w_out, preferred_element_type=jnp.float32).reshape(
        lines_list, residue_length, input_width
    )


def finish_sums(evoformer_block, triangle_output_weight):
    mixed = layer_normalize(jnp.transpose(evoformer_block, (1, 2, 0))).astype(jnp.bfloat16)
    return jnp.einsum(
        "ijc,cz->ijz", mixed, triangle_output_weight, preferred_element_type=jnp.float32
    )


def local_sharded(
    homolog_activity,
    homolog_symbol_ids,
    residue_present_mask,
    pair_state,
    pair_valid_mask,
    symbol_lookup_matrix,
    row_query_weight,
    horizontal_attention_matrix,
    pair_bias_weight,
    horizontal_final_matrix,
    column_query_weight,
    vertical_attention_matrix,
    vertical_final_matrix,
    tensor_mean_lift_matrix,
    outer_product_output_weight,
    triangle_projection_weight,
    triangle_projection_gate,
    triangle_output_gate,
    triangle_output_weight,
):
    sequence_per_device, residue_length, input_width = homolog_activity.shape
    res_dev = pair_state.shape[0]
    group_size = lax.axis_size("axial")
    token_classes = symbol_lookup_matrix.shape[0]
    token_one_hot = (
        homolog_symbol_ids[..., None] == jnp.arange(token_classes, dtype=jnp.int32)
    ).astype(jnp.bfloat16)
    token_embedded = jnp.einsum(
        "slt,tc->slc", token_one_hot, symbol_lookup_matrix, preferred_element_type=jnp.float32
    )
    homolog_starting = homolog_activity.astype(jnp.float32) + token_embedded
    pair_norm = layer_normalize(pair_state).astype(jnp.bfloat16)
    bias_rows = jnp.einsum(
        "ijc,ch->hij", pair_norm, pair_bias_weight, preferred_element_type=jnp.float32
    ).astype(jnp.bfloat16)
    bias_full = lax.all_gather(bias_rows, "axial", axis=1, tiled=True)
    key_bias = 1000000000.0 * (residue_present_mask.astype(jnp.float32) - 1.0)
    extra_axes = bias_full.astype(jnp.float32)[None] + key_bias[None, None, None, :]
    cluster_total = homolog_starting.reshape(
        sequence_per_device // 2, 2, residue_length, input_width
    )
    homolog_across_update = lax.map(
        lambda evoformer_block: gated_attend(
            evoformer_block,
            extra_axes,
            row_query_weight,
            horizontal_attention_matrix,
            horizontal_final_matrix,
        ),
        cluster_total,
    )
    homolog_across_update = homolog_across_update.reshape(
        sequence_per_device, group_size, res_dev, input_width
    ).astype(jnp.bfloat16)
    moved = jnp.swapaxes(
        lax.all_to_all(homolog_across_update, "axial", split_axis=1, concat_axis=0, tiled=True)[
            :, 0
        ],
        0,
        1,
    )
    finished = lax.map(
        lambda item: gated_attend(
            item[None].astype(jnp.float32),
            0.0,
            column_query_weight,
            vertical_attention_matrix,
            vertical_final_matrix,
        )[0],
        moved,
    )
    exchanged = jnp.swapaxes(finished, 0, 1).astype(jnp.bfloat16)[:, None]
    sequence_count = exchanged.shape[0]
    alignment_after_columns = exchanged.reshape(sequence_count, res_dev, input_width)
    tensor_mean_scaler = layer_normalize(alignment_after_columns).astype(jnp.bfloat16)
    split_parts = jnp.einsum(
        "src,cf->rsf",
        tensor_mean_scaler,
        tensor_mean_lift_matrix,
        preferred_element_type=jnp.float32,
    ).astype(jnp.bfloat16)
    first_factor = split_parts[..., :MEAN_HIDDEN_SIZE]
    second_factor = split_parts[..., MEAN_HIDDEN_SIZE:].reshape(
        res_dev, sequence_count * MEAN_HIDDEN_SIZE
    )
    step_rows = 8
    left_blocks = first_factor.reshape(
        res_dev // step_rows, step_rows, sequence_count, MEAN_HIDDEN_SIZE
    )
    piece = lax.all_gather(second_factor, "axial", axis=0, tiled=True)
    count = piece.shape[0]
    right_part = piece.reshape(count, sequence_count, MEAN_HIDDEN_SIZE)

    def one_block(lines_list):
        tensor_mean = (
            jnp.einsum("isc,jsd->ijcd", lines_list, right_part, preferred_element_type=jnp.float32)
            / sequence_count
        )
        tensor_mean = tensor_mean.reshape(
            step_rows, count, MEAN_HIDDEN_SIZE * MEAN_HIDDEN_SIZE
        ).astype(jnp.bfloat16)
        return jnp.einsum(
            "ijf,fz->ijz",
            tensor_mean,
            outer_product_output_weight,
            preferred_element_type=jnp.float32,
        )

    update = lax.map(one_block, left_blocks).reshape(
        res_dev, count, outer_product_output_weight.shape[1]
    )
    pair_one = pair_state.astype(jnp.float32) + update
    tri_norm = layer_normalize(pair_one).astype(jnp.bfloat16)
    proj = jnp.einsum(
        "ikc,cf->fik", tri_norm, triangle_projection_weight, preferred_element_type=jnp.float32
    )
    gates = jnp.einsum(
        "ikc,cf->fik", tri_norm, triangle_projection_gate, preferred_element_type=jnp.float32
    )
    both = (jax.nn.sigmoid(gates) * proj * pair_valid_mask.astype(jnp.float32)[None]).astype(
        jnp.bfloat16
    )
    left_tri = both[:C_TRI]
    right_tri = both[C_TRI:]
    moved_left, moved_right = (
        lax.all_to_all(left_tri, "axial", split_axis=0, concat_axis=1, tiled=True),
        lax.all_to_all(right_tri, "axial", split_axis=0, concat_axis=1, tiled=True),
    )
    partial_sum = jnp.einsum(
        "cik,cjk->cij", moved_left, moved_right, preferred_element_type=jnp.float32
    )
    tri_sum = lax.all_to_all(
        partial_sum.astype(jnp.bfloat16), "axial", split_axis=1, concat_axis=0, tiled=True
    ).astype(partial_sum.dtype)
    tri_update = finish_sums(tri_sum, triangle_output_weight)
    out_gate = jax.nn.sigmoid(
        jnp.einsum(
            "ijc,cz->ijz", tri_norm, triangle_output_gate, preferred_element_type=jnp.float32
        )
    )
    pair_output = (pair_one + out_gate * tri_update).astype(jnp.bfloat16)
    return (alignment_after_columns, pair_output)


BF16 = jnp.bfloat16
F32 = jnp.float32
SMALL_ROWS = 16
FLOPS = 3 * 10**9
PACKET_ORDER = (3, 2, 1)


def mul(lhs, rhs, over=((1,), (0,))):
    return lax.dot_general(lhs, rhs, (over, ((), ())), preferred_element_type=F32)


def iota(shape, axis):
    return lax.broadcasted_iota(jnp.int32, shape, axis)


def zero_one(condition):
    return jnp.where(condition, 1.0, 0.0).astype(BF16)


def normal(x):
    mean = jnp.mean(x, axis=-1, keepdims=True)
    centred = x - mean
    var = jnp.mean(centred * centred, axis=-1, keepdims=True)
    return centred * lax.rsqrt(var + 1e-05)


def sigmoid(x):
    return 1.0 / (1.0 + jnp.exp(-x))


def column_softmax(scores):
    expo = jnp.exp(scores - jnp.max(scores, axis=0, keepdims=True))
    return expo * (1.0 / jnp.sum(expo, axis=0, keepdims=True))


def bias_rows(pair_ref, weight_ref):
    rows, residues, width = pair_ref.shape
    lanes = FOCUS_TOTAL * rows
    spread = zero_one(iota((FOCUS_TOTAL, lanes), 1) // rows == iota((FOCUS_TOTAL, lanes), 0))
    row_of = iota((width, lanes), 1) % rows
    flat = normal(pair_ref[...].astype(F32).reshape(rows * residues, width)).astype(BF16)
    weight = mul(weight_ref[...], spread, ((0,), (0,)))
    bias = jnp.zeros((residues, lanes), F32)
    for i in range(rows):
        one_row = jnp.where(row_of == i, weight, 0.0).astype(BF16)
        bias += mul(flat[i * residues : (i + 1) * residues], one_row)
    return bias


def table_kernel(lanes, count, shift_ref, turn_ref, column_ref):
    shape = column_ref.shape
    column_ref[...] = zero_one(iota(shape, 1) // C_TRI == iota(shape, 0))
    shape = shift_ref.shape
    shift_ref[...] = zero_one(iota(shape, 1) == iota(shape, 0) + lanes)
    shape = turn_ref.shape
    row_at = iota(shape, 0)
    turn_ref[...] = zero_one(
        iota(shape, 1) == (row_at % count) * (shape[0] // count) + row_at // count
    )


def packet_kernel(*refs):
    pair_ref, weight_ref, valid_ref, ids_ref, act_ref, present_ref, shift_ref = refs[:7]
    packet_ref, hidden_ref = refs[7:]
    rows, residues, width = pair_ref.shape
    per, _, features = act_ref.shape
    lanes = FOCUS_TOTAL * rows
    bias = bias_rows(pair_ref, weight_ref)
    extra = jnp.concatenate(
        [
            valid_ref[...].astype(F32),
            ids_ref[...].astype(F32),
            jnp.zeros((SMALL_ROWS - rows - per, residues), F32),
        ],
        axis=0,
    )
    extra = mul(extra.astype(BF16), shift_ref[...])
    empty = jnp.zeros((SMALL_ROWS, 128 - lanes), F32)
    first = jnp.concatenate([bias[:SMALL_ROWS], empty], axis=1) + extra
    second = jnp.concatenate([bias[SMALL_ROWS:], empty], axis=1)
    small = jnp.concatenate([first, second], axis=1).astype(BF16)
    packet_ref[per * residues :, :] = small
    shown = present_ref[...].astype(F32).astype(BF16)
    shown = mul(shown, jnp.ones((1, hidden_ref.shape[1]), BF16), ((0,), (0,)))
    hidden_ref[...] = 1000000000.0 * (shown - 1.0)
    packet_ref[: per * residues, :] = act_ref[...].reshape(per * residues, features)


def split_small(packet, residues, res_dev, per):
    small = packet[per * residues :, :].astype(F32)
    lanes = FOCUS_TOTAL * res_dev
    bias = jnp.concatenate([small[:, :lanes], small[:, 128 : 128 + lanes]], axis=0)
    extra = small[:, lanes : lanes + residues]
    return bias, extra[:res_dev], extra[res_dev : res_dev + per]


def project(x, w_query, w_kvg):
    width = FOCUS_TOTAL * FOCUS_SIZE
    flat = normal(x).astype(BF16)
    turned = ((0,), (1,))
    keys = mul(flat, w_kvg[:, :width]).astype(BF16)
    query = (mul(w_query[...], flat, turned) * FOCUS_SIZE ** (-0.5)).astype(BF16)
    values = mul(w_kvg[:, width : 2 * width], flat, turned).astype(BF16)
    gate = sigmoid(mul(w_kvg[:, 2 * width :], flat, turned))
    return keys, query, values, gate


def attend(keys, query, values, size, extra=None):
    width, tokens = query.shape
    group = min(tokens, 128)
    blocks = group // size
    together = 128 // FOCUS_SIZE
    block_of = iota((1, group), 1) // size
    groups = []
    for start in range(0, tokens, group):
        here = slice(start, start + group)
        heads = []
        for tile in range(0, width, 128):
            apart = []
            for p in range(together):
                row = tile + p * FOCUS_SIZE
                parts = [
                    jnp.zeros((p * FOCUS_SIZE, group), BF16),
                    query[row : row + FOCUS_SIZE, here],
                    jnp.zeros((128 - (p + 1) * FOCUS_SIZE, group), BF16),
                ]
                apart.append(jnp.concatenate([x for x in parts if x.shape[0]], axis=0))
            scores = mul(keys[here, tile : tile + 128], jnp.concatenate(apart, axis=1))
            for p in range(together):
                row = tile + p * FOCUS_SIZE
                full = scores[:, p * group : (p + 1) * group]
                own = full[:size]
                for b in range(1, blocks):
                    own = jnp.where(block_of == b, full[b * size : (b + 1) * size], own)
                if extra is not None:
                    own = own + extra[row // FOCUS_SIZE]
                weights = column_softmax(own)
                weights = jnp.concatenate(
                    [jnp.where(block_of == b, weights, 0.0) for b in range(blocks)], axis=0
                )
                heads.append(mul(values[row : row + FOCUS_SIZE, here], weights.astype(BF16)))
        groups.append(jnp.concatenate(heads, axis=0))
    return jnp.concatenate(groups, axis=1)


def msa_kernel(n, res_dev, *refs):
    packets, turn, hidden_keys, table = refs[:n], refs[n], refs[n + 1], refs[n + 2]
    refs = refs[n + 3 :]
    row_q, row_kvg, row_out, col_q, col_kvg, col_out, lift, outer_w = refs[:8]
    align_ref, update_ref, start, lifted = refs[8:]
    kinds, width = table.shape
    residues, lanes = hidden_keys.shape
    pair_width = outer_w.shape[1]
    per = (packets[0].shape[0] - SMALL_ROWS) // residues
    count = per * n
    tokens = count * residues
    me = lax.axis_index("axial")

    place = iota((FOCUS_TOTAL * res_dev, lanes), 0)
    place = (place // res_dev) * residues + place % res_dev - iota(place.shape, 1)
    bias = jnp.zeros((residues, lanes), F32)
    rows = []
    for packet, r in zip(packets, (0, *PACKET_ORDER)):
        part, _, all_ids = split_small(packet, residues, res_dev, per)
        bias += mul(part.astype(BF16), zero_one(place == -(me ^ r) * res_dev))
        for q in range(per):
            hot = zero_one(iota((kinds, residues), 0).astype(F32) == all_ids[q : q + 1])
            act = packet[q * residues : (q + 1) * residues, :].astype(F32)
            rows.append(act + mul(hot, table[...], ((0,), (0,))))
    zero = jnp.concatenate(rows, axis=0)
    extra = []
    for h in range(FOCUS_TOTAL):
        part = bias + hidden_keys[...]
        part = part[:, h * residues : (h + 1) * residues]
        extra.append(jnp.concatenate([part] * (128 // residues), axis=1))

    halves = range(0, width, 128)
    for half in halves:
        start[half // 128] = zero[:, half : half + 128]
    keys, query, values, gate = project(zero, row_q, row_kvg)
    mixed = (attend(keys, query, values, residues, extra) * gate).astype(BF16)
    mixed = mul(turn[...], mixed, ((1,), (1,))).astype(BF16)
    zero = jnp.concatenate(
        [
            jnp.concatenate(
                [start[half // 128, pl.ds(l, count, stride=residues), :] for l in range(residues)],
                axis=0,
            )
            for half in halves
        ],
        axis=1,
    )
    one = (zero + mul(mixed, row_out[...])).astype(BF16).astype(F32)

    keys, query, values, gate = project(one, col_q, col_kvg)
    mixed = (attend(keys, query, values, count) * gate).astype(BF16)
    align = (one + mul(mixed, col_out[...], ((0,), (0,)))).astype(BF16)
    own = count * res_dev
    row_at, lane_at = iota((own, tokens), 0), iota((own, tokens), 1)
    sequence = row_at // res_dev
    owner = (sequence // per) ^ me
    where_is = jnp.zeros_like(owner)
    for k, r in enumerate(PACKET_ORDER):
        where_is = jnp.where(owner == r, k + 1, where_is)
    pick = zero_one(
        lane_at
        == (row_at % res_dev + me * res_dev) * count + where_is * per + sequence % per
    )
    align_ref[...] = mul(pick, align).reshape(count, res_dev, width).astype(BF16)

    opm = normal(align.astype(F32)).astype(BF16)
    opm = mul(opm, lift[...], ((1,), (1,))).astype(BF16)
    hidden = MEAN_HIDDEN_SIZE
    deep = hidden * count
    spread = zero_one(
        iota((2 * hidden, deep), 1) // count == iota((2 * hidden, deep), 0)
    )
    left = mul(opm, spread)
    left = jnp.where(
        iota((tokens, deep), 0) % count == iota((tokens, deep), 1) % count, left, 0.0
    ).astype(BF16)
    gather = zero_one(iota((residues, tokens), 1) // count == iota((residues, tokens), 0))
    left = mul(gather, left).astype(BF16)
    right = opm[:, hidden:]
    for c in range(0, hidden, 2):
        pair_w = jnp.concatenate(
            [outer_w[(c + k) * hidden : (c + k + 1) * hidden, :] for k in range(2)], axis=1
        )
        part = mul(right, pair_w)
        lifted[c], lifted[c + 1] = part[:, :pair_width], part[:, pair_width:]
    for j in range(0, residues, 2):
        part = jnp.concatenate(
            [
                lifted[:, (j + k) * count : (j + k + 1) * count, :].reshape(deep, pair_width)
                for k in range(2)
            ],
            axis=1,
        )
        part = mul(left, part.astype(BF16)) * (1.0 / count)
        update_ref[j], update_ref[j + 1] = part[:, :pair_width], part[:, pair_width:]


def pair_kernel(*refs):
    pair, packets, update, column, own_mask = refs[0], refs[1:4], *refs[4:7]
    proj, gates, gate_out, w_out, out_ref, state, one, right_at, left_at, valid = refs[7:]
    residues, _, width = pair.shape
    res_dev = own_mask.shape[0]
    per = (packets[0].shape[0] - SMALL_ROWS) // residues
    me = lax.axis_index("axial")
    own_valid = own_mask[...].astype(F32)
    for packet, r in zip((None, *packets), (0, *PACKET_ORDER)):
        shown = split_small(packet, residues, res_dev, per)[1] if r else own_valid
        valid[pl.ds(pl.multiple_of((me ^ r) * res_dev, res_dev), res_dev), :] = shown
    state[...] = pair[...].astype(F32).reshape(residues * residues, width)
    for k in range(residues):
        one[k * residues : (k + 1) * residues, :] = (
            state[pl.ds(k, residues, stride=residues), :] + update[k]
        )

    shown = mul(valid[...].astype(BF16), column[...])
    right_w = jnp.concatenate([proj[:, C_TRI:], gates[:, C_TRI:]], axis=1)
    step = 8
    for k in range(0, residues, step):
        here = slice(k * residues, (k + step) * residues)
        both = mul(normal(one[here, :]).astype(BF16), right_w)
        both = sigmoid(both[:, C_TRI:]) * both[:, :C_TRI]
        for p in range(step):
            part = both[p * residues : (p + 1) * residues]
            part = part * shown[:, (k + p) * C_TRI : (k + p + 1) * C_TRI]
            right_at[(k + p) * residues : (k + p + 1) * residues, :] = part.astype(BF16).astype(F32)

    own = jnp.concatenate(
        [one[pl.ds(me * res_dev + i, residues, stride=residues), :] for i in range(res_dev)],
        axis=0,
    )
    left_w = jnp.concatenate([proj[:, :C_TRI], gates[:, :C_TRI], gate_out[...]], axis=1)
    own_all = mul(normal(own).astype(BF16), left_w)
    own_gate = sigmoid(own_all[:, 2 * C_TRI :])
    left = sigmoid(own_all[:, C_TRI : 2 * C_TRI]) * own_all[:, :C_TRI]
    shown = mul(own_valid.astype(BF16), column[:res_dev, : res_dev * C_TRI], ((0,), (0,)))
    for i in range(res_dev):
        part = left[i * residues : (i + 1) * residues] * shown[:, i * C_TRI : (i + 1) * C_TRI]
        left_at[i * residues : (i + 1) * residues, :] = part.astype(BF16).astype(F32)
    sums = [jnp.zeros((residues, C_TRI), F32) for _ in range(res_dev)]
    for k in range(residues):
        other = right_at[k * residues : (k + 1) * residues, :]
        for i in range(res_dev):
            sums[i] += left_at[i * residues + k : i * residues + k + 1, :] * other
    mixed = normal(jnp.concatenate(sums, axis=0)).astype(BF16)
    result = own + own_gate * mul(mixed, w_out[...])
    out_ref[...] = result.reshape(res_dev, residues, width).astype(BF16)


def call(kernel, out_shape, scratch, vmem_mib, *args, flops=FLOPS):
    vmem = pl.BlockSpec(memory_space=pltpu.VMEM)
    return pl.pallas_call(
        kernel,
        out_shape=out_shape,
        in_specs=[vmem] * len(args),
        out_specs=jax.tree.map(lambda _: vmem, out_shape),
        scratch_shapes=scratch,
        compiler_params=pltpu.CompilerParams(vmem_limit_bytes=vmem_mib * 1024 * 1024),
        cost_estimate=pl.CostEstimate(flops=flops, bytes_accessed=0, transcendentals=0),
    )(*args)


def swap(array, r, n):
    return lax.ppermute(array, "axial", [(i, i ^ r) for i in range(n)])


def local_whole(
    homolog_activity,
    homolog_symbol_ids,
    residue_present_mask,
    pair_state,
    pair_valid_mask,
    symbol_lookup_matrix,
    row_query_weight,
    horizontal_attention_matrix,
    pair_bias_weight,
    horizontal_final_matrix,
    column_query_weight,
    vertical_attention_matrix,
    vertical_final_matrix,
    tensor_mean_lift_matrix,
    outer_product_output_weight,
    triangle_projection_weight,
    triangle_projection_gate,
    triangle_output_gate,
    triangle_output_weight,
):
    n = lax.axis_size("axial")
    per, residues, width = homolog_activity.shape
    res_dev, _, pair_width = pair_state.shape
    count = per * n
    shift, turn, column = call(
        functools.partial(table_kernel, FOCUS_TOTAL * res_dev, count),
        (
            jax.ShapeDtypeStruct((residues, 128), BF16),
            jax.ShapeDtypeStruct((count * residues, count * residues), BF16),
            jax.ShapeDtypeStruct((residues, residues * C_TRI), BF16),
        ),
        [],
        2,
    )
    packet, hidden_keys = call(
        packet_kernel,
        (
            jax.ShapeDtypeStruct((per * residues + SMALL_ROWS, width), BF16),
            jax.ShapeDtypeStruct((residues, FOCUS_TOTAL * residues), F32),
        ),
        [],
        4,
        pair_state,
        pair_bias_weight.T,
        pair_valid_mask,
        homolog_symbol_ids,
        homolog_activity,
        residue_present_mask.reshape(1, residues),
        shift,
    )
    packets = [swap(packet, r, n) for r in PACKET_ORDER]
    pair = lax.all_gather(pair_state, "axial", axis=0, tiled=True)
    alignment, update = call(
        functools.partial(msa_kernel, n, res_dev),
        (
            jax.ShapeDtypeStruct((count, res_dev, width), BF16),
            jax.ShapeDtypeStruct((residues, residues, pair_width), F32),
        ),
        [
            pltpu.VMEM((width // 128, count * residues, 128), F32),
            pltpu.VMEM((MEAN_HIDDEN_SIZE, count * residues, pair_width), F32),
        ],
        16,
        packet,
        *packets,
        turn,
        hidden_keys,
        symbol_lookup_matrix,
        row_query_weight,
        horizontal_attention_matrix,
        horizontal_final_matrix,
        column_query_weight,
        vertical_attention_matrix,
        vertical_final_matrix,
        tensor_mean_lift_matrix.T,
        outer_product_output_weight,
        flops=FLOPS // 3,
    )
    pair_output = call(
        pair_kernel,
        jax.ShapeDtypeStruct((res_dev, residues, pair_width), BF16),
        [
            pltpu.VMEM((residues * residues, pair_width), F32),
            pltpu.VMEM((residues * residues, pair_width), F32),
            pltpu.VMEM((residues * residues, C_TRI), F32),
            pltpu.VMEM((res_dev * residues, C_TRI), F32),
            pltpu.VMEM((residues, residues), F32),
        ],
        16,
        pair,
        *packets,
        update,
        column,
        pair_valid_mask,
        triangle_projection_weight,
        triangle_projection_gate,
        triangle_output_gate,
        triangle_output_weight,
    )
    return (alignment, pair_output)


def local(homolog_activity, homolog_symbol_ids, residue_present_mask, pair_state, *others):
    n = lax.axis_size("axial")
    per, residues, _ = homolog_activity.shape
    small = n == 4 and per * n == 8 and residues == 32
    plan = local_whole if small else local_sharded
    return plan(homolog_activity, homolog_symbol_ids, residue_present_mask, pair_state, *others)


def solution(mesh):
    parts, copied = P(("dp", "axial")), P()
    return jax.shard_map(
        local,
        mesh=mesh,
        in_specs=(parts, parts, P("dp"), parts, parts) + (copied,) * 14,
        out_specs=(P("dp", "axial", None), P(("dp", "axial"), None, None)),
        check_vma=False,
    )
```

```python
import functools

import jax
import jax.numpy as jnp
from jax import lax
from jax.experimental import pallas as pl
from jax.experimental.pallas import tpu as pltpu
from jax.sharding import PartitionSpec as P

FOCUS_TOTAL = 8
FOCUS_SIZE = 32
MEAN_HIDDEN_SIZE = 32
C_TRI = 128


def layer_normalize(attended_entries):
    attended_entries = attended_entries.astype(jnp.float32)
    mean = jnp.mean(attended_entries, axis=-1, keepdims=True)
    centred = attended_entries - mean
    var = jnp.mean(centred * centred, axis=-1, keepdims=True)
    return centred * lax.rsqrt(var + 1e-05)


def gated_attend(evoformer_block, extra_axes, w_query, w_kvg, w_out):
    lines_list, residue_length, input_width = evoformer_block.shape
    width = FOCUS_TOTAL * FOCUS_SIZE
    flat = (
        layer_normalize(evoformer_block)
        .astype(jnp.bfloat16)
        .reshape(lines_list * residue_length, input_width)
    )
    query = (
        jnp.dot(flat, w_query, preferred_element_type=jnp.float32) * FOCUS_SIZE ** (-0.5)
    ).astype(jnp.bfloat16)
    query = query.reshape(lines_list, residue_length, FOCUS_TOTAL, FOCUS_SIZE)
    kvg = jnp.dot(flat, w_kvg, preferred_element_type=jnp.float32)
    keys = (
        kvg[:, :width]
        .astype(jnp.bfloat16)
        .reshape(lines_list, residue_length, FOCUS_TOTAL, FOCUS_SIZE)
    )
    attended_entries = (
        kvg[:, width : 2 * width]
        .astype(jnp.bfloat16)
        .reshape(lines_list, residue_length, FOCUS_TOTAL, FOCUS_SIZE)
    )
    gate = jax.nn.sigmoid(kvg[:, 2 * width :]).reshape(
        lines_list, residue_length, FOCUS_TOTAL, FOCUS_SIZE
    )
    scores = (
        jnp.einsum("bihd,bjhd->bhij", query, keys, preferred_element_type=jnp.float32) + extra_axes
    )
    top = jnp.max(scores, axis=-1, keepdims=True)
    expo = jnp.exp(scores - top)
    weights = (expo / jnp.sum(expo, axis=-1, keepdims=True)).astype(jnp.bfloat16)
    mixed = jnp.einsum(
        "bhij,bjhd->bihd", weights, attended_entries, preferred_element_type=jnp.float32
    )
    mixed = (mixed * gate).astype(jnp.bfloat16).reshape(lines_list * residue_length, width)
    return evoformer_block + jnp.dot(mixed, w_out, preferred_element_type=jnp.float32).reshape(
        lines_list, residue_length, input_width
    )


def finish_sums(evoformer_block, triangle_output_weight):
    mixed = layer_normalize(jnp.transpose(evoformer_block, (1, 2, 0))).astype(jnp.bfloat16)
    return jnp.einsum(
        "ijc,cz->ijz", mixed, triangle_output_weight, preferred_element_type=jnp.float32
    )


def local_sharded(
    homolog_activity,
    homolog_symbol_ids,
    residue_present_mask,
    pair_state,
    pair_valid_mask,
    symbol_lookup_matrix,
    row_query_weight,
    horizontal_attention_matrix,
    pair_bias_weight,
    horizontal_final_matrix,
    column_query_weight,
    vertical_attention_matrix,
    vertical_final_matrix,
    tensor_mean_lift_matrix,
    outer_product_output_weight,
    triangle_projection_weight,
    triangle_projection_gate,
    triangle_output_gate,
    triangle_output_weight,
):
    sequence_per_device, residue_length, input_width = homolog_activity.shape
    res_dev = pair_state.shape[0]
    group_size = lax.axis_size("axial")
    token_classes = symbol_lookup_matrix.shape[0]
    token_one_hot = (
        homolog_symbol_ids[..., None] == jnp.arange(token_classes, dtype=jnp.int32)
    ).astype(jnp.bfloat16)
    token_embedded = jnp.einsum(
        "slt,tc->slc", token_one_hot, symbol_lookup_matrix, preferred_element_type=jnp.float32
    )
    homolog_starting = homolog_activity.astype(jnp.float32) + token_embedded
    pair_norm = layer_normalize(pair_state).astype(jnp.bfloat16)
    bias_rows = jnp.einsum(
        "ijc,ch->hij", pair_norm, pair_bias_weight, preferred_element_type=jnp.float32
    ).astype(jnp.bfloat16)
    bias_full = lax.all_gather(bias_rows, "axial", axis=1, tiled=True)
    key_bias = 1000000000.0 * (residue_present_mask.astype(jnp.float32) - 1.0)
    extra_axes = bias_full.astype(jnp.float32)[None] + key_bias[None, None, None, :]
    cluster_total = homolog_starting.reshape(
        sequence_per_device // 2, 2, residue_length, input_width
    )
    homolog_across_update = lax.map(
        lambda evoformer_block: gated_attend(
            evoformer_block,
            extra_axes,
            row_query_weight,
            horizontal_attention_matrix,
            horizontal_final_matrix,
        ),
        cluster_total,
    )
    homolog_across_update = homolog_across_update.reshape(
        sequence_per_device, group_size, res_dev, input_width
    ).astype(jnp.bfloat16)
    moved = jnp.swapaxes(
        lax.all_to_all(homolog_across_update, "axial", split_axis=1, concat_axis=0, tiled=True)[
            :, 0
        ],
        0,
        1,
    )
    finished = lax.map(
        lambda item: gated_attend(
            item[None].astype(jnp.float32),
            0.0,
            column_query_weight,
            vertical_attention_matrix,
            vertical_final_matrix,
        )[0],
        moved,
    )
    exchanged = jnp.swapaxes(finished, 0, 1).astype(jnp.bfloat16)[:, None]
    sequence_count = exchanged.shape[0]
    alignment_after_columns = exchanged.reshape(sequence_count, res_dev, input_width)
    tensor_mean_scaler = layer_normalize(alignment_after_columns).astype(jnp.bfloat16)
    split_parts = jnp.einsum(
        "src,cf->rsf",
        tensor_mean_scaler,
        tensor_mean_lift_matrix,
        preferred_element_type=jnp.float32,
    ).astype(jnp.bfloat16)
    first_factor = split_parts[..., :MEAN_HIDDEN_SIZE]
    second_factor = split_parts[..., MEAN_HIDDEN_SIZE:].reshape(
        res_dev, sequence_count * MEAN_HIDDEN_SIZE
    )
    step_rows = 8
    left_blocks = first_factor.reshape(
        res_dev // step_rows, step_rows, sequence_count, MEAN_HIDDEN_SIZE
    )
    piece = lax.all_gather(second_factor, "axial", axis=0, tiled=True)
    count = piece.shape[0]
    right_part = piece.reshape(count, sequence_count, MEAN_HIDDEN_SIZE)

    def one_block(lines_list):
        tensor_mean = (
            jnp.einsum("isc,jsd->ijcd", lines_list, right_part, preferred_element_type=jnp.float32)
            / sequence_count
        )
        tensor_mean = tensor_mean.reshape(
            step_rows, count, MEAN_HIDDEN_SIZE * MEAN_HIDDEN_SIZE
        ).astype(jnp.bfloat16)
        return jnp.einsum(
            "ijf,fz->ijz",
            tensor_mean,
            outer_product_output_weight,
            preferred_element_type=jnp.float32,
        )

    update = lax.map(one_block, left_blocks).reshape(
        res_dev, count, outer_product_output_weight.shape[1]
    )
    pair_one = pair_state.astype(jnp.float32) + update
    tri_norm = layer_normalize(pair_one).astype(jnp.bfloat16)
    proj = jnp.einsum(
        "ikc,cf->fik", tri_norm, triangle_projection_weight, preferred_element_type=jnp.float32
    )
    gates = jnp.einsum(
        "ikc,cf->fik", tri_norm, triangle_projection_gate, preferred_element_type=jnp.float32
    )
    both = (jax.nn.sigmoid(gates) * proj * pair_valid_mask.astype(jnp.float32)[None]).astype(
        jnp.bfloat16
    )
    left_tri = both[:C_TRI]
    right_tri = both[C_TRI:]
    moved_left, moved_right = (
        lax.all_to_all(left_tri, "axial", split_axis=0, concat_axis=1, tiled=True),
        lax.all_to_all(right_tri, "axial", split_axis=0, concat_axis=1, tiled=True),
    )
    partial_sum = jnp.einsum(
        "cik,cjk->cij", moved_left, moved_right, preferred_element_type=jnp.float32
    )
    tri_sum = lax.all_to_all(
        partial_sum.astype(jnp.bfloat16), "axial", split_axis=1, concat_axis=0, tiled=True
    ).astype(partial_sum.dtype)
    tri_update = finish_sums(tri_sum, triangle_output_weight)
    out_gate = jax.nn.sigmoid(
        jnp.einsum(
            "ijc,cz->ijz", tri_norm, triangle_output_gate, preferred_element_type=jnp.float32
        )
    )
    pair_output = (pair_one + out_gate * tri_update).astype(jnp.bfloat16)
    return (alignment_after_columns, pair_output)


BF16 = jnp.bfloat16
F32 = jnp.float32
SMALL_ROWS = 16
FLOPS = 3 * 10**9
PACKET_ORDER = (3, 2, 1)
PAIR_ORDER = (2, 1, 3)


def mul(lhs, rhs, over=((1,), (0,))):
    return lax.dot_general(lhs, rhs, (over, ((), ())), preferred_element_type=F32)


def iota(shape, axis):
    return lax.broadcasted_iota(jnp.int32, shape, axis)


def zero_one(condition):
    return jnp.where(condition, 1.0, 0.0).astype(BF16)


def normal(x):
    mean = jnp.mean(x, axis=-1, keepdims=True)
    centred = x - mean
    var = jnp.mean(centred * centred, axis=-1, keepdims=True)
    return centred * lax.rsqrt(var + 1e-05)


def sigmoid(x):
    return 0.5 + 0.5 * jnp.tanh(0.5 * x)


def column_softmax(scores):
    expo = jnp.exp(scores - jnp.max(scores, axis=0, keepdims=True))
    return expo * (1.0 / jnp.sum(expo, axis=0, keepdims=True))


def bias_rows(pair_ref, weight_ref):
    rows, residues, width = pair_ref.shape
    lanes = FOCUS_TOTAL * rows
    spread = zero_one(iota((FOCUS_TOTAL, lanes), 1) // rows == iota((FOCUS_TOTAL, lanes), 0))
    row_of = iota((width, lanes), 1) % rows
    flat = normal(pair_ref[...].astype(F32).reshape(rows * residues, width)).astype(BF16)
    weight = mul(weight_ref[...], spread, ((0,), (0,)))
    bias = jnp.zeros((residues, lanes), F32)
    for i in range(rows):
        one_row = jnp.where(row_of == i, weight, 0.0).astype(BF16)
        bias += mul(flat[i * residues : (i + 1) * residues], one_row)
    return bias


def table_kernel(lanes, count, shift_ref, turn_ref, column_ref):
    shape = column_ref.shape
    column_ref[...] = zero_one(iota(shape, 1) // C_TRI == iota(shape, 0))
    shape = shift_ref.shape
    shift_ref[...] = zero_one(iota(shape, 1) == iota(shape, 0) + lanes)
    shape = turn_ref.shape
    row_at = iota(shape, 0)
    turn_ref[...] = zero_one(
        iota(shape, 1) == (row_at % count) * (shape[0] // count) + row_at // count
    )


def packet_kernel(*refs):
    pair_ref, weight_ref, valid_ref, ids_ref, act_ref, present_ref, shift_ref = refs[:7]
    packet_ref, hidden_ref = refs[7:]
    rows, residues, width = pair_ref.shape
    per, _, features = act_ref.shape
    lanes = FOCUS_TOTAL * rows
    bias = bias_rows(pair_ref, weight_ref)
    extra = jnp.concatenate(
        [
            valid_ref[...].astype(F32),
            ids_ref[...].astype(F32),
            jnp.zeros((SMALL_ROWS - rows - per, residues), F32),
        ],
        axis=0,
    )
    extra = mul(extra.astype(BF16), shift_ref[...])
    empty = jnp.zeros((SMALL_ROWS, 128 - lanes), F32)
    first = jnp.concatenate([bias[:SMALL_ROWS], empty], axis=1) + extra
    second = jnp.concatenate([bias[SMALL_ROWS:], empty], axis=1)
    small = jnp.concatenate([first, second], axis=1).astype(BF16)
    packet_ref[per * residues :, :] = small
    shown = present_ref[...].astype(F32).astype(BF16)
    shown = mul(shown, jnp.ones((1, hidden_ref.shape[1]), BF16), ((0,), (0,)))
    hidden_ref[...] = 1000000000.0 * (shown - 1.0)
    packet_ref[: per * residues, :] = act_ref[...].reshape(per * residues, features)


def split_small(packet, residues, res_dev, per):
    small = packet[per * residues :, :].astype(F32)
    lanes = FOCUS_TOTAL * res_dev
    bias = jnp.concatenate([small[:, :lanes], small[:, 128 : 128 + lanes]], axis=0)
    extra = small[:, lanes : lanes + residues]
    return bias, extra[:res_dev], extra[res_dev : res_dev + per]


def project(x, w_query, w_kvg):
    width = FOCUS_TOTAL * FOCUS_SIZE
    flat = normal(x).astype(BF16)
    turned = ((0,), (1,))
    keys = mul(flat, w_kvg[:, :width]).astype(BF16)
    query = (mul(w_query[...], flat, turned) * FOCUS_SIZE ** (-0.5)).astype(BF16)
    values = mul(w_kvg[:, width : 2 * width], flat, turned).astype(BF16)
    gate = sigmoid(mul(w_kvg[:, 2 * width :], flat, turned))
    return keys, query, values, gate


def attend(keys, query, values, size, extra=None):
    width, tokens = query.shape
    group = min(tokens, 128)
    blocks = group // size
    together = 128 // FOCUS_SIZE
    block_of = iota((1, group), 1) // size
    groups = []
    for start in range(0, tokens, group):
        here = slice(start, start + group)
        heads = []
        for tile in range(0, width, 128):
            apart = []
            for p in range(together):
                row = tile + p * FOCUS_SIZE
                parts = [
                    jnp.zeros((p * FOCUS_SIZE, group), BF16),
                    query[row : row + FOCUS_SIZE, here],
                    jnp.zeros((128 - (p + 1) * FOCUS_SIZE, group), BF16),
                ]
                apart.append(jnp.concatenate([x for x in parts if x.shape[0]], axis=0))
            scores = mul(keys[here, tile : tile + 128], jnp.concatenate(apart, axis=1))
            for p in range(together):
                row = tile + p * FOCUS_SIZE
                full = scores[:, p * group : (p + 1) * group]
                own = full[:size]
                for b in range(1, blocks):
                    own = jnp.where(block_of == b, full[b * size : (b + 1) * size], own)
                if extra is not None:
                    own = own + extra[row // FOCUS_SIZE]
                weights = column_softmax(own)
                weights = jnp.concatenate(
                    [jnp.where(block_of == b, weights, 0.0) for b in range(blocks)], axis=0
                )
                heads.append(mul(values[row : row + FOCUS_SIZE, here], weights.astype(BF16)))
        groups.append(jnp.concatenate(heads, axis=0))
    return jnp.concatenate(groups, axis=1)


def msa_kernel(n, res_dev, *refs):
    packets, turn, hidden_keys, table = refs[:n], refs[n], refs[n + 1], refs[n + 2]
    refs = refs[n + 3 :]
    row_q, row_kvg, row_out, col_q, col_kvg, col_out, lift, outer_w = refs[:8]
    align_ref, update_ref, start, lifted = refs[8:]
    kinds, width = table.shape
    residues, lanes = hidden_keys.shape
    pair_width = outer_w.shape[1]
    per = (packets[0].shape[0] - SMALL_ROWS) // residues
    count = per * n
    tokens = count * residues
    me = lax.axis_index("axial")

    place = iota((FOCUS_TOTAL * res_dev, lanes), 0)
    place = (place // res_dev) * residues + place % res_dev - iota(place.shape, 1)
    bias = jnp.zeros((residues, lanes), F32)
    rows = []
    for packet, r in zip(packets, (0, *PACKET_ORDER)):
        part, _, all_ids = split_small(packet, residues, res_dev, per)
        bias += mul(part.astype(BF16), zero_one(place == -(me ^ r) * res_dev))
        for q in range(per):
            hot = zero_one(iota((kinds, residues), 0).astype(F32) == all_ids[q : q + 1])
            act = packet[q * residues : (q + 1) * residues, :].astype(F32)
            rows.append(act + mul(hot, table[...], ((0,), (0,))))
    zero = jnp.concatenate(rows, axis=0)
    extra = []
    for h in range(FOCUS_TOTAL):
        part = bias + hidden_keys[...]
        part = part[:, h * residues : (h + 1) * residues]
        extra.append(jnp.concatenate([part] * (128 // residues), axis=1))

    halves = range(0, width, 128)
    for half in halves:
        start[half // 128] = zero[:, half : half + 128]
    keys, query, values, gate = project(zero, row_q, row_kvg)
    mixed = (attend(keys, query, values, residues, extra) * gate).astype(BF16)
    mixed = mul(turn[...], mixed, ((1,), (1,))).astype(BF16)
    zero = jnp.concatenate(
        [
            jnp.concatenate(
                [start[half // 128, pl.ds(l, count, stride=residues), :] for l in range(residues)],
                axis=0,
            )
            for half in halves
        ],
        axis=1,
    )
    one = (zero + mul(mixed, row_out[...])).astype(BF16).astype(F32)

    keys, query, values, gate = project(one, col_q, col_kvg)
    mixed = (attend(keys, query, values, count) * gate).astype(BF16)
    align = (one + mul(mixed, col_out[...], ((0,), (0,)))).astype(BF16)
    own = count * res_dev
    row_at, lane_at = iota((own, tokens), 0), iota((own, tokens), 1)
    sequence = row_at // res_dev
    owner = (sequence // per) ^ me
    where_is = jnp.zeros_like(owner)
    for k, r in enumerate(PACKET_ORDER):
        where_is = jnp.where(owner == r, k + 1, where_is)
    pick = zero_one(
        lane_at
        == (row_at % res_dev + me * res_dev) * count + where_is * per + sequence % per
    )
    align_ref[...] = mul(pick, align).reshape(count, res_dev, width).astype(BF16)

    opm = normal(align.astype(F32)).astype(BF16)
    opm = mul(opm, lift[...], ((1,), (1,))).astype(BF16)
    hidden = MEAN_HIDDEN_SIZE
    deep = hidden * count
    spread = zero_one(
        iota((2 * hidden, deep), 1) // count == iota((2 * hidden, deep), 0)
    )
    left = mul(opm, spread)
    left = jnp.where(
        iota((tokens, deep), 0) % count == iota((tokens, deep), 1) % count, left, 0.0
    ).astype(BF16)
    gather = zero_one(iota((residues, tokens), 1) // count == iota((residues, tokens), 0))
    left = mul(gather, left).astype(BF16)
    right = opm[:, hidden:]
    for c in range(0, hidden, 2):
        pair_w = jnp.concatenate(
            [outer_w[(c + k) * hidden : (c + k + 1) * hidden, :] for k in range(2)], axis=1
        )
        part = mul(right, pair_w)
        lifted[c], lifted[c + 1] = part[:, :pair_width], part[:, pair_width:]
    for j in range(0, residues, 2):
        part = jnp.concatenate(
            [
                lifted[:, (j + k) * count : (j + k + 1) * count, :].reshape(deep, pair_width)
                for k in range(2)
            ],
            axis=1,
        )
        part = mul(left, part.astype(BF16)) * (1.0 / count)
        update_ref[j], update_ref[j + 1] = part[:, :pair_width], part[:, pair_width:]


def pair_kernel(*refs):
    pairs, packets, update, column, pair, own_mask = refs[:3], refs[3:6], *refs[6:10]
    proj, gates, gate_out, w_out, out_ref, state, one, right_at, left_at, valid = refs[10:]
    res_dev, residues, width = pair.shape
    per = (packets[0].shape[0] - SMALL_ROWS) // residues
    me = lax.axis_index("axial")
    own_valid = own_mask[...].astype(F32)
    for packet, r in zip((None, *packets), (0, *PACKET_ORDER)):
        shown = split_small(packet, residues, res_dev, per)[1] if r else own_valid
        valid[pl.ds(pl.multiple_of((me ^ r) * res_dev, res_dev), res_dev), :] = shown
    size = res_dev * residues
    for block, r in zip((pair, *pairs), (0, *PAIR_ORDER)):
        state[pl.ds(pl.multiple_of((me ^ r) * size, size), size), :] = (
            block[...].astype(F32).reshape(size, width)
        )
    for k in range(residues):
        one[k * residues : (k + 1) * residues, :] = (
            state[pl.ds(k, residues, stride=residues), :] + update[k]
        )

    shown = mul(valid[...].astype(BF16), column[...])
    right_w = jnp.concatenate([proj[:, C_TRI:], gates[:, C_TRI:]], axis=1)
    step = 8
    for k in range(0, residues, step):
        here = slice(k * residues, (k + step) * residues)
        both = mul(normal(one[here, :]).astype(BF16), right_w)
        both = sigmoid(both[:, C_TRI:]) * both[:, :C_TRI]
        for p in range(step):
            part = both[p * residues : (p + 1) * residues]
            part = part * shown[:, (k + p) * C_TRI : (k + p + 1) * C_TRI]
            right_at[(k + p) * residues : (k + p + 1) * residues, :] = part.astype(BF16).astype(F32)

    own = jnp.concatenate(
        [one[pl.ds(me * res_dev + i, residues, stride=residues), :] for i in range(res_dev)],
        axis=0,
    )
    left_w = jnp.concatenate([proj[:, :C_TRI], gates[:, :C_TRI], gate_out[...]], axis=1)
    own_all = mul(normal(own).astype(BF16), left_w)
    own_gate = sigmoid(own_all[:, 2 * C_TRI :])
    left = sigmoid(own_all[:, C_TRI : 2 * C_TRI]) * own_all[:, :C_TRI]
    shown = mul(own_valid.astype(BF16), column[:res_dev, : res_dev * C_TRI], ((0,), (0,)))
    for i in range(res_dev):
        part = left[i * residues : (i + 1) * residues] * shown[:, i * C_TRI : (i + 1) * C_TRI]
        left_at[i * residues : (i + 1) * residues, :] = part.astype(BF16).astype(F32)
    sums = [jnp.zeros((residues, C_TRI), F32) for _ in range(res_dev)]
    for k in range(residues):
        other = right_at[k * residues : (k + 1) * residues, :]
        for i in range(res_dev):
            sums[i] += left_at[i * residues + k : i * residues + k + 1, :] * other
    mixed = normal(jnp.concatenate(sums, axis=0)).astype(BF16)
    result = own + own_gate * mul(mixed, w_out[...])
    out_ref[...] = result.reshape(res_dev, residues, width).astype(BF16)


def call(kernel, out_shape, scratch, vmem_mib, *args):
    vmem = pl.BlockSpec(memory_space=pltpu.VMEM)
    return pl.pallas_call(
        kernel,
        out_shape=out_shape,
        in_specs=[vmem] * len(args),
        out_specs=jax.tree.map(lambda _: vmem, out_shape),
        scratch_shapes=scratch,
        compiler_params=pltpu.CompilerParams(vmem_limit_bytes=vmem_mib * 1024 * 1024),
        cost_estimate=pl.CostEstimate(flops=FLOPS, bytes_accessed=0, transcendentals=0),
    )(*args)


def swap(array, r, n):
    return lax.ppermute(array, "axial", [(i, i ^ r) for i in range(n)])


def local_whole(
    homolog_activity,
    homolog_symbol_ids,
    residue_present_mask,
    pair_state,
    pair_valid_mask,
    symbol_lookup_matrix,
    row_query_weight,
    horizontal_attention_matrix,
    pair_bias_weight,
    horizontal_final_matrix,
    column_query_weight,
    vertical_attention_matrix,
    vertical_final_matrix,
    tensor_mean_lift_matrix,
    outer_product_output_weight,
    triangle_projection_weight,
    triangle_projection_gate,
    triangle_output_gate,
    triangle_output_weight,
):
    n = lax.axis_size("axial")
    per, residues, width = homolog_activity.shape
    res_dev, _, pair_width = pair_state.shape
    count = per * n
    shift, turn, column = call(
        functools.partial(table_kernel, FOCUS_TOTAL * res_dev, count),
        (
            jax.ShapeDtypeStruct((residues, 128), BF16),
            jax.ShapeDtypeStruct((count * residues, count * residues), BF16),
            jax.ShapeDtypeStruct((residues, residues * C_TRI), BF16),
        ),
        [],
        2,
    )
    packet, hidden_keys = call(
        packet_kernel,
        (
            jax.ShapeDtypeStruct((per * residues + SMALL_ROWS, width), BF16),
            jax.ShapeDtypeStruct((residues, FOCUS_TOTAL * residues), F32),
        ),
        [],
        4,
        pair_state,
        pair_bias_weight.T,
        pair_valid_mask,
        homolog_symbol_ids,
        homolog_activity,
        residue_present_mask.reshape(1, residues),
        shift,
    )
    packets = [swap(packet, r, n) for r in PACKET_ORDER]
    _, later = lax.optimization_barrier((packet, pair_state))
    pairs = [swap(later, r, n) for r in PAIR_ORDER]
    alignment, update = call(
        functools.partial(msa_kernel, n, res_dev),
        (
            jax.ShapeDtypeStruct((count, res_dev, width), BF16),
            jax.ShapeDtypeStruct((residues, residues, pair_width), F32),
        ),
        [
            pltpu.VMEM((width // 128, count * residues, 128), F32),
            pltpu.VMEM((MEAN_HIDDEN_SIZE, count * residues, pair_width), F32),
        ],
        16,
        packet,
        *packets,
        turn,
        hidden_keys,
        symbol_lookup_matrix,
        row_query_weight,
        horizontal_attention_matrix,
        horizontal_final_matrix,
        column_query_weight,
        vertical_attention_matrix,
        vertical_final_matrix,
        tensor_mean_lift_matrix.T,
        outer_product_output_weight,
    )
    pair_output = call(
        pair_kernel,
        jax.ShapeDtypeStruct((res_dev, residues, pair_width), BF16),
        [
            pltpu.VMEM((residues * residues, pair_width), F32),
            pltpu.VMEM((residues * residues, pair_width), F32),
            pltpu.VMEM((residues * residues, C_TRI), F32),
            pltpu.VMEM((res_dev * residues, C_TRI), F32),
            pltpu.VMEM((residues, residues), F32),
        ],
        16,
        *pairs,
        *packets,
        update,
        column,
        pair_state,
        pair_valid_mask,
        triangle_projection_weight,
        triangle_projection_gate,
        triangle_output_gate,
        triangle_output_weight,
    )
    return (alignment, pair_output)


def local(homolog_activity, homolog_symbol_ids, residue_present_mask, pair_state, *others):
    n = lax.axis_size("axial")
    per, residues, _ = homolog_activity.shape
    small = n == 4 and per * n == 8 and residues == 32
    plan = local_whole if small else local_sharded
    return plan(homolog_activity, homolog_symbol_ids, residue_present_mask, pair_state, *others)


def solution(mesh):
    parts, copied = P(("dp", "axial")), P()
    return jax.shard_map(
        local,
        mesh=mesh,
        in_specs=(parts, parts, P("dp"), parts, parts) + (copied,) * 14,
        out_specs=(P("dp", "axial", None), P(("dp", "axial"), None, None)),
        check_vma=False,
    )
```

```python
import functools

import jax
import jax.numpy as jnp
from jax import lax
from jax.experimental import pallas as pl
from jax.experimental.pallas import tpu as pltpu
from jax.sharding import PartitionSpec as P

FOCUS_TOTAL = 8
FOCUS_SIZE = 32
MEAN_HIDDEN_SIZE = 32
C_TRI = 128


def layer_normalize(attended_entries):
    attended_entries = attended_entries.astype(jnp.float32)
    mean = jnp.mean(attended_entries, axis=-1, keepdims=True)
    centred = attended_entries - mean
    var = jnp.mean(centred * centred, axis=-1, keepdims=True)
    return centred * lax.rsqrt(var + 1e-05)


def gated_attend(evoformer_block, extra_axes, w_query, w_kvg, w_out):
    lines_list, residue_length, input_width = evoformer_block.shape
    width = FOCUS_TOTAL * FOCUS_SIZE
    flat = (
        layer_normalize(evoformer_block)
        .astype(jnp.bfloat16)
        .reshape(lines_list * residue_length, input_width)
    )
    query = (
        jnp.dot(flat, w_query, preferred_element_type=jnp.float32) * FOCUS_SIZE ** (-0.5)
    ).astype(jnp.bfloat16)
    query = query.reshape(lines_list, residue_length, FOCUS_TOTAL, FOCUS_SIZE)
    kvg = jnp.dot(flat, w_kvg, preferred_element_type=jnp.float32)
    keys = (
        kvg[:, :width]
        .astype(jnp.bfloat16)
        .reshape(lines_list, residue_length, FOCUS_TOTAL, FOCUS_SIZE)
    )
    attended_entries = (
        kvg[:, width : 2 * width]
        .astype(jnp.bfloat16)
        .reshape(lines_list, residue_length, FOCUS_TOTAL, FOCUS_SIZE)
    )
    gate = jax.nn.sigmoid(kvg[:, 2 * width :]).reshape(
        lines_list, residue_length, FOCUS_TOTAL, FOCUS_SIZE
    )
    scores = (
        jnp.einsum("bihd,bjhd->bhij", query, keys, preferred_element_type=jnp.float32) + extra_axes
    )
    top = jnp.max(scores, axis=-1, keepdims=True)
    expo = jnp.exp(scores - top)
    weights = (expo / jnp.sum(expo, axis=-1, keepdims=True)).astype(jnp.bfloat16)
    mixed = jnp.einsum(
        "bhij,bjhd->bihd", weights, attended_entries, preferred_element_type=jnp.float32
    )
    mixed = (mixed * gate).astype(jnp.bfloat16).reshape(lines_list * residue_length, width)
    return evoformer_block + jnp.dot(mixed, w_out, preferred_element_type=jnp.float32).reshape(
        lines_list, residue_length, input_width
    )


def finish_sums(evoformer_block, triangle_output_weight):
    mixed = layer_normalize(jnp.transpose(evoformer_block, (1, 2, 0))).astype(jnp.bfloat16)
    return jnp.einsum(
        "ijc,cz->ijz", mixed, triangle_output_weight, preferred_element_type=jnp.float32
    )


def local_sharded(
    homolog_activity,
    homolog_symbol_ids,
    residue_present_mask,
    pair_state,
    pair_valid_mask,
    symbol_lookup_matrix,
    row_query_weight,
    horizontal_attention_matrix,
    pair_bias_weight,
    horizontal_final_matrix,
    column_query_weight,
    vertical_attention_matrix,
    vertical_final_matrix,
    tensor_mean_lift_matrix,
    outer_product_output_weight,
    triangle_projection_weight,
    triangle_projection_gate,
    triangle_output_gate,
    triangle_output_weight,
):
    sequence_per_device, residue_length, input_width = homolog_activity.shape
    res_dev = pair_state.shape[0]
    group_size = lax.axis_size("axial")
    token_classes = symbol_lookup_matrix.shape[0]
    token_one_hot = (
        homolog_symbol_ids[..., None] == jnp.arange(token_classes, dtype=jnp.int32)
    ).astype(jnp.bfloat16)
    token_embedded = jnp.einsum(
        "slt,tc->slc", token_one_hot, symbol_lookup_matrix, preferred_element_type=jnp.float32
    )
    homolog_starting = homolog_activity.astype(jnp.float32) + token_embedded
    pair_norm = layer_normalize(pair_state).astype(jnp.bfloat16)
    bias_rows = jnp.einsum(
        "ijc,ch->hij", pair_norm, pair_bias_weight, preferred_element_type=jnp.float32
    ).astype(jnp.bfloat16)
    bias_full = lax.all_gather(bias_rows, "axial", axis=1, tiled=True)
    key_bias = 1000000000.0 * (residue_present_mask.astype(jnp.float32) - 1.0)
    extra_axes = bias_full.astype(jnp.float32)[None] + key_bias[None, None, None, :]
    cluster_total = homolog_starting.reshape(
        sequence_per_device // 2, 2, residue_length, input_width
    )
    homolog_across_update = lax.map(
        lambda evoformer_block: gated_attend(
            evoformer_block,
            extra_axes,
            row_query_weight,
            horizontal_attention_matrix,
            horizontal_final_matrix,
        ),
        cluster_total,
    )
    homolog_across_update = homolog_across_update.reshape(
        sequence_per_device, group_size, res_dev, input_width
    ).astype(jnp.bfloat16)
    moved = jnp.swapaxes(
        lax.all_to_all(homolog_across_update, "axial", split_axis=1, concat_axis=0, tiled=True)[
            :, 0
        ],
        0,
        1,
    )
    finished = lax.map(
        lambda item: gated_attend(
            item[None].astype(jnp.float32),
            0.0,
            column_query_weight,
            vertical_attention_matrix,
            vertical_final_matrix,
        )[0],
        moved,
    )
    exchanged = jnp.swapaxes(finished, 0, 1).astype(jnp.bfloat16)[:, None]
    sequence_count = exchanged.shape[0]
    alignment_after_columns = exchanged.reshape(sequence_count, res_dev, input_width)
    tensor_mean_scaler = layer_normalize(alignment_after_columns).astype(jnp.bfloat16)
    split_parts = jnp.einsum(
        "src,cf->rsf",
        tensor_mean_scaler,
        tensor_mean_lift_matrix,
        preferred_element_type=jnp.float32,
    ).astype(jnp.bfloat16)
    first_factor = split_parts[..., :MEAN_HIDDEN_SIZE]
    second_factor = split_parts[..., MEAN_HIDDEN_SIZE:].reshape(
        res_dev, sequence_count * MEAN_HIDDEN_SIZE
    )
    step_rows = 8
    left_blocks = first_factor.reshape(
        res_dev // step_rows, step_rows, sequence_count, MEAN_HIDDEN_SIZE
    )
    piece = lax.all_gather(second_factor, "axial", axis=0, tiled=True)
    count = piece.shape[0]
    right_part = piece.reshape(count, sequence_count, MEAN_HIDDEN_SIZE)

    def one_block(lines_list):
        tensor_mean = (
            jnp.einsum("isc,jsd->ijcd", lines_list, right_part, preferred_element_type=jnp.float32)
            / sequence_count
        )
        tensor_mean = tensor_mean.reshape(
            step_rows, count, MEAN_HIDDEN_SIZE * MEAN_HIDDEN_SIZE
        ).astype(jnp.bfloat16)
        return jnp.einsum(
            "ijf,fz->ijz",
            tensor_mean,
            outer_product_output_weight,
            preferred_element_type=jnp.float32,
        )

    update = lax.map(one_block, left_blocks).reshape(
        res_dev, count, outer_product_output_weight.shape[1]
    )
    pair_one = pair_state.astype(jnp.float32) + update
    tri_norm = layer_normalize(pair_one).astype(jnp.bfloat16)
    proj = jnp.einsum(
        "ikc,cf->fik", tri_norm, triangle_projection_weight, preferred_element_type=jnp.float32
    )
    gates = jnp.einsum(
        "ikc,cf->fik", tri_norm, triangle_projection_gate, preferred_element_type=jnp.float32
    )
    both = (jax.nn.sigmoid(gates) * proj * pair_valid_mask.astype(jnp.float32)[None]).astype(
        jnp.bfloat16
    )
    left_tri = both[:C_TRI]
    right_tri = both[C_TRI:]
    moved_left, moved_right = (
        lax.all_to_all(left_tri, "axial", split_axis=0, concat_axis=1, tiled=True),
        lax.all_to_all(right_tri, "axial", split_axis=0, concat_axis=1, tiled=True),
    )
    partial_sum = jnp.einsum(
        "cik,cjk->cij", moved_left, moved_right, preferred_element_type=jnp.float32
    )
    tri_sum = lax.all_to_all(
        partial_sum.astype(jnp.bfloat16), "axial", split_axis=1, concat_axis=0, tiled=True
    ).astype(partial_sum.dtype)
    tri_update = finish_sums(tri_sum, triangle_output_weight)
    out_gate = jax.nn.sigmoid(
        jnp.einsum(
            "ijc,cz->ijz", tri_norm, triangle_output_gate, preferred_element_type=jnp.float32
        )
    )
    pair_output = (pair_one + out_gate * tri_update).astype(jnp.bfloat16)
    return (alignment_after_columns, pair_output)


BF16 = jnp.bfloat16
F32 = jnp.float32
SMALL_ROWS = 16
FLOPS = 3 * 10**9
PACKET_ORDER = (3, 2, 1)
PAIR_ORDER = (2, 1, 3)


def mul(lhs, rhs, over=((1,), (0,))):
    return lax.dot_general(lhs, rhs, (over, ((), ())), preferred_element_type=F32)


def iota(shape, axis):
    return lax.broadcasted_iota(jnp.int32, shape, axis)


def zero_one(condition):
    return jnp.where(condition, 1.0, 0.0).astype(BF16)


def normal(x):
    mean = jnp.mean(x, axis=-1, keepdims=True)
    centred = x - mean
    var = jnp.mean(centred * centred, axis=-1, keepdims=True)
    return centred * lax.rsqrt(var + 1e-05)


def sigmoid(x):
    return 0.5 + 0.5 * jnp.tanh(0.5 * x)


def column_softmax(scores):
    expo = jnp.exp(scores - jnp.max(scores, axis=0, keepdims=True))
    return expo * (1.0 / jnp.sum(expo, axis=0, keepdims=True))


def bias_rows(pair_ref, weight_ref):
    rows, residues, width = pair_ref.shape
    lanes = FOCUS_TOTAL * rows
    spread = zero_one(iota((FOCUS_TOTAL, lanes), 1) // rows == iota((FOCUS_TOTAL, lanes), 0))
    row_of = iota((width, lanes), 1) % rows
    flat = normal(pair_ref[...].astype(F32).reshape(rows * residues, width)).astype(BF16)
    weight = mul(weight_ref[...], spread, ((0,), (0,)))
    bias = jnp.zeros((residues, lanes), F32)
    for i in range(rows):
        one_row = jnp.where(row_of == i, weight, 0.0).astype(BF16)
        bias += mul(flat[i * residues : (i + 1) * residues], one_row)
    return bias


def table_kernel(lanes, count, shift_ref, turn_ref, column_ref):
    shape = column_ref.shape
    column_ref[...] = zero_one(iota(shape, 1) // C_TRI == iota(shape, 0))
    shape = shift_ref.shape
    shift_ref[...] = zero_one(iota(shape, 1) == iota(shape, 0) + lanes)
    shape = turn_ref.shape
    row_at = iota(shape, 0)
    turn_ref[...] = zero_one(
        iota(shape, 1) == (row_at % count) * (shape[0] // count) + row_at // count
    )


def packet_kernel(*refs):
    pair_ref, weight_ref, valid_ref, ids_ref, act_ref, present_ref, shift_ref = refs[:7]
    packet_ref, hidden_ref = refs[7:]
    rows, residues, width = pair_ref.shape
    per, _, features = act_ref.shape
    lanes = FOCUS_TOTAL * rows
    bias = bias_rows(pair_ref, weight_ref)
    extra = jnp.concatenate(
        [
            valid_ref[...].astype(F32),
            ids_ref[...].astype(F32),
            jnp.zeros((SMALL_ROWS - rows - per, residues), F32),
        ],
        axis=0,
    )
    extra = mul(extra.astype(BF16), shift_ref[...])
    empty = jnp.zeros((SMALL_ROWS, 128 - lanes), F32)
    first = jnp.concatenate([bias[:SMALL_ROWS], empty], axis=1) + extra
    second = jnp.concatenate([bias[SMALL_ROWS:], empty], axis=1)
    small = jnp.concatenate([first, second], axis=1).astype(BF16)
    packet_ref[per * residues :, :] = small
    shown = present_ref[...].astype(F32).astype(BF16)
    shown = mul(shown, jnp.ones((1, hidden_ref.shape[1]), BF16), ((0,), (0,)))
    hidden_ref[...] = 1000000000.0 * (shown - 1.0)
    packet_ref[: per * residues, :] = act_ref[...].reshape(per * residues, features)


def split_small(packet, residues, res_dev, per):
    small = packet[per * residues :, :].astype(F32)
    lanes = FOCUS_TOTAL * res_dev
    bias = jnp.concatenate([small[:, :lanes], small[:, 128 : 128 + lanes]], axis=0)
    extra = small[:, lanes : lanes + residues]
    return bias, extra[:res_dev], extra[res_dev : res_dev + per]


def head_masks(width):
    return [
        zero_one(iota((1, width), 1) // FOCUS_SIZE == h) for h in range(FOCUS_TOTAL)
    ]


def project(x, w_query, w_kvg):
    width = FOCUS_TOTAL * FOCUS_SIZE
    flat = normal(x).astype(BF16)
    query = (mul(flat, w_query[...]) * FOCUS_SIZE ** (-0.5)).astype(BF16)
    keys = mul(flat, w_kvg[:, :width]).astype(BF16)
    values = mul(flat, w_kvg[:, width : 2 * width]).astype(BF16)
    gate = sigmoid(mul(flat, w_kvg[:, 2 * width :]))
    return query, keys, values, gate


def msa_kernel(n, res_dev, *refs):
    packets, turn, hidden_keys, table = refs[:n], refs[n], refs[n + 1], refs[n + 2]
    refs = refs[n + 3 :]
    row_q, row_kvg, row_out, col_q, col_kvg, col_out, lift, outer_w = refs[:8]
    align_ref, update_ref, lifted = refs[8:]
    kinds, width = table.shape
    residues, lanes = hidden_keys.shape
    pair_width = outer_w.shape[1]
    per = (packets[0].shape[0] - SMALL_ROWS) // residues
    count = per * n
    tokens = count * residues
    me = lax.axis_index("axial")

    place = iota((FOCUS_TOTAL * res_dev, lanes), 0)
    place = (place // res_dev) * residues + place % res_dev - iota(place.shape, 1)
    bias = jnp.zeros((residues, lanes), F32)
    rows = []
    for packet, r in zip(packets, (0, *PACKET_ORDER)):
        part, _, all_ids = split_small(packet, residues, res_dev, per)
        bias += mul(part.astype(BF16), zero_one(place == -(me ^ r) * res_dev))
        for q in range(per):
            hot = zero_one(iota((kinds, residues), 0).astype(F32) == all_ids[q : q + 1])
            act = packet[q * residues : (q + 1) * residues, :].astype(F32)
            rows.append(act + mul(hot, table[...], ((0,), (0,))))
    zero = jnp.concatenate(rows, axis=0)
    extra = bias + hidden_keys[...]
    masks = head_masks(width)

    query, keys, values, gate = project(zero, row_q, row_kvg)
    rows = []
    for s in range(count):
        here = slice(s * residues, (s + 1) * residues)
        spread = jnp.concatenate([query[here] * mask for mask in masks], axis=0)
        weights = column_softmax(mul(keys[here], spread, ((1,), (1,))) + extra).astype(BF16)
        heads = mul(weights, values[here], ((0,), (0,)))
        mixed = heads[:residues]
        for h in range(1, FOCUS_TOTAL):
            part = heads[h * residues : (h + 1) * residues]
            mixed = jnp.where(iota((1, width), 1) // FOCUS_SIZE == h, part, mixed)
        rows.append(mixed)
    mixed = (jnp.concatenate(rows, axis=0) * gate).astype(BF16)
    msa_one = (zero + mul(mixed, row_out[...])).astype(BF16)

    one = mul(turn[...], msa_one)
    query, keys, values, gate = project(one, col_q, col_kvg)
    group = min(tokens, 128)
    sites = group // count
    block_of = iota((1, group), 1) // count
    groups = []
    for g in range(tokens // group):
        here = slice(g * group, (g + 1) * group)
        all_weights, all_values = [], []
        for mask in masks:
            full = mul(keys[here], query[here] * mask, ((1,), (1,)))
            scores = full[:count]
            for b in range(1, sites):
                scores = jnp.where(block_of == b, full[b * count : (b + 1) * count], scores)
            weights = column_softmax(scores)
            weights = jnp.concatenate(
                [jnp.where(block_of == b, weights, 0.0) for b in range(sites)], axis=0
            )
            all_weights.append(weights.astype(BF16))
            all_values.append(values[here] * mask)
        groups.append(
            mul(
                jnp.concatenate(all_weights, axis=0),
                jnp.concatenate(all_values, axis=0),
                ((0,), (0,)),
            )
        )
    mixed = (jnp.concatenate(groups, axis=0) * gate).astype(BF16)
    align = (one + mul(mixed, col_out[...])).astype(BF16)
    own = count * res_dev
    row_at, lane_at = iota((own, tokens), 0), iota((own, tokens), 1)
    sequence = row_at // res_dev
    owner = (sequence // per) ^ me
    where_is = jnp.zeros_like(owner)
    for k, r in enumerate(PACKET_ORDER):
        where_is = jnp.where(owner == r, k + 1, where_is)
    pick = zero_one(
        lane_at
        == (row_at % res_dev + me * res_dev) * count + where_is * per + sequence % per
    )
    align_ref[...] = mul(pick, align).reshape(count, res_dev, width).astype(BF16)

    opm = normal(align.astype(F32)).astype(BF16)
    opm = mul(opm, lift[...], ((1,), (1,))).astype(BF16)
    hidden = MEAN_HIDDEN_SIZE
    deep = hidden * count
    spread = zero_one(
        iota((2 * hidden, deep), 1) // count == iota((2 * hidden, deep), 0)
    )
    left = mul(opm, spread)
    left = jnp.where(
        iota((tokens, deep), 0) % count == iota((tokens, deep), 1) % count, left, 0.0
    ).astype(BF16)
    gather = zero_one(iota((residues, tokens), 1) // count == iota((residues, tokens), 0))
    left = mul(gather, left).astype(BF16)
    right = opm[:, hidden:]
    for c in range(0, hidden, 2):
        pair_w = jnp.concatenate(
            [outer_w[(c + k) * hidden : (c + k + 1) * hidden, :] for k in range(2)], axis=1
        )
        part = mul(right, pair_w)
        lifted[c], lifted[c + 1] = part[:, :pair_width], part[:, pair_width:]
    for j in range(0, residues, 2):
        part = jnp.concatenate(
            [
                lifted[:, (j + k) * count : (j + k + 1) * count, :].reshape(deep, pair_width)
                for k in range(2)
            ],
            axis=1,
        )
        part = mul(left, part.astype(BF16)) * (1.0 / count)
        update_ref[j], update_ref[j + 1] = part[:, :pair_width], part[:, pair_width:]


def pair_kernel(*refs):
    pairs, packets, update, column, pair, own_mask = refs[:3], refs[3:6], *refs[6:10]
    proj, gates, gate_out, w_out, out_ref, state, one, right_at, left_at, valid = refs[10:]
    res_dev, residues, width = pair.shape
    per = (packets[0].shape[0] - SMALL_ROWS) // residues
    me = lax.axis_index("axial")
    own_valid = own_mask[...].astype(F32)
    for packet, r in zip((None, *packets), (0, *PACKET_ORDER)):
        shown = split_small(packet, residues, res_dev, per)[1] if r else own_valid
        valid[pl.ds(pl.multiple_of((me ^ r) * res_dev, res_dev), res_dev), :] = shown
    size = res_dev * residues
    for block, r in zip((pair, *pairs), (0, *PAIR_ORDER)):
        state[pl.ds(pl.multiple_of((me ^ r) * size, size), size), :] = (
            block[...].astype(F32).reshape(size, width)
        )
    for k in range(residues):
        one[k * residues : (k + 1) * residues, :] = (
            state[pl.ds(k, residues, stride=residues), :] + update[k]
        )

    shown = mul(valid[...].astype(BF16), column[...])
    right_w = jnp.concatenate([proj[:, C_TRI:], gates[:, C_TRI:]], axis=1)
    step = 8
    for k in range(0, residues, step):
        here = slice(k * residues, (k + step) * residues)
        both = mul(normal(one[here, :]).astype(BF16), right_w)
        both = sigmoid(both[:, C_TRI:]) * both[:, :C_TRI]
        for p in range(step):
            part = both[p * residues : (p + 1) * residues]
            part = part * shown[:, (k + p) * C_TRI : (k + p + 1) * C_TRI]
            right_at[(k + p) * residues : (k + p + 1) * residues, :] = part.astype(BF16).astype(F32)

    own = jnp.concatenate(
        [one[pl.ds(me * res_dev + i, residues, stride=residues), :] for i in range(res_dev)],
        axis=0,
    )
    left_w = jnp.concatenate([proj[:, :C_TRI], gates[:, :C_TRI], gate_out[...]], axis=1)
    own_all = mul(normal(own).astype(BF16), left_w)
    own_gate = sigmoid(own_all[:, 2 * C_TRI :])
    left = sigmoid(own_all[:, C_TRI : 2 * C_TRI]) * own_all[:, :C_TRI]
    shown = mul(own_valid.astype(BF16), column[:res_dev, : res_dev * C_TRI], ((0,), (0,)))
    for i in range(res_dev):
        part = left[i * residues : (i + 1) * residues] * shown[:, i * C_TRI : (i + 1) * C_TRI]
        left_at[i * residues : (i + 1) * residues, :] = part.astype(BF16).astype(F32)
    sums = [jnp.zeros((residues, C_TRI), F32) for _ in range(res_dev)]
    for k in range(residues):
        other = right_at[k * residues : (k + 1) * residues, :]
        for i in range(res_dev):
            sums[i] += left_at[i * residues + k : i * residues + k + 1, :] * other
    mixed = normal(jnp.concatenate(sums, axis=0)).astype(BF16)
    result = own + own_gate * mul(mixed, w_out[...])
    out_ref[...] = result.reshape(res_dev, residues, width).astype(BF16)


def call(kernel, out_shape, scratch, vmem_mib, *args):
    vmem = pl.BlockSpec(memory_space=pltpu.VMEM)
    return pl.pallas_call(
        kernel,
        out_shape=out_shape,
        in_specs=[vmem] * len(args),
        out_specs=jax.tree.map(lambda _: vmem, out_shape),
        scratch_shapes=scratch,
        compiler_params=pltpu.CompilerParams(vmem_limit_bytes=vmem_mib * 1024 * 1024),
        cost_estimate=pl.CostEstimate(flops=FLOPS, bytes_accessed=0, transcendentals=0),
    )(*args)


def swap(array, r, n):
    return lax.ppermute(array, "axial", [(i, i ^ r) for i in range(n)])


def local_whole(
    homolog_activity,
    homolog_symbol_ids,
    residue_present_mask,
    pair_state,
    pair_valid_mask,
    symbol_lookup_matrix,
    row_query_weight,
    horizontal_attention_matrix,
    pair_bias_weight,
    horizontal_final_matrix,
    column_query_weight,
    vertical_attention_matrix,
    vertical_final_matrix,
    tensor_mean_lift_matrix,
    outer_product_output_weight,
    triangle_projection_weight,
    triangle_projection_gate,
    triangle_output_gate,
    triangle_output_weight,
):
    n = lax.axis_size("axial")
    per, residues, width = homolog_activity.shape
    res_dev, _, pair_width = pair_state.shape
    count = per * n
    shift, turn, column = call(
        functools.partial(table_kernel, FOCUS_TOTAL * res_dev, count),
        (
            jax.ShapeDtypeStruct((residues, 128), BF16),
            jax.ShapeDtypeStruct((count * residues, count * residues), BF16),
            jax.ShapeDtypeStruct((residues, residues * C_TRI), BF16),
        ),
        [],
        2,
    )
    packet, hidden_keys = call(
        packet_kernel,
        (
            jax.ShapeDtypeStruct((per * residues + SMALL_ROWS, width), BF16),
            jax.ShapeDtypeStruct((residues, FOCUS_TOTAL * residues), F32),
        ),
        [],
        4,
        pair_state,
        pair_bias_weight.T,
        pair_valid_mask,
        homolog_symbol_ids,
        homolog_activity,
        residue_present_mask.reshape(1, residues),
        shift,
    )
    packets = [swap(packet, r, n) for r in PACKET_ORDER]
    _, later = lax.optimization_barrier((packet, pair_state))
    pairs = [swap(later, r, n) for r in PAIR_ORDER]
    alignment, update = call(
        functools.partial(msa_kernel, n, res_dev),
        (
            jax.ShapeDtypeStruct((count, res_dev, width), BF16),
            jax.ShapeDtypeStruct((residues, residues, pair_width), F32),
        ),
        [
            pltpu.VMEM((MEAN_HIDDEN_SIZE, count * residues, pair_width), F32),
        ],
        16,
        packet,
        *packets,
        turn,
        hidden_keys,
        symbol_lookup_matrix,
        row_query_weight,
        horizontal_attention_matrix,
        horizontal_final_matrix,
        column_query_weight,
        vertical_attention_matrix,
        vertical_final_matrix,
        tensor_mean_lift_matrix.T,
        outer_product_output_weight,
    )
    pair_output = call(
        pair_kernel,
        jax.ShapeDtypeStruct((res_dev, residues, pair_width), BF16),
        [
            pltpu.VMEM((residues * residues, pair_width), F32),
            pltpu.VMEM((residues * residues, pair_width), F32),
            pltpu.VMEM((residues * residues, C_TRI), F32),
            pltpu.VMEM((res_dev * residues, C_TRI), F32),
            pltpu.VMEM((residues, residues), F32),
        ],
        16,
        *pairs,
        *packets,
        update,
        column,
        pair_state,
        pair_valid_mask,
        triangle_projection_weight,
        triangle_projection_gate,
        triangle_output_gate,
        triangle_output_weight,
    )
    return (alignment, pair_output)


def local(homolog_activity, homolog_symbol_ids, residue_present_mask, pair_state, *others):
    n = lax.axis_size("axial")
    per, residues, _ = homolog_activity.shape
    small = n == 4 and per * n == 8 and residues == 32
    plan = local_whole if small else local_sharded
    return plan(homolog_activity, homolog_symbol_ids, residue_present_mask, pair_state, *others)


def solution(mesh):
    parts, copied = P(("dp", "axial")), P()
    return jax.shard_map(
        local,
        mesh=mesh,
        in_specs=(parts, parts, P("dp"), parts, parts) + (copied,) * 14,
        out_specs=(P("dp", "axial", None), P(("dp", "axial"), None, None)),
        check_vma=False,
    )
```

```python
import functools

import jax
import jax.numpy as jnp
from jax import lax
from jax.experimental import pallas as pl
from jax.experimental.pallas import tpu as pltpu
from jax.sharding import PartitionSpec as P

FOCUS_TOTAL = 8
FOCUS_SIZE = 32
MEAN_HIDDEN_SIZE = 32
C_TRI = 128


def layer_normalize(attended_entries):
    attended_entries = attended_entries.astype(jnp.float32)
    mean = jnp.mean(attended_entries, axis=-1, keepdims=True)
    centred = attended_entries - mean
    var = jnp.mean(centred * centred, axis=-1, keepdims=True)
    return centred * lax.rsqrt(var + 1e-05)


def gated_attend(evoformer_block, extra_axes, w_query, w_kvg, w_out):
    lines_list, residue_length, input_width = evoformer_block.shape
    width = FOCUS_TOTAL * FOCUS_SIZE
    flat = (
        layer_normalize(evoformer_block)
        .astype(jnp.bfloat16)
        .reshape(lines_list * residue_length, input_width)
    )
    query = (
        jnp.dot(flat, w_query, preferred_element_type=jnp.float32) * FOCUS_SIZE ** (-0.5)
    ).astype(jnp.bfloat16)
    query = query.reshape(lines_list, residue_length, FOCUS_TOTAL, FOCUS_SIZE)
    kvg = jnp.dot(flat, w_kvg, preferred_element_type=jnp.float32)
    keys = (
        kvg[:, :width]
        .astype(jnp.bfloat16)
        .reshape(lines_list, residue_length, FOCUS_TOTAL, FOCUS_SIZE)
    )
    attended_entries = (
        kvg[:, width : 2 * width]
        .astype(jnp.bfloat16)
        .reshape(lines_list, residue_length, FOCUS_TOTAL, FOCUS_SIZE)
    )
    gate = jax.nn.sigmoid(kvg[:, 2 * width :]).reshape(
        lines_list, residue_length, FOCUS_TOTAL, FOCUS_SIZE
    )
    scores = (
        jnp.einsum("bihd,bjhd->bhij", query, keys, preferred_element_type=jnp.float32) + extra_axes
    )
    top = jnp.max(scores, axis=-1, keepdims=True)
    expo = jnp.exp(scores - top)
    weights = (expo / jnp.sum(expo, axis=-1, keepdims=True)).astype(jnp.bfloat16)
    mixed = jnp.einsum(
        "bhij,bjhd->bihd", weights, attended_entries, preferred_element_type=jnp.float32
    )
    mixed = (mixed * gate).astype(jnp.bfloat16).reshape(lines_list * residue_length, width)
    return evoformer_block + jnp.dot(mixed, w_out, preferred_element_type=jnp.float32).reshape(
        lines_list, residue_length, input_width
    )


def finish_sums(evoformer_block, triangle_output_weight):
    mixed = layer_normalize(jnp.transpose(evoformer_block, (1, 2, 0))).astype(jnp.bfloat16)
    return jnp.einsum(
        "ijc,cz->ijz", mixed, triangle_output_weight, preferred_element_type=jnp.float32
    )


def local_sharded(
    homolog_activity,
    homolog_symbol_ids,
    residue_present_mask,
    pair_state,
    pair_valid_mask,
    symbol_lookup_matrix,
    row_query_weight,
    horizontal_attention_matrix,
    pair_bias_weight,
    horizontal_final_matrix,
    column_query_weight,
    vertical_attention_matrix,
    vertical_final_matrix,
    tensor_mean_lift_matrix,
    outer_product_output_weight,
    triangle_projection_weight,
    triangle_projection_gate,
    triangle_output_gate,
    triangle_output_weight,
):
    sequence_per_device, residue_length, input_width = homolog_activity.shape
    res_dev = pair_state.shape[0]
    group_size = lax.axis_size("axial")
    token_classes = symbol_lookup_matrix.shape[0]
    token_one_hot = (
        homolog_symbol_ids[..., None] == jnp.arange(token_classes, dtype=jnp.int32)
    ).astype(jnp.bfloat16)
    token_embedded = jnp.einsum(
        "slt,tc->slc", token_one_hot, symbol_lookup_matrix, preferred_element_type=jnp.float32
    )
    homolog_starting = homolog_activity.astype(jnp.float32) + token_embedded
    pair_norm = layer_normalize(pair_state).astype(jnp.bfloat16)
    bias_rows = jnp.einsum(
        "ijc,ch->hij", pair_norm, pair_bias_weight, preferred_element_type=jnp.float32
    ).astype(jnp.bfloat16)
    bias_full = lax.all_gather(bias_rows, "axial", axis=1, tiled=True)
    key_bias = 1000000000.0 * (residue_present_mask.astype(jnp.float32) - 1.0)
    extra_axes = bias_full.astype(jnp.float32)[None] + key_bias[None, None, None, :]
    cluster_total = homolog_starting.reshape(
        sequence_per_device // 2, 2, residue_length, input_width
    )
    homolog_across_update = lax.map(
        lambda evoformer_block: gated_attend(
            evoformer_block,
            extra_axes,
            row_query_weight,
            horizontal_attention_matrix,
            horizontal_final_matrix,
        ),
        cluster_total,
    )
    homolog_across_update = homolog_across_update.reshape(
        sequence_per_device, group_size, res_dev, input_width
    ).astype(jnp.bfloat16)
    moved = jnp.swapaxes(
        lax.all_to_all(homolog_across_update, "axial", split_axis=1, concat_axis=0, tiled=True)[
            :, 0
        ],
        0,
        1,
    )
    finished = lax.map(
        lambda item: gated_attend(
            item[None].astype(jnp.float32),
            0.0,
            column_query_weight,
            vertical_attention_matrix,
            vertical_final_matrix,
        )[0],
        moved,
    )
    exchanged = jnp.swapaxes(finished, 0, 1).astype(jnp.bfloat16)[:, None]
    sequence_count = exchanged.shape[0]
    alignment_after_columns = exchanged.reshape(sequence_count, res_dev, input_width)
    tensor_mean_scaler = layer_normalize(alignment_after_columns).astype(jnp.bfloat16)
    split_parts = jnp.einsum(
        "src,cf->rsf",
        tensor_mean_scaler,
        tensor_mean_lift_matrix,
        preferred_element_type=jnp.float32,
    ).astype(jnp.bfloat16)
    first_factor = split_parts[..., :MEAN_HIDDEN_SIZE]
    second_factor = split_parts[..., MEAN_HIDDEN_SIZE:].reshape(
        res_dev, sequence_count * MEAN_HIDDEN_SIZE
    )
    step_rows = 8
    left_blocks = first_factor.reshape(
        res_dev // step_rows, step_rows, sequence_count, MEAN_HIDDEN_SIZE
    )
    piece = lax.all_gather(second_factor, "axial", axis=0, tiled=True)
    count = piece.shape[0]
    right_part = piece.reshape(count, sequence_count, MEAN_HIDDEN_SIZE)

    def one_block(lines_list):
        tensor_mean = (
            jnp.einsum("isc,jsd->ijcd", lines_list, right_part, preferred_element_type=jnp.float32)
            / sequence_count
        )
        tensor_mean = tensor_mean.reshape(
            step_rows, count, MEAN_HIDDEN_SIZE * MEAN_HIDDEN_SIZE
        ).astype(jnp.bfloat16)
        return jnp.einsum(
            "ijf,fz->ijz",
            tensor_mean,
            outer_product_output_weight,
            preferred_element_type=jnp.float32,
        )

    update = lax.map(one_block, left_blocks).reshape(
        res_dev, count, outer_product_output_weight.shape[1]
    )
    pair_one = pair_state.astype(jnp.float32) + update
    tri_norm = layer_normalize(pair_one).astype(jnp.bfloat16)
    proj = jnp.einsum(
        "ikc,cf->fik", tri_norm, triangle_projection_weight, preferred_element_type=jnp.float32
    )
    gates = jnp.einsum(
        "ikc,cf->fik", tri_norm, triangle_projection_gate, preferred_element_type=jnp.float32
    )
    both = (jax.nn.sigmoid(gates) * proj * pair_valid_mask.astype(jnp.float32)[None]).astype(
        jnp.bfloat16
    )
    left_tri = both[:C_TRI]
    right_tri = both[C_TRI:]
    moved_left, moved_right = (
        lax.all_to_all(left_tri, "axial", split_axis=0, concat_axis=1, tiled=True),
        lax.all_to_all(right_tri, "axial", split_axis=0, concat_axis=1, tiled=True),
    )
    partial_sum = jnp.einsum(
        "cik,cjk->cij", moved_left, moved_right, preferred_element_type=jnp.float32
    )
    tri_sum = lax.all_to_all(
        partial_sum.astype(jnp.bfloat16), "axial", split_axis=1, concat_axis=0, tiled=True
    ).astype(partial_sum.dtype)
    tri_update = finish_sums(tri_sum, triangle_output_weight)
    out_gate = jax.nn.sigmoid(
        jnp.einsum(
            "ijc,cz->ijz", tri_norm, triangle_output_gate, preferred_element_type=jnp.float32
        )
    )
    pair_output = (pair_one + out_gate * tri_update).astype(jnp.bfloat16)
    return (alignment_after_columns, pair_output)


BF16 = jnp.bfloat16
F32 = jnp.float32
SMALL_ROWS = 16
FLOPS = 3 * 10**9
PACKET_ORDER = (2, 3, 1)
PAIR_ORDER = (3, 1, 2)


def mul(lhs, rhs, over=((1,), (0,))):
    return lax.dot_general(lhs, rhs, (over, ((), ())), preferred_element_type=F32)


def iota(shape, axis):
    return lax.broadcasted_iota(jnp.int32, shape, axis)


def zero_one(condition):
    return jnp.where(condition, 1.0, 0.0).astype(BF16)


def normal(x):
    mean = jnp.mean(x, axis=-1, keepdims=True)
    centred = x - mean
    var = jnp.mean(centred * centred, axis=-1, keepdims=True)
    return centred * lax.rsqrt(var + 1e-05)


def sigmoid(x):
    return 0.5 + 0.5 * jnp.tanh(0.5 * x)


def column_softmax(scores):
    expo = jnp.exp(scores - jnp.max(scores, axis=0, keepdims=True))
    return expo * (1.0 / jnp.sum(expo, axis=0, keepdims=True))


def bias_rows(pair_ref, weight_ref):
    rows, residues, width = pair_ref.shape
    lanes = FOCUS_TOTAL * rows
    spread = zero_one(iota((FOCUS_TOTAL, lanes), 1) // rows == iota((FOCUS_TOTAL, lanes), 0))
    row_of = iota((width, lanes), 1) % rows
    flat = normal(pair_ref[...].astype(F32).reshape(rows * residues, width)).astype(BF16)
    weight = mul(weight_ref[...], spread, ((0,), (0,)))
    bias = jnp.zeros((residues, lanes), F32)
    for i in range(rows):
        one_row = jnp.where(row_of == i, weight, 0.0).astype(BF16)
        bias += mul(flat[i * residues : (i + 1) * residues], one_row)
    return bias


def table_kernel(lanes, count, shift_ref, turn_ref, column_ref):
    shape = column_ref.shape
    column_ref[...] = zero_one(iota(shape, 1) // C_TRI == iota(shape, 0))
    shape = shift_ref.shape
    shift_ref[...] = zero_one(iota(shape, 1) == iota(shape, 0) + lanes)
    shape = turn_ref.shape
    row_at = iota(shape, 0)
    turn_ref[...] = zero_one(
        iota(shape, 1) == (row_at % count) * (shape[0] // count) + row_at // count
    )


def packet_kernel(*refs):
    pair_ref, weight_ref, valid_ref, ids_ref, act_ref, present_ref, shift_ref = refs[:7]
    packet_ref, hidden_ref = refs[7:]
    rows, residues, width = pair_ref.shape
    per, _, features = act_ref.shape
    lanes = FOCUS_TOTAL * rows
    bias = bias_rows(pair_ref, weight_ref)
    extra = jnp.concatenate(
        [
            valid_ref[...].astype(F32),
            ids_ref[...].astype(F32),
            jnp.zeros((SMALL_ROWS - rows - per, residues), F32),
        ],
        axis=0,
    )
    extra = mul(extra.astype(BF16), shift_ref[...])
    empty = jnp.zeros((SMALL_ROWS, 128 - lanes), F32)
    first = jnp.concatenate([bias[:SMALL_ROWS], empty], axis=1) + extra
    second = jnp.concatenate([bias[SMALL_ROWS:], empty], axis=1)
    small = jnp.concatenate([first, second], axis=1).astype(BF16)
    packet_ref[per * residues :, :] = small
    shown = present_ref[...].astype(F32).astype(BF16)
    shown = mul(shown, jnp.ones((1, hidden_ref.shape[1]), BF16), ((0,), (0,)))
    hidden_ref[...] = 1000000000.0 * (shown - 1.0)
    packet_ref[: per * residues, :] = act_ref[...].reshape(per * residues, features)


def split_small(packet, residues, res_dev, per):
    small = packet[per * residues :, :].astype(F32)
    lanes = FOCUS_TOTAL * res_dev
    bias = jnp.concatenate([small[:, :lanes], small[:, 128 : 128 + lanes]], axis=0)
    extra = small[:, lanes : lanes + residues]
    return bias, extra[:res_dev], extra[res_dev : res_dev + per]


def head_masks(width):
    return [
        zero_one(iota((1, width), 1) // FOCUS_SIZE == h) for h in range(FOCUS_TOTAL)
    ]


def project(x, w_query, w_kvg):
    width = FOCUS_TOTAL * FOCUS_SIZE
    flat = normal(x).astype(BF16)
    query = (mul(flat, w_query[...]) * FOCUS_SIZE ** (-0.5)).astype(BF16)
    keys = mul(flat, w_kvg[:, :width]).astype(BF16)
    values = mul(flat, w_kvg[:, width : 2 * width]).astype(BF16)
    gate = sigmoid(mul(flat, w_kvg[:, 2 * width :]))
    return query, keys, values, gate


def msa_kernel(n, res_dev, *refs):
    packets, turn, hidden_keys, table = refs[:n], refs[n], refs[n + 1], refs[n + 2]
    refs = refs[n + 3 :]
    row_q, row_kvg, row_out, col_q, col_kvg, col_out, lift, outer_w = refs[:8]
    align_ref, update_ref, lifted = refs[8:]
    kinds, width = table.shape
    residues, lanes = hidden_keys.shape
    pair_width = outer_w.shape[1]
    per = (packets[0].shape[0] - SMALL_ROWS) // residues
    count = per * n
    tokens = count * residues
    me = lax.axis_index("axial")

    place = iota((FOCUS_TOTAL * res_dev, lanes), 0)
    place = (place // res_dev) * residues + place % res_dev - iota(place.shape, 1)
    bias = jnp.zeros((residues, lanes), F32)
    rows = []
    for packet, r in zip(packets, (0, *PACKET_ORDER)):
        part, _, all_ids = split_small(packet, residues, res_dev, per)
        bias += mul(part.astype(BF16), zero_one(place == -(me ^ r) * res_dev))
        for q in range(per):
            hot = zero_one(iota((kinds, residues), 0).astype(F32) == all_ids[q : q + 1])
            act = packet[q * residues : (q + 1) * residues, :].astype(F32)
            rows.append(act + mul(hot, table[...], ((0,), (0,))))
    zero = jnp.concatenate(rows, axis=0)
    extra = bias + hidden_keys[...]
    masks = head_masks(width)

    query, keys, values, gate = project(zero, row_q, row_kvg)
    rows = []
    for s in range(count):
        here = slice(s * residues, (s + 1) * residues)
        spread = jnp.concatenate([query[here] * mask for mask in masks], axis=0)
        weights = column_softmax(mul(keys[here], spread, ((1,), (1,))) + extra).astype(BF16)
        heads = mul(weights, values[here], ((0,), (0,)))
        mixed = heads[:residues]
        for h in range(1, FOCUS_TOTAL):
            part = heads[h * residues : (h + 1) * residues]
            mixed = jnp.where(iota((1, width), 1) // FOCUS_SIZE == h, part, mixed)
        rows.append(mixed)
    mixed = (jnp.concatenate(rows, axis=0) * gate).astype(BF16)
    msa_one = (zero + mul(mixed, row_out[...])).astype(BF16)

    one = mul(turn[...], msa_one)
    query, keys, values, gate = project(one, col_q, col_kvg)
    group = min(tokens, 128)
    sites = group // count
    block_of = iota((1, group), 1) // count
    groups = []
    for g in range(tokens // group):
        here = slice(g * group, (g + 1) * group)
        all_weights, all_values = [], []
        for mask in masks:
            full = mul(keys[here], query[here] * mask, ((1,), (1,)))
            scores = full[:count]
            for b in range(1, sites):
                scores = jnp.where(block_of == b, full[b * count : (b + 1) * count], scores)
            weights = column_softmax(scores)
            weights = jnp.concatenate(
                [jnp.where(block_of == b, weights, 0.0) for b in range(sites)], axis=0
            )
            all_weights.append(weights.astype(BF16))
            all_values.append(values[here] * mask)
        groups.append(
            mul(
                jnp.concatenate(all_weights, axis=0),
                jnp.concatenate(all_values, axis=0),
                ((0,), (0,)),
            )
        )
    mixed = (jnp.concatenate(groups, axis=0) * gate).astype(BF16)
    align = (one + mul(mixed, col_out[...])).astype(BF16)
    align_ref[...] = align

    opm = normal(align.astype(F32)).astype(BF16)
    opm = mul(opm, lift[...], ((1,), (1,))).astype(BF16)
    hidden = MEAN_HIDDEN_SIZE
    deep = hidden * count
    spread = zero_one(
        iota((2 * hidden, deep), 1) // count == iota((2 * hidden, deep), 0)
    )
    left = mul(opm, spread)
    left = jnp.where(
        iota((tokens, deep), 0) % count == iota((tokens, deep), 1) % count, left, 0.0
    ).astype(BF16)
    gather = zero_one(iota((residues, tokens), 1) // count == iota((residues, tokens), 0))
    left = mul(gather, left).astype(BF16)
    right = opm[:, hidden:]
    for c in range(0, hidden, 2):
        pair_w = jnp.concatenate(
            [outer_w[(c + k) * hidden : (c + k + 1) * hidden, :] for k in range(2)], axis=1
        )
        part = mul(right, pair_w)
        lifted[c], lifted[c + 1] = part[:, :pair_width], part[:, pair_width:]
    for j in range(0, residues, 2):
        part = jnp.concatenate(
            [
                lifted[:, (j + k) * count : (j + k + 1) * count, :].reshape(deep, pair_width)
                for k in range(2)
            ],
            axis=1,
        )
        part = mul(left, part.astype(BF16)) * (1.0 / count)
        update_ref[j], update_ref[j + 1] = part[:, :pair_width], part[:, pair_width:]


def pair_kernel(*refs):
    pairs, packets, update, align, column, pair, own_mask = refs[:3], refs[3:6], *refs[6:11]
    proj, gates, gate_out, w_out, align_ref, out_ref = refs[11:17]
    state, one, right_at, left_at, valid = refs[17:]
    res_dev, residues, width = pair.shape
    per = (packets[0].shape[0] - SMALL_ROWS) // residues
    me = lax.axis_index("axial")
    own_valid = own_mask[...].astype(F32)
    for packet, r in zip((None, *packets), (0, *PACKET_ORDER)):
        shown = split_small(packet, residues, res_dev, per)[1] if r else own_valid
        valid[pl.ds(pl.multiple_of((me ^ r) * res_dev, res_dev), res_dev), :] = shown
    tokens, features = align.shape
    count = tokens // residues
    own = count * res_dev
    row_at, lane_at = iota((own, tokens), 0), iota((own, tokens), 1)
    sequence = row_at // res_dev
    owner = (sequence // per) ^ me
    where_is = jnp.zeros_like(owner)
    for k, r in enumerate(PACKET_ORDER):
        where_is = jnp.where(owner == r, k + 1, where_is)
    pick = zero_one(
        lane_at
        == (row_at % res_dev + me * res_dev) * count + where_is * per + sequence % per
    )
    align_ref[...] = mul(pick, align[...]).reshape(count, res_dev, features).astype(BF16)

    size = res_dev * residues
    for block, r in zip((pair, *pairs), (0, *PAIR_ORDER)):
        state[pl.ds(pl.multiple_of((me ^ r) * size, size), size), :] = (
            block[...].astype(F32).reshape(size, width)
        )
    for k in range(residues):
        one[k * residues : (k + 1) * residues, :] = (
            state[pl.ds(k, residues, stride=residues), :] + update[k]
        )

    shown = mul(valid[...].astype(BF16), column[...])
    right_w = jnp.concatenate([proj[:, C_TRI:], gates[:, C_TRI:]], axis=1)
    step = 8
    for k in range(0, residues, step):
        here = slice(k * residues, (k + step) * residues)
        both = mul(normal(one[here, :]).astype(BF16), right_w)
        both = sigmoid(both[:, C_TRI:]) * both[:, :C_TRI]
        for p in range(step):
            part = both[p * residues : (p + 1) * residues]
            part = part * shown[:, (k + p) * C_TRI : (k + p + 1) * C_TRI]
            right_at[(k + p) * residues : (k + p + 1) * residues, :] = part.astype(BF16).astype(F32)

    own = jnp.concatenate(
        [one[pl.ds(me * res_dev + i, residues, stride=residues), :] for i in range(res_dev)],
        axis=0,
    )
    left_w = jnp.concatenate([proj[:, :C_TRI], gates[:, :C_TRI], gate_out[...]], axis=1)
    own_all = mul(normal(own).astype(BF16), left_w)
    own_gate = sigmoid(own_all[:, 2 * C_TRI :])
    left = sigmoid(own_all[:, C_TRI : 2 * C_TRI]) * own_all[:, :C_TRI]
    shown = mul(own_valid.astype(BF16), column[:res_dev, : res_dev * C_TRI], ((0,), (0,)))
    for i in range(res_dev):
        part = left[i * residues : (i + 1) * residues] * shown[:, i * C_TRI : (i + 1) * C_TRI]
        left_at[i * residues : (i + 1) * residues, :] = part.astype(BF16).astype(F32)
    sums = [jnp.zeros((residues, C_TRI), F32) for _ in range(res_dev)]
    for k in range(residues):
        other = right_at[k * residues : (k + 1) * residues, :]
        for i in range(res_dev):
            sums[i] += left_at[i * residues + k : i * residues + k + 1, :] * other
    mixed = normal(jnp.concatenate(sums, axis=0)).astype(BF16)
    result = own + own_gate * mul(mixed, w_out[...])
    out_ref[...] = result.reshape(res_dev, residues, width).astype(BF16)


def call(kernel, out_shape, scratch, vmem_mib, *args):
    vmem = pl.BlockSpec(memory_space=pltpu.VMEM)
    return pl.pallas_call(
        kernel,
        out_shape=out_shape,
        in_specs=[vmem] * len(args),
        out_specs=jax.tree.map(lambda _: vmem, out_shape),
        scratch_shapes=scratch,
        compiler_params=pltpu.CompilerParams(vmem_limit_bytes=vmem_mib * 1024 * 1024),
        cost_estimate=pl.CostEstimate(flops=FLOPS, bytes_accessed=0, transcendentals=0),
    )(*args)


def swap(array, r, n):
    return lax.ppermute(array, "axial", [(i, i ^ r) for i in range(n)])


def local_whole(
    homolog_activity,
    homolog_symbol_ids,
    residue_present_mask,
    pair_state,
    pair_valid_mask,
    symbol_lookup_matrix,
    row_query_weight,
    horizontal_attention_matrix,
    pair_bias_weight,
    horizontal_final_matrix,
    column_query_weight,
    vertical_attention_matrix,
    vertical_final_matrix,
    tensor_mean_lift_matrix,
    outer_product_output_weight,
    triangle_projection_weight,
    triangle_projection_gate,
    triangle_output_gate,
    triangle_output_weight,
):
    n = lax.axis_size("axial")
    per, residues, width = homolog_activity.shape
    res_dev, _, pair_width = pair_state.shape
    count = per * n
    shift, turn, column = call(
        functools.partial(table_kernel, FOCUS_TOTAL * res_dev, count),
        (
            jax.ShapeDtypeStruct((residues, 128), BF16),
            jax.ShapeDtypeStruct((count * residues, count * residues), BF16),
            jax.ShapeDtypeStruct((residues, residues * C_TRI), BF16),
        ),
        [],
        2,
    )
    packet, hidden_keys = call(
        packet_kernel,
        (
            jax.ShapeDtypeStruct((per * residues + SMALL_ROWS, width), BF16),
            jax.ShapeDtypeStruct((residues, FOCUS_TOTAL * residues), F32),
        ),
        [],
        4,
        pair_state,
        pair_bias_weight.T,
        pair_valid_mask,
        homolog_symbol_ids,
        homolog_activity,
        residue_present_mask.reshape(1, residues),
        shift,
    )
    packets = [swap(packet, r, n) for r in PACKET_ORDER]
    _, later = lax.optimization_barrier((packet, pair_state))
    pairs = [swap(later, r, n) for r in PAIR_ORDER]
    align, update = call(
        functools.partial(msa_kernel, n, res_dev),
        (
            jax.ShapeDtypeStruct((count * residues, width), BF16),
            jax.ShapeDtypeStruct((residues, residues, pair_width), F32),
        ),
        [
            pltpu.VMEM((MEAN_HIDDEN_SIZE, count * residues, pair_width), F32),
        ],
        16,
        packet,
        *packets,
        turn,
        hidden_keys,
        symbol_lookup_matrix,
        row_query_weight,
        horizontal_attention_matrix,
        horizontal_final_matrix,
        column_query_weight,
        vertical_attention_matrix,
        vertical_final_matrix,
        tensor_mean_lift_matrix.T,
        outer_product_output_weight,
    )
    return call(
        pair_kernel,
        (
            jax.ShapeDtypeStruct((count, res_dev, width), BF16),
            jax.ShapeDtypeStruct((res_dev, residues, pair_width), BF16),
        ),
        [
            pltpu.VMEM((residues * residues, pair_width), F32),
            pltpu.VMEM((residues * residues, pair_width), F32),
            pltpu.VMEM((residues * residues, C_TRI), F32),
            pltpu.VMEM((res_dev * residues, C_TRI), F32),
            pltpu.VMEM((residues, residues), F32),
        ],
        16,
        *pairs,
        *packets,
        update,
        align,
        column,
        pair_state,
        pair_valid_mask,
        triangle_projection_weight,
        triangle_projection_gate,
        triangle_output_gate,
        triangle_output_weight,
    )


def local(homolog_activity, homolog_symbol_ids, residue_present_mask, pair_state, *others):
    n = lax.axis_size("axial")
    per, residues, _ = homolog_activity.shape
    small = n == 4 and per * n == 8 and residues == 32
    plan = local_whole if small else local_sharded
    return plan(homolog_activity, homolog_symbol_ids, residue_present_mask, pair_state, *others)


def solution(mesh):
    parts, copied = P(("dp", "axial")), P()
    return jax.shard_map(
        local,
        mesh=mesh,
        in_specs=(parts, parts, P("dp"), parts, parts) + (copied,) * 14,
        out_specs=(P("dp", "axial", None), P(("dp", "axial"), None, None)),
        check_vma=False,
    )
```

```python
import functools

import jax
import jax.numpy as jnp
from jax import lax
from jax.experimental import pallas as pl
from jax.experimental.pallas import tpu as pltpu
from jax.sharding import PartitionSpec as P

FOCUS_TOTAL = 8
FOCUS_SIZE = 32
MEAN_HIDDEN_SIZE = 32
C_TRI = 128


def layer_normalize(attended_entries):
    attended_entries = attended_entries.astype(jnp.float32)
    mean = jnp.mean(attended_entries, axis=-1, keepdims=True)
    centred = attended_entries - mean
    var = jnp.mean(centred * centred, axis=-1, keepdims=True)
    return centred * lax.rsqrt(var + 1e-05)


def gated_attend(evoformer_block, extra_axes, w_query, w_kvg, w_out):
    lines_list, residue_length, input_width = evoformer_block.shape
    width = FOCUS_TOTAL * FOCUS_SIZE
    flat = (
        layer_normalize(evoformer_block)
        .astype(jnp.bfloat16)
        .reshape(lines_list * residue_length, input_width)
    )
    query = (
        jnp.dot(flat, w_query, preferred_element_type=jnp.float32) * FOCUS_SIZE ** (-0.5)
    ).astype(jnp.bfloat16)
    query = query.reshape(lines_list, residue_length, FOCUS_TOTAL, FOCUS_SIZE)
    kvg = jnp.dot(flat, w_kvg, preferred_element_type=jnp.float32)
    keys = (
        kvg[:, :width]
        .astype(jnp.bfloat16)
        .reshape(lines_list, residue_length, FOCUS_TOTAL, FOCUS_SIZE)
    )
    attended_entries = (
        kvg[:, width : 2 * width]
        .astype(jnp.bfloat16)
        .reshape(lines_list, residue_length, FOCUS_TOTAL, FOCUS_SIZE)
    )
    gate = jax.nn.sigmoid(kvg[:, 2 * width :]).reshape(
        lines_list, residue_length, FOCUS_TOTAL, FOCUS_SIZE
    )
    scores = (
        jnp.einsum("bihd,bjhd->bhij", query, keys, preferred_element_type=jnp.float32) + extra_axes
    )
    top = jnp.max(scores, axis=-1, keepdims=True)
    expo = jnp.exp(scores - top)
    weights = (expo / jnp.sum(expo, axis=-1, keepdims=True)).astype(jnp.bfloat16)
    mixed = jnp.einsum(
        "bhij,bjhd->bihd", weights, attended_entries, preferred_element_type=jnp.float32
    )
    mixed = (mixed * gate).astype(jnp.bfloat16).reshape(lines_list * residue_length, width)
    return evoformer_block + jnp.dot(mixed, w_out, preferred_element_type=jnp.float32).reshape(
        lines_list, residue_length, input_width
    )


def finish_sums(evoformer_block, triangle_output_weight):
    mixed = layer_normalize(jnp.transpose(evoformer_block, (1, 2, 0))).astype(jnp.bfloat16)
    return jnp.einsum(
        "ijc,cz->ijz", mixed, triangle_output_weight, preferred_element_type=jnp.float32
    )


def local_sharded(
    homolog_activity,
    homolog_symbol_ids,
    residue_present_mask,
    pair_state,
    pair_valid_mask,
    symbol_lookup_matrix,
    row_query_weight,
    horizontal_attention_matrix,
    pair_bias_weight,
    horizontal_final_matrix,
    column_query_weight,
    vertical_attention_matrix,
    vertical_final_matrix,
    tensor_mean_lift_matrix,
    outer_product_output_weight,
    triangle_projection_weight,
    triangle_projection_gate,
    triangle_output_gate,
    triangle_output_weight,
):
    sequence_per_device, residue_length, input_width = homolog_activity.shape
    res_dev = pair_state.shape[0]
    group_size = lax.axis_size("axial")
    token_classes = symbol_lookup_matrix.shape[0]
    token_one_hot = (
        homolog_symbol_ids[..., None] == jnp.arange(token_classes, dtype=jnp.int32)
    ).astype(jnp.bfloat16)
    token_embedded = jnp.einsum(
        "slt,tc->slc", token_one_hot, symbol_lookup_matrix, preferred_element_type=jnp.float32
    )
    homolog_starting = homolog_activity.astype(jnp.float32) + token_embedded
    pair_norm = layer_normalize(pair_state).astype(jnp.bfloat16)
    bias_rows = jnp.einsum(
        "ijc,ch->hij", pair_norm, pair_bias_weight, preferred_element_type=jnp.float32
    ).astype(jnp.bfloat16)
    bias_full = lax.all_gather(bias_rows, "axial", axis=1, tiled=True)
    key_bias = 1000000000.0 * (residue_present_mask.astype(jnp.float32) - 1.0)
    extra_axes = bias_full.astype(jnp.float32)[None] + key_bias[None, None, None, :]
    cluster_total = homolog_starting.reshape(
        sequence_per_device // 2, 2, residue_length, input_width
    )
    homolog_across_update = lax.map(
        lambda evoformer_block: gated_attend(
            evoformer_block,
            extra_axes,
            row_query_weight,
            horizontal_attention_matrix,
            horizontal_final_matrix,
        ),
        cluster_total,
    )
    homolog_across_update = homolog_across_update.reshape(
        sequence_per_device, group_size, res_dev, input_width
    ).astype(jnp.bfloat16)
    moved = jnp.swapaxes(
        lax.all_to_all(homolog_across_update, "axial", split_axis=1, concat_axis=0, tiled=True)[
            :, 0
        ],
        0,
        1,
    )
    finished = lax.map(
        lambda item: gated_attend(
            item[None].astype(jnp.float32),
            0.0,
            column_query_weight,
            vertical_attention_matrix,
            vertical_final_matrix,
        )[0],
        moved,
    )
    exchanged = jnp.swapaxes(finished, 0, 1).astype(jnp.bfloat16)[:, None]
    sequence_count = exchanged.shape[0]
    alignment_after_columns = exchanged.reshape(sequence_count, res_dev, input_width)
    tensor_mean_scaler = layer_normalize(alignment_after_columns).astype(jnp.bfloat16)
    split_parts = jnp.einsum(
        "src,cf->rsf",
        tensor_mean_scaler,
        tensor_mean_lift_matrix,
        preferred_element_type=jnp.float32,
    ).astype(jnp.bfloat16)
    first_factor = split_parts[..., :MEAN_HIDDEN_SIZE]
    second_factor = split_parts[..., MEAN_HIDDEN_SIZE:].reshape(
        res_dev, sequence_count * MEAN_HIDDEN_SIZE
    )
    step_rows = 8
    left_blocks = first_factor.reshape(
        res_dev // step_rows, step_rows, sequence_count, MEAN_HIDDEN_SIZE
    )
    piece = lax.all_gather(second_factor, "axial", axis=0, tiled=True)
    count = piece.shape[0]
    right_part = piece.reshape(count, sequence_count, MEAN_HIDDEN_SIZE)

    def one_block(lines_list):
        tensor_mean = (
            jnp.einsum("isc,jsd->ijcd", lines_list, right_part, preferred_element_type=jnp.float32)
            / sequence_count
        )
        tensor_mean = tensor_mean.reshape(
            step_rows, count, MEAN_HIDDEN_SIZE * MEAN_HIDDEN_SIZE
        ).astype(jnp.bfloat16)
        return jnp.einsum(
            "ijf,fz->ijz",
            tensor_mean,
            outer_product_output_weight,
            preferred_element_type=jnp.float32,
        )

    update = lax.map(one_block, left_blocks).reshape(
        res_dev, count, outer_product_output_weight.shape[1]
    )
    pair_one = pair_state.astype(jnp.float32) + update
    tri_norm = layer_normalize(pair_one).astype(jnp.bfloat16)
    proj = jnp.einsum(
        "ikc,cf->fik", tri_norm, triangle_projection_weight, preferred_element_type=jnp.float32
    )
    gates = jnp.einsum(
        "ikc,cf->fik", tri_norm, triangle_projection_gate, preferred_element_type=jnp.float32
    )
    both = (jax.nn.sigmoid(gates) * proj * pair_valid_mask.astype(jnp.float32)[None]).astype(
        jnp.bfloat16
    )
    left_tri = both[:C_TRI]
    right_tri = both[C_TRI:]
    moved_left, moved_right = (
        lax.all_to_all(left_tri, "axial", split_axis=0, concat_axis=1, tiled=True),
        lax.all_to_all(right_tri, "axial", split_axis=0, concat_axis=1, tiled=True),
    )
    partial_sum = jnp.einsum(
        "cik,cjk->cij", moved_left, moved_right, preferred_element_type=jnp.float32
    )
    tri_sum = lax.all_to_all(
        partial_sum.astype(jnp.bfloat16), "axial", split_axis=1, concat_axis=0, tiled=True
    ).astype(partial_sum.dtype)
    tri_update = finish_sums(tri_sum, triangle_output_weight)
    out_gate = jax.nn.sigmoid(
        jnp.einsum(
            "ijc,cz->ijz", tri_norm, triangle_output_gate, preferred_element_type=jnp.float32
        )
    )
    pair_output = (pair_one + out_gate * tri_update).astype(jnp.bfloat16)
    return (alignment_after_columns, pair_output)


BF16 = jnp.bfloat16
F32 = jnp.float32
SMALL_ROWS = 16
OUTER_CHUNKS = 4
FLOPS = 3 * 10**9
PACKET_ORDER = (2, 3, 1)
PAIR_ORDER = (3, 1, 2)


def mul(lhs, rhs, over=((1,), (0,))):
    return lax.dot_general(lhs, rhs, (over, ((), ())), preferred_element_type=F32)


def iota(shape, axis):
    return lax.broadcasted_iota(jnp.int32, shape, axis)


def zero_one(condition):
    return jnp.where(condition, 1.0, 0.0).astype(BF16)


def normal(x):
    mean = jnp.mean(x, axis=-1, keepdims=True)
    centred = x - mean
    var = jnp.mean(centred * centred, axis=-1, keepdims=True)
    return centred * lax.rsqrt(var + 1e-05)


def sigmoid(x):
    return 0.5 + 0.5 * jnp.tanh(0.5 * x)


def column_softmax(scores):
    expo = jnp.exp(scores - jnp.max(scores, axis=0, keepdims=True))
    return expo * (1.0 / jnp.sum(expo, axis=0, keepdims=True))


def bias_rows(pair_ref, weight_ref):
    rows, residues, width = pair_ref.shape
    lanes = FOCUS_TOTAL * rows
    spread = zero_one(iota((FOCUS_TOTAL, lanes), 1) // rows == iota((FOCUS_TOTAL, lanes), 0))
    row_of = iota((width, lanes), 1) % rows
    flat = normal(pair_ref[...].astype(F32).reshape(rows * residues, width)).astype(BF16)
    weight = mul(weight_ref[...], spread, ((0,), (0,)))
    bias = jnp.zeros((residues, lanes), F32)
    for i in range(rows):
        one_row = jnp.where(row_of == i, weight, 0.0).astype(BF16)
        bias += mul(flat[i * residues : (i + 1) * residues], one_row)
    return bias


def table_kernel(lanes, count, shift_ref, turn_ref, column_ref):
    shape = column_ref.shape
    column_ref[...] = zero_one(iota(shape, 1) // C_TRI == iota(shape, 0))
    shape = shift_ref.shape
    shift_ref[...] = zero_one(iota(shape, 1) == iota(shape, 0) + lanes)
    shape = turn_ref.shape
    row_at = iota(shape, 0)
    turn_ref[...] = zero_one(
        iota(shape, 1) == (row_at % count) * (shape[0] // count) + row_at // count
    )


def packet_kernel(*refs):
    pair_ref, weight_ref, valid_ref, ids_ref, act_ref, present_ref, shift_ref = refs[:7]
    packet_ref, hidden_ref = refs[7:]
    rows, residues, width = pair_ref.shape
    per, _, features = act_ref.shape
    lanes = FOCUS_TOTAL * rows
    bias = bias_rows(pair_ref, weight_ref)
    extra = jnp.concatenate(
        [
            valid_ref[...].astype(F32),
            ids_ref[...].astype(F32),
            jnp.zeros((SMALL_ROWS - rows - per, residues), F32),
        ],
        axis=0,
    )
    extra = mul(extra.astype(BF16), shift_ref[...])
    empty = jnp.zeros((SMALL_ROWS, 128 - lanes), F32)
    first = jnp.concatenate([bias[:SMALL_ROWS], empty], axis=1) + extra
    second = jnp.concatenate([bias[SMALL_ROWS:], empty], axis=1)
    small = jnp.concatenate([first, second], axis=1).astype(BF16)
    packet_ref[per * residues :, :] = small
    shown = present_ref[...].astype(F32).astype(BF16)
    shown = mul(shown, jnp.ones((1, hidden_ref.shape[1]), BF16), ((0,), (0,)))
    hidden_ref[...] = 1000000000.0 * (shown - 1.0)
    packet_ref[: per * residues, :] = act_ref[...].reshape(per * residues, features)


def split_small(packet, residues, res_dev, per):
    small = packet[per * residues :, :].astype(F32)
    lanes = FOCUS_TOTAL * res_dev
    bias = jnp.concatenate([small[:, :lanes], small[:, 128 : 128 + lanes]], axis=0)
    extra = small[:, lanes : lanes + residues]
    return bias, extra[:res_dev], extra[res_dev : res_dev + per]


def head_masks(width):
    return [
        zero_one(iota((1, width), 1) // FOCUS_SIZE == h) for h in range(FOCUS_TOTAL)
    ]


def project(x, w_query, w_kvg):
    width = FOCUS_TOTAL * FOCUS_SIZE
    flat = normal(x).astype(BF16)
    query = (mul(flat, w_query[...]) * FOCUS_SIZE ** (-0.5)).astype(BF16)
    keys = mul(flat, w_kvg[:, :width]).astype(BF16)
    values = mul(flat, w_kvg[:, width : 2 * width]).astype(BF16)
    gate = sigmoid(mul(flat, w_kvg[:, 2 * width :]))
    return query, keys, values, gate


def msa_kernel(n, res_dev, *refs):
    packets, turn, hidden_keys, table = refs[:n], refs[n], refs[n + 1], refs[n + 2]
    refs = refs[n + 3 :]
    row_q, row_kvg, row_out, col_q, col_kvg, col_out, lift, outer_w = refs[:8]
    align_ref, update_ref, lifted_chunks = *refs[8:10], refs[10:]
    kinds, width = table.shape
    residues, lanes = hidden_keys.shape
    pair_width = outer_w.shape[1]
    per = (packets[0].shape[0] - SMALL_ROWS) // residues
    count = per * n
    tokens = count * residues
    me = lax.axis_index("axial")

    place = iota((FOCUS_TOTAL * res_dev, lanes), 0)
    place = (place // res_dev) * residues + place % res_dev - iota(place.shape, 1)
    bias = jnp.zeros((residues, lanes), F32)
    rows = []
    for packet, r in zip(packets, (0, *PACKET_ORDER)):
        part, _, all_ids = split_small(packet, residues, res_dev, per)
        bias += mul(part.astype(BF16), zero_one(place == -(me ^ r) * res_dev))
        for q in range(per):
            hot = zero_one(iota((kinds, residues), 0).astype(F32) == all_ids[q : q + 1])
            act = packet[q * residues : (q + 1) * residues, :].astype(F32)
            rows.append(act + mul(hot, table[...], ((0,), (0,))))
    zero = jnp.concatenate(rows, axis=0)
    extra = bias + hidden_keys[...]
    masks = head_masks(width)

    query, keys, values, gate = project(zero, row_q, row_kvg)
    rows = []
    for s in range(count):
        here = slice(s * residues, (s + 1) * residues)
        spread = jnp.concatenate([query[here] * mask for mask in masks], axis=0)
        weights = column_softmax(mul(keys[here], spread, ((1,), (1,))) + extra).astype(BF16)
        heads = mul(weights, values[here], ((0,), (0,)))
        mixed = heads[:residues]
        for h in range(1, FOCUS_TOTAL):
            part = heads[h * residues : (h + 1) * residues]
            mixed = jnp.where(iota((1, width), 1) // FOCUS_SIZE == h, part, mixed)
        rows.append(mixed)
    mixed = (jnp.concatenate(rows, axis=0) * gate).astype(BF16)
    msa_one = (zero + mul(mixed, row_out[...])).astype(BF16)

    one = mul(turn[...], msa_one)
    query, keys, values, gate = project(one, col_q, col_kvg)
    group = min(tokens, 128)
    sites = group // count
    block_of = iota((1, group), 1) // count
    groups = []
    for g in range(tokens // group):
        here = slice(g * group, (g + 1) * group)
        all_weights, all_values = [], []
        for mask in masks:
            full = mul(keys[here], query[here] * mask, ((1,), (1,)))
            scores = full[:count]
            for b in range(1, sites):
                scores = jnp.where(block_of == b, full[b * count : (b + 1) * count], scores)
            weights = column_softmax(scores)
            weights = jnp.concatenate(
                [jnp.where(block_of == b, weights, 0.0) for b in range(sites)], axis=0
            )
            all_weights.append(weights.astype(BF16))
            all_values.append(values[here] * mask)
        groups.append(
            mul(
                jnp.concatenate(all_weights, axis=0),
                jnp.concatenate(all_values, axis=0),
                ((0,), (0,)),
            )
        )
    mixed = (jnp.concatenate(groups, axis=0) * gate).astype(BF16)
    align = (one + mul(mixed, col_out[...])).astype(BF16)
    own = count * res_dev
    row_at, lane_at = iota((own, tokens), 0), iota((own, tokens), 1)
    sequence = row_at // res_dev
    owner = (sequence // per) ^ me
    where_is = jnp.zeros_like(owner)
    for k, r in enumerate(PACKET_ORDER):
        where_is = jnp.where(owner == r, k + 1, where_is)
    pick = zero_one(
        lane_at
        == (row_at % res_dev + me * res_dev) * count + where_is * per + sequence % per
    )
    align_ref[...] = mul(pick, align).reshape(count, res_dev, width).astype(BF16)

    opm = normal(align.astype(F32)).astype(BF16)
    opm = mul(opm, lift[...], ((1,), (1,))).astype(BF16)
    hidden = MEAN_HIDDEN_SIZE
    deep = hidden * count
    spread = zero_one(
        iota((2 * hidden, deep), 1) // count == iota((2 * hidden, deep), 0)
    )
    left = mul(opm, spread)
    left = jnp.where(
        iota((tokens, deep), 0) % count == iota((tokens, deep), 1) % count, left, 0.0
    ).astype(BF16)
    gather = zero_one(iota((residues, tokens), 1) // count == iota((residues, tokens), 0))
    left = mul(gather, left).astype(BF16)
    right = opm[:, hidden:]
    pairs_w = [
        jnp.concatenate(
            [outer_w[(c + k) * hidden : (c + k + 1) * hidden, :] for k in range(2)], axis=1
        )
        for c in range(0, hidden, 2)
    ]
    step = residues // OUTER_CHUNKS
    for chunk, lifted in enumerate(lifted_chunks):
        part_right = right[chunk * step * count : (chunk + 1) * step * count]
        for c in range(0, hidden, 2):
            part = mul(part_right, pairs_w[c // 2])
            lifted[c], lifted[c + 1] = part[:, :pair_width], part[:, pair_width:]
        for j in range(0, step, 2):
            part = jnp.concatenate(
                [
                    lifted[:, (j + k) * count : (j + k + 1) * count, :].reshape(deep, pair_width)
                    for k in range(2)
                ],
                axis=1,
            )
            part = mul(left, part.astype(BF16)) * (1.0 / count)
            for k in range(2):
                update_ref[chunk * step + j + k] = part[:, k * pair_width : (k + 1) * pair_width]


def pair_kernel(*refs):
    pairs, packets, update, column, pair, own_mask = refs[:3], refs[3:6], *refs[6:10]
    proj, gates, gate_out, w_out, out_ref, state, one, right_at, left_at, valid = refs[10:]
    res_dev, residues, width = pair.shape
    per = (packets[0].shape[0] - SMALL_ROWS) // residues
    me = lax.axis_index("axial")
    own_valid = own_mask[...].astype(F32)
    for packet, r in zip((None, *packets), (0, *PACKET_ORDER)):
        shown = split_small(packet, residues, res_dev, per)[1] if r else own_valid
        valid[pl.ds(pl.multiple_of((me ^ r) * res_dev, res_dev), res_dev), :] = shown
    size = res_dev * residues
    for block, r in zip((pair, *pairs), (0, *PAIR_ORDER)):
        state[pl.ds(pl.multiple_of((me ^ r) * size, size), size), :] = (
            block[...].astype(F32).reshape(size, width)
        )
    for k in range(residues):
        one[k * residues : (k + 1) * residues, :] = (
            state[pl.ds(k, residues, stride=residues), :] + update[k]
        )

    shown = mul(valid[...].astype(BF16), column[...])
    right_w = jnp.concatenate([proj[:, C_TRI:], gates[:, C_TRI:]], axis=1)
    step = 8
    for k in range(0, residues, step):
        here = slice(k * residues, (k + step) * residues)
        both = mul(normal(one[here, :]).astype(BF16), right_w)
        both = sigmoid(both[:, C_TRI:]) * both[:, :C_TRI]
        for p in range(step):
            part = both[p * residues : (p + 1) * residues]
            part = part * shown[:, (k + p) * C_TRI : (k + p + 1) * C_TRI]
            right_at[(k + p) * residues : (k + p + 1) * residues, :] = part.astype(BF16).astype(F32)

    own = jnp.concatenate(
        [one[pl.ds(me * res_dev + i, residues, stride=residues), :] for i in range(res_dev)],
        axis=0,
    )
    left_w = jnp.concatenate([proj[:, :C_TRI], gates[:, :C_TRI], gate_out[...]], axis=1)
    own_all = mul(normal(own).astype(BF16), left_w)
    own_gate = sigmoid(own_all[:, 2 * C_TRI :])
    left = sigmoid(own_all[:, C_TRI : 2 * C_TRI]) * own_all[:, :C_TRI]
    shown = mul(own_valid.astype(BF16), column[:res_dev, : res_dev * C_TRI], ((0,), (0,)))
    for i in range(res_dev):
        part = left[i * residues : (i + 1) * residues] * shown[:, i * C_TRI : (i + 1) * C_TRI]
        left_at[i * residues : (i + 1) * residues, :] = part.astype(BF16).astype(F32)
    sums = [jnp.zeros((residues, C_TRI), F32) for _ in range(res_dev)]
    for k in range(residues):
        other = right_at[k * residues : (k + 1) * residues, :]
        for i in range(res_dev):
            sums[i] += left_at[i * residues + k : i * residues + k + 1, :] * other
    mixed = normal(jnp.concatenate(sums, axis=0)).astype(BF16)
    result = own + own_gate * mul(mixed, w_out[...])
    out_ref[...] = result.reshape(res_dev, residues, width).astype(BF16)


def call(kernel, out_shape, scratch, vmem_mib, *args):
    vmem = pl.BlockSpec(memory_space=pltpu.VMEM)
    return pl.pallas_call(
        kernel,
        out_shape=out_shape,
        in_specs=[vmem] * len(args),
        out_specs=jax.tree.map(lambda _: vmem, out_shape),
        scratch_shapes=scratch,
        compiler_params=pltpu.CompilerParams(vmem_limit_bytes=vmem_mib * 1024 * 1024),
        cost_estimate=pl.CostEstimate(flops=FLOPS, bytes_accessed=0, transcendentals=0),
    )(*args)


def swap(array, r, n):
    return lax.ppermute(array, "axial", [(i, i ^ r) for i in range(n)])


def local_whole(
    homolog_activity,
    homolog_symbol_ids,
    residue_present_mask,
    pair_state,
    pair_valid_mask,
    symbol_lookup_matrix,
    row_query_weight,
    horizontal_attention_matrix,
    pair_bias_weight,
    horizontal_final_matrix,
    column_query_weight,
    vertical_attention_matrix,
    vertical_final_matrix,
    tensor_mean_lift_matrix,
    outer_product_output_weight,
    triangle_projection_weight,
    triangle_projection_gate,
    triangle_output_gate,
    triangle_output_weight,
):
    n = lax.axis_size("axial")
    per, residues, width = homolog_activity.shape
    res_dev, _, pair_width = pair_state.shape
    count = per * n
    shift, turn, column = call(
        functools.partial(table_kernel, FOCUS_TOTAL * res_dev, count),
        (
            jax.ShapeDtypeStruct((residues, 128), BF16),
            jax.ShapeDtypeStruct((count * residues, count * residues), BF16),
            jax.ShapeDtypeStruct((residues, residues * C_TRI), BF16),
        ),
        [],
        2,
    )
    packet, hidden_keys = call(
        packet_kernel,
        (
            jax.ShapeDtypeStruct((per * residues + SMALL_ROWS, width), BF16),
            jax.ShapeDtypeStruct((residues, FOCUS_TOTAL * residues), F32),
        ),
        [],
        4,
        pair_state,
        pair_bias_weight.T,
        pair_valid_mask,
        homolog_symbol_ids,
        homolog_activity,
        residue_present_mask.reshape(1, residues),
        shift,
    )
    packets = [swap(packet, r, n) for r in PACKET_ORDER]
    _, later = lax.optimization_barrier((packet, pair_state))
    pairs = [swap(later, r, n) for r in PAIR_ORDER]
    alignment, update = call(
        functools.partial(msa_kernel, n, res_dev),
        (
            jax.ShapeDtypeStruct((count, res_dev, width), BF16),
            jax.ShapeDtypeStruct((residues, residues, pair_width), F32),
        ),
        [
            pltpu.VMEM((MEAN_HIDDEN_SIZE, count * residues // OUTER_CHUNKS, pair_width), F32)
            for _ in range(OUTER_CHUNKS)
        ],
        16,
        packet,
        *packets,
        turn,
        hidden_keys,
        symbol_lookup_matrix,
        row_query_weight,
        horizontal_attention_matrix,
        horizontal_final_matrix,
        column_query_weight,
        vertical_attention_matrix,
        vertical_final_matrix,
        tensor_mean_lift_matrix.T,
        outer_product_output_weight,
    )
    pair_output = call(
        pair_kernel,
        jax.ShapeDtypeStruct((res_dev, residues, pair_width), BF16),
        [
            pltpu.VMEM((residues * residues, pair_width), F32),
            pltpu.VMEM((residues * residues, pair_width), F32),
            pltpu.VMEM((residues * residues, C_TRI), F32),
            pltpu.VMEM((res_dev * residues, C_TRI), F32),
            pltpu.VMEM((residues, residues), F32),
        ],
        16,
        *pairs,
        *packets,
        update,
        column,
        pair_state,
        pair_valid_mask,
        triangle_projection_weight,
        triangle_projection_gate,
        triangle_output_gate,
        triangle_output_weight,
    )
    return (alignment, pair_output)


def local(homolog_activity, homolog_symbol_ids, residue_present_mask, pair_state, *others):
    n = lax.axis_size("axial")
    per, residues, _ = homolog_activity.shape
    small = n == 4 and per * n == 8 and residues == 32
    plan = local_whole if small else local_sharded
    return plan(homolog_activity, homolog_symbol_ids, residue_present_mask, pair_state, *others)


def solution(mesh):
    parts, copied = P(("dp", "axial")), P()
    return jax.shard_map(
        local,
        mesh=mesh,
        in_specs=(parts, parts, P("dp"), parts, parts) + (copied,) * 14,
        out_specs=(P("dp", "axial", None), P(("dp", "axial"), None, None)),
        check_vma=False,
    )
```

```python
import functools

import jax
import jax.numpy as jnp
from jax import lax
from jax.experimental import pallas as pl
from jax.experimental.pallas import tpu as pltpu
from jax.sharding import PartitionSpec as P

FOCUS_TOTAL = 8
FOCUS_SIZE = 32
MEAN_HIDDEN_SIZE = 32
C_TRI = 128


def layer_normalize(attended_entries):
    attended_entries = attended_entries.astype(jnp.float32)
    mean = jnp.mean(attended_entries, axis=-1, keepdims=True)
    centred = attended_entries - mean
    var = jnp.mean(centred * centred, axis=-1, keepdims=True)
    return centred * lax.rsqrt(var + 1e-05)


def gated_attend(evoformer_block, extra_axes, w_query, w_kvg, w_out):
    lines_list, residue_length, input_width = evoformer_block.shape
    width = FOCUS_TOTAL * FOCUS_SIZE
    flat = (
        layer_normalize(evoformer_block)
        .astype(jnp.bfloat16)
        .reshape(lines_list * residue_length, input_width)
    )
    query = (
        jnp.dot(flat, w_query, preferred_element_type=jnp.float32) * FOCUS_SIZE ** (-0.5)
    ).astype(jnp.bfloat16)
    query = query.reshape(lines_list, residue_length, FOCUS_TOTAL, FOCUS_SIZE)
    kvg = jnp.dot(flat, w_kvg, preferred_element_type=jnp.float32)
    keys = (
        kvg[:, :width]
        .astype(jnp.bfloat16)
        .reshape(lines_list, residue_length, FOCUS_TOTAL, FOCUS_SIZE)
    )
    attended_entries = (
        kvg[:, width : 2 * width]
        .astype(jnp.bfloat16)
        .reshape(lines_list, residue_length, FOCUS_TOTAL, FOCUS_SIZE)
    )
    gate = jax.nn.sigmoid(kvg[:, 2 * width :]).reshape(
        lines_list, residue_length, FOCUS_TOTAL, FOCUS_SIZE
    )
    scores = (
        jnp.einsum("bihd,bjhd->bhij", query, keys, preferred_element_type=jnp.float32) + extra_axes
    )
    top = jnp.max(scores, axis=-1, keepdims=True)
    expo = jnp.exp(scores - top)
    weights = (expo / jnp.sum(expo, axis=-1, keepdims=True)).astype(jnp.bfloat16)
    mixed = jnp.einsum(
        "bhij,bjhd->bihd", weights, attended_entries, preferred_element_type=jnp.float32
    )
    mixed = (mixed * gate).astype(jnp.bfloat16).reshape(lines_list * residue_length, width)
    return evoformer_block + jnp.dot(mixed, w_out, preferred_element_type=jnp.float32).reshape(
        lines_list, residue_length, input_width
    )


def finish_sums(evoformer_block, triangle_output_weight):
    mixed = layer_normalize(jnp.transpose(evoformer_block, (1, 2, 0))).astype(jnp.bfloat16)
    return jnp.einsum(
        "ijc,cz->ijz", mixed, triangle_output_weight, preferred_element_type=jnp.float32
    )


def local_sharded(
    homolog_activity,
    homolog_symbol_ids,
    residue_present_mask,
    pair_state,
    pair_valid_mask,
    symbol_lookup_matrix,
    row_query_weight,
    horizontal_attention_matrix,
    pair_bias_weight,
    horizontal_final_matrix,
    column_query_weight,
    vertical_attention_matrix,
    vertical_final_matrix,
    tensor_mean_lift_matrix,
    outer_product_output_weight,
    triangle_projection_weight,
    triangle_projection_gate,
    triangle_output_gate,
    triangle_output_weight,
):
    sequence_per_device, residue_length, input_width = homolog_activity.shape
    res_dev = pair_state.shape[0]
    group_size = lax.axis_size("axial")
    token_classes = symbol_lookup_matrix.shape[0]
    token_one_hot = (
        homolog_symbol_ids[..., None] == jnp.arange(token_classes, dtype=jnp.int32)
    ).astype(jnp.bfloat16)
    token_embedded = jnp.einsum(
        "slt,tc->slc", token_one_hot, symbol_lookup_matrix, preferred_element_type=jnp.float32
    )
    homolog_starting = homolog_activity.astype(jnp.float32) + token_embedded
    pair_norm = layer_normalize(pair_state).astype(jnp.bfloat16)
    bias_rows = jnp.einsum(
        "ijc,ch->hij", pair_norm, pair_bias_weight, preferred_element_type=jnp.float32
    ).astype(jnp.bfloat16)
    bias_full = lax.all_gather(bias_rows, "axial", axis=1, tiled=True)
    key_bias = 1000000000.0 * (residue_present_mask.astype(jnp.float32) - 1.0)
    extra_axes = bias_full.astype(jnp.float32)[None] + key_bias[None, None, None, :]
    cluster_total = homolog_starting.reshape(
        sequence_per_device // 2, 2, residue_length, input_width
    )
    homolog_across_update = lax.map(
        lambda evoformer_block: gated_attend(
            evoformer_block,
            extra_axes,
            row_query_weight,
            horizontal_attention_matrix,
            horizontal_final_matrix,
        ),
        cluster_total,
    )
    homolog_across_update = homolog_across_update.reshape(
        sequence_per_device, group_size, res_dev, input_width
    ).astype(jnp.bfloat16)
    moved = jnp.swapaxes(
        lax.all_to_all(homolog_across_update, "axial", split_axis=1, concat_axis=0, tiled=True)[
            :, 0
        ],
        0,
        1,
    )
    finished = lax.map(
        lambda item: gated_attend(
            item[None].astype(jnp.float32),
            0.0,
            column_query_weight,
            vertical_attention_matrix,
            vertical_final_matrix,
        )[0],
        moved,
    )
    exchanged = jnp.swapaxes(finished, 0, 1).astype(jnp.bfloat16)[:, None]
    sequence_count = exchanged.shape[0]
    alignment_after_columns = exchanged.reshape(sequence_count, res_dev, input_width)
    tensor_mean_scaler = layer_normalize(alignment_after_columns).astype(jnp.bfloat16)
    split_parts = jnp.einsum(
        "src,cf->rsf",
        tensor_mean_scaler,
        tensor_mean_lift_matrix,
        preferred_element_type=jnp.float32,
    ).astype(jnp.bfloat16)
    first_factor = split_parts[..., :MEAN_HIDDEN_SIZE]
    second_factor = split_parts[..., MEAN_HIDDEN_SIZE:].reshape(
        res_dev, sequence_count * MEAN_HIDDEN_SIZE
    )
    step_rows = 8
    left_blocks = first_factor.reshape(
        res_dev // step_rows, step_rows, sequence_count, MEAN_HIDDEN_SIZE
    )
    piece = lax.all_gather(second_factor, "axial", axis=0, tiled=True)
    count = piece.shape[0]
    right_part = piece.reshape(count, sequence_count, MEAN_HIDDEN_SIZE)

    def one_block(lines_list):
        tensor_mean = (
            jnp.einsum("isc,jsd->ijcd", lines_list, right_part, preferred_element_type=jnp.float32)
            / sequence_count
        )
        tensor_mean = tensor_mean.reshape(
            step_rows, count, MEAN_HIDDEN_SIZE * MEAN_HIDDEN_SIZE
        ).astype(jnp.bfloat16)
        return jnp.einsum(
            "ijf,fz->ijz",
            tensor_mean,
            outer_product_output_weight,
            preferred_element_type=jnp.float32,
        )

    update = lax.map(one_block, left_blocks).reshape(
        res_dev, count, outer_product_output_weight.shape[1]
    )
    pair_one = pair_state.astype(jnp.float32) + update
    tri_norm = layer_normalize(pair_one).astype(jnp.bfloat16)
    proj = jnp.einsum(
        "ikc,cf->fik", tri_norm, triangle_projection_weight, preferred_element_type=jnp.float32
    )
    gates = jnp.einsum(
        "ikc,cf->fik", tri_norm, triangle_projection_gate, preferred_element_type=jnp.float32
    )
    both = (jax.nn.sigmoid(gates) * proj * pair_valid_mask.astype(jnp.float32)[None]).astype(
        jnp.bfloat16
    )
    left_tri = both[:C_TRI]
    right_tri = both[C_TRI:]
    moved_left, moved_right = (
        lax.all_to_all(left_tri, "axial", split_axis=0, concat_axis=1, tiled=True),
        lax.all_to_all(right_tri, "axial", split_axis=0, concat_axis=1, tiled=True),
    )
    partial_sum = jnp.einsum(
        "cik,cjk->cij", moved_left, moved_right, preferred_element_type=jnp.float32
    )
    tri_sum = lax.all_to_all(
        partial_sum.astype(jnp.bfloat16), "axial", split_axis=1, concat_axis=0, tiled=True
    ).astype(partial_sum.dtype)
    tri_update = finish_sums(tri_sum, triangle_output_weight)
    out_gate = jax.nn.sigmoid(
        jnp.einsum(
            "ijc,cz->ijz", tri_norm, triangle_output_gate, preferred_element_type=jnp.float32
        )
    )
    pair_output = (pair_one + out_gate * tri_update).astype(jnp.bfloat16)
    return (alignment_after_columns, pair_output)


BF16 = jnp.bfloat16
F32 = jnp.float32
SMALL_ROWS = 16
FLOPS = 3 * 10**9
PACKET_ORDER = (2, 3, 1)
PAIR_ORDER = (3, 1, 2)


def mul(lhs, rhs, over=((1,), (0,))):
    return lax.dot_general(lhs, rhs, (over, ((), ())), preferred_element_type=F32)


def iota(shape, axis):
    return lax.broadcasted_iota(jnp.int32, shape, axis)


def zero_one(condition):
    return jnp.where(condition, 1.0, 0.0).astype(BF16)


def normal(x):
    mean = jnp.mean(x, axis=-1, keepdims=True)
    centred = x - mean
    var = jnp.mean(centred * centred, axis=-1, keepdims=True)
    return centred * lax.rsqrt(var + 1e-05)


def sigmoid(x):
    return 0.5 + 0.5 * jnp.tanh(0.5 * x)


def column_softmax(scores):
    expo = jnp.exp(scores - jnp.max(scores, axis=0, keepdims=True))
    return expo * (1.0 / jnp.sum(expo, axis=0, keepdims=True))


def bias_rows(pair_ref, weight_ref):
    rows, residues, width = pair_ref.shape
    lanes = FOCUS_TOTAL * rows
    spread = zero_one(iota((FOCUS_TOTAL, lanes), 1) // rows == iota((FOCUS_TOTAL, lanes), 0))
    row_of = iota((width, lanes), 1) % rows
    flat = normal(pair_ref[...].astype(F32).reshape(rows * residues, width)).astype(BF16)
    weight = mul(weight_ref[...], spread, ((0,), (0,)))
    bias = jnp.zeros((residues, lanes), F32)
    for i in range(rows):
        one_row = jnp.where(row_of == i, weight, 0.0).astype(BF16)
        bias += mul(flat[i * residues : (i + 1) * residues], one_row)
    return bias


def table_kernel(lanes, count, shift_ref, turn_ref, column_ref):
    shape = column_ref.shape
    column_ref[...] = zero_one(iota(shape, 1) // C_TRI == iota(shape, 0))
    shape = shift_ref.shape
    shift_ref[...] = zero_one(iota(shape, 1) == iota(shape, 0) + lanes)
    shape = turn_ref.shape
    row_at = iota(shape, 0)
    turn_ref[...] = zero_one(
        iota(shape, 1) == (row_at % count) * (shape[0] // count) + row_at // count
    )


def packet_kernel(*refs):
    pair_ref, weight_ref, valid_ref, ids_ref, act_ref, present_ref, shift_ref = refs[:7]
    packet_ref, hidden_ref = refs[7:]
    rows, residues, width = pair_ref.shape
    per, _, features = act_ref.shape
    lanes = FOCUS_TOTAL * rows
    bias = bias_rows(pair_ref, weight_ref)
    extra = jnp.concatenate(
        [
            valid_ref[...].astype(F32),
            ids_ref[...].astype(F32),
            jnp.zeros((SMALL_ROWS - rows - per, residues), F32),
        ],
        axis=0,
    )
    extra = mul(extra.astype(BF16), shift_ref[...])
    empty = jnp.zeros((SMALL_ROWS, 128 - lanes), F32)
    first = jnp.concatenate([bias[:SMALL_ROWS], empty], axis=1) + extra
    second = jnp.concatenate([bias[SMALL_ROWS:], empty], axis=1)
    small = jnp.concatenate([first, second], axis=1).astype(BF16)
    packet_ref[per * residues :, :] = small
    shown = present_ref[...].astype(F32).astype(BF16)
    shown = mul(shown, jnp.ones((1, hidden_ref.shape[1]), BF16), ((0,), (0,)))
    hidden_ref[...] = 1000000000.0 * (shown - 1.0)
    packet_ref[: per * residues, :] = act_ref[...].reshape(per * residues, features)


def split_small(packet, residues, res_dev, per):
    small = packet[per * residues :, :].astype(F32)
    lanes = FOCUS_TOTAL * res_dev
    bias = jnp.concatenate([small[:, :lanes], small[:, 128 : 128 + lanes]], axis=0)
    extra = small[:, lanes : lanes + residues]
    return bias, extra[:res_dev], extra[res_dev : res_dev + per]


def head_masks(width):
    return [
        zero_one(iota((1, width), 1) // FOCUS_SIZE == h) for h in range(FOCUS_TOTAL)
    ]


def project(x, w_query, w_kvg):
    width = FOCUS_TOTAL * FOCUS_SIZE
    flat = normal(x).astype(BF16)
    query = (mul(flat, w_query[...]) * FOCUS_SIZE ** (-0.5)).astype(BF16)
    keys = mul(flat, w_kvg[:, :width]).astype(BF16)
    values = mul(flat, w_kvg[:, width : 2 * width]).astype(BF16)
    gate = sigmoid(mul(flat, w_kvg[:, 2 * width :]))
    return query, keys, values, gate


def msa_kernel(n, res_dev, *refs):
    packets, turn, hidden_keys, table = refs[:n], refs[n], refs[n + 1], refs[n + 2]
    refs = refs[n + 3 :]
    row_q, row_kvg, row_out, col_q, col_kvg, col_out, lift, outer_w = refs[:8]
    align_ref, update_ref, lifted = refs[8:]
    kinds, width = table.shape
    residues, lanes = hidden_keys.shape
    pair_width = outer_w.shape[1]
    per = (packets[0].shape[0] - SMALL_ROWS) // residues
    count = per * n
    tokens = count * residues
    me = lax.axis_index("axial")

    place = iota((FOCUS_TOTAL * res_dev, lanes), 0)
    place = (place // res_dev) * residues + place % res_dev - iota(place.shape, 1)
    bias = jnp.zeros((residues, lanes), F32)
    rows = []
    for packet, r in zip(packets, (0, *PACKET_ORDER)):
        part, _, all_ids = split_small(packet, residues, res_dev, per)
        bias += mul(part.astype(BF16), zero_one(place == -(me ^ r) * res_dev))
        for q in range(per):
            hot = zero_one(iota((kinds, residues), 0).astype(F32) == all_ids[q : q + 1])
            act = packet[q * residues : (q + 1) * residues, :].astype(F32)
            rows.append(act + mul(hot, table[...], ((0,), (0,))))
    zero = jnp.concatenate(rows, axis=0)
    extra = bias + hidden_keys[...]
    masks = head_masks(width)

    query, keys, values, gate = project(zero, row_q, row_kvg)
    rows = []
    for s in range(count):
        here = slice(s * residues, (s + 1) * residues)
        spread = jnp.concatenate([query[here] * mask for mask in masks], axis=0)
        weights = column_softmax(mul(keys[here], spread, ((1,), (1,))) + extra).astype(BF16)
        heads = mul(weights, values[here], ((0,), (0,)))
        mixed = heads[:residues]
        for h in range(1, FOCUS_TOTAL):
            part = heads[h * residues : (h + 1) * residues]
            mixed = jnp.where(iota((1, width), 1) // FOCUS_SIZE == h, part, mixed)
        rows.append(mixed)
    mixed = (jnp.concatenate(rows, axis=0) * gate).astype(BF16)
    msa_one = (zero + mul(mixed, row_out[...])).astype(BF16)

    one = mul(turn[...], msa_one)
    query, keys, values, gate = project(one, col_q, col_kvg)
    group = min(tokens, 128)
    sites = group // count
    block_of = iota((1, group), 1) // count
    groups = []
    for g in range(tokens // group):
        here = slice(g * group, (g + 1) * group)
        all_weights, all_values = [], []
        for mask in masks:
            full = mul(keys[here], query[here] * mask, ((1,), (1,)))
            scores = full[:count]
            for b in range(1, sites):
                scores = jnp.where(block_of == b, full[b * count : (b + 1) * count], scores)
            weights = column_softmax(scores)
            weights = jnp.concatenate(
                [jnp.where(block_of == b, weights, 0.0) for b in range(sites)], axis=0
            )
            all_weights.append(weights.astype(BF16))
            all_values.append(values[here] * mask)
        groups.append(
            mul(
                jnp.concatenate(all_weights, axis=0),
                jnp.concatenate(all_values, axis=0),
                ((0,), (0,)),
            )
        )
    mixed = (jnp.concatenate(groups, axis=0) * gate).astype(BF16)
    align = (one + mul(mixed, col_out[...])).astype(BF16)
    own = count * res_dev
    row_at, lane_at = iota((own, tokens), 0), iota((own, tokens), 1)
    sequence = row_at // res_dev
    owner = (sequence // per) ^ me
    where_is = jnp.zeros_like(owner)
    for k, r in enumerate(PACKET_ORDER):
        where_is = jnp.where(owner == r, k + 1, where_is)
    pick = zero_one(
        lane_at
        == (row_at % res_dev + me * res_dev) * count + where_is * per + sequence % per
    )
    align_ref[...] = mul(pick, align).reshape(count, res_dev, width).astype(BF16)

    opm = normal(align.astype(F32)).astype(BF16)
    opm = mul(opm, lift[...], ((1,), (1,))).astype(BF16)
    hidden = MEAN_HIDDEN_SIZE
    deep = hidden * count
    spread = zero_one(
        iota((2 * hidden, deep), 1) // count == iota((2 * hidden, deep), 0)
    )
    left = mul(opm, spread)
    left = jnp.where(
        iota((tokens, deep), 0) % count == iota((tokens, deep), 1) % count, left, 0.0
    ).astype(BF16)
    gather = zero_one(iota((residues, tokens), 1) // count == iota((residues, tokens), 0))
    left = mul(gather, left).astype(BF16)
    right = opm[:, hidden:]
    for c in range(0, hidden, 2):
        pair_w = jnp.concatenate(
            [outer_w[(c + k) * hidden : (c + k + 1) * hidden, :] for k in range(2)], axis=1
        )
        part = mul(right, pair_w)
        lifted[c], lifted[c + 1] = part[:, :pair_width], part[:, pair_width:]
    for j in range(0, residues, 2):
        part = jnp.concatenate(
            [
                lifted[:, (j + k) * count : (j + k + 1) * count, :].reshape(deep, pair_width)
                for k in range(2)
            ],
            axis=1,
        )
        part = mul(left, part.astype(BF16)) * (1.0 / count)
        update_ref[j], update_ref[j + 1] = part[:, :pair_width], part[:, pair_width:]


def pair_kernel(*refs):
    pairs, packets, update, column, pair, own_mask = refs[:3], refs[3:6], *refs[6:10]
    proj, gates, gate_out, w_out, out_ref, state, one, right_at, left_at, valid = refs[10:]
    res_dev, residues, width = pair.shape
    per = (packets[0].shape[0] - SMALL_ROWS) // residues
    me = lax.axis_index("axial")
    own_valid = own_mask[...].astype(F32)
    for packet, r in zip((None, *packets), (0, *PACKET_ORDER)):
        shown = split_small(packet, residues, res_dev, per)[1] if r else own_valid
        valid[pl.ds(pl.multiple_of((me ^ r) * res_dev, res_dev), res_dev), :] = shown
    size = res_dev * residues
    for block, r in zip((pair, *pairs), (0, *PAIR_ORDER)):
        state[pl.ds(pl.multiple_of((me ^ r) * size, size), size), :] = (
            block[...].astype(F32).reshape(size, width)
        )
    for k in range(residues):
        one[k * residues : (k + 1) * residues, :] = (
            state[pl.ds(k, residues, stride=residues), :] + update[k]
        )

    shown = mul(valid[...].astype(BF16), column[...])
    right_w = jnp.concatenate([proj[:, C_TRI:], gates[:, C_TRI:]], axis=1)
    step = 8
    for k in range(0, residues, step):
        here = slice(k * residues, (k + step) * residues)
        both = mul(normal(one[here, :]).astype(BF16), right_w)
        both = sigmoid(both[:, C_TRI:]) * both[:, :C_TRI]
        for p in range(step):
            part = both[p * residues : (p + 1) * residues]
            part = part * shown[:, (k + p) * C_TRI : (k + p + 1) * C_TRI]
            right_at[(k + p) * residues : (k + p + 1) * residues, :] = part.astype(BF16).astype(F32)

    own = jnp.concatenate(
        [one[pl.ds(me * res_dev + i, residues, stride=residues), :] for i in range(res_dev)],
        axis=0,
    )
    left_w = jnp.concatenate([proj[:, :C_TRI], gates[:, :C_TRI], gate_out[...]], axis=1)
    own_all = mul(normal(own).astype(BF16), left_w)
    own_gate = sigmoid(own_all[:, 2 * C_TRI :])
    left = sigmoid(own_all[:, C_TRI : 2 * C_TRI]) * own_all[:, :C_TRI]
    shown = mul(own_valid.astype(BF16), column[:res_dev, : res_dev * C_TRI], ((0,), (0,)))
    for i in range(res_dev):
        part = left[i * residues : (i + 1) * residues] * shown[:, i * C_TRI : (i + 1) * C_TRI]
        left_at[i * residues : (i + 1) * residues, :] = part.astype(BF16).astype(F32)
    sums = [jnp.zeros((residues, C_TRI), F32) for _ in range(res_dev)]
    for k in range(residues):
        other = right_at[k * residues : (k + 1) * residues, :]
        for i in range(res_dev):
            sums[i] += left_at[i * residues + k : i * residues + k + 1, :] * other
    mixed = normal(jnp.concatenate(sums, axis=0)).astype(BF16)
    result = own + own_gate * mul(mixed, w_out[...])
    out_ref[...] = result.reshape(res_dev, residues, width).astype(BF16)


def call(kernel, out_shape, scratch, vmem_mib, *args):
    vmem = pl.BlockSpec(memory_space=pltpu.VMEM)
    return pl.pallas_call(
        kernel,
        out_shape=out_shape,
        in_specs=[vmem] * len(args),
        out_specs=jax.tree.map(lambda _: vmem, out_shape),
        scratch_shapes=scratch,
        compiler_params=pltpu.CompilerParams(vmem_limit_bytes=vmem_mib * 1024 * 1024),
        cost_estimate=pl.CostEstimate(flops=FLOPS, bytes_accessed=0, transcendentals=0),
    )(*args)


def swap(array, r, n):
    return lax.ppermute(array, "axial", [(i, i ^ r) for i in range(n)])


def local_whole(
    homolog_activity,
    homolog_symbol_ids,
    residue_present_mask,
    pair_state,
    pair_valid_mask,
    symbol_lookup_matrix,
    row_query_weight,
    horizontal_attention_matrix,
    pair_bias_weight,
    horizontal_final_matrix,
    column_query_weight,
    vertical_attention_matrix,
    vertical_final_matrix,
    tensor_mean_lift_matrix,
    outer_product_output_weight,
    triangle_projection_weight,
    triangle_projection_gate,
    triangle_output_gate,
    triangle_output_weight,
):
    n = lax.axis_size("axial")
    per, residues, width = homolog_activity.shape
    res_dev, _, pair_width = pair_state.shape
    count = per * n
    shift, turn, column = call(
        functools.partial(table_kernel, FOCUS_TOTAL * res_dev, count),
        (
            jax.ShapeDtypeStruct((residues, 128), BF16),
            jax.ShapeDtypeStruct((count * residues, count * residues), BF16),
            jax.ShapeDtypeStruct((residues, residues * C_TRI), BF16),
        ),
        [],
        2,
    )
    packet, hidden_keys = call(
        packet_kernel,
        (
            jax.ShapeDtypeStruct((per * residues + SMALL_ROWS, width), BF16),
            jax.ShapeDtypeStruct((residues, FOCUS_TOTAL * residues), F32),
        ),
        [],
        4,
        pair_state,
        pair_bias_weight.T,
        pair_valid_mask,
        homolog_symbol_ids,
        homolog_activity,
        residue_present_mask.reshape(1, residues),
        shift,
    )
    packets = [swap(packet, r, n) for r in PACKET_ORDER]
    _, later = lax.optimization_barrier((packet, pair_state))
    pairs = [swap(later, r, n) for r in PAIR_ORDER]
    alignment, update = call(
        functools.partial(msa_kernel, n, res_dev),
        (
            jax.ShapeDtypeStruct((count, res_dev, width), BF16),
            jax.ShapeDtypeStruct((residues, residues, pair_width), F32),
        ),
        [
            pltpu.VMEM((MEAN_HIDDEN_SIZE, count * residues, pair_width), F32),
        ],
        16,
        packet,
        *packets,
        turn,
        hidden_keys,
        symbol_lookup_matrix,
        row_query_weight,
        horizontal_attention_matrix,
        horizontal_final_matrix,
        column_query_weight,
        vertical_attention_matrix,
        vertical_final_matrix,
        tensor_mean_lift_matrix.T,
        outer_product_output_weight,
    )
    pair_output = call(
        pair_kernel,
        jax.ShapeDtypeStruct((res_dev, residues, pair_width), BF16),
        [
            pltpu.VMEM((residues * residues, pair_width), F32),
            pltpu.VMEM((residues * residues, pair_width), F32),
            pltpu.VMEM((residues * residues, C_TRI), F32),
            pltpu.VMEM((res_dev * residues, C_TRI), F32),
            pltpu.VMEM((residues, residues), F32),
        ],
        16,
        *pairs,
        *packets,
        update,
        column,
        pair_state,
        pair_valid_mask,
        triangle_projection_weight,
        triangle_projection_gate,
        triangle_output_gate,
        triangle_output_weight,
    )
    return (alignment, pair_output)


def local(homolog_activity, homolog_symbol_ids, residue_present_mask, pair_state, *others):
    n = lax.axis_size("axial")
    per, residues, _ = homolog_activity.shape
    small = n == 4 and per * n == 8 and residues == 32
    plan = local_whole if small else local_sharded
    return plan(homolog_activity, homolog_symbol_ids, residue_present_mask, pair_state, *others)


def solution(mesh):
    parts, copied = P(("dp", "axial")), P()
    return jax.shard_map(
        local,
        mesh=mesh,
        in_specs=(parts, parts, P("dp"), parts, parts) + (copied,) * 14,
        out_specs=(P("dp", "axial", None), P(("dp", "axial"), None, None)),
        check_vma=False,
    )
```

```python
import functools

import jax
import jax.numpy as jnp
from jax import lax
from jax.experimental import pallas as pl
from jax.experimental.pallas import tpu as pltpu
from jax.sharding import PartitionSpec as P

FOCUS_TOTAL = 8
FOCUS_SIZE = 32
MEAN_HIDDEN_SIZE = 32
C_TRI = 128


def layer_normalize(attended_entries):
    attended_entries = attended_entries.astype(jnp.float32)
    mean = jnp.mean(attended_entries, axis=-1, keepdims=True)
    centred = attended_entries - mean
    var = jnp.mean(centred * centred, axis=-1, keepdims=True)
    return centred * lax.rsqrt(var + 1e-05)


def gated_attend(evoformer_block, extra_axes, w_query, w_kvg, w_out):
    lines_list, residue_length, input_width = evoformer_block.shape
    width = FOCUS_TOTAL * FOCUS_SIZE
    flat = (
        layer_normalize(evoformer_block)
        .astype(jnp.bfloat16)
        .reshape(lines_list * residue_length, input_width)
    )
    query = (
        jnp.dot(flat, w_query, preferred_element_type=jnp.float32) * FOCUS_SIZE ** (-0.5)
    ).astype(jnp.bfloat16)
    query = query.reshape(lines_list, residue_length, FOCUS_TOTAL, FOCUS_SIZE)
    kvg = jnp.dot(flat, w_kvg, preferred_element_type=jnp.float32)
    keys = (
        kvg[:, :width]
        .astype(jnp.bfloat16)
        .reshape(lines_list, residue_length, FOCUS_TOTAL, FOCUS_SIZE)
    )
    attended_entries = (
        kvg[:, width : 2 * width]
        .astype(jnp.bfloat16)
        .reshape(lines_list, residue_length, FOCUS_TOTAL, FOCUS_SIZE)
    )
    gate = jax.nn.sigmoid(kvg[:, 2 * width :]).reshape(
        lines_list, residue_length, FOCUS_TOTAL, FOCUS_SIZE
    )
    scores = (
        jnp.einsum("bihd,bjhd->bhij", query, keys, preferred_element_type=jnp.float32) + extra_axes
    )
    top = jnp.max(scores, axis=-1, keepdims=True)
    expo = jnp.exp(scores - top)
    weights = (expo / jnp.sum(expo, axis=-1, keepdims=True)).astype(jnp.bfloat16)
    mixed = jnp.einsum(
        "bhij,bjhd->bihd", weights, attended_entries, preferred_element_type=jnp.float32
    )
    mixed = (mixed * gate).astype(jnp.bfloat16).reshape(lines_list * residue_length, width)
    return evoformer_block + jnp.dot(mixed, w_out, preferred_element_type=jnp.float32).reshape(
        lines_list, residue_length, input_width
    )


def finish_sums(evoformer_block, triangle_output_weight):
    mixed = layer_normalize(jnp.transpose(evoformer_block, (1, 2, 0))).astype(jnp.bfloat16)
    return jnp.einsum(
        "ijc,cz->ijz", mixed, triangle_output_weight, preferred_element_type=jnp.float32
    )


def local_sharded(
    homolog_activity,
    homolog_symbol_ids,
    residue_present_mask,
    pair_state,
    pair_valid_mask,
    symbol_lookup_matrix,
    row_query_weight,
    horizontal_attention_matrix,
    pair_bias_weight,
    horizontal_final_matrix,
    column_query_weight,
    vertical_attention_matrix,
    vertical_final_matrix,
    tensor_mean_lift_matrix,
    outer_product_output_weight,
    triangle_projection_weight,
    triangle_projection_gate,
    triangle_output_gate,
    triangle_output_weight,
):
    sequence_per_device, residue_length, input_width = homolog_activity.shape
    res_dev = pair_state.shape[0]
    group_size = lax.axis_size("axial")
    token_classes = symbol_lookup_matrix.shape[0]
    token_one_hot = (
        homolog_symbol_ids[..., None] == jnp.arange(token_classes, dtype=jnp.int32)
    ).astype(jnp.bfloat16)
    token_embedded = jnp.einsum(
        "slt,tc->slc", token_one_hot, symbol_lookup_matrix, preferred_element_type=jnp.float32
    )
    homolog_starting = homolog_activity.astype(jnp.float32) + token_embedded
    pair_norm = layer_normalize(pair_state).astype(jnp.bfloat16)
    bias_rows = jnp.einsum(
        "ijc,ch->hij", pair_norm, pair_bias_weight, preferred_element_type=jnp.float32
    ).astype(jnp.bfloat16)
    bias_full = lax.all_gather(bias_rows, "axial", axis=1, tiled=True)
    key_bias = 1000000000.0 * (residue_present_mask.astype(jnp.float32) - 1.0)
    extra_axes = bias_full.astype(jnp.float32)[None] + key_bias[None, None, None, :]
    cluster_total = homolog_starting.reshape(
        sequence_per_device // 2, 2, residue_length, input_width
    )
    homolog_across_update = lax.map(
        lambda evoformer_block: gated_attend(
            evoformer_block,
            extra_axes,
            row_query_weight,
            horizontal_attention_matrix,
            horizontal_final_matrix,
        ),
        cluster_total,
    )
    homolog_across_update = homolog_across_update.reshape(
        sequence_per_device, group_size, res_dev, input_width
    ).astype(jnp.bfloat16)
    moved = jnp.swapaxes(
        lax.all_to_all(homolog_across_update, "axial", split_axis=1, concat_axis=0, tiled=True)[
            :, 0
        ],
        0,
        1,
    )
    finished = lax.map(
        lambda item: gated_attend(
            item[None].astype(jnp.float32),
            0.0,
            column_query_weight,
            vertical_attention_matrix,
            vertical_final_matrix,
        )[0],
        moved,
    )
    exchanged = jnp.swapaxes(finished, 0, 1).astype(jnp.bfloat16)[:, None]
    sequence_count = exchanged.shape[0]
    alignment_after_columns = exchanged.reshape(sequence_count, res_dev, input_width)
    tensor_mean_scaler = layer_normalize(alignment_after_columns).astype(jnp.bfloat16)
    split_parts = jnp.einsum(
        "src,cf->rsf",
        tensor_mean_scaler,
        tensor_mean_lift_matrix,
        preferred_element_type=jnp.float32,
    ).astype(jnp.bfloat16)
    first_factor = split_parts[..., :MEAN_HIDDEN_SIZE]
    second_factor = split_parts[..., MEAN_HIDDEN_SIZE:].reshape(
        res_dev, sequence_count * MEAN_HIDDEN_SIZE
    )
    step_rows = 8
    left_blocks = first_factor.reshape(
        res_dev // step_rows, step_rows, sequence_count, MEAN_HIDDEN_SIZE
    )
    piece = lax.all_gather(second_factor, "axial", axis=0, tiled=True)
    count = piece.shape[0]
    right_part = piece.reshape(count, sequence_count, MEAN_HIDDEN_SIZE)

    def one_block(lines_list):
        tensor_mean = (
            jnp.einsum("isc,jsd->ijcd", lines_list, right_part, preferred_element_type=jnp.float32)
            / sequence_count
        )
        tensor_mean = tensor_mean.reshape(
            step_rows, count, MEAN_HIDDEN_SIZE * MEAN_HIDDEN_SIZE
        ).astype(jnp.bfloat16)
        return jnp.einsum(
            "ijf,fz->ijz",
            tensor_mean,
            outer_product_output_weight,
            preferred_element_type=jnp.float32,
        )

    update = lax.map(one_block, left_blocks).reshape(
        res_dev, count, outer_product_output_weight.shape[1]
    )
    pair_one = pair_state.astype(jnp.float32) + update
    tri_norm = layer_normalize(pair_one).astype(jnp.bfloat16)
    proj = jnp.einsum(
        "ikc,cf->fik", tri_norm, triangle_projection_weight, preferred_element_type=jnp.float32
    )
    gates = jnp.einsum(
        "ikc,cf->fik", tri_norm, triangle_projection_gate, preferred_element_type=jnp.float32
    )
    both = (jax.nn.sigmoid(gates) * proj * pair_valid_mask.astype(jnp.float32)[None]).astype(
        jnp.bfloat16
    )
    left_tri = both[:C_TRI]
    right_tri = both[C_TRI:]
    moved_left, moved_right = (
        lax.all_to_all(left_tri, "axial", split_axis=0, concat_axis=1, tiled=True),
        lax.all_to_all(right_tri, "axial", split_axis=0, concat_axis=1, tiled=True),
    )
    partial_sum = jnp.einsum(
        "cik,cjk->cij", moved_left, moved_right, preferred_element_type=jnp.float32
    )
    tri_sum = lax.all_to_all(
        partial_sum.astype(jnp.bfloat16), "axial", split_axis=1, concat_axis=0, tiled=True
    ).astype(partial_sum.dtype)
    tri_update = finish_sums(tri_sum, triangle_output_weight)
    out_gate = jax.nn.sigmoid(
        jnp.einsum(
            "ijc,cz->ijz", tri_norm, triangle_output_gate, preferred_element_type=jnp.float32
        )
    )
    pair_output = (pair_one + out_gate * tri_update).astype(jnp.bfloat16)
    return (alignment_after_columns, pair_output)


BF16 = jnp.bfloat16
F32 = jnp.float32
SMALL_ROWS = 16
FLOPS = 3 * 10**9
PACKET_ORDER = (2, 3, 1)
PAIR_ORDER = (3, 1, 2)


def mul(lhs, rhs, over=((1,), (0,))):
    return lax.dot_general(lhs, rhs, (over, ((), ())), preferred_element_type=F32)


def iota(shape, axis):
    return lax.broadcasted_iota(jnp.int32, shape, axis)


def zero_one(condition):
    return jnp.where(condition, 1.0, 0.0).astype(BF16)


def normal(x):
    mean = jnp.mean(x, axis=-1, keepdims=True)
    centred = x - mean
    var = jnp.mean(centred * centred, axis=-1, keepdims=True)
    return centred * lax.rsqrt(var + 1e-05)


def sigmoid(x):
    return 0.5 + 0.5 * jnp.tanh(0.5 * x)


def column_softmax(scores):
    expo = jnp.exp(scores - jnp.max(scores, axis=0, keepdims=True))
    return expo * (1.0 / jnp.sum(expo, axis=0, keepdims=True))


def bias_rows(pair_ref, weight_ref):
    rows, residues, width = pair_ref.shape
    lanes = FOCUS_TOTAL * rows
    spread = zero_one(iota((FOCUS_TOTAL, lanes), 1) // rows == iota((FOCUS_TOTAL, lanes), 0))
    row_of = iota((width, lanes), 1) % rows
    flat = normal(pair_ref[...].astype(F32).reshape(rows * residues, width)).astype(BF16)
    weight = mul(weight_ref[...], spread, ((0,), (0,)))
    bias = jnp.zeros((residues, lanes), F32)
    for i in range(rows):
        one_row = jnp.where(row_of == i, weight, 0.0).astype(BF16)
        bias += mul(flat[i * residues : (i + 1) * residues], one_row)
    return bias


def table_kernel(lanes, count, shift_ref, turn_ref, column_ref):
    shape = column_ref.shape
    column_ref[...] = zero_one(iota(shape, 1) // C_TRI == iota(shape, 0))
    shape = shift_ref.shape
    shift_ref[...] = zero_one(iota(shape, 1) == iota(shape, 0) + lanes)
    shape = turn_ref.shape
    row_at = iota(shape, 0)
    turn_ref[...] = zero_one(
        iota(shape, 1) == (row_at % count) * (shape[0] // count) + row_at // count
    )


def packet_kernel(*refs):
    pair_ref, weight_ref, valid_ref, ids_ref, act_ref, present_ref, shift_ref = refs[:7]
    packet_ref, hidden_ref = refs[7:]
    rows, residues, width = pair_ref.shape
    per, _, features = act_ref.shape
    lanes = FOCUS_TOTAL * rows
    bias = bias_rows(pair_ref, weight_ref)
    extra = jnp.concatenate(
        [
            valid_ref[...].astype(F32),
            ids_ref[...].astype(F32),
            jnp.zeros((SMALL_ROWS - rows - per, residues), F32),
        ],
        axis=0,
    )
    extra = mul(extra.astype(BF16), shift_ref[...])
    empty = jnp.zeros((SMALL_ROWS, 128 - lanes), F32)
    first = jnp.concatenate([bias[:SMALL_ROWS], empty], axis=1) + extra
    second = jnp.concatenate([bias[SMALL_ROWS:], empty], axis=1)
    small = jnp.concatenate([first, second], axis=1).astype(BF16)
    packet_ref[per * residues :, :] = small
    shown = present_ref[...].astype(F32).astype(BF16)
    shown = mul(shown, jnp.ones((1, hidden_ref.shape[1]), BF16), ((0,), (0,)))
    hidden_ref[...] = 1000000000.0 * (shown - 1.0)
    packet_ref[: per * residues, :] = act_ref[...].reshape(per * residues, features)


def split_small(packet, residues, res_dev, per):
    small = packet[per * residues :, :].astype(F32)
    lanes = FOCUS_TOTAL * res_dev
    bias = jnp.concatenate([small[:, :lanes], small[:, 128 : 128 + lanes]], axis=0)
    extra = small[:, lanes : lanes + residues]
    return bias, extra[:res_dev], extra[res_dev : res_dev + per]


def head_masks():
    return [zero_one(iota((1, 128), 1) // FOCUS_SIZE == h) for h in range(128 // FOCUS_SIZE)]


def project(x, w_query, w_kvg):
    width = FOCUS_TOTAL * FOCUS_SIZE
    flat = normal(x).astype(BF16)
    query = (mul(flat, w_query[...]) * FOCUS_SIZE ** (-0.5)).astype(BF16)
    keys = mul(flat, w_kvg[:, :width]).astype(BF16)
    values = mul(flat, w_kvg[:, width : 2 * width]).astype(BF16)
    gate = sigmoid(mul(flat, w_kvg[:, 2 * width :]))
    return query, keys, values, gate


def msa_kernel(n, res_dev, *refs):
    packets, turn, hidden_keys, table = refs[:n], refs[n], refs[n + 1], refs[n + 2]
    refs = refs[n + 3 :]
    row_q, row_kvg, row_out, col_q, col_kvg, col_out, lift, outer_w = refs[:8]
    align_ref, update_ref, lifted = refs[8:]
    kinds, width = table.shape
    residues, lanes = hidden_keys.shape
    pair_width = outer_w.shape[1]
    per = (packets[0].shape[0] - SMALL_ROWS) // residues
    count = per * n
    tokens = count * residues
    me = lax.axis_index("axial")

    place = iota((FOCUS_TOTAL * res_dev, lanes), 0)
    place = (place // res_dev) * residues + place % res_dev - iota(place.shape, 1)
    bias = jnp.zeros((residues, lanes), F32)
    rows = []
    for packet, r in zip(packets, (0, *PACKET_ORDER)):
        part, _, all_ids = split_small(packet, residues, res_dev, per)
        bias += mul(part.astype(BF16), zero_one(place == -(me ^ r) * res_dev))
        for q in range(per):
            hot = zero_one(iota((kinds, residues), 0).astype(F32) == all_ids[q : q + 1])
            act = packet[q * residues : (q + 1) * residues, :].astype(F32)
            rows.append(act + mul(hot, table[...], ((0,), (0,))))
    zero = jnp.concatenate(rows, axis=0)
    extra = bias + hidden_keys[...]
    masks = head_masks()
    tiles = [slice(t, t + 128) for t in range(0, width, 128)]
    per_tile = len(masks) * residues

    query, keys, values, gate = project(zero, row_q, row_kvg)
    rows = []
    for s in range(count):
        here = slice(s * residues, (s + 1) * residues)
        parts = []
        for t, tile in enumerate(tiles):
            spread = jnp.concatenate([query[here, tile] * mask for mask in masks], axis=0)
            scores = mul(keys[here, tile], spread, ((1,), (1,)))
            scores = scores + extra[:, t * per_tile : (t + 1) * per_tile]
            weights = column_softmax(scores).astype(BF16)
            heads = mul(weights, values[here, tile], ((0,), (0,)))
            mixed = heads[:residues]
            for h in range(1, len(masks)):
                part = heads[h * residues : (h + 1) * residues]
                mixed = jnp.where(iota((1, 128), 1) // FOCUS_SIZE == h, part, mixed)
            parts.append(mixed)
        rows.append(jnp.concatenate(parts, axis=1))
    mixed = (jnp.concatenate(rows, axis=0) * gate).astype(BF16)
    msa_one = (zero + mul(mixed, row_out[...])).astype(BF16)

    one = mul(turn[...], msa_one)
    query, keys, values, gate = project(one, col_q, col_kvg)
    group = min(tokens, 128)
    sites = group // count
    block_of = iota((1, group), 1) // count
    groups = []
    for g in range(tokens // group):
        here = slice(g * group, (g + 1) * group)
        parts = []
        for tile in tiles:
            all_weights, all_values = [], []
            for mask in masks:
                full = mul(keys[here, tile], query[here, tile] * mask, ((1,), (1,)))
                scores = full[:count]
                for b in range(1, sites):
                    scores = jnp.where(block_of == b, full[b * count : (b + 1) * count], scores)
                weights = column_softmax(scores)
                weights = jnp.concatenate(
                    [jnp.where(block_of == b, weights, 0.0) for b in range(sites)], axis=0
                )
                all_weights.append(weights.astype(BF16))
                all_values.append(values[here, tile] * mask)
            parts.append(
                mul(
                    jnp.concatenate(all_weights, axis=0),
                    jnp.concatenate(all_values, axis=0),
                    ((0,), (0,)),
                )
            )
        groups.append(jnp.concatenate(parts, axis=1))
    mixed = (jnp.concatenate(groups, axis=0) * gate).astype(BF16)
    align = (one + mul(mixed, col_out[...])).astype(BF16)
    own = count * res_dev
    row_at, lane_at = iota((own, tokens), 0), iota((own, tokens), 1)
    sequence = row_at // res_dev
    owner = (sequence // per) ^ me
    where_is = jnp.zeros_like(owner)
    for k, r in enumerate(PACKET_ORDER):
        where_is = jnp.where(owner == r, k + 1, where_is)
    pick = zero_one(
        lane_at
        == (row_at % res_dev + me * res_dev) * count + where_is * per + sequence % per
    )
    align_ref[...] = mul(pick, align).reshape(count, res_dev, width).astype(BF16)

    opm = normal(align.astype(F32)).astype(BF16)
    opm = mul(opm, lift[...], ((1,), (1,))).astype(BF16)
    hidden = MEAN_HIDDEN_SIZE
    deep = hidden * count
    spread = zero_one(
        iota((2 * hidden, deep), 1) // count == iota((2 * hidden, deep), 0)
    )
    left = mul(opm, spread)
    left = jnp.where(
        iota((tokens, deep), 0) % count == iota((tokens, deep), 1) % count, left, 0.0
    ).astype(BF16)
    gather = zero_one(iota((residues, tokens), 1) // count == iota((residues, tokens), 0))
    left = mul(gather, left).astype(BF16)
    right = opm[:, hidden:]
    for c in range(0, hidden, 2):
        pair_w = jnp.concatenate(
            [outer_w[(c + k) * hidden : (c + k + 1) * hidden, :] for k in range(2)], axis=1
        )
        part = mul(right, pair_w)
        lifted[c], lifted[c + 1] = part[:, :pair_width], part[:, pair_width:]
    for j in range(0, residues, 2):
        part = jnp.concatenate(
            [
                lifted[:, (j + k) * count : (j + k + 1) * count, :].reshape(deep, pair_width)
                for k in range(2)
            ],
            axis=1,
        )
        part = mul(left, part.astype(BF16)) * (1.0 / count)
        update_ref[j], update_ref[j + 1] = part[:, :pair_width], part[:, pair_width:]


def pair_kernel(*refs):
    pairs, packets, update, column, pair, own_mask = refs[:3], refs[3:6], *refs[6:10]
    proj, gates, gate_out, w_out, out_ref, state, one, left_at, valid = refs[10:]
    res_dev, residues, width = pair.shape
    per = (packets[0].shape[0] - SMALL_ROWS) // residues
    me = lax.axis_index("axial")
    own_valid = own_mask[...].astype(F32)
    for packet, r in zip((None, *packets), (0, *PACKET_ORDER)):
        shown = split_small(packet, residues, res_dev, per)[1] if r else own_valid
        valid[pl.ds(pl.multiple_of((me ^ r) * res_dev, res_dev), res_dev), :] = shown
    size = res_dev * residues
    for block, r in zip((pair, *pairs), (0, *PAIR_ORDER)):
        state[pl.ds(pl.multiple_of((me ^ r) * size, size), size), :] = (
            block[...].astype(F32).reshape(size, width)
        )
    for k in range(residues):
        one[k * residues : (k + 1) * residues, :] = (
            state[pl.ds(k, residues, stride=residues), :] + update[k]
        )

    own = jnp.concatenate(
        [one[pl.ds(me * res_dev + i, residues, stride=residues), :] for i in range(res_dev)],
        axis=0,
    )
    left_w = jnp.concatenate([proj[:, :C_TRI], gates[:, :C_TRI], gate_out[...]], axis=1)
    own_all = mul(normal(own).astype(BF16), left_w)
    own_gate = sigmoid(own_all[:, 2 * C_TRI :])
    left = sigmoid(own_all[:, C_TRI : 2 * C_TRI]) * own_all[:, :C_TRI]
    shown = mul(own_valid.astype(BF16), column[:res_dev, : res_dev * C_TRI], ((0,), (0,)))
    for i in range(res_dev):
        part = left[i * residues : (i + 1) * residues] * shown[:, i * C_TRI : (i + 1) * C_TRI]
        left_at[i * residues : (i + 1) * residues, :] = part.astype(BF16).astype(F32)

    sums = [jnp.zeros((residues, C_TRI), F32) for _ in range(res_dev)]
    shown = mul(valid[...].astype(BF16), column[...])
    right_w = jnp.concatenate([proj[:, C_TRI:], gates[:, C_TRI:]], axis=1)
    step = 8
    for k in range(0, residues, step):
        here = slice(k * residues, (k + step) * residues)
        both = mul(normal(one[here, :]).astype(BF16), right_w)
        both = sigmoid(both[:, C_TRI:]) * both[:, :C_TRI]
        for p in range(step):
            part = both[p * residues : (p + 1) * residues]
            part = part * shown[:, (k + p) * C_TRI : (k + p + 1) * C_TRI]
            other = part.astype(BF16).astype(F32)
            for i in range(res_dev):
                at = i * residues + k + p
                sums[i] += left_at[at : at + 1, :] * other
    mixed = normal(jnp.concatenate(sums, axis=0)).astype(BF16)
    result = own + own_gate * mul(mixed, w_out[...])
    out_ref[...] = result.reshape(res_dev, residues, width).astype(BF16)


def call(kernel, out_shape, scratch, vmem_mib, *args):
    vmem = pl.BlockSpec(memory_space=pltpu.VMEM)
    return pl.pallas_call(
        kernel,
        out_shape=out_shape,
        in_specs=[vmem] * len(args),
        out_specs=jax.tree.map(lambda _: vmem, out_shape),
        scratch_shapes=scratch,
        compiler_params=pltpu.CompilerParams(vmem_limit_bytes=vmem_mib * 1024 * 1024),
        cost_estimate=pl.CostEstimate(flops=FLOPS, bytes_accessed=0, transcendentals=0),
    )(*args)


def swap(array, r, n):
    return lax.ppermute(array, "axial", [(i, i ^ r) for i in range(n)])


def local_whole(
    homolog_activity,
    homolog_symbol_ids,
    residue_present_mask,
    pair_state,
    pair_valid_mask,
    symbol_lookup_matrix,
    row_query_weight,
    horizontal_attention_matrix,
    pair_bias_weight,
    horizontal_final_matrix,
    column_query_weight,
    vertical_attention_matrix,
    vertical_final_matrix,
    tensor_mean_lift_matrix,
    outer_product_output_weight,
    triangle_projection_weight,
    triangle_projection_gate,
    triangle_output_gate,
    triangle_output_weight,
):
    n = lax.axis_size("axial")
    per, residues, width = homolog_activity.shape
    res_dev, _, pair_width = pair_state.shape
    count = per * n
    shift, turn, column = call(
        functools.partial(table_kernel, FOCUS_TOTAL * res_dev, count),
        (
            jax.ShapeDtypeStruct((residues, 128), BF16),
            jax.ShapeDtypeStruct((count * residues, count * residues), BF16),
            jax.ShapeDtypeStruct((residues, residues * C_TRI), BF16),
        ),
        [],
        2,
    )
    packet, hidden_keys = call(
        packet_kernel,
        (
            jax.ShapeDtypeStruct((per * residues + SMALL_ROWS, width), BF16),
            jax.ShapeDtypeStruct((residues, FOCUS_TOTAL * residues), F32),
        ),
        [],
        4,
        pair_state,
        pair_bias_weight.T,
        pair_valid_mask,
        homolog_symbol_ids,
        homolog_activity,
        residue_present_mask.reshape(1, residues),
        shift,
    )
    packets = [swap(packet, r, n) for r in PACKET_ORDER]
    _, later = lax.optimization_barrier((packet, pair_state))
    pairs = [swap(later, r, n) for r in PAIR_ORDER]
    alignment, update = call(
        functools.partial(msa_kernel, n, res_dev),
        (
            jax.ShapeDtypeStruct((count, res_dev, width), BF16),
            jax.ShapeDtypeStruct((residues, residues, pair_width), F32),
        ),
        [
            pltpu.VMEM((MEAN_HIDDEN_SIZE, count * residues, pair_width), F32),
        ],
        16,
        packet,
        *packets,
        turn,
        hidden_keys,
        symbol_lookup_matrix,
        row_query_weight,
        horizontal_attention_matrix,
        horizontal_final_matrix,
        column_query_weight,
        vertical_attention_matrix,
        vertical_final_matrix,
        tensor_mean_lift_matrix.T,
        outer_product_output_weight,
    )
    pair_output = call(
        pair_kernel,
        jax.ShapeDtypeStruct((res_dev, residues, pair_width), BF16),
        [
            pltpu.VMEM((residues * residues, pair_width), F32),
            pltpu.VMEM((residues * residues, pair_width), F32),
            pltpu.VMEM((res_dev * residues, C_TRI), F32),
            pltpu.VMEM((residues, residues), F32),
        ],
        16,
        *pairs,
        *packets,
        update,
        column,
        pair_state,
        pair_valid_mask,
        triangle_projection_weight,
        triangle_projection_gate,
        triangle_output_gate,
        triangle_output_weight,
    )
    return (alignment, pair_output)


def local(homolog_activity, homolog_symbol_ids, residue_present_mask, pair_state, *others):
    n = lax.axis_size("axial")
    per, residues, _ = homolog_activity.shape
    small = n == 4 and per * n == 8 and residues == 32
    plan = local_whole if small else local_sharded
    return plan(homolog_activity, homolog_symbol_ids, residue_present_mask, pair_state, *others)


def solution(mesh):
    parts, copied = P(("dp", "axial")), P()
    return jax.shard_map(
        local,
        mesh=mesh,
        in_specs=(parts, parts, P("dp"), parts, parts) + (copied,) * 14,
        out_specs=(P("dp", "axial", None), P(("dp", "axial"), None, None)),
        check_vma=False,
    )
```

```python
import functools

import jax
import jax.numpy as jnp
from jax import lax
from jax.experimental import pallas as pl
from jax.experimental.pallas import tpu as pltpu
from jax.sharding import PartitionSpec as P

FOCUS_TOTAL = 8
FOCUS_SIZE = 32
MEAN_HIDDEN_SIZE = 32
C_TRI = 128


def layer_normalize(attended_entries):
    attended_entries = attended_entries.astype(jnp.float32)
    mean = jnp.mean(attended_entries, axis=-1, keepdims=True)
    centred = attended_entries - mean
    var = jnp.mean(centred * centred, axis=-1, keepdims=True)
    return centred * lax.rsqrt(var + 1e-05)


def gated_attend(evoformer_block, extra_axes, w_query, w_kvg, w_out):
    lines_list, residue_length, input_width = evoformer_block.shape
    width = FOCUS_TOTAL * FOCUS_SIZE
    flat = (
        layer_normalize(evoformer_block)
        .astype(jnp.bfloat16)
        .reshape(lines_list * residue_length, input_width)
    )
    query = (
        jnp.dot(flat, w_query, preferred_element_type=jnp.float32) * FOCUS_SIZE ** (-0.5)
    ).astype(jnp.bfloat16)
    query = query.reshape(lines_list, residue_length, FOCUS_TOTAL, FOCUS_SIZE)
    kvg = jnp.dot(flat, w_kvg, preferred_element_type=jnp.float32)
    keys = (
        kvg[:, :width]
        .astype(jnp.bfloat16)
        .reshape(lines_list, residue_length, FOCUS_TOTAL, FOCUS_SIZE)
    )
    attended_entries = (
        kvg[:, width : 2 * width]
        .astype(jnp.bfloat16)
        .reshape(lines_list, residue_length, FOCUS_TOTAL, FOCUS_SIZE)
    )
    gate = jax.nn.sigmoid(kvg[:, 2 * width :]).reshape(
        lines_list, residue_length, FOCUS_TOTAL, FOCUS_SIZE
    )
    scores = (
        jnp.einsum("bihd,bjhd->bhij", query, keys, preferred_element_type=jnp.float32) + extra_axes
    )
    top = jnp.max(scores, axis=-1, keepdims=True)
    expo = jnp.exp(scores - top)
    weights = (expo / jnp.sum(expo, axis=-1, keepdims=True)).astype(jnp.bfloat16)
    mixed = jnp.einsum(
        "bhij,bjhd->bihd", weights, attended_entries, preferred_element_type=jnp.float32
    )
    mixed = (mixed * gate).astype(jnp.bfloat16).reshape(lines_list * residue_length, width)
    return evoformer_block + jnp.dot(mixed, w_out, preferred_element_type=jnp.float32).reshape(
        lines_list, residue_length, input_width
    )


def finish_sums(evoformer_block, triangle_output_weight):
    mixed = layer_normalize(jnp.transpose(evoformer_block, (1, 2, 0))).astype(jnp.bfloat16)
    return jnp.einsum(
        "ijc,cz->ijz", mixed, triangle_output_weight, preferred_element_type=jnp.float32
    )


def local_sharded(
    homolog_activity,
    homolog_symbol_ids,
    residue_present_mask,
    pair_state,
    pair_valid_mask,
    symbol_lookup_matrix,
    row_query_weight,
    horizontal_attention_matrix,
    pair_bias_weight,
    horizontal_final_matrix,
    column_query_weight,
    vertical_attention_matrix,
    vertical_final_matrix,
    tensor_mean_lift_matrix,
    outer_product_output_weight,
    triangle_projection_weight,
    triangle_projection_gate,
    triangle_output_gate,
    triangle_output_weight,
):
    sequence_per_device, residue_length, input_width = homolog_activity.shape
    res_dev = pair_state.shape[0]
    group_size = lax.axis_size("axial")
    token_classes = symbol_lookup_matrix.shape[0]
    token_one_hot = (
        homolog_symbol_ids[..., None] == jnp.arange(token_classes, dtype=jnp.int32)
    ).astype(jnp.bfloat16)
    token_embedded = jnp.einsum(
        "slt,tc->slc", token_one_hot, symbol_lookup_matrix, preferred_element_type=jnp.float32
    )
    homolog_starting = homolog_activity.astype(jnp.float32) + token_embedded
    pair_norm = layer_normalize(pair_state).astype(jnp.bfloat16)
    bias_rows = jnp.einsum(
        "ijc,ch->hij", pair_norm, pair_bias_weight, preferred_element_type=jnp.float32
    ).astype(jnp.bfloat16)
    bias_full = lax.all_gather(bias_rows, "axial", axis=1, tiled=True)
    key_bias = 1000000000.0 * (residue_present_mask.astype(jnp.float32) - 1.0)
    extra_axes = bias_full.astype(jnp.float32)[None] + key_bias[None, None, None, :]
    cluster_total = homolog_starting.reshape(
        sequence_per_device // 2, 2, residue_length, input_width
    )
    homolog_across_update = lax.map(
        lambda evoformer_block: gated_attend(
            evoformer_block,
            extra_axes,
            row_query_weight,
            horizontal_attention_matrix,
            horizontal_final_matrix,
        ),
        cluster_total,
    )
    homolog_across_update = homolog_across_update.reshape(
        sequence_per_device, group_size, res_dev, input_width
    ).astype(jnp.bfloat16)
    moved = jnp.swapaxes(
        lax.all_to_all(homolog_across_update, "axial", split_axis=1, concat_axis=0, tiled=True)[
            :, 0
        ],
        0,
        1,
    )
    finished = lax.map(
        lambda item: gated_attend(
            item[None].astype(jnp.float32),
            0.0,
            column_query_weight,
            vertical_attention_matrix,
            vertical_final_matrix,
        )[0],
        moved,
    )
    exchanged = jnp.swapaxes(finished, 0, 1).astype(jnp.bfloat16)[:, None]
    sequence_count = exchanged.shape[0]
    alignment_after_columns = exchanged.reshape(sequence_count, res_dev, input_width)
    tensor_mean_scaler = layer_normalize(alignment_after_columns).astype(jnp.bfloat16)
    split_parts = jnp.einsum(
        "src,cf->rsf",
        tensor_mean_scaler,
        tensor_mean_lift_matrix,
        preferred_element_type=jnp.float32,
    ).astype(jnp.bfloat16)
    first_factor = split_parts[..., :MEAN_HIDDEN_SIZE]
    second_factor = split_parts[..., MEAN_HIDDEN_SIZE:].reshape(
        res_dev, sequence_count * MEAN_HIDDEN_SIZE
    )
    step_rows = 8
    left_blocks = first_factor.reshape(
        res_dev // step_rows, step_rows, sequence_count, MEAN_HIDDEN_SIZE
    )
    piece = lax.all_gather(second_factor, "axial", axis=0, tiled=True)
    count = piece.shape[0]
    right_part = piece.reshape(count, sequence_count, MEAN_HIDDEN_SIZE)

    def one_block(lines_list):
        tensor_mean = (
            jnp.einsum("isc,jsd->ijcd", lines_list, right_part, preferred_element_type=jnp.float32)
            / sequence_count
        )
        tensor_mean = tensor_mean.reshape(
            step_rows, count, MEAN_HIDDEN_SIZE * MEAN_HIDDEN_SIZE
        ).astype(jnp.bfloat16)
        return jnp.einsum(
            "ijf,fz->ijz",
            tensor_mean,
            outer_product_output_weight,
            preferred_element_type=jnp.float32,
        )

    update = lax.map(one_block, left_blocks).reshape(
        res_dev, count, outer_product_output_weight.shape[1]
    )
    pair_one = pair_state.astype(jnp.float32) + update
    tri_norm = layer_normalize(pair_one).astype(jnp.bfloat16)
    proj = jnp.einsum(
        "ikc,cf->fik", tri_norm, triangle_projection_weight, preferred_element_type=jnp.float32
    )
    gates = jnp.einsum(
        "ikc,cf->fik", tri_norm, triangle_projection_gate, preferred_element_type=jnp.float32
    )
    both = (jax.nn.sigmoid(gates) * proj * pair_valid_mask.astype(jnp.float32)[None]).astype(
        jnp.bfloat16
    )
    left_tri = both[:C_TRI]
    right_tri = both[C_TRI:]
    moved_left, moved_right = (
        lax.all_to_all(left_tri, "axial", split_axis=0, concat_axis=1, tiled=True),
        lax.all_to_all(right_tri, "axial", split_axis=0, concat_axis=1, tiled=True),
    )
    partial_sum = jnp.einsum(
        "cik,cjk->cij", moved_left, moved_right, preferred_element_type=jnp.float32
    )
    tri_sum = lax.all_to_all(
        partial_sum.astype(jnp.bfloat16), "axial", split_axis=1, concat_axis=0, tiled=True
    ).astype(partial_sum.dtype)
    tri_update = finish_sums(tri_sum, triangle_output_weight)
    out_gate = jax.nn.sigmoid(
        jnp.einsum(
            "ijc,cz->ijz", tri_norm, triangle_output_gate, preferred_element_type=jnp.float32
        )
    )
    pair_output = (pair_one + out_gate * tri_update).astype(jnp.bfloat16)
    return (alignment_after_columns, pair_output)


BF16 = jnp.bfloat16
F32 = jnp.float32
SMALL_ROWS = 16
FLOPS = 3 * 10**9
PACKET_ORDER = (2, 3, 1)
PAIR_ORDER = (3, 1, 2)


def mul(lhs, rhs, over=((1,), (0,))):
    return lax.dot_general(lhs, rhs, (over, ((), ())), preferred_element_type=F32)


def iota(shape, axis):
    return lax.broadcasted_iota(jnp.int32, shape, axis)


def zero_one(condition):
    return jnp.where(condition, 1.0, 0.0).astype(BF16)


def normal(x):
    mean = jnp.mean(x, axis=-1, keepdims=True)
    centred = x - mean
    var = jnp.mean(centred * centred, axis=-1, keepdims=True)
    return centred * lax.rsqrt(var + 1e-05)


def sigmoid(x):
    return 0.5 + 0.5 * jnp.tanh(0.5 * x)


def column_softmax(scores):
    expo = jnp.exp(scores - jnp.max(scores, axis=0, keepdims=True))
    return expo * (1.0 / jnp.sum(expo, axis=0, keepdims=True))


def bias_rows(pair_ref, weight_ref):
    rows, residues, width = pair_ref.shape
    lanes = FOCUS_TOTAL * rows
    spread = zero_one(iota((FOCUS_TOTAL, lanes), 1) // rows == iota((FOCUS_TOTAL, lanes), 0))
    row_of = iota((width, lanes), 1) % rows
    flat = normal(pair_ref[...].astype(F32).reshape(rows * residues, width)).astype(BF16)
    weight = mul(weight_ref[...], spread, ((0,), (0,)))
    bias = jnp.zeros((residues, lanes), F32)
    for i in range(rows):
        one_row = jnp.where(row_of == i, weight, 0.0).astype(BF16)
        bias += mul(flat[i * residues : (i + 1) * residues], one_row)
    return bias


def table_kernel(lanes, count, shift_ref, turn_ref, column_ref):
    shape = column_ref.shape
    column_ref[...] = zero_one(iota(shape, 1) // C_TRI == iota(shape, 0))
    shape = shift_ref.shape
    shift_ref[...] = zero_one(iota(shape, 1) == iota(shape, 0) + lanes)
    shape = turn_ref.shape
    row_at = iota(shape, 0)
    turn_ref[...] = zero_one(
        iota(shape, 1) == (row_at % count) * (shape[0] // count) + row_at // count
    )


def packet_kernel(*refs):
    pair_ref, weight_ref, valid_ref, ids_ref, act_ref, present_ref, shift_ref = refs[:7]
    packet_ref, hidden_ref = refs[7:]
    rows, residues, width = pair_ref.shape
    per, _, features = act_ref.shape
    lanes = FOCUS_TOTAL * rows
    bias = bias_rows(pair_ref, weight_ref)
    extra = jnp.concatenate(
        [
            valid_ref[...].astype(F32),
            ids_ref[...].astype(F32),
            jnp.zeros((SMALL_ROWS - rows - per, residues), F32),
        ],
        axis=0,
    )
    extra = mul(extra.astype(BF16), shift_ref[...])
    empty = jnp.zeros((SMALL_ROWS, 128 - lanes), F32)
    first = jnp.concatenate([bias[:SMALL_ROWS], empty], axis=1) + extra
    second = jnp.concatenate([bias[SMALL_ROWS:], empty], axis=1)
    small = jnp.concatenate([first, second], axis=1).astype(BF16)
    packet_ref[per * residues :, :] = small
    shown = present_ref[...].astype(F32).astype(BF16)
    shown = mul(shown, jnp.ones((1, hidden_ref.shape[1]), BF16), ((0,), (0,)))
    hidden_ref[...] = 1000000000.0 * (shown - 1.0)
    packet_ref[: per * residues, :] = act_ref[...].reshape(per * residues, features)


def split_small(packet, residues, res_dev, per):
    small = packet[per * residues :, :].astype(F32)
    lanes = FOCUS_TOTAL * res_dev
    bias = jnp.concatenate([small[:, :lanes], small[:, 128 : 128 + lanes]], axis=0)
    extra = small[:, lanes : lanes + residues]
    return bias, extra[:res_dev], extra[res_dev : res_dev + per]


def head_masks(width):
    return [
        zero_one(iota((1, width), 1) // FOCUS_SIZE == h) for h in range(FOCUS_TOTAL)
    ]


def project(x, w_query, w_kvg):
    width = FOCUS_TOTAL * FOCUS_SIZE
    flat = normal(x).astype(BF16)
    query = (mul(flat, w_query[...]) * FOCUS_SIZE ** (-0.5)).astype(BF16)
    keys = mul(flat, w_kvg[:, :width]).astype(BF16)
    values = mul(flat, w_kvg[:, width : 2 * width]).astype(BF16)
    gate = sigmoid(mul(flat, w_kvg[:, 2 * width :]))
    return query, keys, values, gate


def msa_kernel(n, res_dev, *refs):
    packets, turn, hidden_keys, table = refs[:n], refs[n], refs[n + 1], refs[n + 2]
    refs = refs[n + 3 :]
    row_q, row_kvg, row_out, col_q, col_kvg, col_out, lift, outer_w = refs[:8]
    align_ref, update_ref, lifted = refs[8:]
    kinds, width = table.shape
    residues, lanes = hidden_keys.shape
    pair_width = outer_w.shape[1]
    per = (packets[0].shape[0] - SMALL_ROWS) // residues
    count = per * n
    tokens = count * residues
    me = lax.axis_index("axial")

    place = iota((FOCUS_TOTAL * res_dev, lanes), 0)
    place = (place // res_dev) * residues + place % res_dev - iota(place.shape, 1)
    parts, places, acts, ids = [], [], [], []
    for packet, r in zip(packets, (0, *PACKET_ORDER)):
        part, _, all_ids = split_small(packet, residues, res_dev, per)
        parts.append(part)
        places.append(zero_one(place == -(me ^ r) * res_dev))
        acts.append(packet[: per * residues, :])
        ids += [all_ids[q : q + 1] for q in range(per)]
    bias = mul(jnp.concatenate(parts, axis=1).astype(BF16), jnp.concatenate(places, axis=0))
    hot = zero_one(iota((kinds, tokens), 0).astype(F32) == jnp.concatenate(ids, axis=1))
    zero = jnp.concatenate(acts, axis=0).astype(F32) + mul(hot, table[...], ((0,), (0,)))
    extra = bias + hidden_keys[...]
    masks = head_masks(width)

    query, keys, values, gate = project(zero, row_q, row_kvg)
    rows = []
    for s in range(count):
        here = slice(s * residues, (s + 1) * residues)
        spread = jnp.concatenate([query[here] * mask for mask in masks], axis=0)
        weights = column_softmax(mul(keys[here], spread, ((1,), (1,))) + extra).astype(BF16)
        heads = mul(weights, values[here], ((0,), (0,)))
        mixed = heads[:residues]
        for h in range(1, FOCUS_TOTAL):
            part = heads[h * residues : (h + 1) * residues]
            mixed = jnp.where(iota((1, width), 1) // FOCUS_SIZE == h, part, mixed)
        rows.append(mixed)
    mixed = (jnp.concatenate(rows, axis=0) * gate).astype(BF16)
    msa_one = (zero + mul(mixed, row_out[...])).astype(BF16)

    one = mul(turn[...], msa_one)
    query, keys, values, gate = project(one, col_q, col_kvg)
    group = min(tokens, 128)
    sites = group // count
    block_of = iota((1, group), 1) // count
    groups = []
    for g in range(tokens // group):
        here = slice(g * group, (g + 1) * group)
        all_weights, all_values = [], []
        for h in range(0, FOCUS_TOTAL, 2):
            two = jnp.concatenate([query[here] * masks[h + k] for k in range(2)], axis=0)
            two = mul(keys[here], two, ((1,), (1,)))
            for k in range(2):
                full = two[:, k * group : (k + 1) * group]
                scores = full[:count]
                for b in range(1, sites):
                    scores = jnp.where(block_of == b, full[b * count : (b + 1) * count], scores)
                weights = column_softmax(scores)
                weights = jnp.concatenate(
                    [jnp.where(block_of == b, weights, 0.0) for b in range(sites)], axis=0
                )
                all_weights.append(weights.astype(BF16))
                all_values.append(values[here] * masks[h + k])
        groups.append(
            mul(
                jnp.concatenate(all_weights, axis=0),
                jnp.concatenate(all_values, axis=0),
                ((0,), (0,)),
            )
        )
    mixed = (jnp.concatenate(groups, axis=0) * gate).astype(BF16)
    align = (one + mul(mixed, col_out[...])).astype(BF16)
    own = count * res_dev
    row_at, lane_at = iota((own, tokens), 0), iota((own, tokens), 1)
    sequence = row_at // res_dev
    owner = (sequence // per) ^ me
    where_is = jnp.zeros_like(owner)
    for k, r in enumerate(PACKET_ORDER):
        where_is = jnp.where(owner == r, k + 1, where_is)
    pick = zero_one(
        lane_at
        == (row_at % res_dev + me * res_dev) * count + where_is * per + sequence % per
    )
    align_ref[...] = mul(pick, align).reshape(count, res_dev, width).astype(BF16)

    opm = normal(align.astype(F32)).astype(BF16)
    opm = mul(opm, lift[...], ((1,), (1,))).astype(BF16)
    hidden = MEAN_HIDDEN_SIZE
    deep = hidden * count
    spread = zero_one(
        iota((2 * hidden, deep), 1) // count == iota((2 * hidden, deep), 0)
    )
    left = mul(opm, spread)
    left = jnp.where(
        iota((tokens, deep), 0) % count == iota((tokens, deep), 1) % count, left, 0.0
    ).astype(BF16)
    gather = zero_one(iota((residues, tokens), 1) // count == iota((residues, tokens), 0))
    left = mul(gather, left).astype(BF16)
    right = opm[:, hidden:]
    for c in range(0, hidden, 2):
        pair_w = jnp.concatenate(
            [outer_w[(c + k) * hidden : (c + k + 1) * hidden, :] for k in range(2)], axis=1
        )
        part = mul(right, pair_w)
        lifted[c], lifted[c + 1] = part[:, :pair_width], part[:, pair_width:]
    for j in range(0, residues, 2):
        part = jnp.concatenate(
            [
                lifted[:, (j + k) * count : (j + k + 1) * count, :].reshape(deep, pair_width)
                for k in range(2)
            ],
            axis=1,
        )
        part = mul(left, part.astype(BF16)) * (1.0 / count)
        update_ref[j], update_ref[j + 1] = part[:, :pair_width], part[:, pair_width:]


def pair_kernel(*refs):
    pairs, packets, update, column, pair, own_mask = refs[:3], refs[3:6], *refs[6:10]
    proj, gates, gate_out, w_out, out_ref, state, one, right_at, left_at, valid = refs[10:]
    res_dev, residues, width = pair.shape
    per = (packets[0].shape[0] - SMALL_ROWS) // residues
    me = lax.axis_index("axial")
    own_valid = own_mask[...].astype(F32)
    for packet, r in zip((None, *packets), (0, *PACKET_ORDER)):
        shown = split_small(packet, residues, res_dev, per)[1] if r else own_valid
        valid[pl.ds(pl.multiple_of((me ^ r) * res_dev, res_dev), res_dev), :] = shown
    size = res_dev * residues
    for block, r in zip((pair, *pairs), (0, *PAIR_ORDER)):
        state[pl.ds(pl.multiple_of((me ^ r) * size, size), size), :] = (
            block[...].astype(F32).reshape(size, width)
        )
    for k in range(residues):
        one[k * residues : (k + 1) * residues, :] = (
            state[pl.ds(k, residues, stride=residues), :] + update[k]
        )

    shown = mul(valid[...].astype(BF16), column[...])
    right_w = jnp.concatenate([proj[:, C_TRI:], gates[:, C_TRI:]], axis=1)
    step = 8
    for k in range(0, residues, step):
        here = slice(k * residues, (k + step) * residues)
        both = mul(normal(one[here, :]).astype(BF16), right_w)
        both = sigmoid(both[:, C_TRI:]) * both[:, :C_TRI]
        for p in range(step):
            part = both[p * residues : (p + 1) * residues]
            part = part * shown[:, (k + p) * C_TRI : (k + p + 1) * C_TRI]
            right_at[(k + p) * residues : (k + p + 1) * residues, :] = part.astype(BF16).astype(F32)

    own = jnp.concatenate(
        [one[pl.ds(me * res_dev + i, residues, stride=residues), :] for i in range(res_dev)],
        axis=0,
    )
    left_w = jnp.concatenate([proj[:, :C_TRI], gates[:, :C_TRI], gate_out[...]], axis=1)
    own_all = mul(normal(own).astype(BF16), left_w)
    own_gate = sigmoid(own_all[:, 2 * C_TRI :])
    left = sigmoid(own_all[:, C_TRI : 2 * C_TRI]) * own_all[:, :C_TRI]
    shown = mul(own_valid.astype(BF16), column[:res_dev, : res_dev * C_TRI], ((0,), (0,)))
    for i in range(res_dev):
        part = left[i * residues : (i + 1) * residues] * shown[:, i * C_TRI : (i + 1) * C_TRI]
        left_at[i * residues : (i + 1) * residues, :] = part.astype(BF16).astype(F32)
    sums = [jnp.zeros((residues, C_TRI), F32) for _ in range(res_dev)]
    for k in range(residues):
        other = right_at[k * residues : (k + 1) * residues, :]
        for i in range(res_dev):
            sums[i] += left_at[i * residues + k : i * residues + k + 1, :] * other
    mixed = normal(jnp.concatenate(sums, axis=0)).astype(BF16)
    result = own + own_gate * mul(mixed, w_out[...])
    out_ref[...] = result.reshape(res_dev, residues, width).astype(BF16)


def call(kernel, out_shape, scratch, vmem_mib, *args):
    vmem = pl.BlockSpec(memory_space=pltpu.VMEM)
    return pl.pallas_call(
        kernel,
        out_shape=out_shape,
        in_specs=[vmem] * len(args),
        out_specs=jax.tree.map(lambda _: vmem, out_shape),
        scratch_shapes=scratch,
        compiler_params=pltpu.CompilerParams(vmem_limit_bytes=vmem_mib * 1024 * 1024),
        cost_estimate=pl.CostEstimate(flops=FLOPS, bytes_accessed=0, transcendentals=0),
    )(*args)


def swap(array, r, n):
    return lax.ppermute(array, "axial", [(i, i ^ r) for i in range(n)])


def local_whole(
    homolog_activity,
    homolog_symbol_ids,
    residue_present_mask,
    pair_state,
    pair_valid_mask,
    symbol_lookup_matrix,
    row_query_weight,
    horizontal_attention_matrix,
    pair_bias_weight,
    horizontal_final_matrix,
    column_query_weight,
    vertical_attention_matrix,
    vertical_final_matrix,
    tensor_mean_lift_matrix,
    outer_product_output_weight,
    triangle_projection_weight,
    triangle_projection_gate,
    triangle_output_gate,
    triangle_output_weight,
):
    n = lax.axis_size("axial")
    per, residues, width = homolog_activity.shape
    res_dev, _, pair_width = pair_state.shape
    count = per * n
    shift, turn, column = call(
        functools.partial(table_kernel, FOCUS_TOTAL * res_dev, count),
        (
            jax.ShapeDtypeStruct((residues, 128), BF16),
            jax.ShapeDtypeStruct((count * residues, count * residues), BF16),
            jax.ShapeDtypeStruct((residues, residues * C_TRI), BF16),
        ),
        [],
        2,
    )
    packet, hidden_keys = call(
        packet_kernel,
        (
            jax.ShapeDtypeStruct((per * residues + SMALL_ROWS, width), BF16),
            jax.ShapeDtypeStruct((residues, FOCUS_TOTAL * residues), F32),
        ),
        [],
        4,
        pair_state,
        pair_bias_weight.T,
        pair_valid_mask,
        homolog_symbol_ids,
        homolog_activity,
        residue_present_mask.reshape(1, residues),
        shift,
    )
    packets = [swap(packet, r, n) for r in PACKET_ORDER]
    _, later = lax.optimization_barrier((packet, pair_state))
    pairs = [swap(later, r, n) for r in PAIR_ORDER]
    alignment, update = call(
        functools.partial(msa_kernel, n, res_dev),
        (
            jax.ShapeDtypeStruct((count, res_dev, width), BF16),
            jax.ShapeDtypeStruct((residues, residues, pair_width), F32),
        ),
        [
            pltpu.VMEM((MEAN_HIDDEN_SIZE, count * residues, pair_width), F32),
        ],
        16,
        packet,
        *packets,
        turn,
        hidden_keys,
        symbol_lookup_matrix,
        row_query_weight,
        horizontal_attention_matrix,
        horizontal_final_matrix,
        column_query_weight,
        vertical_attention_matrix,
        vertical_final_matrix,
        tensor_mean_lift_matrix.T,
        outer_product_output_weight,
    )
    pair_output = call(
        pair_kernel,
        jax.ShapeDtypeStruct((res_dev, residues, pair_width), BF16),
        [
            pltpu.VMEM((residues * residues, pair_width), F32),
            pltpu.VMEM((residues * residues, pair_width), F32),
            pltpu.VMEM((residues * residues, C_TRI), F32),
            pltpu.VMEM((res_dev * residues, C_TRI), F32),
            pltpu.VMEM((residues, residues), F32),
        ],
        16,
        *pairs,
        *packets,
        update,
        column,
        pair_state,
        pair_valid_mask,
        triangle_projection_weight,
        triangle_projection_gate,
        triangle_output_gate,
        triangle_output_weight,
    )
    return (alignment, pair_output)


def local(homolog_activity, homolog_symbol_ids, residue_present_mask, pair_state, *others):
    n = lax.axis_size("axial")
    per, residues, _ = homolog_activity.shape
    small = n == 4 and per * n == 8 and residues == 32
    plan = local_whole if small else local_sharded
    return plan(homolog_activity, homolog_symbol_ids, residue_present_mask, pair_state, *others)


def solution(mesh):
    parts, copied = P(("dp", "axial")), P()
    return jax.shard_map(
        local,
        mesh=mesh,
        in_specs=(parts, parts, P("dp"), parts, parts) + (copied,) * 14,
        out_specs=(P("dp", "axial", None), P(("dp", "axial"), None, None)),
        check_vma=False,
    )
```

```python
import functools

import jax
import jax.numpy as jnp
from jax import lax
from jax.experimental import pallas as pl
from jax.experimental.pallas import tpu as pltpu
from jax.sharding import PartitionSpec as P

FOCUS_TOTAL = 8
FOCUS_SIZE = 32
MEAN_HIDDEN_SIZE = 32
C_TRI = 128


def layer_normalize(attended_entries):
    attended_entries = attended_entries.astype(jnp.float32)
    mean = jnp.mean(attended_entries, axis=-1, keepdims=True)
    centred = attended_entries - mean
    var = jnp.mean(centred * centred, axis=-1, keepdims=True)
    return centred * lax.rsqrt(var + 1e-05)


def gated_attend(evoformer_block, extra_axes, w_query, w_kvg, w_out):
    lines_list, residue_length, input_width = evoformer_block.shape
    width = FOCUS_TOTAL * FOCUS_SIZE
    flat = (
        layer_normalize(evoformer_block)
        .astype(jnp.bfloat16)
        .reshape(lines_list * residue_length, input_width)
    )
    query = (
        jnp.dot(flat, w_query, preferred_element_type=jnp.float32) * FOCUS_SIZE ** (-0.5)
    ).astype(jnp.bfloat16)
    query = query.reshape(lines_list, residue_length, FOCUS_TOTAL, FOCUS_SIZE)
    kvg = jnp.dot(flat, w_kvg, preferred_element_type=jnp.float32)
    keys = (
        kvg[:, :width]
        .astype(jnp.bfloat16)
        .reshape(lines_list, residue_length, FOCUS_TOTAL, FOCUS_SIZE)
    )
    attended_entries = (
        kvg[:, width : 2 * width]
        .astype(jnp.bfloat16)
        .reshape(lines_list, residue_length, FOCUS_TOTAL, FOCUS_SIZE)
    )
    gate = jax.nn.sigmoid(kvg[:, 2 * width :]).reshape(
        lines_list, residue_length, FOCUS_TOTAL, FOCUS_SIZE
    )
    scores = (
        jnp.einsum("bihd,bjhd->bhij", query, keys, preferred_element_type=jnp.float32) + extra_axes
    )
    top = jnp.max(scores, axis=-1, keepdims=True)
    expo = jnp.exp(scores - top)
    weights = (expo / jnp.sum(expo, axis=-1, keepdims=True)).astype(jnp.bfloat16)
    mixed = jnp.einsum(
        "bhij,bjhd->bihd", weights, attended_entries, preferred_element_type=jnp.float32
    )
    mixed = (mixed * gate).astype(jnp.bfloat16).reshape(lines_list * residue_length, width)
    return evoformer_block + jnp.dot(mixed, w_out, preferred_element_type=jnp.float32).reshape(
        lines_list, residue_length, input_width
    )


def finish_sums(evoformer_block, triangle_output_weight):
    mixed = layer_normalize(jnp.transpose(evoformer_block, (1, 2, 0))).astype(jnp.bfloat16)
    return jnp.einsum(
        "ijc,cz->ijz", mixed, triangle_output_weight, preferred_element_type=jnp.float32
    )


def local_sharded(
    homolog_activity,
    homolog_symbol_ids,
    residue_present_mask,
    pair_state,
    pair_valid_mask,
    symbol_lookup_matrix,
    row_query_weight,
    horizontal_attention_matrix,
    pair_bias_weight,
    horizontal_final_matrix,
    column_query_weight,
    vertical_attention_matrix,
    vertical_final_matrix,
    tensor_mean_lift_matrix,
    outer_product_output_weight,
    triangle_projection_weight,
    triangle_projection_gate,
    triangle_output_gate,
    triangle_output_weight,
):
    sequence_per_device, residue_length, input_width = homolog_activity.shape
    res_dev = pair_state.shape[0]
    group_size = lax.axis_size("axial")
    token_classes = symbol_lookup_matrix.shape[0]
    token_one_hot = (
        homolog_symbol_ids[..., None] == jnp.arange(token_classes, dtype=jnp.int32)
    ).astype(jnp.bfloat16)
    token_embedded = jnp.einsum(
        "slt,tc->slc", token_one_hot, symbol_lookup_matrix, preferred_element_type=jnp.float32
    )
    homolog_starting = homolog_activity.astype(jnp.float32) + token_embedded
    pair_norm = layer_normalize(pair_state).astype(jnp.bfloat16)
    bias_rows = jnp.einsum(
        "ijc,ch->hij", pair_norm, pair_bias_weight, preferred_element_type=jnp.float32
    ).astype(jnp.bfloat16)
    bias_full = lax.all_gather(bias_rows, "axial", axis=1, tiled=True)
    key_bias = 1000000000.0 * (residue_present_mask.astype(jnp.float32) - 1.0)
    extra_axes = bias_full.astype(jnp.float32)[None] + key_bias[None, None, None, :]
    cluster_total = homolog_starting.reshape(
        sequence_per_device // 2, 2, residue_length, input_width
    )
    homolog_across_update = lax.map(
        lambda evoformer_block: gated_attend(
            evoformer_block,
            extra_axes,
            row_query_weight,
            horizontal_attention_matrix,
            horizontal_final_matrix,
        ),
        cluster_total,
    )
    homolog_across_update = homolog_across_update.reshape(
        sequence_per_device, group_size, res_dev, input_width
    ).astype(jnp.bfloat16)
    moved = jnp.swapaxes(
        lax.all_to_all(homolog_across_update, "axial", split_axis=1, concat_axis=0, tiled=True)[
            :, 0
        ],
        0,
        1,
    )
    finished = lax.map(
        lambda item: gated_attend(
            item[None].astype(jnp.float32),
            0.0,
            column_query_weight,
            vertical_attention_matrix,
            vertical_final_matrix,
        )[0],
        moved,
    )
    exchanged = jnp.swapaxes(finished, 0, 1).astype(jnp.bfloat16)[:, None]
    sequence_count = exchanged.shape[0]
    alignment_after_columns = exchanged.reshape(sequence_count, res_dev, input_width)
    tensor_mean_scaler = layer_normalize(alignment_after_columns).astype(jnp.bfloat16)
    split_parts = jnp.einsum(
        "src,cf->rsf",
        tensor_mean_scaler,
        tensor_mean_lift_matrix,
        preferred_element_type=jnp.float32,
    ).astype(jnp.bfloat16)
    first_factor = split_parts[..., :MEAN_HIDDEN_SIZE]
    second_factor = split_parts[..., MEAN_HIDDEN_SIZE:].reshape(
        res_dev, sequence_count * MEAN_HIDDEN_SIZE
    )
    step_rows = 8
    left_blocks = first_factor.reshape(
        res_dev // step_rows, step_rows, sequence_count, MEAN_HIDDEN_SIZE
    )
    piece = lax.all_gather(second_factor, "axial", axis=0, tiled=True)
    count = piece.shape[0]
    right_part = piece.reshape(count, sequence_count, MEAN_HIDDEN_SIZE)

    def one_block(lines_list):
        tensor_mean = (
            jnp.einsum("isc,jsd->ijcd", lines_list, right_part, preferred_element_type=jnp.float32)
            / sequence_count
        )
        tensor_mean = tensor_mean.reshape(
            step_rows, count, MEAN_HIDDEN_SIZE * MEAN_HIDDEN_SIZE
        ).astype(jnp.bfloat16)
        return jnp.einsum(
            "ijf,fz->ijz",
            tensor_mean,
            outer_product_output_weight,
            preferred_element_type=jnp.float32,
        )

    update = lax.map(one_block, left_blocks).reshape(
        res_dev, count, outer_product_output_weight.shape[1]
    )
    pair_one = pair_state.astype(jnp.float32) + update
    tri_norm = layer_normalize(pair_one).astype(jnp.bfloat16)
    proj = jnp.einsum(
        "ikc,cf->fik", tri_norm, triangle_projection_weight, preferred_element_type=jnp.float32
    )
    gates = jnp.einsum(
        "ikc,cf->fik", tri_norm, triangle_projection_gate, preferred_element_type=jnp.float32
    )
    both = (jax.nn.sigmoid(gates) * proj * pair_valid_mask.astype(jnp.float32)[None]).astype(
        jnp.bfloat16
    )
    left_tri = both[:C_TRI]
    right_tri = both[C_TRI:]
    moved_left, moved_right = (
        lax.all_to_all(left_tri, "axial", split_axis=0, concat_axis=1, tiled=True),
        lax.all_to_all(right_tri, "axial", split_axis=0, concat_axis=1, tiled=True),
    )
    partial_sum = jnp.einsum(
        "cik,cjk->cij", moved_left, moved_right, preferred_element_type=jnp.float32
    )
    tri_sum = lax.all_to_all(
        partial_sum.astype(jnp.bfloat16), "axial", split_axis=1, concat_axis=0, tiled=True
    ).astype(partial_sum.dtype)
    tri_update = finish_sums(tri_sum, triangle_output_weight)
    out_gate = jax.nn.sigmoid(
        jnp.einsum(
            "ijc,cz->ijz", tri_norm, triangle_output_gate, preferred_element_type=jnp.float32
        )
    )
    pair_output = (pair_one + out_gate * tri_update).astype(jnp.bfloat16)
    return (alignment_after_columns, pair_output)


BF16 = jnp.bfloat16
F32 = jnp.float32
SMALL_ROWS = 16
FLOPS = 3 * 10**9
PACKET_ORDER = (2, 3, 1)
PAIR_ORDER = (3, 1, 2)


def mul(lhs, rhs, over=((1,), (0,))):
    return lax.dot_general(lhs, rhs, (over, ((), ())), preferred_element_type=F32)


def iota(shape, axis):
    return lax.broadcasted_iota(jnp.int32, shape, axis)


def zero_one(condition):
    return jnp.where(condition, 1.0, 0.0).astype(BF16)


def normal(x):
    mean = jnp.mean(x, axis=-1, keepdims=True)
    centred = x - mean
    var = jnp.mean(centred * centred, axis=-1, keepdims=True)
    return centred * lax.rsqrt(var + 1e-05)


def sigmoid(x):
    return 0.5 + 0.5 * jnp.tanh(0.5 * x)


def column_softmax(scores):
    expo = jnp.exp(scores - jnp.max(scores, axis=0, keepdims=True))
    return expo * (1.0 / jnp.sum(expo, axis=0, keepdims=True))


def bias_rows(pair_ref, weight_ref):
    rows, residues, width = pair_ref.shape
    lanes = FOCUS_TOTAL * rows
    spread = zero_one(iota((FOCUS_TOTAL, lanes), 1) // rows == iota((FOCUS_TOTAL, lanes), 0))
    row_of = iota((width, lanes), 1) % rows
    flat = normal(pair_ref[...].astype(F32).reshape(rows * residues, width)).astype(BF16)
    weight = mul(weight_ref[...], spread, ((0,), (0,)))
    bias = jnp.zeros((residues, lanes), F32)
    for i in range(rows):
        one_row = jnp.where(row_of == i, weight, 0.0).astype(BF16)
        bias += mul(flat[i * residues : (i + 1) * residues], one_row)
    return bias


def table_kernel(lanes, count, shift_ref, turn_ref, column_ref):
    shape = column_ref.shape
    column_ref[...] = zero_one(iota(shape, 1) // C_TRI == iota(shape, 0))
    shape = shift_ref.shape
    shift_ref[...] = zero_one(iota(shape, 1) == iota(shape, 0) + lanes)
    shape = turn_ref.shape
    row_at = iota(shape, 0)
    turn_ref[...] = zero_one(
        iota(shape, 1) == (row_at % count) * (shape[0] // count) + row_at // count
    )


def packet_kernel(*refs):
    pair_ref, weight_ref, valid_ref, ids_ref, act_ref, present_ref, shift_ref = refs[:7]
    packet_ref, hidden_ref = refs[7:]
    rows, residues, width = pair_ref.shape
    per, _, features = act_ref.shape
    lanes = FOCUS_TOTAL * rows
    bias = bias_rows(pair_ref, weight_ref)
    extra = jnp.concatenate(
        [
            valid_ref[...].astype(F32),
            ids_ref[...].astype(F32),
            jnp.zeros((SMALL_ROWS - rows - per, residues), F32),
        ],
        axis=0,
    )
    extra = mul(extra.astype(BF16), shift_ref[...])
    empty = jnp.zeros((SMALL_ROWS, 128 - lanes), F32)
    first = jnp.concatenate([bias[:SMALL_ROWS], empty], axis=1) + extra
    second = jnp.concatenate([bias[SMALL_ROWS:], empty], axis=1)
    small = jnp.concatenate([first, second], axis=1).astype(BF16)
    packet_ref[per * residues :, :] = small
    shown = present_ref[...].astype(F32).astype(BF16)
    shown = mul(shown, jnp.ones((1, hidden_ref.shape[1]), BF16), ((0,), (0,)))
    hidden_ref[...] = 1000000000.0 * (shown - 1.0)
    packet_ref[: per * residues, :] = act_ref[...].reshape(per * residues, features)


def split_small(packet, residues, res_dev, per):
    small = packet[per * residues :, :].astype(F32)
    lanes = FOCUS_TOTAL * res_dev
    bias = jnp.concatenate([small[:, :lanes], small[:, 128 : 128 + lanes]], axis=0)
    extra = small[:, lanes : lanes + residues]
    return bias, extra[:res_dev], extra[res_dev : res_dev + per]


def head_masks(width):
    return [
        zero_one(iota((1, width), 1) // FOCUS_SIZE == h) for h in range(FOCUS_TOTAL)
    ]


def project(x, w_query, w_kvg):
    width = FOCUS_TOTAL * FOCUS_SIZE
    flat = normal(x).astype(BF16)
    query = (mul(flat, w_query[...]) * FOCUS_SIZE ** (-0.5)).astype(BF16)
    keys = mul(flat, w_kvg[:, :width]).astype(BF16)
    values = mul(flat, w_kvg[:, width : 2 * width]).astype(BF16)
    gate = sigmoid(mul(flat, w_kvg[:, 2 * width :]))
    return query, keys, values, gate


def msa_kernel(n, res_dev, *refs):
    packets, turn, hidden_keys, table = refs[:n], refs[n], refs[n + 1], refs[n + 2]
    refs = refs[n + 3 :]
    row_q, row_kvg, row_out, col_q, col_kvg, col_out, lift, outer_w = refs[:8]
    align_ref, update_ref, lifted = refs[8:]
    kinds, width = table.shape
    residues, lanes = hidden_keys.shape
    pair_width = outer_w.shape[1]
    per = (packets[0].shape[0] - SMALL_ROWS) // residues
    count = per * n
    tokens = count * residues
    me = lax.axis_index("axial")

    place = iota((FOCUS_TOTAL * res_dev, lanes), 0)
    place = (place // res_dev) * residues + place % res_dev - iota(place.shape, 1)
    bias = jnp.zeros((residues, lanes), F32)
    rows = []
    for packet, r in zip(packets, (0, *PACKET_ORDER)):
        part, _, all_ids = split_small(packet, residues, res_dev, per)
        bias += mul(part.astype(BF16), zero_one(place == -(me ^ r) * res_dev))
        for q in range(per):
            hot = zero_one(iota((kinds, residues), 0).astype(F32) == all_ids[q : q + 1])
            act = packet[q * residues : (q + 1) * residues, :].astype(F32)
            rows.append(act + mul(hot, table[...], ((0,), (0,))))
    zero = jnp.concatenate(rows, axis=0)
    extra = bias + hidden_keys[...]
    masks = head_masks(width)

    query, keys, values, gate = project(zero, row_q, row_kvg)
    rows = []
    for s in range(count):
        here = slice(s * residues, (s + 1) * residues)
        spread = jnp.concatenate([query[here] * mask for mask in masks], axis=0)
        weights = column_softmax(mul(keys[here], spread, ((1,), (1,))) + extra).astype(BF16)
        heads = mul(weights, values[here], ((0,), (0,)))
        mixed = heads[:residues]
        for h in range(1, FOCUS_TOTAL):
            part = heads[h * residues : (h + 1) * residues]
            mixed = jnp.where(iota((1, width), 1) // FOCUS_SIZE == h, part, mixed)
        rows.append(mixed)
    mixed = (jnp.concatenate(rows, axis=0) * gate).astype(BF16)
    msa_one = (zero + mul(mixed, row_out[...])).astype(BF16)

    one = mul(turn[...], msa_one)
    query, keys, values, gate = project(one, col_q, col_kvg)
    group = min(tokens, 128)
    sites = group // count
    block_of = iota((1, group), 1) // count
    groups = []
    for g in range(tokens // group):
        here = slice(g * group, (g + 1) * group)
        all_weights, all_values = [], []
        for mask in masks:
            full = mul(keys[here], query[here] * mask, ((1,), (1,)))
            scores = full[:count]
            for b in range(1, sites):
                scores = jnp.where(block_of == b, full[b * count : (b + 1) * count], scores)
            weights = column_softmax(scores)
            weights = jnp.concatenate(
                [jnp.where(block_of == b, weights, 0.0) for b in range(sites)], axis=0
            )
            all_weights.append(weights.astype(BF16))
            all_values.append(values[here] * mask)
        groups.append(
            mul(
                jnp.concatenate(all_weights, axis=0),
                jnp.concatenate(all_values, axis=0),
                ((0,), (0,)),
            )
        )
    mixed = (jnp.concatenate(groups, axis=0) * gate).astype(BF16)
    align = (one + mul(mixed, col_out[...])).astype(BF16)
    own = count * res_dev
    row_at, lane_at = iota((own, tokens), 0), iota((own, tokens), 1)
    sequence = row_at // res_dev
    owner = (sequence // per) ^ me
    where_is = jnp.zeros_like(owner)
    for k, r in enumerate(PACKET_ORDER):
        where_is = jnp.where(owner == r, k + 1, where_is)
    pick = zero_one(
        lane_at
        == (row_at % res_dev + me * res_dev) * count + where_is * per + sequence % per
    )
    align_ref[...] = mul(pick, align).reshape(count, res_dev, width).astype(BF16)

    opm = normal(align.astype(F32)).astype(BF16)
    opm = mul(opm, lift[...], ((1,), (1,))).astype(BF16)
    hidden = MEAN_HIDDEN_SIZE
    deep = hidden * count
    spread = zero_one(
        iota((2 * hidden, deep), 1) // count == iota((2 * hidden, deep), 0)
    )
    left = mul(opm, spread)
    left = jnp.where(
        iota((tokens, deep), 0) % count == iota((tokens, deep), 1) % count, left, 0.0
    ).astype(BF16)
    gather = zero_one(iota((residues, tokens), 1) // count == iota((residues, tokens), 0))
    left = mul(gather, left).astype(BF16)
    right = opm[:, hidden:]

    def lift_two(c, _):
        rows = outer_w[pl.ds(pl.multiple_of(c * 2 * hidden, 2 * hidden), 2 * hidden), :]
        part = mul(right, jnp.concatenate([rows[:hidden], rows[hidden:]], axis=1))
        lifted[2 * c], lifted[2 * c + 1] = part[:, :pair_width], part[:, pair_width:]
        return _

    def update_two(j, _):
        rows = lifted[:, pl.ds(pl.multiple_of(j * 2 * count, 2 * count), 2 * count), :]
        part = jnp.concatenate(
            [rows[:, k * count : (k + 1) * count].reshape(deep, pair_width) for k in range(2)],
            axis=1,
        )
        part = mul(left, part.astype(BF16)) * (1.0 / count)
        update_ref[2 * j], update_ref[2 * j + 1] = part[:, :pair_width], part[:, pair_width:]
        return _

    lax.fori_loop(0, hidden // 2, lift_two, 0, unroll=4)
    lax.fori_loop(0, residues // 2, update_two, 0, unroll=4)


def pair_kernel(*refs):
    pairs, packets, update, column, pair, own_mask = refs[:3], refs[3:6], *refs[6:10]
    proj, gates, gate_out, w_out, out_ref, state, one, right_at, left_at, valid = refs[10:]
    res_dev, residues, width = pair.shape
    per = (packets[0].shape[0] - SMALL_ROWS) // residues
    me = lax.axis_index("axial")
    own_valid = own_mask[...].astype(F32)
    for packet, r in zip((None, *packets), (0, *PACKET_ORDER)):
        shown = split_small(packet, residues, res_dev, per)[1] if r else own_valid
        valid[pl.ds(pl.multiple_of((me ^ r) * res_dev, res_dev), res_dev), :] = shown
    size = res_dev * residues
    for block, r in zip((pair, *pairs), (0, *PAIR_ORDER)):
        state[pl.ds(pl.multiple_of((me ^ r) * size, size), size), :] = (
            block[...].astype(F32).reshape(size, width)
        )
    for k in range(residues):
        one[k * residues : (k + 1) * residues, :] = (
            state[pl.ds(k, residues, stride=residues), :] + update[k]
        )

    shown = mul(valid[...].astype(BF16), column[...])
    right_w = jnp.concatenate([proj[:, C_TRI:], gates[:, C_TRI:]], axis=1)
    step = 8
    for k in range(0, residues, step):
        here = slice(k * residues, (k + step) * residues)
        both = mul(normal(one[here, :]).astype(BF16), right_w)
        both = sigmoid(both[:, C_TRI:]) * both[:, :C_TRI]
        for p in range(step):
            part = both[p * residues : (p + 1) * residues]
            part = part * shown[:, (k + p) * C_TRI : (k + p + 1) * C_TRI]
            right_at[(k + p) * residues : (k + p + 1) * residues, :] = part.astype(BF16).astype(F32)

    own = jnp.concatenate(
        [one[pl.ds(me * res_dev + i, residues, stride=residues), :] for i in range(res_dev)],
        axis=0,
    )
    left_w = jnp.concatenate([proj[:, :C_TRI], gates[:, :C_TRI], gate_out[...]], axis=1)
    own_all = mul(normal(own).astype(BF16), left_w)
    own_gate = sigmoid(own_all[:, 2 * C_TRI :])
    left = sigmoid(own_all[:, C_TRI : 2 * C_TRI]) * own_all[:, :C_TRI]
    shown = mul(own_valid.astype(BF16), column[:res_dev, : res_dev * C_TRI], ((0,), (0,)))
    for i in range(res_dev):
        part = left[i * residues : (i + 1) * residues] * shown[:, i * C_TRI : (i + 1) * C_TRI]
        left_at[i * residues : (i + 1) * residues, :] = part.astype(BF16).astype(F32)

    def add_k(k, sums):
        other = right_at[pl.ds(pl.multiple_of(k * residues, residues), residues), :]
        return [
            sums[i] + left_at[pl.ds(i * residues + k, 1), :] * other for i in range(res_dev)
        ]

    sums = [jnp.zeros((residues, C_TRI), F32) for _ in range(res_dev)]
    sums = lax.fori_loop(0, residues, add_k, sums, unroll=4)
    mixed = normal(jnp.concatenate(sums, axis=0)).astype(BF16)
    result = own + own_gate * mul(mixed, w_out[...])
    out_ref[...] = result.reshape(res_dev, residues, width).astype(BF16)


def call(kernel, out_shape, scratch, vmem_mib, *args):
    vmem = pl.BlockSpec(memory_space=pltpu.VMEM)
    return pl.pallas_call(
        kernel,
        out_shape=out_shape,
        in_specs=[vmem] * len(args),
        out_specs=jax.tree.map(lambda _: vmem, out_shape),
        scratch_shapes=scratch,
        compiler_params=pltpu.CompilerParams(vmem_limit_bytes=vmem_mib * 1024 * 1024),
        cost_estimate=pl.CostEstimate(flops=FLOPS, bytes_accessed=0, transcendentals=0),
    )(*args)


def swap(array, r, n):
    return lax.ppermute(array, "axial", [(i, i ^ r) for i in range(n)])


def local_whole(
    homolog_activity,
    homolog_symbol_ids,
    residue_present_mask,
    pair_state,
    pair_valid_mask,
    symbol_lookup_matrix,
    row_query_weight,
    horizontal_attention_matrix,
    pair_bias_weight,
    horizontal_final_matrix,
    column_query_weight,
    vertical_attention_matrix,
    vertical_final_matrix,
    tensor_mean_lift_matrix,
    outer_product_output_weight,
    triangle_projection_weight,
    triangle_projection_gate,
    triangle_output_gate,
    triangle_output_weight,
):
    n = lax.axis_size("axial")
    per, residues, width = homolog_activity.shape
    res_dev, _, pair_width = pair_state.shape
    count = per * n
    shift, turn, column = call(
        functools.partial(table_kernel, FOCUS_TOTAL * res_dev, count),
        (
            jax.ShapeDtypeStruct((residues, 128), BF16),
            jax.ShapeDtypeStruct((count * residues, count * residues), BF16),
            jax.ShapeDtypeStruct((residues, residues * C_TRI), BF16),
        ),
        [],
        2,
    )
    packet, hidden_keys = call(
        packet_kernel,
        (
            jax.ShapeDtypeStruct((per * residues + SMALL_ROWS, width), BF16),
            jax.ShapeDtypeStruct((residues, FOCUS_TOTAL * residues), F32),
        ),
        [],
        4,
        pair_state,
        pair_bias_weight.T,
        pair_valid_mask,
        homolog_symbol_ids,
        homolog_activity,
        residue_present_mask.reshape(1, residues),
        shift,
    )
    packets = [swap(packet, r, n) for r in PACKET_ORDER]
    _, later = lax.optimization_barrier((packet, pair_state))
    pairs = [swap(later, r, n) for r in PAIR_ORDER]
    alignment, update = call(
        functools.partial(msa_kernel, n, res_dev),
        (
            jax.ShapeDtypeStruct((count, res_dev, width), BF16),
            jax.ShapeDtypeStruct((residues, residues, pair_width), F32),
        ),
        [
            pltpu.VMEM((MEAN_HIDDEN_SIZE, count * residues, pair_width), F32),
        ],
        16,
        packet,
        *packets,
        turn,
        hidden_keys,
        symbol_lookup_matrix,
        row_query_weight,
        horizontal_attention_matrix,
        horizontal_final_matrix,
        column_query_weight,
        vertical_attention_matrix,
        vertical_final_matrix,
        tensor_mean_lift_matrix.T,
        outer_product_output_weight,
    )
    pair_output = call(
        pair_kernel,
        jax.ShapeDtypeStruct((res_dev, residues, pair_width), BF16),
        [
            pltpu.VMEM((residues * residues, pair_width), F32),
            pltpu.VMEM((residues * residues, pair_width), F32),
            pltpu.VMEM((residues * residues, C_TRI), F32),
            pltpu.VMEM((res_dev * residues, C_TRI), F32),
            pltpu.VMEM((residues, residues), F32),
        ],
        16,
        *pairs,
        *packets,
        update,
        column,
        pair_state,
        pair_valid_mask,
        triangle_projection_weight,
        triangle_projection_gate,
        triangle_output_gate,
        triangle_output_weight,
    )
    return (alignment, pair_output)


def local(homolog_activity, homolog_symbol_ids, residue_present_mask, pair_state, *others):
    n = lax.axis_size("axial")
    per, residues, _ = homolog_activity.shape
    small = n == 4 and per * n == 8 and residues == 32
    plan = local_whole if small else local_sharded
    return plan(homolog_activity, homolog_symbol_ids, residue_present_mask, pair_state, *others)


def solution(mesh):
    parts, copied = P(("dp", "axial")), P()
    return jax.shard_map(
        local,
        mesh=mesh,
        in_specs=(parts, parts, P("dp"), parts, parts) + (copied,) * 14,
        out_specs=(P("dp", "axial", None), P(("dp", "axial"), None, None)),
        check_vma=False,
    )
```

```python
import functools

import jax
import jax.numpy as jnp
from jax import lax
from jax.experimental import pallas as pl
from jax.experimental.pallas import tpu as pltpu
from jax.sharding import PartitionSpec as P

FOCUS_TOTAL = 8
FOCUS_SIZE = 32
MEAN_HIDDEN_SIZE = 32
C_TRI = 128


def layer_normalize(attended_entries):
    attended_entries = attended_entries.astype(jnp.float32)
    mean = jnp.mean(attended_entries, axis=-1, keepdims=True)
    centred = attended_entries - mean
    var = jnp.mean(centred * centred, axis=-1, keepdims=True)
    return centred * lax.rsqrt(var + 1e-05)


def gated_attend(evoformer_block, extra_axes, w_query, w_kvg, w_out):
    lines_list, residue_length, input_width = evoformer_block.shape
    width = FOCUS_TOTAL * FOCUS_SIZE
    flat = (
        layer_normalize(evoformer_block)
        .astype(jnp.bfloat16)
        .reshape(lines_list * residue_length, input_width)
    )
    query = (
        jnp.dot(flat, w_query, preferred_element_type=jnp.float32) * FOCUS_SIZE ** (-0.5)
    ).astype(jnp.bfloat16)
    query = query.reshape(lines_list, residue_length, FOCUS_TOTAL, FOCUS_SIZE)
    kvg = jnp.dot(flat, w_kvg, preferred_element_type=jnp.float32)
    keys = (
        kvg[:, :width]
        .astype(jnp.bfloat16)
        .reshape(lines_list, residue_length, FOCUS_TOTAL, FOCUS_SIZE)
    )
    attended_entries = (
        kvg[:, width : 2 * width]
        .astype(jnp.bfloat16)
        .reshape(lines_list, residue_length, FOCUS_TOTAL, FOCUS_SIZE)
    )
    gate = jax.nn.sigmoid(kvg[:, 2 * width :]).reshape(
        lines_list, residue_length, FOCUS_TOTAL, FOCUS_SIZE
    )
    scores = (
        jnp.einsum("bihd,bjhd->bhij", query, keys, preferred_element_type=jnp.float32) + extra_axes
    )
    top = jnp.max(scores, axis=-1, keepdims=True)
    expo = jnp.exp(scores - top)
    weights = (expo / jnp.sum(expo, axis=-1, keepdims=True)).astype(jnp.bfloat16)
    mixed = jnp.einsum(
        "bhij,bjhd->bihd", weights, attended_entries, preferred_element_type=jnp.float32
    )
    mixed = (mixed * gate).astype(jnp.bfloat16).reshape(lines_list * residue_length, width)
    return evoformer_block + jnp.dot(mixed, w_out, preferred_element_type=jnp.float32).reshape(
        lines_list, residue_length, input_width
    )


def finish_sums(evoformer_block, triangle_output_weight):
    mixed = layer_normalize(jnp.transpose(evoformer_block, (1, 2, 0))).astype(jnp.bfloat16)
    return jnp.einsum(
        "ijc,cz->ijz", mixed, triangle_output_weight, preferred_element_type=jnp.float32
    )


def local_sharded(
    homolog_activity,
    homolog_symbol_ids,
    residue_present_mask,
    pair_state,
    pair_valid_mask,
    symbol_lookup_matrix,
    row_query_weight,
    horizontal_attention_matrix,
    pair_bias_weight,
    horizontal_final_matrix,
    column_query_weight,
    vertical_attention_matrix,
    vertical_final_matrix,
    tensor_mean_lift_matrix,
    outer_product_output_weight,
    triangle_projection_weight,
    triangle_projection_gate,
    triangle_output_gate,
    triangle_output_weight,
):
    sequence_per_device, residue_length, input_width = homolog_activity.shape
    res_dev = pair_state.shape[0]
    group_size = lax.axis_size("axial")
    token_classes = symbol_lookup_matrix.shape[0]
    token_one_hot = (
        homolog_symbol_ids[..., None] == jnp.arange(token_classes, dtype=jnp.int32)
    ).astype(jnp.bfloat16)
    token_embedded = jnp.einsum(
        "slt,tc->slc", token_one_hot, symbol_lookup_matrix, preferred_element_type=jnp.float32
    )
    homolog_starting = homolog_activity.astype(jnp.float32) + token_embedded
    pair_norm = layer_normalize(pair_state).astype(jnp.bfloat16)
    bias_rows = jnp.einsum(
        "ijc,ch->hij", pair_norm, pair_bias_weight, preferred_element_type=jnp.float32
    ).astype(jnp.bfloat16)
    bias_full = lax.all_gather(bias_rows, "axial", axis=1, tiled=True)
    key_bias = 1000000000.0 * (residue_present_mask.astype(jnp.float32) - 1.0)
    extra_axes = bias_full.astype(jnp.float32)[None] + key_bias[None, None, None, :]
    cluster_total = homolog_starting.reshape(
        sequence_per_device // 2, 2, residue_length, input_width
    )
    homolog_across_update = lax.map(
        lambda evoformer_block: gated_attend(
            evoformer_block,
            extra_axes,
            row_query_weight,
            horizontal_attention_matrix,
            horizontal_final_matrix,
        ),
        cluster_total,
    )
    homolog_across_update = homolog_across_update.reshape(
        sequence_per_device, group_size, res_dev, input_width
    ).astype(jnp.bfloat16)
    moved = jnp.swapaxes(
        lax.all_to_all(homolog_across_update, "axial", split_axis=1, concat_axis=0, tiled=True)[
            :, 0
        ],
        0,
        1,
    )
    finished = lax.map(
        lambda item: gated_attend(
            item[None].astype(jnp.float32),
            0.0,
            column_query_weight,
            vertical_attention_matrix,
            vertical_final_matrix,
        )[0],
        moved,
    )
    exchanged = jnp.swapaxes(finished, 0, 1).astype(jnp.bfloat16)[:, None]
    sequence_count = exchanged.shape[0]
    alignment_after_columns = exchanged.reshape(sequence_count, res_dev, input_width)
    tensor_mean_scaler = layer_normalize(alignment_after_columns).astype(jnp.bfloat16)
    split_parts = jnp.einsum(
        "src,cf->rsf",
        tensor_mean_scaler,
        tensor_mean_lift_matrix,
        preferred_element_type=jnp.float32,
    ).astype(jnp.bfloat16)
    first_factor = split_parts[..., :MEAN_HIDDEN_SIZE]
    second_factor = split_parts[..., MEAN_HIDDEN_SIZE:].reshape(
        res_dev, sequence_count * MEAN_HIDDEN_SIZE
    )
    step_rows = 8
    left_blocks = first_factor.reshape(
        res_dev // step_rows, step_rows, sequence_count, MEAN_HIDDEN_SIZE
    )
    piece = lax.all_gather(second_factor, "axial", axis=0, tiled=True)
    count = piece.shape[0]
    right_part = piece.reshape(count, sequence_count, MEAN_HIDDEN_SIZE)

    def one_block(lines_list):
        tensor_mean = (
            jnp.einsum("isc,jsd->ijcd", lines_list, right_part, preferred_element_type=jnp.float32)
            / sequence_count
        )
        tensor_mean = tensor_mean.reshape(
            step_rows, count, MEAN_HIDDEN_SIZE * MEAN_HIDDEN_SIZE
        ).astype(jnp.bfloat16)
        return jnp.einsum(
            "ijf,fz->ijz",
            tensor_mean,
            outer_product_output_weight,
            preferred_element_type=jnp.float32,
        )

    update = lax.map(one_block, left_blocks).reshape(
        res_dev, count, outer_product_output_weight.shape[1]
    )
    pair_one = pair_state.astype(jnp.float32) + update
    tri_norm = layer_normalize(pair_one).astype(jnp.bfloat16)
    proj = jnp.einsum(
        "ikc,cf->fik", tri_norm, triangle_projection_weight, preferred_element_type=jnp.float32
    )
    gates = jnp.einsum(
        "ikc,cf->fik", tri_norm, triangle_projection_gate, preferred_element_type=jnp.float32
    )
    both = (jax.nn.sigmoid(gates) * proj * pair_valid_mask.astype(jnp.float32)[None]).astype(
        jnp.bfloat16
    )
    left_tri = both[:C_TRI]
    right_tri = both[C_TRI:]
    moved_left, moved_right = (
        lax.all_to_all(left_tri, "axial", split_axis=0, concat_axis=1, tiled=True),
        lax.all_to_all(right_tri, "axial", split_axis=0, concat_axis=1, tiled=True),
    )
    partial_sum = jnp.einsum(
        "cik,cjk->cij", moved_left, moved_right, preferred_element_type=jnp.float32
    )
    tri_sum = lax.all_to_all(
        partial_sum.astype(jnp.bfloat16), "axial", split_axis=1, concat_axis=0, tiled=True
    ).astype(partial_sum.dtype)
    tri_update = finish_sums(tri_sum, triangle_output_weight)
    out_gate = jax.nn.sigmoid(
        jnp.einsum(
            "ijc,cz->ijz", tri_norm, triangle_output_gate, preferred_element_type=jnp.float32
        )
    )
    pair_output = (pair_one + out_gate * tri_update).astype(jnp.bfloat16)
    return (alignment_after_columns, pair_output)


BF16 = jnp.bfloat16
F32 = jnp.float32
SMALL_ROWS = 16
FLOPS = 3 * 10**9
PACKET_ORDER = (2, 3, 1)
PAIR_ORDER = (3, 1, 2)


def mul(lhs, rhs, over=((1,), (0,))):
    return lax.dot_general(lhs, rhs, (over, ((), ())), preferred_element_type=F32)


def iota(shape, axis):
    return lax.broadcasted_iota(jnp.int32, shape, axis)


def zero_one(condition):
    return jnp.where(condition, 1.0, 0.0).astype(BF16)


def normal(x):
    mean = jnp.mean(x, axis=-1, keepdims=True)
    centred = x - mean
    var = jnp.mean(centred * centred, axis=-1, keepdims=True)
    return centred * lax.rsqrt(var + 1e-05)


def sigmoid(x):
    return 0.5 + 0.5 * jnp.tanh(0.5 * x)


def column_softmax(scores):
    expo = jnp.exp(scores - jnp.max(scores, axis=0, keepdims=True))
    return expo * (1.0 / jnp.sum(expo, axis=0, keepdims=True))


def bias_rows(pair_ref, weight_ref):
    rows, residues, width = pair_ref.shape
    lanes = FOCUS_TOTAL * rows
    spread = zero_one(iota((FOCUS_TOTAL, lanes), 1) // rows == iota((FOCUS_TOTAL, lanes), 0))
    row_of = iota((width, lanes), 1) % rows
    flat = normal(pair_ref[...].astype(F32).reshape(rows * residues, width)).astype(BF16)
    weight = mul(weight_ref[...], spread, ((0,), (0,)))
    bias = jnp.zeros((residues, lanes), F32)
    for i in range(rows):
        one_row = jnp.where(row_of == i, weight, 0.0).astype(BF16)
        bias += mul(flat[i * residues : (i + 1) * residues], one_row)
    return bias


def table_kernel(lanes, count, shift_ref, turn_ref, column_ref):
    shape = column_ref.shape
    column_ref[...] = zero_one(iota(shape, 1) // C_TRI == iota(shape, 0))
    shape = shift_ref.shape
    shift_ref[...] = zero_one(iota(shape, 1) == iota(shape, 0) + lanes)
    shape = turn_ref.shape
    row_at = iota(shape, 0)
    turn_ref[...] = zero_one(
        iota(shape, 1) == (row_at % count) * (shape[0] // count) + row_at // count
    )


def packet_kernel(*refs):
    pair_ref, weight_ref, valid_ref, ids_ref, act_ref, present_ref, shift_ref = refs[:7]
    packet_ref, hidden_ref = refs[7:]
    rows, residues, width = pair_ref.shape
    per, _, features = act_ref.shape
    lanes = FOCUS_TOTAL * rows
    bias = bias_rows(pair_ref, weight_ref)
    extra = jnp.concatenate(
        [
            valid_ref[...].astype(F32),
            ids_ref[...].astype(F32),
            jnp.zeros((SMALL_ROWS - rows - per, residues), F32),
        ],
        axis=0,
    )
    extra = mul(extra.astype(BF16), shift_ref[...])
    empty = jnp.zeros((SMALL_ROWS, 128 - lanes), F32)
    first = jnp.concatenate([bias[:SMALL_ROWS], empty], axis=1) + extra
    second = jnp.concatenate([bias[SMALL_ROWS:], empty], axis=1)
    small = jnp.concatenate([first, second], axis=1).astype(BF16)
    packet_ref[per * residues :, :] = small
    shown = present_ref[...].astype(F32).astype(BF16)
    shown = mul(shown, jnp.ones((1, hidden_ref.shape[1]), BF16), ((0,), (0,)))
    hidden_ref[...] = 1000000000.0 * (shown - 1.0)
    packet_ref[: per * residues, :] = act_ref[...].reshape(per * residues, features)


def split_small(packet, residues, res_dev, per):
    small = packet[per * residues :, :].astype(F32)
    lanes = FOCUS_TOTAL * res_dev
    bias = jnp.concatenate([small[:, :lanes], small[:, 128 : 128 + lanes]], axis=0)
    extra = small[:, lanes : lanes + residues]
    return bias, extra[:res_dev], extra[res_dev : res_dev + per]


def head_masks(width):
    return [
        zero_one(iota((1, width), 1) // FOCUS_SIZE == h) for h in range(FOCUS_TOTAL)
    ]


def project(x, w_query, w_kvg):
    width = FOCUS_TOTAL * FOCUS_SIZE
    flat = normal(x).astype(BF16)
    query = (mul(flat, w_query[...]) * FOCUS_SIZE ** (-0.5)).astype(BF16)
    keys = mul(flat, w_kvg[:, :width]).astype(BF16)
    values = mul(flat, w_kvg[:, width : 2 * width]).astype(BF16)
    gate = sigmoid(mul(flat, w_kvg[:, 2 * width :]))
    return query, keys, values, gate


def msa_kernel(n, res_dev, *refs):
    packets, turn, hidden_keys, table = refs[:n], refs[n], refs[n + 1], refs[n + 2]
    refs = refs[n + 3 :]
    row_q, row_kvg, row_out, col_q, col_kvg, col_out, lift, outer_w = refs[:8]
    align_ref, update_ref, lifted = refs[8:]
    kinds, width = table.shape
    residues, lanes = hidden_keys.shape
    pair_width = outer_w.shape[1]
    per = (packets[0].shape[0] - SMALL_ROWS) // residues
    count = per * n
    tokens = count * residues
    me = lax.axis_index("axial")

    place = iota((FOCUS_TOTAL * res_dev, lanes), 0)
    place = (place // res_dev) * residues + place % res_dev - iota(place.shape, 1)
    bias = jnp.zeros((residues, lanes), F32)
    rows = []
    for packet, r in zip(packets, (0, *PACKET_ORDER)):
        part, _, all_ids = split_small(packet, residues, res_dev, per)
        bias += mul(part.astype(BF16), zero_one(place == -(me ^ r) * res_dev))
        for q in range(per):
            hot = zero_one(iota((kinds, residues), 0).astype(F32) == all_ids[q : q + 1])
            act = packet[q * residues : (q + 1) * residues, :].astype(F32)
            rows.append(act + mul(hot, table[...], ((0,), (0,))))
    zero = jnp.concatenate(rows, axis=0)
    extra = bias + hidden_keys[...]
    masks = head_masks(width)

    query, keys, values, gate = project(zero, row_q, row_kvg)
    rows = []
    for s in range(count):
        here = slice(s * residues, (s + 1) * residues)
        spread = jnp.concatenate([query[here] * mask for mask in masks], axis=0)
        weights = column_softmax(mul(keys[here], spread, ((1,), (1,))) + extra).astype(BF16)
        heads = mul(weights, values[here], ((0,), (0,)))
        mixed = heads[:residues]
        for h in range(1, FOCUS_TOTAL):
            part = heads[h * residues : (h + 1) * residues]
            mixed = jnp.where(iota((1, width), 1) // FOCUS_SIZE == h, part, mixed)
        rows.append(mixed)
    mixed = (jnp.concatenate(rows, axis=0) * gate).astype(BF16)
    msa_one = (zero + mul(mixed, row_out[...])).astype(BF16)

    one = mul(turn[...], msa_one)
    query, keys, values, gate = project(one, col_q, col_kvg)
    group = min(tokens, 128)
    sites = group // count
    block_of = iota((1, group), 1) // count
    groups = []
    for g in range(tokens // group):
        here = slice(g * group, (g + 1) * group)
        all_weights, all_values = [], []
        for mask in masks:
            full = mul(keys[here], query[here] * mask, ((1,), (1,)))
            scores = full[:count]
            for b in range(1, sites):
                scores = jnp.where(block_of == b, full[b * count : (b + 1) * count], scores)
            weights = column_softmax(scores)
            weights = jnp.concatenate(
                [jnp.where(block_of == b, weights, 0.0) for b in range(sites)], axis=0
            )
            all_weights.append(weights.astype(BF16))
            all_values.append(values[here] * mask)
        groups.append(
            mul(
                jnp.concatenate(all_weights, axis=0),
                jnp.concatenate(all_values, axis=0),
                ((0,), (0,)),
            )
        )
    mixed = (jnp.concatenate(groups, axis=0) * gate).astype(BF16)
    align = (one + mul(mixed, col_out[...])).astype(BF16)
    own = count * res_dev
    row_at, lane_at = iota((own, tokens), 0), iota((own, tokens), 1)
    sequence = row_at // res_dev
    owner = (sequence // per) ^ me
    where_is = jnp.zeros_like(owner)
    for k, r in enumerate(PACKET_ORDER):
        where_is = jnp.where(owner == r, k + 1, where_is)
    pick = zero_one(
        lane_at
        == (row_at % res_dev + me * res_dev) * count + where_is * per + sequence % per
    )
    align_ref[...] = mul(pick, align).reshape(count, res_dev, width).astype(BF16)

    opm = normal(align.astype(F32)).astype(BF16)
    opm = mul(opm, lift[...], ((1,), (1,))).astype(BF16)
    hidden = MEAN_HIDDEN_SIZE
    right = opm[:, hidden:]
    for c in range(0, hidden, 2):
        pair_w = jnp.concatenate(
            [outer_w[(c + k) * hidden : (c + k + 1) * hidden, :] for k in range(2)], axis=1
        )
        part = mul(right, pair_w)
        lifted[c], lifted[c + 1] = part[:, :pair_width], part[:, pair_width:]
    deep = hidden * count
    spread = zero_one(
        iota((2 * hidden, deep), 1) // count == iota((2 * hidden, deep), 0)
    )
    left = mul(opm, spread)
    left = jnp.where(
        iota((tokens, deep), 0) % count == iota((tokens, deep), 1) % count, left, 0.0
    ).astype(BF16)
    gather = zero_one(iota((residues, tokens), 1) // count == iota((residues, tokens), 0))
    left = mul(gather, left).astype(BF16)
    for j in range(0, residues, 2):
        part = jnp.concatenate(
            [
                lifted[:, (j + k) * count : (j + k + 1) * count, :].reshape(deep, pair_width)
                for k in range(2)
            ],
            axis=1,
        )
        part = mul(left, part.astype(BF16)) * (1.0 / count)
        for k in range(2):
            at = slice((j + k) * residues, (j + k + 1) * residues)
            update_ref[at, :] = part[:, k * pair_width : (k + 1) * pair_width]


def pair_kernel(*refs):
    pairs, packets, update, column, pair, own_mask = refs[:3], refs[3:6], *refs[6:10]
    proj, gates, gate_out, w_out, out_ref, state, one, right_at, left_at, valid = refs[10:]
    res_dev, residues, width = pair.shape
    per = (packets[0].shape[0] - SMALL_ROWS) // residues
    me = lax.axis_index("axial")
    own_valid = own_mask[...].astype(F32)
    for packet, r in zip((None, *packets), (0, *PACKET_ORDER)):
        shown = split_small(packet, residues, res_dev, per)[1] if r else own_valid
        valid[pl.ds(pl.multiple_of((me ^ r) * res_dev, res_dev), res_dev), :] = shown
    own = jnp.concatenate(
        [
            pair[i].astype(F32) + update[pl.ds(me * res_dev + i, residues, stride=residues), :]
            for i in range(res_dev)
        ],
        axis=0,
    )
    left_w = jnp.concatenate([proj[:, :C_TRI], gates[:, :C_TRI], gate_out[...]], axis=1)
    own_all = mul(normal(own).astype(BF16), left_w)
    own_gate = sigmoid(own_all[:, 2 * C_TRI :])
    left = sigmoid(own_all[:, C_TRI : 2 * C_TRI]) * own_all[:, :C_TRI]
    shown = mul(own_valid.astype(BF16), column[:res_dev, : res_dev * C_TRI], ((0,), (0,)))
    for i in range(res_dev):
        part = left[i * residues : (i + 1) * residues] * shown[:, i * C_TRI : (i + 1) * C_TRI]
        left_at[i * residues : (i + 1) * residues, :] = part.astype(BF16).astype(F32)
    size = res_dev * residues
    for block, r in zip((pair, *pairs), (0, *PAIR_ORDER)):
        state[pl.ds(pl.multiple_of((me ^ r) * size, size), size), :] = (
            block[...].astype(F32).reshape(size, width)
        )
    for k in range(residues):
        one[k * residues : (k + 1) * residues, :] = (
            state[pl.ds(k, residues, stride=residues), :]
            + update[k * residues : (k + 1) * residues, :]
        )

    shown = mul(valid[...].astype(BF16), column[...])
    right_w = jnp.concatenate([proj[:, C_TRI:], gates[:, C_TRI:]], axis=1)
    step = 8
    for k in range(0, residues, step):
        here = slice(k * residues, (k + step) * residues)
        both = mul(normal(one[here, :]).astype(BF16), right_w)
        both = sigmoid(both[:, C_TRI:]) * both[:, :C_TRI]
        for p in range(step):
            part = both[p * residues : (p + 1) * residues]
            part = part * shown[:, (k + p) * C_TRI : (k + p + 1) * C_TRI]
            right_at[(k + p) * residues : (k + p + 1) * residues, :] = part.astype(BF16).astype(F32)

    sums = [jnp.zeros((residues, C_TRI), F32) for _ in range(res_dev)]
    for k in range(residues):
        other = right_at[k * residues : (k + 1) * residues, :]
        for i in range(res_dev):
            sums[i] += left_at[i * residues + k : i * residues + k + 1, :] * other
    mixed = normal(jnp.concatenate(sums, axis=0)).astype(BF16)
    result = own + own_gate * mul(mixed, w_out[...])
    out_ref[...] = result.reshape(res_dev, residues, width).astype(BF16)


def call(kernel, out_shape, scratch, vmem_mib, *args):
    vmem = pl.BlockSpec(memory_space=pltpu.VMEM)
    return pl.pallas_call(
        kernel,
        out_shape=out_shape,
        in_specs=[vmem] * len(args),
        out_specs=jax.tree.map(lambda _: vmem, out_shape),
        scratch_shapes=scratch,
        compiler_params=pltpu.CompilerParams(vmem_limit_bytes=vmem_mib * 1024 * 1024),
        cost_estimate=pl.CostEstimate(flops=FLOPS, bytes_accessed=0, transcendentals=0),
    )(*args)


def swap(array, r, n):
    return lax.ppermute(array, "axial", [(i, i ^ r) for i in range(n)])


def local_whole(
    homolog_activity,
    homolog_symbol_ids,
    residue_present_mask,
    pair_state,
    pair_valid_mask,
    symbol_lookup_matrix,
    row_query_weight,
    horizontal_attention_matrix,
    pair_bias_weight,
    horizontal_final_matrix,
    column_query_weight,
    vertical_attention_matrix,
    vertical_final_matrix,
    tensor_mean_lift_matrix,
    outer_product_output_weight,
    triangle_projection_weight,
    triangle_projection_gate,
    triangle_output_gate,
    triangle_output_weight,
):
    n = lax.axis_size("axial")
    per, residues, width = homolog_activity.shape
    res_dev, _, pair_width = pair_state.shape
    count = per * n
    shift, turn, column = call(
        functools.partial(table_kernel, FOCUS_TOTAL * res_dev, count),
        (
            jax.ShapeDtypeStruct((residues, 128), BF16),
            jax.ShapeDtypeStruct((count * residues, count * residues), BF16),
            jax.ShapeDtypeStruct((residues, residues * C_TRI), BF16),
        ),
        [],
        2,
    )
    packet, hidden_keys = call(
        packet_kernel,
        (
            jax.ShapeDtypeStruct((per * residues + SMALL_ROWS, width), BF16),
            jax.ShapeDtypeStruct((residues, FOCUS_TOTAL * residues), F32),
        ),
        [],
        4,
        pair_state,
        pair_bias_weight.T,
        pair_valid_mask,
        homolog_symbol_ids,
        homolog_activity,
        residue_present_mask.reshape(1, residues),
        shift,
    )
    packets = [swap(packet, r, n) for r in PACKET_ORDER]
    _, later = lax.optimization_barrier((packet, pair_state))
    pairs = [swap(later, r, n) for r in PAIR_ORDER]
    alignment, update = call(
        functools.partial(msa_kernel, n, res_dev),
        (
            jax.ShapeDtypeStruct((count, res_dev, width), BF16),
            jax.ShapeDtypeStruct((residues * residues, pair_width), F32),
        ),
        [
            pltpu.VMEM((MEAN_HIDDEN_SIZE, count * residues, pair_width), F32),
        ],
        16,
        packet,
        *packets,
        turn,
        hidden_keys,
        symbol_lookup_matrix,
        row_query_weight,
        horizontal_attention_matrix,
        horizontal_final_matrix,
        column_query_weight,
        vertical_attention_matrix,
        vertical_final_matrix,
        tensor_mean_lift_matrix.T,
        outer_product_output_weight,
    )
    pair_output = call(
        pair_kernel,
        jax.ShapeDtypeStruct((res_dev, residues, pair_width), BF16),
        [
            pltpu.VMEM((residues * residues, pair_width), F32),
            pltpu.VMEM((residues * residues, pair_width), F32),
            pltpu.VMEM((residues * residues, C_TRI), F32),
            pltpu.VMEM((res_dev * residues, C_TRI), F32),
            pltpu.VMEM((residues, residues), F32),
        ],
        16,
        *pairs,
        *packets,
        update,
        column,
        pair_state,
        pair_valid_mask,
        triangle_projection_weight,
        triangle_projection_gate,
        triangle_output_gate,
        triangle_output_weight,
    )
    return (alignment, pair_output)


def local(homolog_activity, homolog_symbol_ids, residue_present_mask, pair_state, *others):
    n = lax.axis_size("axial")
    per, residues, _ = homolog_activity.shape
    small = n == 4 and per * n == 8 and residues == 32
    plan = local_whole if small else local_sharded
    return plan(homolog_activity, homolog_symbol_ids, residue_present_mask, pair_state, *others)


def solution(mesh):
    parts, copied = P(("dp", "axial")), P()
    return jax.shard_map(
        local,
        mesh=mesh,
        in_specs=(parts, parts, P("dp"), parts, parts) + (copied,) * 14,
        out_specs=(P("dp", "axial", None), P(("dp", "axial"), None, None)),
        check_vma=False,
    )
```

```python
import functools

import jax
import jax.numpy as jnp
from jax import lax
from jax.experimental import pallas as pl
from jax.experimental.pallas import tpu as pltpu
from jax.sharding import PartitionSpec as P

FOCUS_TOTAL = 8
FOCUS_SIZE = 32
MEAN_HIDDEN_SIZE = 32
C_TRI = 128


def layer_normalize(attended_entries):
    attended_entries = attended_entries.astype(jnp.float32)
    mean = jnp.mean(attended_entries, axis=-1, keepdims=True)
    centred = attended_entries - mean
    var = jnp.mean(centred * centred, axis=-1, keepdims=True)
    return centred * lax.rsqrt(var + 1e-05)


def gated_attend(evoformer_block, extra_axes, w_query, w_kvg, w_out):
    lines_list, residue_length, input_width = evoformer_block.shape
    width = FOCUS_TOTAL * FOCUS_SIZE
    flat = (
        layer_normalize(evoformer_block)
        .astype(jnp.bfloat16)
        .reshape(lines_list * residue_length, input_width)
    )
    query = (
        jnp.dot(flat, w_query, preferred_element_type=jnp.float32) * FOCUS_SIZE ** (-0.5)
    ).astype(jnp.bfloat16)
    query = query.reshape(lines_list, residue_length, FOCUS_TOTAL, FOCUS_SIZE)
    kvg = jnp.dot(flat, w_kvg, preferred_element_type=jnp.float32)
    keys = (
        kvg[:, :width]
        .astype(jnp.bfloat16)
        .reshape(lines_list, residue_length, FOCUS_TOTAL, FOCUS_SIZE)
    )
    attended_entries = (
        kvg[:, width : 2 * width]
        .astype(jnp.bfloat16)
        .reshape(lines_list, residue_length, FOCUS_TOTAL, FOCUS_SIZE)
    )
    gate = jax.nn.sigmoid(kvg[:, 2 * width :]).reshape(
        lines_list, residue_length, FOCUS_TOTAL, FOCUS_SIZE
    )
    scores = (
        jnp.einsum("bihd,bjhd->bhij", query, keys, preferred_element_type=jnp.float32) + extra_axes
    )
    top = jnp.max(scores, axis=-1, keepdims=True)
    expo = jnp.exp(scores - top)
    weights = (expo / jnp.sum(expo, axis=-1, keepdims=True)).astype(jnp.bfloat16)
    mixed = jnp.einsum(
        "bhij,bjhd->bihd", weights, attended_entries, preferred_element_type=jnp.float32
    )
    mixed = (mixed * gate).astype(jnp.bfloat16).reshape(lines_list * residue_length, width)
    return evoformer_block + jnp.dot(mixed, w_out, preferred_element_type=jnp.float32).reshape(
        lines_list, residue_length, input_width
    )


def finish_sums(evoformer_block, triangle_output_weight):
    mixed = layer_normalize(jnp.transpose(evoformer_block, (1, 2, 0))).astype(jnp.bfloat16)
    return jnp.einsum(
        "ijc,cz->ijz", mixed, triangle_output_weight, preferred_element_type=jnp.float32
    )


def local_sharded(
    homolog_activity,
    homolog_symbol_ids,
    residue_present_mask,
    pair_state,
    pair_valid_mask,
    symbol_lookup_matrix,
    row_query_weight,
    horizontal_attention_matrix,
    pair_bias_weight,
    horizontal_final_matrix,
    column_query_weight,
    vertical_attention_matrix,
    vertical_final_matrix,
    tensor_mean_lift_matrix,
    outer_product_output_weight,
    triangle_projection_weight,
    triangle_projection_gate,
    triangle_output_gate,
    triangle_output_weight,
):
    sequence_per_device, residue_length, input_width = homolog_activity.shape
    res_dev = pair_state.shape[0]
    group_size = lax.axis_size("axial")
    token_classes = symbol_lookup_matrix.shape[0]
    token_one_hot = (
        homolog_symbol_ids[..., None] == jnp.arange(token_classes, dtype=jnp.int32)
    ).astype(jnp.bfloat16)
    token_embedded = jnp.einsum(
        "slt,tc->slc", token_one_hot, symbol_lookup_matrix, preferred_element_type=jnp.float32
    )
    homolog_starting = homolog_activity.astype(jnp.float32) + token_embedded
    pair_norm = layer_normalize(pair_state).astype(jnp.bfloat16)
    bias_rows = jnp.einsum(
        "ijc,ch->hij", pair_norm, pair_bias_weight, preferred_element_type=jnp.float32
    ).astype(jnp.bfloat16)
    bias_full = lax.all_gather(bias_rows, "axial", axis=1, tiled=True)
    key_bias = 1000000000.0 * (residue_present_mask.astype(jnp.float32) - 1.0)
    extra_axes = bias_full.astype(jnp.float32)[None] + key_bias[None, None, None, :]
    cluster_total = homolog_starting.reshape(
        sequence_per_device // 2, 2, residue_length, input_width
    )
    homolog_across_update = lax.map(
        lambda evoformer_block: gated_attend(
            evoformer_block,
            extra_axes,
            row_query_weight,
            horizontal_attention_matrix,
            horizontal_final_matrix,
        ),
        cluster_total,
    )
    homolog_across_update = homolog_across_update.reshape(
        sequence_per_device, group_size, res_dev, input_width
    ).astype(jnp.bfloat16)
    moved = jnp.swapaxes(
        lax.all_to_all(homolog_across_update, "axial", split_axis=1, concat_axis=0, tiled=True)[
            :, 0
        ],
        0,
        1,
    )
    finished = lax.map(
        lambda item: gated_attend(
            item[None].astype(jnp.float32),
            0.0,
            column_query_weight,
            vertical_attention_matrix,
            vertical_final_matrix,
        )[0],
        moved,
    )
    exchanged = jnp.swapaxes(finished, 0, 1).astype(jnp.bfloat16)[:, None]
    sequence_count = exchanged.shape[0]
    alignment_after_columns = exchanged.reshape(sequence_count, res_dev, input_width)
    tensor_mean_scaler = layer_normalize(alignment_after_columns).astype(jnp.bfloat16)
    split_parts = jnp.einsum(
        "src,cf->rsf",
        tensor_mean_scaler,
        tensor_mean_lift_matrix,
        preferred_element_type=jnp.float32,
    ).astype(jnp.bfloat16)
    first_factor = split_parts[..., :MEAN_HIDDEN_SIZE]
    second_factor = split_parts[..., MEAN_HIDDEN_SIZE:].reshape(
        res_dev, sequence_count * MEAN_HIDDEN_SIZE
    )
    step_rows = 8
    left_blocks = first_factor.reshape(
        res_dev // step_rows, step_rows, sequence_count, MEAN_HIDDEN_SIZE
    )
    piece = lax.all_gather(second_factor, "axial", axis=0, tiled=True)
    count = piece.shape[0]
    right_part = piece.reshape(count, sequence_count, MEAN_HIDDEN_SIZE)

    def one_block(lines_list):
        tensor_mean = (
            jnp.einsum("isc,jsd->ijcd", lines_list, right_part, preferred_element_type=jnp.float32)
            / sequence_count
        )
        tensor_mean = tensor_mean.reshape(
            step_rows, count, MEAN_HIDDEN_SIZE * MEAN_HIDDEN_SIZE
        ).astype(jnp.bfloat16)
        return jnp.einsum(
            "ijf,fz->ijz",
            tensor_mean,
            outer_product_output_weight,
            preferred_element_type=jnp.float32,
        )

    update = lax.map(one_block, left_blocks).reshape(
        res_dev, count, outer_product_output_weight.shape[1]
    )
    pair_one = pair_state.astype(jnp.float32) + update
    tri_norm = layer_normalize(pair_one).astype(jnp.bfloat16)
    proj = jnp.einsum(
        "ikc,cf->fik", tri_norm, triangle_projection_weight, preferred_element_type=jnp.float32
    )
    gates = jnp.einsum(
        "ikc,cf->fik", tri_norm, triangle_projection_gate, preferred_element_type=jnp.float32
    )
    both = (jax.nn.sigmoid(gates) * proj * pair_valid_mask.astype(jnp.float32)[None]).astype(
        jnp.bfloat16
    )
    left_tri = both[:C_TRI]
    right_tri = both[C_TRI:]
    moved_left, moved_right = (
        lax.all_to_all(left_tri, "axial", split_axis=0, concat_axis=1, tiled=True),
        lax.all_to_all(right_tri, "axial", split_axis=0, concat_axis=1, tiled=True),
    )
    partial_sum = jnp.einsum(
        "cik,cjk->cij", moved_left, moved_right, preferred_element_type=jnp.float32
    )
    tri_sum = lax.all_to_all(
        partial_sum.astype(jnp.bfloat16), "axial", split_axis=1, concat_axis=0, tiled=True
    ).astype(partial_sum.dtype)
    tri_update = finish_sums(tri_sum, triangle_output_weight)
    out_gate = jax.nn.sigmoid(
        jnp.einsum(
            "ijc,cz->ijz", tri_norm, triangle_output_gate, preferred_element_type=jnp.float32
        )
    )
    pair_output = (pair_one + out_gate * tri_update).astype(jnp.bfloat16)
    return (alignment_after_columns, pair_output)


BF16 = jnp.bfloat16
F32 = jnp.float32
SMALL_ROWS = 16
FLOPS = 3 * 10**9
PACKET_ORDER = (2, 1, 3)
PAIR_ORDER = (2, 3)


def mul(lhs, rhs, over=((1,), (0,))):
    return lax.dot_general(lhs, rhs, (over, ((), ())), preferred_element_type=F32)


def iota(shape, axis):
    return lax.broadcasted_iota(jnp.int32, shape, axis)


def zero_one(condition):
    return jnp.where(condition, 1.0, 0.0).astype(BF16)


def normal(x):
    mean = jnp.mean(x, axis=-1, keepdims=True)
    centred = x - mean
    var = jnp.mean(centred * centred, axis=-1, keepdims=True)
    return centred * lax.rsqrt(var + 1e-05)


def sigmoid(x):
    return 0.5 + 0.5 * jnp.tanh(0.5 * x)


def column_softmax(scores):
    expo = jnp.exp(scores - jnp.max(scores, axis=0, keepdims=True))
    return expo * (1.0 / jnp.sum(expo, axis=0, keepdims=True))


def bias_rows(pair_ref, weight_ref):
    rows, residues, width = pair_ref.shape
    lanes = FOCUS_TOTAL * rows
    spread = zero_one(iota((FOCUS_TOTAL, lanes), 1) // rows == iota((FOCUS_TOTAL, lanes), 0))
    row_of = iota((width, lanes), 1) % rows
    flat = normal(pair_ref[...].astype(F32).reshape(rows * residues, width)).astype(BF16)
    weight = mul(weight_ref[...], spread, ((0,), (0,)))
    bias = jnp.zeros((residues, lanes), F32)
    for i in range(rows):
        one_row = jnp.where(row_of == i, weight, 0.0).astype(BF16)
        bias += mul(flat[i * residues : (i + 1) * residues], one_row)
    return bias


def table_kernel(lanes, count, shift_ref, turn_ref, column_ref):
    shape = column_ref.shape
    column_ref[...] = zero_one(iota(shape, 1) // C_TRI == iota(shape, 0))
    shape = shift_ref.shape
    shift_ref[...] = zero_one(iota(shape, 1) == iota(shape, 0) + lanes)
    shape = turn_ref.shape
    row_at = iota(shape, 0)
    turn_ref[...] = zero_one(
        iota(shape, 1) == (row_at % count) * (shape[0] // count) + row_at // count
    )


def packet_kernel(*refs):
    pair_ref, weight_ref, valid_ref, ids_ref, act_ref, present_ref, shift_ref = refs[:7]
    packet_ref, hidden_ref, full_ref = refs[7:]
    rows, residues, width = pair_ref.shape
    per, _, features = act_ref.shape
    lanes = FOCUS_TOTAL * rows
    bias = bias_rows(pair_ref, weight_ref)
    extra = jnp.concatenate(
        [
            valid_ref[...].astype(F32),
            ids_ref[...].astype(F32),
            jnp.zeros((SMALL_ROWS - rows - per, residues), F32),
        ],
        axis=0,
    )
    extra = mul(extra.astype(BF16), shift_ref[...])
    empty = jnp.zeros((SMALL_ROWS, 128 - lanes), F32)
    first = jnp.concatenate([bias[:SMALL_ROWS], empty], axis=1) + extra
    second = jnp.concatenate([bias[SMALL_ROWS:], empty], axis=1)
    small = jnp.concatenate([first, second], axis=1).astype(BF16)
    top = per * residues
    packet_ref[top:, :] = small
    full_ref[top : top + SMALL_ROWS, :] = small
    full_ref[:top, :] = act_ref[...].reshape(top, features)
    for k in range(2):
        half = pair_ref[k * rows // 2 : (k + 1) * rows // 2].reshape(rows * residues // 2, width)
        full_ref[top + SMALL_ROWS :, k * width : (k + 1) * width] = half
    shown = present_ref[...].astype(F32).astype(BF16)
    shown = mul(shown, jnp.ones((1, hidden_ref.shape[1]), BF16), ((0,), (0,)))
    hidden_ref[...] = 1000000000.0 * (shown - 1.0)
    packet_ref[: per * residues, :] = act_ref[...].reshape(per * residues, features)


def split_small(packet, residues, res_dev, per):
    small = packet[per * residues : per * residues + SMALL_ROWS, :].astype(F32)
    lanes = FOCUS_TOTAL * res_dev
    bias = jnp.concatenate([small[:, :lanes], small[:, 128 : 128 + lanes]], axis=0)
    extra = small[:, lanes : lanes + residues]
    return bias, extra[:res_dev], extra[res_dev : res_dev + per]


def head_masks(width):
    return [
        zero_one(iota((1, width), 1) // FOCUS_SIZE == h) for h in range(FOCUS_TOTAL)
    ]


def project(x, w_query, w_kvg):
    width = FOCUS_TOTAL * FOCUS_SIZE
    flat = normal(x).astype(BF16)
    query = (mul(flat, w_query[...]) * FOCUS_SIZE ** (-0.5)).astype(BF16)
    keys = mul(flat, w_kvg[:, :width]).astype(BF16)
    values = mul(flat, w_kvg[:, width : 2 * width]).astype(BF16)
    gate = sigmoid(mul(flat, w_kvg[:, 2 * width :]))
    return query, keys, values, gate


def msa_kernel(n, res_dev, *refs):
    packets, turn, hidden_keys, table = refs[:n], refs[n], refs[n + 1], refs[n + 2]
    refs = refs[n + 3 :]
    row_q, row_kvg, row_out, col_q, col_kvg, col_out, lift, outer_w = refs[:8]
    align_ref, update_ref, lifted = refs[8:]
    kinds, width = table.shape
    residues, lanes = hidden_keys.shape
    pair_width = outer_w.shape[1]
    per = (packets[0].shape[0] - SMALL_ROWS) // residues
    count = per * n
    tokens = count * residues
    me = lax.axis_index("axial")

    place = iota((FOCUS_TOTAL * res_dev, lanes), 0)
    place = (place // res_dev) * residues + place % res_dev - iota(place.shape, 1)
    bias = jnp.zeros((residues, lanes), F32)
    rows = []
    for packet, r in zip(packets, (0, *PACKET_ORDER)):
        part, _, all_ids = split_small(packet, residues, res_dev, per)
        bias += mul(part.astype(BF16), zero_one(place == -(me ^ r) * res_dev))
        for q in range(per):
            hot = zero_one(iota((kinds, residues), 0).astype(F32) == all_ids[q : q + 1])
            act = packet[q * residues : (q + 1) * residues, :].astype(F32)
            rows.append(act + mul(hot, table[...], ((0,), (0,))))
    zero = jnp.concatenate(rows, axis=0)
    extra = bias + hidden_keys[...]
    masks = head_masks(width)

    query, keys, values, gate = project(zero, row_q, row_kvg)
    rows = []
    for s in range(count):
        here = slice(s * residues, (s + 1) * residues)
        spread = jnp.concatenate([query[here] * mask for mask in masks], axis=0)
        weights = column_softmax(mul(keys[here], spread, ((1,), (1,))) + extra).astype(BF16)
        heads = mul(weights, values[here], ((0,), (0,)))
        mixed = heads[:residues]
        for h in range(1, FOCUS_TOTAL):
            part = heads[h * residues : (h + 1) * residues]
            mixed = jnp.where(iota((1, width), 1) // FOCUS_SIZE == h, part, mixed)
        rows.append(mixed)
    mixed = (jnp.concatenate(rows, axis=0) * gate).astype(BF16)
    msa_one = (zero + mul(mixed, row_out[...])).astype(BF16)

    one = mul(turn[...], msa_one)
    query, keys, values, gate = project(one, col_q, col_kvg)
    group = min(tokens, 128)
    sites = group // count
    block_of = iota((1, group), 1) // count
    groups = []
    for g in range(tokens // group):
        here = slice(g * group, (g + 1) * group)
        all_weights, all_values = [], []
        for mask in masks:
            full = mul(keys[here], query[here] * mask, ((1,), (1,)))
            scores = full[:count]
            for b in range(1, sites):
                scores = jnp.where(block_of == b, full[b * count : (b + 1) * count], scores)
            weights = column_softmax(scores)
            weights = jnp.concatenate(
                [jnp.where(block_of == b, weights, 0.0) for b in range(sites)], axis=0
            )
            all_weights.append(weights.astype(BF16))
            all_values.append(values[here] * mask)
        groups.append(
            mul(
                jnp.concatenate(all_weights, axis=0),
                jnp.concatenate(all_values, axis=0),
                ((0,), (0,)),
            )
        )
    mixed = (jnp.concatenate(groups, axis=0) * gate).astype(BF16)
    align = (one + mul(mixed, col_out[...])).astype(BF16)
    own = count * res_dev
    row_at, lane_at = iota((own, tokens), 0), iota((own, tokens), 1)
    sequence = row_at // res_dev
    owner = (sequence // per) ^ me
    where_is = jnp.zeros_like(owner)
    for k, r in enumerate(PACKET_ORDER):
        where_is = jnp.where(owner == r, k + 1, where_is)
    pick = zero_one(
        lane_at
        == (row_at % res_dev + me * res_dev) * count + where_is * per + sequence % per
    )
    align_ref[...] = mul(pick, align).reshape(count, res_dev, width).astype(BF16)

    opm = normal(align.astype(F32)).astype(BF16)
    opm = mul(opm, lift[...], ((1,), (1,))).astype(BF16)
    hidden = MEAN_HIDDEN_SIZE
    deep = hidden * count
    spread = zero_one(
        iota((2 * hidden, deep), 1) // count == iota((2 * hidden, deep), 0)
    )
    left = mul(opm, spread)
    left = jnp.where(
        iota((tokens, deep), 0) % count == iota((tokens, deep), 1) % count, left, 0.0
    ).astype(BF16)
    gather = zero_one(iota((residues, tokens), 1) // count == iota((residues, tokens), 0))
    left = mul(gather, left).astype(BF16)
    right = opm[:, hidden:]
    for c in range(0, hidden, 2):
        pair_w = jnp.concatenate(
            [outer_w[(c + k) * hidden : (c + k + 1) * hidden, :] for k in range(2)], axis=1
        )
        part = mul(right, pair_w)
        lifted[c], lifted[c + 1] = part[:, :pair_width], part[:, pair_width:]
    for j in range(0, residues, 2):
        part = jnp.concatenate(
            [
                lifted[:, (j + k) * count : (j + k + 1) * count, :].reshape(deep, pair_width)
                for k in range(2)
            ],
            axis=1,
        )
        part = mul(left, part.astype(BF16)) * (1.0 / count)
        for k in range(2):
            at = slice((j + k) * residues, (j + k + 1) * residues)
            update_ref[at, :] = part[:, k * pair_width : (k + 1) * pair_width]


def pair_kernel(*refs):
    pairs, packets, update, column, pair, own_mask = refs[:2], refs[2:5], *refs[5:9]
    proj, gates, gate_out, w_out, out_ref, state, one, right_at, left_at, valid = refs[9:]
    res_dev, residues, width = pair.shape
    per = (packets[0].shape[0] - SMALL_ROWS) // residues
    me = lax.axis_index("axial")
    own_valid = own_mask[...].astype(F32)
    for packet, r in zip((None, *packets), (0, *PACKET_ORDER)):
        shown = split_small(packet, residues, res_dev, per)[1] if r else own_valid
        valid[pl.ds(pl.multiple_of((me ^ r) * res_dev, res_dev), res_dev), :] = shown
    own = jnp.concatenate(
        [
            pair[i].astype(F32) + update[pl.ds(me * res_dev + i, residues, stride=residues), :]
            for i in range(res_dev)
        ],
        axis=0,
    )
    left_w = jnp.concatenate([proj[:, :C_TRI], gates[:, :C_TRI], gate_out[...]], axis=1)
    own_all = mul(normal(own).astype(BF16), left_w)
    own_gate = sigmoid(own_all[:, 2 * C_TRI :])
    left = sigmoid(own_all[:, C_TRI : 2 * C_TRI]) * own_all[:, :C_TRI]
    shown = mul(own_valid.astype(BF16), column[:res_dev, : res_dev * C_TRI], ((0,), (0,)))
    for i in range(res_dev):
        part = left[i * residues : (i + 1) * residues] * shown[:, i * C_TRI : (i + 1) * C_TRI]
        left_at[i * residues : (i + 1) * residues, :] = part.astype(BF16).astype(F32)
    size = res_dev * residues
    beside = packets[PACKET_ORDER.index(1)][per * residues + SMALL_ROWS :, :]
    beside = jnp.concatenate([beside[:, :width], beside[:, width:]], axis=0)
    blocks = [pair[...].reshape(size, width), beside]
    blocks += [block[...].reshape(size, width) for block in pairs]
    for block, r in zip(blocks, (0, 1, *PAIR_ORDER)):
        state[pl.ds(pl.multiple_of((me ^ r) * size, size), size), :] = block.astype(F32)
    for k in range(residues):
        one[k * residues : (k + 1) * residues, :] = (
            state[pl.ds(k, residues, stride=residues), :]
            + update[k * residues : (k + 1) * residues, :]
        )

    shown = mul(valid[...].astype(BF16), column[...])
    right_w = jnp.concatenate([proj[:, C_TRI:], gates[:, C_TRI:]], axis=1)
    step = 8
    for k in range(0, residues, step):
        here = slice(k * residues, (k + step) * residues)
        both = mul(normal(one[here, :]).astype(BF16), right_w)
        both = sigmoid(both[:, C_TRI:]) * both[:, :C_TRI]
        for p in range(step):
            part = both[p * residues : (p + 1) * residues]
            part = part * shown[:, (k + p) * C_TRI : (k + p + 1) * C_TRI]
            right_at[(k + p) * residues : (k + p + 1) * residues, :] = part.astype(BF16).astype(F32)

    sums = [jnp.zeros((residues, C_TRI), F32) for _ in range(res_dev)]
    for k in range(residues):
        other = right_at[k * residues : (k + 1) * residues, :]
        for i in range(res_dev):
            sums[i] += left_at[i * residues + k : i * residues + k + 1, :] * other
    mixed = normal(jnp.concatenate(sums, axis=0)).astype(BF16)
    result = own + own_gate * mul(mixed, w_out[...])
    out_ref[...] = result.reshape(res_dev, residues, width).astype(BF16)


def call(kernel, out_shape, scratch, vmem_mib, *args):
    vmem = pl.BlockSpec(memory_space=pltpu.VMEM)
    return pl.pallas_call(
        kernel,
        out_shape=out_shape,
        in_specs=[vmem] * len(args),
        out_specs=jax.tree.map(lambda _: vmem, out_shape),
        scratch_shapes=scratch,
        compiler_params=pltpu.CompilerParams(vmem_limit_bytes=vmem_mib * 1024 * 1024),
        cost_estimate=pl.CostEstimate(flops=FLOPS, bytes_accessed=0, transcendentals=0),
    )(*args)


def swap(array, r, n):
    return lax.ppermute(array, "axial", [(i, i ^ r) for i in range(n)])


def local_whole(
    homolog_activity,
    homolog_symbol_ids,
    residue_present_mask,
    pair_state,
    pair_valid_mask,
    symbol_lookup_matrix,
    row_query_weight,
    horizontal_attention_matrix,
    pair_bias_weight,
    horizontal_final_matrix,
    column_query_weight,
    vertical_attention_matrix,
    vertical_final_matrix,
    tensor_mean_lift_matrix,
    outer_product_output_weight,
    triangle_projection_weight,
    triangle_projection_gate,
    triangle_output_gate,
    triangle_output_weight,
):
    n = lax.axis_size("axial")
    per, residues, width = homolog_activity.shape
    res_dev, _, pair_width = pair_state.shape
    count = per * n
    shift, turn, column = call(
        functools.partial(table_kernel, FOCUS_TOTAL * res_dev, count),
        (
            jax.ShapeDtypeStruct((residues, 128), BF16),
            jax.ShapeDtypeStruct((count * residues, count * residues), BF16),
            jax.ShapeDtypeStruct((residues, residues * C_TRI), BF16),
        ),
        [],
        2,
    )
    packet, hidden_keys, full = call(
        packet_kernel,
        (
            jax.ShapeDtypeStruct((per * residues + SMALL_ROWS, width), BF16),
            jax.ShapeDtypeStruct((residues, FOCUS_TOTAL * residues), F32),
            jax.ShapeDtypeStruct(
                (per * residues + SMALL_ROWS + res_dev * residues // 2, width), BF16
            ),
        ),
        [],
        4,
        pair_state,
        pair_bias_weight.T,
        pair_valid_mask,
        homolog_symbol_ids,
        homolog_activity,
        residue_present_mask.reshape(1, residues),
        shift,
    )
    packets = [swap(full if r == 1 else packet, r, n) for r in PACKET_ORDER]
    _, later = lax.optimization_barrier((packet, pair_state))
    pairs = [swap(later, r, n) for r in PAIR_ORDER]
    alignment, update = call(
        functools.partial(msa_kernel, n, res_dev),
        (
            jax.ShapeDtypeStruct((count, res_dev, width), BF16),
            jax.ShapeDtypeStruct((residues * residues, pair_width), F32),
        ),
        [
            pltpu.VMEM((MEAN_HIDDEN_SIZE, count * residues, pair_width), F32),
        ],
        16,
        packet,
        *packets,
        turn,
        hidden_keys,
        symbol_lookup_matrix,
        row_query_weight,
        horizontal_attention_matrix,
        horizontal_final_matrix,
        column_query_weight,
        vertical_attention_matrix,
        vertical_final_matrix,
        tensor_mean_lift_matrix.T,
        outer_product_output_weight,
    )
    pair_output = call(
        pair_kernel,
        jax.ShapeDtypeStruct((res_dev, residues, pair_width), BF16),
        [
            pltpu.VMEM((residues * residues, pair_width), F32),
            pltpu.VMEM((residues * residues, pair_width), F32),
            pltpu.VMEM((residues * residues, C_TRI), F32),
            pltpu.VMEM((res_dev * residues, C_TRI), F32),
            pltpu.VMEM((residues, residues), F32),
        ],
        16,
        *pairs,
        *packets,
        update,
        column,
        pair_state,
        pair_valid_mask,
        triangle_projection_weight,
        triangle_projection_gate,
        triangle_output_gate,
        triangle_output_weight,
    )
    return (alignment, pair_output)


def local(homolog_activity, homolog_symbol_ids, residue_present_mask, pair_state, *others):
    n = lax.axis_size("axial")
    per, residues, _ = homolog_activity.shape
    small = n == 4 and per * n == 8 and residues == 32
    plan = local_whole if small else local_sharded
    return plan(homolog_activity, homolog_symbol_ids, residue_present_mask, pair_state, *others)


def solution(mesh):
    parts, copied = P(("dp", "axial")), P()
    return jax.shard_map(
        local,
        mesh=mesh,
        in_specs=(parts, parts, P("dp"), parts, parts) + (copied,) * 14,
        out_specs=(P("dp", "axial", None), P(("dp", "axial"), None, None)),
        check_vma=False,
    )
```

```python
import functools

import jax
import jax.numpy as jnp
from jax import lax
from jax.experimental import pallas as pl
from jax.experimental.pallas import tpu as pltpu
from jax.sharding import PartitionSpec as P

FOCUS_TOTAL = 8
FOCUS_SIZE = 32
MEAN_HIDDEN_SIZE = 32
C_TRI = 128


def layer_normalize(attended_entries):
    attended_entries = attended_entries.astype(jnp.float32)
    mean = jnp.mean(attended_entries, axis=-1, keepdims=True)
    centred = attended_entries - mean
    var = jnp.mean(centred * centred, axis=-1, keepdims=True)
    return centred * lax.rsqrt(var + 1e-05)


def gated_attend(evoformer_block, extra_axes, w_query, w_kvg, w_out):
    lines_list, residue_length, input_width = evoformer_block.shape
    width = FOCUS_TOTAL * FOCUS_SIZE
    flat = (
        layer_normalize(evoformer_block)
        .astype(jnp.bfloat16)
        .reshape(lines_list * residue_length, input_width)
    )
    query = (
        jnp.dot(flat, w_query, preferred_element_type=jnp.float32) * FOCUS_SIZE ** (-0.5)
    ).astype(jnp.bfloat16)
    query = query.reshape(lines_list, residue_length, FOCUS_TOTAL, FOCUS_SIZE)
    kvg = jnp.dot(flat, w_kvg, preferred_element_type=jnp.float32)
    keys = (
        kvg[:, :width]
        .astype(jnp.bfloat16)
        .reshape(lines_list, residue_length, FOCUS_TOTAL, FOCUS_SIZE)
    )
    attended_entries = (
        kvg[:, width : 2 * width]
        .astype(jnp.bfloat16)
        .reshape(lines_list, residue_length, FOCUS_TOTAL, FOCUS_SIZE)
    )
    gate = jax.nn.sigmoid(kvg[:, 2 * width :]).reshape(
        lines_list, residue_length, FOCUS_TOTAL, FOCUS_SIZE
    )
    scores = (
        jnp.einsum("bihd,bjhd->bhij", query, keys, preferred_element_type=jnp.float32) + extra_axes
    )
    top = jnp.max(scores, axis=-1, keepdims=True)
    expo = jnp.exp(scores - top)
    weights = (expo / jnp.sum(expo, axis=-1, keepdims=True)).astype(jnp.bfloat16)
    mixed = jnp.einsum(
        "bhij,bjhd->bihd", weights, attended_entries, preferred_element_type=jnp.float32
    )
    mixed = (mixed * gate).astype(jnp.bfloat16).reshape(lines_list * residue_length, width)
    return evoformer_block + jnp.dot(mixed, w_out, preferred_element_type=jnp.float32).reshape(
        lines_list, residue_length, input_width
    )


def finish_sums(evoformer_block, triangle_output_weight):
    mixed = layer_normalize(jnp.transpose(evoformer_block, (1, 2, 0))).astype(jnp.bfloat16)
    return jnp.einsum(
        "ijc,cz->ijz", mixed, triangle_output_weight, preferred_element_type=jnp.float32
    )


def local_sharded(
    homolog_activity,
    homolog_symbol_ids,
    residue_present_mask,
    pair_state,
    pair_valid_mask,
    symbol_lookup_matrix,
    row_query_weight,
    horizontal_attention_matrix,
    pair_bias_weight,
    horizontal_final_matrix,
    column_query_weight,
    vertical_attention_matrix,
    vertical_final_matrix,
    tensor_mean_lift_matrix,
    outer_product_output_weight,
    triangle_projection_weight,
    triangle_projection_gate,
    triangle_output_gate,
    triangle_output_weight,
):
    sequence_per_device, residue_length, input_width = homolog_activity.shape
    res_dev = pair_state.shape[0]
    group_size = lax.axis_size("axial")
    token_classes = symbol_lookup_matrix.shape[0]
    token_one_hot = (
        homolog_symbol_ids[..., None] == jnp.arange(token_classes, dtype=jnp.int32)
    ).astype(jnp.bfloat16)
    token_embedded = jnp.einsum(
        "slt,tc->slc", token_one_hot, symbol_lookup_matrix, preferred_element_type=jnp.float32
    )
    homolog_starting = homolog_activity.astype(jnp.float32) + token_embedded
    pair_norm = layer_normalize(pair_state).astype(jnp.bfloat16)
    bias_rows = jnp.einsum(
        "ijc,ch->hij", pair_norm, pair_bias_weight, preferred_element_type=jnp.float32
    ).astype(jnp.bfloat16)
    bias_full = lax.all_gather(bias_rows, "axial", axis=1, tiled=True)
    key_bias = 1000000000.0 * (residue_present_mask.astype(jnp.float32) - 1.0)
    extra_axes = bias_full.astype(jnp.float32)[None] + key_bias[None, None, None, :]
    cluster_total = homolog_starting.reshape(
        sequence_per_device // 2, 2, residue_length, input_width
    )
    homolog_across_update = lax.map(
        lambda evoformer_block: gated_attend(
            evoformer_block,
            extra_axes,
            row_query_weight,
            horizontal_attention_matrix,
            horizontal_final_matrix,
        ),
        cluster_total,
    )
    homolog_across_update = homolog_across_update.reshape(
        sequence_per_device, group_size, res_dev, input_width
    ).astype(jnp.bfloat16)
    moved = jnp.swapaxes(
        lax.all_to_all(homolog_across_update, "axial", split_axis=1, concat_axis=0, tiled=True)[
            :, 0
        ],
        0,
        1,
    )
    finished = lax.map(
        lambda item: gated_attend(
            item[None].astype(jnp.float32),
            0.0,
            column_query_weight,
            vertical_attention_matrix,
            vertical_final_matrix,
        )[0],
        moved,
    )
    exchanged = jnp.swapaxes(finished, 0, 1).astype(jnp.bfloat16)[:, None]
    sequence_count = exchanged.shape[0]
    alignment_after_columns = exchanged.reshape(sequence_count, res_dev, input_width)
    tensor_mean_scaler = layer_normalize(alignment_after_columns).astype(jnp.bfloat16)
    split_parts = jnp.einsum(
        "src,cf->rsf",
        tensor_mean_scaler,
        tensor_mean_lift_matrix,
        preferred_element_type=jnp.float32,
    ).astype(jnp.bfloat16)
    first_factor = split_parts[..., :MEAN_HIDDEN_SIZE]
    second_factor = split_parts[..., MEAN_HIDDEN_SIZE:].reshape(
        res_dev, sequence_count * MEAN_HIDDEN_SIZE
    )
    step_rows = 8
    left_blocks = first_factor.reshape(
        res_dev // step_rows, step_rows, sequence_count, MEAN_HIDDEN_SIZE
    )
    piece = lax.all_gather(second_factor, "axial", axis=0, tiled=True)
    count = piece.shape[0]
    right_part = piece.reshape(count, sequence_count, MEAN_HIDDEN_SIZE)

    def one_block(lines_list):
        tensor_mean = (
            jnp.einsum("isc,jsd->ijcd", lines_list, right_part, preferred_element_type=jnp.float32)
            / sequence_count
        )
        tensor_mean = tensor_mean.reshape(
            step_rows, count, MEAN_HIDDEN_SIZE * MEAN_HIDDEN_SIZE
        ).astype(jnp.bfloat16)
        return jnp.einsum(
            "ijf,fz->ijz",
            tensor_mean,
            outer_product_output_weight,
            preferred_element_type=jnp.float32,
        )

    update = lax.map(one_block, left_blocks).reshape(
        res_dev, count, outer_product_output_weight.shape[1]
    )
    pair_one = pair_state.astype(jnp.float32) + update
    tri_norm = layer_normalize(pair_one).astype(jnp.bfloat16)
    proj = jnp.einsum(
        "ikc,cf->fik", tri_norm, triangle_projection_weight, preferred_element_type=jnp.float32
    )
    gates = jnp.einsum(
        "ikc,cf->fik", tri_norm, triangle_projection_gate, preferred_element_type=jnp.float32
    )
    both = (jax.nn.sigmoid(gates) * proj * pair_valid_mask.astype(jnp.float32)[None]).astype(
        jnp.bfloat16
    )
    left_tri = both[:C_TRI]
    right_tri = both[C_TRI:]
    moved_left, moved_right = (
        lax.all_to_all(left_tri, "axial", split_axis=0, concat_axis=1, tiled=True),
        lax.all_to_all(right_tri, "axial", split_axis=0, concat_axis=1, tiled=True),
    )
    partial_sum = jnp.einsum(
        "cik,cjk->cij", moved_left, moved_right, preferred_element_type=jnp.float32
    )
    tri_sum = lax.all_to_all(
        partial_sum.astype(jnp.bfloat16), "axial", split_axis=1, concat_axis=0, tiled=True
    ).astype(partial_sum.dtype)
    tri_update = finish_sums(tri_sum, triangle_output_weight)
    out_gate = jax.nn.sigmoid(
        jnp.einsum(
            "ijc,cz->ijz", tri_norm, triangle_output_gate, preferred_element_type=jnp.float32
        )
    )
    pair_output = (pair_one + out_gate * tri_update).astype(jnp.bfloat16)
    return (alignment_after_columns, pair_output)


BF16 = jnp.bfloat16
F32 = jnp.float32
SMALL_ROWS = 16
FLOPS = 3 * 10**9
PACKET_ORDER = (2, 3, 1)
PAIR_ORDER = (3, 1, 2)


def mul(lhs, rhs, over=((1,), (0,))):
    return lax.dot_general(lhs, rhs, (over, ((), ())), preferred_element_type=F32)


def iota(shape, axis):
    return lax.broadcasted_iota(jnp.int32, shape, axis)


def zero_one(condition):
    return jnp.where(condition, 1.0, 0.0).astype(BF16)


def normal(x):
    mean = jnp.mean(x, axis=-1, keepdims=True)
    centred = x - mean
    var = jnp.mean(centred * centred, axis=-1, keepdims=True)
    return centred * lax.rsqrt(var + 1e-05)


def sigmoid(x):
    return 0.5 + 0.5 * jnp.tanh(0.5 * x)


def column_softmax(scores):
    expo = jnp.exp(scores - jnp.max(scores, axis=0, keepdims=True))
    return expo * (1.0 / jnp.sum(expo, axis=0, keepdims=True))


def bias_rows(pair_ref, weight_ref):
    rows, residues, width = pair_ref.shape
    lanes = FOCUS_TOTAL * rows
    spread = zero_one(iota((FOCUS_TOTAL, lanes), 1) // rows == iota((FOCUS_TOTAL, lanes), 0))
    row_of = iota((width, lanes), 1) % rows
    flat = normal(pair_ref[...].astype(F32).reshape(rows * residues, width)).astype(BF16)
    weight = mul(weight_ref[...], spread, ((0,), (0,)))
    side_by_side = [flat[i * residues : (i + 1) * residues] for i in range(rows)]
    one_row = [jnp.where(row_of == i, weight, 0.0).astype(BF16) for i in range(rows)]
    bias = mul(jnp.concatenate(side_by_side, axis=1), jnp.concatenate(one_row, axis=0))
    return bias


def table_kernel(lanes, count, shift_ref, turn_ref, column_ref):
    shape = column_ref.shape
    column_ref[...] = zero_one(iota(shape, 1) // C_TRI == iota(shape, 0))
    shape = shift_ref.shape
    shift_ref[...] = zero_one(iota(shape, 1) == iota(shape, 0) + lanes)
    shape = turn_ref.shape
    row_at = iota(shape, 0)
    turn_ref[...] = zero_one(
        iota(shape, 1) == (row_at % count) * (shape[0] // count) + row_at // count
    )


def packet_kernel(*refs):
    pair_ref, weight_ref, valid_ref, ids_ref, act_ref, present_ref, shift_ref = refs[:7]
    packet_ref, hidden_ref = refs[7:]
    rows, residues, width = pair_ref.shape
    per, _, features = act_ref.shape
    lanes = FOCUS_TOTAL * rows
    bias = bias_rows(pair_ref, weight_ref)
    extra = jnp.concatenate(
        [
            valid_ref[...].astype(F32),
            ids_ref[...].astype(F32),
            jnp.zeros((SMALL_ROWS - rows - per, residues), F32),
        ],
        axis=0,
    )
    extra = mul(extra.astype(BF16), shift_ref[...])
    empty = jnp.zeros((SMALL_ROWS, 128 - lanes), F32)
    first = jnp.concatenate([bias[:SMALL_ROWS], empty], axis=1) + extra
    second = jnp.concatenate([bias[SMALL_ROWS:], empty], axis=1)
    small = jnp.concatenate([first, second], axis=1).astype(BF16)
    packet_ref[per * residues :, :] = small
    shown = present_ref[...].astype(F32).astype(BF16)
    shown = mul(shown, jnp.ones((1, hidden_ref.shape[1]), BF16), ((0,), (0,)))
    hidden_ref[...] = 1000000000.0 * (shown - 1.0)
    packet_ref[: per * residues, :] = act_ref[...].reshape(per * residues, features)


def split_small(packet, residues, res_dev, per):
    small = packet[per * residues :, :].astype(F32)
    lanes = FOCUS_TOTAL * res_dev
    bias = jnp.concatenate([small[:, :lanes], small[:, 128 : 128 + lanes]], axis=0)
    extra = small[:, lanes : lanes + residues]
    return bias, extra[:res_dev], extra[res_dev : res_dev + per]


def head_masks(width):
    return [
        zero_one(iota((1, width), 1) // FOCUS_SIZE == h) for h in range(FOCUS_TOTAL)
    ]


def project(x, w_query, w_kvg):
    width = FOCUS_TOTAL * FOCUS_SIZE
    flat = normal(x).astype(BF16)
    query = (mul(flat, w_query[...]) * FOCUS_SIZE ** (-0.5)).astype(BF16)
    keys = mul(flat, w_kvg[:, :width]).astype(BF16)
    values = mul(flat, w_kvg[:, width : 2 * width]).astype(BF16)
    gate = sigmoid(mul(flat, w_kvg[:, 2 * width :]))
    return query, keys, values, gate


def msa_kernel(n, res_dev, *refs):
    packets, turn, hidden_keys, table = refs[:n], refs[n], refs[n + 1], refs[n + 2]
    refs = refs[n + 3 :]
    row_q, row_kvg, row_out, col_q, col_kvg, col_out, lift, outer_w = refs[:8]
    align_ref, update_ref, lifted = refs[8:]
    kinds, width = table.shape
    residues, lanes = hidden_keys.shape
    pair_width = outer_w.shape[1]
    per = (packets[0].shape[0] - SMALL_ROWS) // residues
    count = per * n
    tokens = count * residues
    me = lax.axis_index("axial")

    place = iota((FOCUS_TOTAL * res_dev, lanes), 0)
    place = (place // res_dev) * residues + place % res_dev - iota(place.shape, 1)
    bias = jnp.zeros((residues, lanes), F32)
    rows = []
    for packet, r in zip(packets, (0, *PACKET_ORDER)):
        part, _, all_ids = split_small(packet, residues, res_dev, per)
        bias += mul(part.astype(BF16), zero_one(place == -(me ^ r) * res_dev))
        for q in range(per):
            hot = zero_one(iota((kinds, residues), 0).astype(F32) == all_ids[q : q + 1])
            act = packet[q * residues : (q + 1) * residues, :].astype(F32)
            rows.append(act + mul(hot, table[...], ((0,), (0,))))
    zero = jnp.concatenate(rows, axis=0)
    extra = bias + hidden_keys[...]
    masks = head_masks(width)

    query, keys, values, gate = project(zero, row_q, row_kvg)
    rows = []
    for s in range(count):
        here = slice(s * residues, (s + 1) * residues)
        spread = jnp.concatenate([query[here] * mask for mask in masks], axis=0)
        weights = column_softmax(mul(keys[here], spread, ((1,), (1,))) + extra).astype(BF16)
        heads = mul(weights, values[here], ((0,), (0,)))
        mixed = heads[:residues]
        for h in range(1, FOCUS_TOTAL):
            part = heads[h * residues : (h + 1) * residues]
            mixed = jnp.where(iota((1, width), 1) // FOCUS_SIZE == h, part, mixed)
        rows.append(mixed)
    mixed = (jnp.concatenate(rows, axis=0) * gate).astype(BF16)
    msa_one = (zero + mul(mixed, row_out[...])).astype(BF16)

    one = mul(turn[...], msa_one)
    query, keys, values, gate = project(one, col_q, col_kvg)
    group = min(tokens, 128)
    sites = group // count
    block_of = iota((1, group), 1) // count
    groups = []
    for g in range(tokens // group):
        here = slice(g * group, (g + 1) * group)
        all_weights, all_values = [], []
        for mask in masks:
            full = mul(keys[here], query[here] * mask, ((1,), (1,)))
            scores = full[:count]
            for b in range(1, sites):
                scores = jnp.where(block_of == b, full[b * count : (b + 1) * count], scores)
            weights = column_softmax(scores)
            weights = jnp.concatenate(
                [jnp.where(block_of == b, weights, 0.0) for b in range(sites)], axis=0
            )
            all_weights.append(weights.astype(BF16))
            all_values.append(values[here] * mask)
        groups.append(
            mul(
                jnp.concatenate(all_weights, axis=0),
                jnp.concatenate(all_values, axis=0),
                ((0,), (0,)),
            )
        )
    mixed = (jnp.concatenate(groups, axis=0) * gate).astype(BF16)
    align = (one + mul(mixed, col_out[...])).astype(BF16)
    own = count * res_dev
    row_at, lane_at = iota((own, tokens), 0), iota((own, tokens), 1)
    sequence = row_at // res_dev
    owner = (sequence // per) ^ me
    where_is = jnp.zeros_like(owner)
    for k, r in enumerate(PACKET_ORDER):
        where_is = jnp.where(owner == r, k + 1, where_is)
    pick = zero_one(
        lane_at
        == (row_at % res_dev + me * res_dev) * count + where_is * per + sequence % per
    )
    align_ref[...] = mul(pick, align).reshape(count, res_dev, width).astype(BF16)

    opm = normal(align.astype(F32)).astype(BF16)
    opm = mul(opm, lift[...], ((1,), (1,))).astype(BF16)
    hidden = MEAN_HIDDEN_SIZE
    deep = hidden * count
    spread = zero_one(
        iota((2 * hidden, deep), 1) // count == iota((2 * hidden, deep), 0)
    )
    left = mul(opm, spread)
    left = jnp.where(
        iota((tokens, deep), 0) % count == iota((tokens, deep), 1) % count, left, 0.0
    ).astype(BF16)
    gather = zero_one(iota((residues, tokens), 1) // count == iota((residues, tokens), 0))
    left = mul(gather, left).astype(BF16)
    right = opm[:, hidden:]
    for c in range(0, hidden, 2):
        pair_w = jnp.concatenate(
            [outer_w[(c + k) * hidden : (c + k + 1) * hidden, :] for k in range(2)], axis=1
        )
        part = mul(right, pair_w)
        lifted[c], lifted[c + 1] = part[:, :pair_width], part[:, pair_width:]
    for j in range(0, residues, 2):
        part = jnp.concatenate(
            [
                lifted[:, (j + k) * count : (j + k + 1) * count, :].reshape(deep, pair_width)
                for k in range(2)
            ],
            axis=1,
        )
        part = mul(left, part.astype(BF16)) * (1.0 / count)
        for k in range(2):
            at = slice((j + k) * residues, (j + k + 1) * residues)
            update_ref[at, :] = part[:, k * pair_width : (k + 1) * pair_width]


def pair_kernel(*refs):
    pairs, packets, update, column, pair, own_mask = refs[:3], refs[3:6], *refs[6:10]
    proj, gates, gate_out, w_out, out_ref, state, one, right_at, left_at, valid = refs[10:]
    res_dev, residues, width = pair.shape
    per = (packets[0].shape[0] - SMALL_ROWS) // residues
    me = lax.axis_index("axial")
    own_valid = own_mask[...].astype(F32)
    for packet, r in zip((None, *packets), (0, *PACKET_ORDER)):
        shown = split_small(packet, residues, res_dev, per)[1] if r else own_valid
        valid[pl.ds(pl.multiple_of((me ^ r) * res_dev, res_dev), res_dev), :] = shown
    own = jnp.concatenate(
        [
            pair[i].astype(F32) + update[pl.ds(me * res_dev + i, residues, stride=residues), :]
            for i in range(res_dev)
        ],
        axis=0,
    )
    left_w = jnp.concatenate([proj[:, :C_TRI], gates[:, :C_TRI], gate_out[...]], axis=1)
    own_all = mul(normal(own).astype(BF16), left_w)
    own_gate = sigmoid(own_all[:, 2 * C_TRI :])
    left = sigmoid(own_all[:, C_TRI : 2 * C_TRI]) * own_all[:, :C_TRI]
    shown = mul(own_valid.astype(BF16), column[:res_dev, : res_dev * C_TRI], ((0,), (0,)))
    for i in range(res_dev):
        part = left[i * residues : (i + 1) * residues] * shown[:, i * C_TRI : (i + 1) * C_TRI]
        left_at[i * residues : (i + 1) * residues, :] = part.astype(BF16).astype(F32)
    size = res_dev * residues
    for block, r in zip((pair, *pairs), (0, *PAIR_ORDER)):
        state[pl.ds(pl.multiple_of((me ^ r) * size, size), size), :] = (
            block[...].astype(F32).reshape(size, width)
        )
    for k in range(residues):
        one[k * residues : (k + 1) * residues, :] = (
            state[pl.ds(k, residues, stride=residues), :]
            + update[k * residues : (k + 1) * residues, :]
        )

    shown = mul(valid[...].astype(BF16), column[...])
    right_w = jnp.concatenate([proj[:, C_TRI:], gates[:, C_TRI:]], axis=1)
    step = 8
    for k in range(0, residues, step):
        here = slice(k * residues, (k + step) * residues)
        both = mul(normal(one[here, :]).astype(BF16), right_w)
        both = sigmoid(both[:, C_TRI:]) * both[:, :C_TRI]
        for p in range(step):
            part = both[p * residues : (p + 1) * residues]
            part = part * shown[:, (k + p) * C_TRI : (k + p + 1) * C_TRI]
            right_at[(k + p) * residues : (k + p + 1) * residues, :] = part.astype(BF16).astype(F32)

    sums = [jnp.zeros((residues, C_TRI), F32) for _ in range(res_dev)]
    for k in range(residues):
        other = right_at[k * residues : (k + 1) * residues, :]
        for i in range(res_dev):
            sums[i] += left_at[i * residues + k : i * residues + k + 1, :] * other
    mixed = normal(jnp.concatenate(sums, axis=0)).astype(BF16)
    result = own + own_gate * mul(mixed, w_out[...])
    out_ref[...] = result.reshape(res_dev, residues, width).astype(BF16)


def call(kernel, out_shape, scratch, vmem_mib, *args):
    vmem = pl.BlockSpec(memory_space=pltpu.VMEM)
    return pl.pallas_call(
        kernel,
        out_shape=out_shape,
        in_specs=[vmem] * len(args),
        out_specs=jax.tree.map(lambda _: vmem, out_shape),
        scratch_shapes=scratch,
        compiler_params=pltpu.CompilerParams(vmem_limit_bytes=vmem_mib * 1024 * 1024),
        cost_estimate=pl.CostEstimate(flops=FLOPS, bytes_accessed=0, transcendentals=0),
    )(*args)


def swap(array, r, n):
    return lax.ppermute(array, "axial", [(i, i ^ r) for i in range(n)])


def local_whole(
    homolog_activity,
    homolog_symbol_ids,
    residue_present_mask,
    pair_state,
    pair_valid_mask,
    symbol_lookup_matrix,
    row_query_weight,
    horizontal_attention_matrix,
    pair_bias_weight,
    horizontal_final_matrix,
    column_query_weight,
    vertical_attention_matrix,
    vertical_final_matrix,
    tensor_mean_lift_matrix,
    outer_product_output_weight,
    triangle_projection_weight,
    triangle_projection_gate,
    triangle_output_gate,
    triangle_output_weight,
):
    n = lax.axis_size("axial")
    per, residues, width = homolog_activity.shape
    res_dev, _, pair_width = pair_state.shape
    count = per * n
    shift, turn, column = call(
        functools.partial(table_kernel, FOCUS_TOTAL * res_dev, count),
        (
            jax.ShapeDtypeStruct((residues, 128), BF16),
            jax.ShapeDtypeStruct((count * residues, count * residues), BF16),
            jax.ShapeDtypeStruct((residues, residues * C_TRI), BF16),
        ),
        [],
        2,
    )
    packet, hidden_keys = call(
        packet_kernel,
        (
            jax.ShapeDtypeStruct((per * residues + SMALL_ROWS, width), BF16),
            jax.ShapeDtypeStruct((residues, FOCUS_TOTAL * residues), F32),
        ),
        [],
        4,
        pair_state,
        pair_bias_weight.T,
        pair_valid_mask,
        homolog_symbol_ids,
        homolog_activity,
        residue_present_mask.reshape(1, residues),
        shift,
    )
    packets = [swap(packet, r, n) for r in PACKET_ORDER]
    _, later = lax.optimization_barrier((packet, pair_state))
    pairs = [swap(later, r, n) for r in PAIR_ORDER]
    alignment, update = call(
        functools.partial(msa_kernel, n, res_dev),
        (
            jax.ShapeDtypeStruct((count, res_dev, width), BF16),
            jax.ShapeDtypeStruct((residues * residues, pair_width), F32),
        ),
        [
            pltpu.VMEM((MEAN_HIDDEN_SIZE, count * residues, pair_width), F32),
        ],
        16,
        packet,
        *packets,
        turn,
        hidden_keys,
        symbol_lookup_matrix,
        row_query_weight,
        horizontal_attention_matrix,
        horizontal_final_matrix,
        column_query_weight,
        vertical_attention_matrix,
        vertical_final_matrix,
        tensor_mean_lift_matrix.T,
        outer_product_output_weight,
    )
    pair_output = call(
        pair_kernel,
        jax.ShapeDtypeStruct((res_dev, residues, pair_width), BF16),
        [
            pltpu.VMEM((residues * residues, pair_width), F32),
            pltpu.VMEM((residues * residues, pair_width), F32),
            pltpu.VMEM((residues * residues, C_TRI), F32),
            pltpu.VMEM((res_dev * residues, C_TRI), F32),
            pltpu.VMEM((residues, residues), F32),
        ],
        16,
        *pairs,
        *packets,
        update,
        column,
        pair_state,
        pair_valid_mask,
        triangle_projection_weight,
        triangle_projection_gate,
        triangle_output_gate,
        triangle_output_weight,
    )
    return (alignment, pair_output)


def local(homolog_activity, homolog_symbol_ids, residue_present_mask, pair_state, *others):
    n = lax.axis_size("axial")
    per, residues, _ = homolog_activity.shape
    small = n == 4 and per * n == 8 and residues == 32
    plan = local_whole if small else local_sharded
    return plan(homolog_activity, homolog_symbol_ids, residue_present_mask, pair_state, *others)


def solution(mesh):
    parts, copied = P(("dp", "axial")), P()
    return jax.shard_map(
        local,
        mesh=mesh,
        in_specs=(parts, parts, P("dp"), parts, parts) + (copied,) * 14,
        out_specs=(P("dp", "axial", None), P(("dp", "axial"), None, None)),
        check_vma=False,
    )
```

```python
import functools

import jax
import jax.numpy as jnp
from jax import lax
from jax.experimental import pallas as pl
from jax.experimental.pallas import tpu as pltpu
from jax.sharding import PartitionSpec as P

FOCUS_TOTAL = 8
FOCUS_SIZE = 32
MEAN_HIDDEN_SIZE = 32
C_TRI = 128


def layer_normalize(attended_entries):
    attended_entries = attended_entries.astype(jnp.float32)
    mean = jnp.mean(attended_entries, axis=-1, keepdims=True)
    centred = attended_entries - mean
    var = jnp.mean(centred * centred, axis=-1, keepdims=True)
    return centred * lax.rsqrt(var + 1e-05)


def gated_attend(evoformer_block, extra_axes, w_query, w_kvg, w_out):
    lines_list, residue_length, input_width = evoformer_block.shape
    width = FOCUS_TOTAL * FOCUS_SIZE
    flat = (
        layer_normalize(evoformer_block)
        .astype(jnp.bfloat16)
        .reshape(lines_list * residue_length, input_width)
    )
    query = (
        jnp.dot(flat, w_query, preferred_element_type=jnp.float32) * FOCUS_SIZE ** (-0.5)
    ).astype(jnp.bfloat16)
    query = query.reshape(lines_list, residue_length, FOCUS_TOTAL, FOCUS_SIZE)
    kvg = jnp.dot(flat, w_kvg, preferred_element_type=jnp.float32)
    keys = (
        kvg[:, :width]
        .astype(jnp.bfloat16)
        .reshape(lines_list, residue_length, FOCUS_TOTAL, FOCUS_SIZE)
    )
    attended_entries = (
        kvg[:, width : 2 * width]
        .astype(jnp.bfloat16)
        .reshape(lines_list, residue_length, FOCUS_TOTAL, FOCUS_SIZE)
    )
    gate = jax.nn.sigmoid(kvg[:, 2 * width :]).reshape(
        lines_list, residue_length, FOCUS_TOTAL, FOCUS_SIZE
    )
    scores = (
        jnp.einsum("bihd,bjhd->bhij", query, keys, preferred_element_type=jnp.float32) + extra_axes
    )
    top = jnp.max(scores, axis=-1, keepdims=True)
    expo = jnp.exp(scores - top)
    weights = (expo / jnp.sum(expo, axis=-1, keepdims=True)).astype(jnp.bfloat16)
    mixed = jnp.einsum(
        "bhij,bjhd->bihd", weights, attended_entries, preferred_element_type=jnp.float32
    )
    mixed = (mixed * gate).astype(jnp.bfloat16).reshape(lines_list * residue_length, width)
    return evoformer_block + jnp.dot(mixed, w_out, preferred_element_type=jnp.float32).reshape(
        lines_list, residue_length, input_width
    )


def finish_sums(evoformer_block, triangle_output_weight):
    mixed = layer_normalize(jnp.transpose(evoformer_block, (1, 2, 0))).astype(jnp.bfloat16)
    return jnp.einsum(
        "ijc,cz->ijz", mixed, triangle_output_weight, preferred_element_type=jnp.float32
    )


def local_sharded(
    homolog_activity,
    homolog_symbol_ids,
    residue_present_mask,
    pair_state,
    pair_valid_mask,
    symbol_lookup_matrix,
    row_query_weight,
    horizontal_attention_matrix,
    pair_bias_weight,
    horizontal_final_matrix,
    column_query_weight,
    vertical_attention_matrix,
    vertical_final_matrix,
    tensor_mean_lift_matrix,
    outer_product_output_weight,
    triangle_projection_weight,
    triangle_projection_gate,
    triangle_output_gate,
    triangle_output_weight,
):
    sequence_per_device, residue_length, input_width = homolog_activity.shape
    res_dev = pair_state.shape[0]
    group_size = lax.axis_size("axial")
    token_classes = symbol_lookup_matrix.shape[0]
    token_one_hot = (
        homolog_symbol_ids[..., None] == jnp.arange(token_classes, dtype=jnp.int32)
    ).astype(jnp.bfloat16)
    token_embedded = jnp.einsum(
        "slt,tc->slc", token_one_hot, symbol_lookup_matrix, preferred_element_type=jnp.float32
    )
    homolog_starting = homolog_activity.astype(jnp.float32) + token_embedded
    pair_norm = layer_normalize(pair_state).astype(jnp.bfloat16)
    bias_rows = jnp.einsum(
        "ijc,ch->hij", pair_norm, pair_bias_weight, preferred_element_type=jnp.float32
    ).astype(jnp.bfloat16)
    bias_full = lax.all_gather(bias_rows, "axial", axis=1, tiled=True)
    key_bias = 1000000000.0 * (residue_present_mask.astype(jnp.float32) - 1.0)
    extra_axes = bias_full.astype(jnp.float32)[None] + key_bias[None, None, None, :]
    cluster_total = homolog_starting.reshape(
        sequence_per_device // 2, 2, residue_length, input_width
    )
    homolog_across_update = lax.map(
        lambda evoformer_block: gated_attend(
            evoformer_block,
            extra_axes,
            row_query_weight,
            horizontal_attention_matrix,
            horizontal_final_matrix,
        ),
        cluster_total,
    )
    homolog_across_update = homolog_across_update.reshape(
        sequence_per_device, group_size, res_dev, input_width
    ).astype(jnp.bfloat16)
    moved = jnp.swapaxes(
        lax.all_to_all(homolog_across_update, "axial", split_axis=1, concat_axis=0, tiled=True)[
            :, 0
        ],
        0,
        1,
    )
    finished = lax.map(
        lambda item: gated_attend(
            item[None].astype(jnp.float32),
            0.0,
            column_query_weight,
            vertical_attention_matrix,
            vertical_final_matrix,
        )[0],
        moved,
    )
    exchanged = jnp.swapaxes(finished, 0, 1).astype(jnp.bfloat16)[:, None]
    sequence_count = exchanged.shape[0]
    alignment_after_columns = exchanged.reshape(sequence_count, res_dev, input_width)
    tensor_mean_scaler = layer_normalize(alignment_after_columns).astype(jnp.bfloat16)
    split_parts = jnp.einsum(
        "src,cf->rsf",
        tensor_mean_scaler,
        tensor_mean_lift_matrix,
        preferred_element_type=jnp.float32,
    ).astype(jnp.bfloat16)
    first_factor = split_parts[..., :MEAN_HIDDEN_SIZE]
    second_factor = split_parts[..., MEAN_HIDDEN_SIZE:].reshape(
        res_dev, sequence_count * MEAN_HIDDEN_SIZE
    )
    step_rows = 8
    left_blocks = first_factor.reshape(
        res_dev // step_rows, step_rows, sequence_count, MEAN_HIDDEN_SIZE
    )
    piece = lax.all_gather(second_factor, "axial", axis=0, tiled=True)
    count = piece.shape[0]
    right_part = piece.reshape(count, sequence_count, MEAN_HIDDEN_SIZE)

    def one_block(lines_list):
        tensor_mean = (
            jnp.einsum("isc,jsd->ijcd", lines_list, right_part, preferred_element_type=jnp.float32)
            / sequence_count
        )
        tensor_mean = tensor_mean.reshape(
            step_rows, count, MEAN_HIDDEN_SIZE * MEAN_HIDDEN_SIZE
        ).astype(jnp.bfloat16)
        return jnp.einsum(
            "ijf,fz->ijz",
            tensor_mean,
            outer_product_output_weight,
            preferred_element_type=jnp.float32,
        )

    update = lax.map(one_block, left_blocks).reshape(
        res_dev, count, outer_product_output_weight.shape[1]
    )
    pair_one = pair_state.astype(jnp.float32) + update
    tri_norm = layer_normalize(pair_one).astype(jnp.bfloat16)
    proj = jnp.einsum(
        "ikc,cf->fik", tri_norm, triangle_projection_weight, preferred_element_type=jnp.float32
    )
    gates = jnp.einsum(
        "ikc,cf->fik", tri_norm, triangle_projection_gate, preferred_element_type=jnp.float32
    )
    both = (jax.nn.sigmoid(gates) * proj * pair_valid_mask.astype(jnp.float32)[None]).astype(
        jnp.bfloat16
    )
    left_tri = both[:C_TRI]
    right_tri = both[C_TRI:]
    moved_left, moved_right = (
        lax.all_to_all(left_tri, "axial", split_axis=0, concat_axis=1, tiled=True),
        lax.all_to_all(right_tri, "axial", split_axis=0, concat_axis=1, tiled=True),
    )
    partial_sum = jnp.einsum(
        "cik,cjk->cij", moved_left, moved_right, preferred_element_type=jnp.float32
    )
    tri_sum = lax.all_to_all(
        partial_sum.astype(jnp.bfloat16), "axial", split_axis=1, concat_axis=0, tiled=True
    ).astype(partial_sum.dtype)
    tri_update = finish_sums(tri_sum, triangle_output_weight)
    out_gate = jax.nn.sigmoid(
        jnp.einsum(
            "ijc,cz->ijz", tri_norm, triangle_output_gate, preferred_element_type=jnp.float32
        )
    )
    pair_output = (pair_one + out_gate * tri_update).astype(jnp.bfloat16)
    return (alignment_after_columns, pair_output)


BF16 = jnp.bfloat16
F32 = jnp.float32
SMALL_ROWS = 16
FLOPS = 3 * 10**9
PACKET_ORDER = (2, 3, 1)
PAIR_ORDER = (3, 1, 2)


def mul(lhs, rhs, over=((1,), (0,))):
    return lax.dot_general(lhs, rhs, (over, ((), ())), preferred_element_type=F32)


def iota(shape, axis):
    return lax.broadcasted_iota(jnp.int32, shape, axis)


def zero_one(condition):
    return jnp.where(condition, 1.0, 0.0).astype(BF16)


def normal(x):
    mean = jnp.mean(x, axis=-1, keepdims=True)
    centred = x - mean
    var = jnp.mean(centred * centred, axis=-1, keepdims=True)
    return centred * lax.rsqrt(var + 1e-05)


def sigmoid(x):
    return 0.5 + 0.5 * jnp.tanh(0.5 * x)


def column_softmax(scores):
    expo = jnp.exp(scores - jnp.max(scores, axis=0, keepdims=True))
    return expo * (1.0 / jnp.sum(expo, axis=0, keepdims=True))


def bias_rows(pair_ref, weight_ref):
    rows, residues, width = pair_ref.shape
    lanes = FOCUS_TOTAL * rows
    spread = zero_one(iota((FOCUS_TOTAL, lanes), 1) // rows == iota((FOCUS_TOTAL, lanes), 0))
    row_of = iota((width, lanes), 1) % rows
    flat = normal(pair_ref[...].astype(F32).reshape(rows * residues, width)).astype(BF16)
    weight = mul(weight_ref[...], spread, ((0,), (0,)))
    side_by_side = [flat[i * residues : (i + 1) * residues] for i in range(rows)]
    one_row = [jnp.where(row_of == i, weight, 0.0).astype(BF16) for i in range(rows)]
    bias = mul(jnp.concatenate(side_by_side, axis=1), jnp.concatenate(one_row, axis=0))
    return bias


def table_kernel(lanes, count, shift_ref, turn_ref, column_ref):
    shape = column_ref.shape
    column_ref[...] = zero_one(iota(shape, 1) // C_TRI == iota(shape, 0))
    shape = shift_ref.shape
    shift_ref[...] = zero_one(iota(shape, 1) == iota(shape, 0) + lanes)
    shape = turn_ref.shape
    row_at = iota(shape, 0)
    turn_ref[...] = zero_one(
        iota(shape, 1) == (row_at % count) * (shape[0] // count) + row_at // count
    )


def packet_kernel(*refs):
    pair_ref, weight_ref, valid_ref, ids_ref, act_ref, present_ref, shift_ref = refs[:7]
    packet_ref, hidden_ref = refs[7:]
    rows, residues, width = pair_ref.shape
    per, _, features = act_ref.shape
    lanes = FOCUS_TOTAL * rows
    bias = bias_rows(pair_ref, weight_ref)
    extra = jnp.concatenate(
        [
            valid_ref[...].astype(F32),
            ids_ref[...].astype(F32),
            jnp.zeros((SMALL_ROWS - rows - per, residues), F32),
        ],
        axis=0,
    )
    extra = mul(extra.astype(BF16), shift_ref[...])
    empty = jnp.zeros((SMALL_ROWS, 128 - lanes), F32)
    first = jnp.concatenate([bias[:SMALL_ROWS], empty], axis=1) + extra
    second = jnp.concatenate([bias[SMALL_ROWS:], empty], axis=1)
    small = jnp.concatenate([first, second], axis=1).astype(BF16)
    packet_ref[per * residues :, :] = small
    shown = present_ref[...].astype(F32).astype(BF16)
    shown = mul(shown, jnp.ones((1, hidden_ref.shape[1]), BF16), ((0,), (0,)))
    hidden_ref[...] = 1000000000.0 * (shown - 1.0)
    packet_ref[: per * residues, :] = act_ref[...].reshape(per * residues, features)


def split_small(packet, residues, res_dev, per):
    small = packet[per * residues :, :].astype(F32)
    lanes = FOCUS_TOTAL * res_dev
    bias = jnp.concatenate([small[:, :lanes], small[:, 128 : 128 + lanes]], axis=0)
    extra = small[:, lanes : lanes + residues]
    return bias, extra[:res_dev], extra[res_dev : res_dev + per]


def head_masks(width):
    return [
        zero_one(iota((1, width), 1) // FOCUS_SIZE == h) for h in range(FOCUS_TOTAL)
    ]


def project(x, w_query, w_kvg):
    width = FOCUS_TOTAL * FOCUS_SIZE
    flat = normal(x).astype(BF16)
    query = (mul(flat, w_query[...]) * FOCUS_SIZE ** (-0.5)).astype(BF16)
    keys = mul(flat, w_kvg[:, :width]).astype(BF16)
    values = mul(flat, w_kvg[:, width : 2 * width]).astype(BF16)
    gate = sigmoid(mul(flat, w_kvg[:, 2 * width :]))
    return query, keys, values, gate


def msa_kernel(n, res_dev, *refs):
    packets, turn, hidden_keys, table = refs[:n], refs[n], refs[n + 1], refs[n + 2]
    refs = refs[n + 3 :]
    row_q, row_kvg, row_out, col_q, col_kvg, col_out, lift, outer_w = refs[:8]
    align_ref, update_ref, lifted = refs[8:]
    kinds, width = table.shape
    residues, lanes = hidden_keys.shape
    pair_width = outer_w.shape[1]
    per = (packets[0].shape[0] - SMALL_ROWS) // residues
    count = per * n
    tokens = count * residues
    me = lax.axis_index("axial")

    place = iota((FOCUS_TOTAL * res_dev, lanes), 0)
    place = (place // res_dev) * residues + place % res_dev - iota(place.shape, 1)
    bias = jnp.zeros((residues, lanes), F32)
    rows = []
    for packet, r in zip(packets, (0, *PACKET_ORDER)):
        part, _, all_ids = split_small(packet, residues, res_dev, per)
        bias += mul(part.astype(BF16), zero_one(place == -(me ^ r) * res_dev))
        for q in range(per):
            hot = zero_one(iota((kinds, residues), 0).astype(F32) == all_ids[q : q + 1])
            act = packet[q * residues : (q + 1) * residues, :].astype(F32)
            rows.append(act + mul(hot, table[...], ((0,), (0,))))
    zero = jnp.concatenate(rows, axis=0)
    extra = bias + hidden_keys[...]
    masks = head_masks(width)

    query, keys, values, gate = project(zero, row_q, row_kvg)
    rows = []
    for s in range(count):
        here = slice(s * residues, (s + 1) * residues)
        spread = jnp.concatenate([query[here] * mask for mask in masks], axis=0)
        weights = column_softmax(mul(keys[here], spread, ((1,), (1,))) + extra).astype(BF16)
        heads = mul(weights, values[here], ((0,), (0,)))
        mixed = heads[:residues]
        for h in range(1, FOCUS_TOTAL):
            part = heads[h * residues : (h + 1) * residues]
            mixed = jnp.where(iota((1, width), 1) // FOCUS_SIZE == h, part, mixed)
        rows.append(mixed)
    mixed = (jnp.concatenate(rows, axis=0) * gate).astype(BF16)
    msa_one = (zero + mul(mixed, row_out[...])).astype(BF16)

    one = mul(turn[...], msa_one)
    query, keys, values, gate = project(one, col_q, col_kvg)
    group = min(tokens, 128)
    sites = group // count
    block_of = iota((1, group), 1) // count
    groups = []
    for g in range(tokens // group):
        here = slice(g * group, (g + 1) * group)
        all_weights, all_values = [], []
        for mask in masks:
            full = mul(keys[here], query[here] * mask, ((1,), (1,)))
            scores = full[:count]
            for b in range(1, sites):
                scores = jnp.where(block_of == b, full[b * count : (b + 1) * count], scores)
            weights = column_softmax(scores)
            weights = jnp.concatenate(
                [jnp.where(block_of == b, weights, 0.0) for b in range(sites)], axis=0
            )
            all_weights.append(weights.astype(BF16))
            all_values.append(values[here] * mask)
        groups.append(
            mul(
                jnp.concatenate(all_weights, axis=0),
                jnp.concatenate(all_values, axis=0),
                ((0,), (0,)),
            )
        )
    mixed = (jnp.concatenate(groups, axis=0) * gate).astype(BF16)
    align = (one + mul(mixed, col_out[...])).astype(BF16)
    own = count * res_dev
    row_at, lane_at = iota((own, tokens), 0), iota((own, tokens), 1)
    sequence = row_at // res_dev
    owner = (sequence // per) ^ me
    where_is = jnp.zeros_like(owner)
    for k, r in enumerate(PACKET_ORDER):
        where_is = jnp.where(owner == r, k + 1, where_is)
    pick = zero_one(
        lane_at
        == (row_at % res_dev + me * res_dev) * count + where_is * per + sequence % per
    )
    align_ref[...] = mul(pick, align).reshape(count, res_dev, width).astype(BF16)

    opm = normal(align.astype(F32)).astype(BF16)
    opm = mul(opm, lift[...], ((1,), (1,))).astype(BF16)
    hidden = MEAN_HIDDEN_SIZE
    deep = hidden * count
    spread = zero_one(
        iota((2 * hidden, deep), 1) // count == iota((2 * hidden, deep), 0)
    )
    left = mul(opm, spread)
    left = jnp.where(
        iota((tokens, deep), 0) % count == iota((tokens, deep), 1) % count, left, 0.0
    ).astype(BF16)
    gather = zero_one(iota((residues, tokens), 1) // count == iota((residues, tokens), 0))
    left = mul(gather, left).astype(BF16)
    right = opm[:, hidden:]
    for c in range(0, hidden, 4):
        four_w = jnp.concatenate(
            [outer_w[(c + k) * hidden : (c + k + 1) * hidden, :] for k in range(4)], axis=1
        )
        part = mul(right, four_w)
        for k in range(4):
            lifted[c + k] = part[:, k * pair_width : (k + 1) * pair_width]
    for j in range(0, residues, 4):
        part = jnp.concatenate(
            [
                lifted[:, (j + k) * count : (j + k + 1) * count, :].reshape(deep, pair_width)
                for k in range(4)
            ],
            axis=1,
        )
        part = mul(left, part.astype(BF16)) * (1.0 / count)
        for k in range(4):
            at = slice((j + k) * residues, (j + k + 1) * residues)
            update_ref[at, :] = part[:, k * pair_width : (k + 1) * pair_width]


def pair_kernel(*refs):
    pairs, packets, update, column, pair, own_mask = refs[:3], refs[3:6], *refs[6:10]
    proj, gates, gate_out, w_out, out_ref, state, one, right_at, left_at, valid = refs[10:]
    res_dev, residues, width = pair.shape
    per = (packets[0].shape[0] - SMALL_ROWS) // residues
    me = lax.axis_index("axial")
    own_valid = own_mask[...].astype(F32)
    for packet, r in zip((None, *packets), (0, *PACKET_ORDER)):
        shown = split_small(packet, residues, res_dev, per)[1] if r else own_valid
        valid[pl.ds(pl.multiple_of((me ^ r) * res_dev, res_dev), res_dev), :] = shown
    own = jnp.concatenate(
        [
            pair[i].astype(F32) + update[pl.ds(me * res_dev + i, residues, stride=residues), :]
            for i in range(res_dev)
        ],
        axis=0,
    )
    left_w = jnp.concatenate([proj[:, :C_TRI], gates[:, :C_TRI], gate_out[...]], axis=1)
    own_all = mul(normal(own).astype(BF16), left_w)
    own_gate = sigmoid(own_all[:, 2 * C_TRI :])
    left = sigmoid(own_all[:, C_TRI : 2 * C_TRI]) * own_all[:, :C_TRI]
    shown = mul(own_valid.astype(BF16), column[:res_dev, : res_dev * C_TRI], ((0,), (0,)))
    for i in range(res_dev):
        part = left[i * residues : (i + 1) * residues] * shown[:, i * C_TRI : (i + 1) * C_TRI]
        left_at[i * residues : (i + 1) * residues, :] = part.astype(BF16).astype(F32)
    size = res_dev * residues
    for block, r in zip((pair, *pairs), (0, *PAIR_ORDER)):
        state[pl.ds(pl.multiple_of((me ^ r) * size, size), size), :] = (
            block[...].astype(F32).reshape(size, width)
        )
    for k in range(residues):
        one[k * residues : (k + 1) * residues, :] = (
            state[pl.ds(k, residues, stride=residues), :]
            + update[k * residues : (k + 1) * residues, :]
        )

    shown = mul(valid[...].astype(BF16), column[...])
    right_w = jnp.concatenate([proj[:, C_TRI:], gates[:, C_TRI:]], axis=1)
    step = min(residues, 16)
    for k in range(0, residues, step):
        here = slice(k * residues, (k + step) * residues)
        both = mul(normal(one[here, :]).astype(BF16), right_w)
        both = sigmoid(both[:, C_TRI:]) * both[:, :C_TRI]
        for p in range(step):
            part = both[p * residues : (p + 1) * residues]
            part = part * shown[:, (k + p) * C_TRI : (k + p + 1) * C_TRI]
            right_at[(k + p) * residues : (k + p + 1) * residues, :] = part.astype(BF16).astype(F32)

    sums = [jnp.zeros((residues, C_TRI), F32) for _ in range(res_dev)]
    for k in range(residues):
        other = right_at[k * residues : (k + 1) * residues, :]
        for i in range(res_dev):
            sums[i] += left_at[i * residues + k : i * residues + k + 1, :] * other
    mixed = normal(jnp.concatenate(sums, axis=0)).astype(BF16)
    result = own + own_gate * mul(mixed, w_out[...])
    out_ref[...] = result.reshape(res_dev, residues, width).astype(BF16)


def call(kernel, out_shape, scratch, vmem_mib, *args):
    vmem = pl.BlockSpec(memory_space=pltpu.VMEM)
    return pl.pallas_call(
        kernel,
        out_shape=out_shape,
        in_specs=[vmem] * len(args),
        out_specs=jax.tree.map(lambda _: vmem, out_shape),
        scratch_shapes=scratch,
        compiler_params=pltpu.CompilerParams(vmem_limit_bytes=vmem_mib * 1024 * 1024),
        cost_estimate=pl.CostEstimate(flops=FLOPS, bytes_accessed=0, transcendentals=0),
    )(*args)


def swap(array, r, n):
    return lax.ppermute(array, "axial", [(i, i ^ r) for i in range(n)])


def local_whole(
    homolog_activity,
    homolog_symbol_ids,
    residue_present_mask,
    pair_state,
    pair_valid_mask,
    symbol_lookup_matrix,
    row_query_weight,
    horizontal_attention_matrix,
    pair_bias_weight,
    horizontal_final_matrix,
    column_query_weight,
    vertical_attention_matrix,
    vertical_final_matrix,
    tensor_mean_lift_matrix,
    outer_product_output_weight,
    triangle_projection_weight,
    triangle_projection_gate,
    triangle_output_gate,
    triangle_output_weight,
):
    n = lax.axis_size("axial")
    per, residues, width = homolog_activity.shape
    res_dev, _, pair_width = pair_state.shape
    count = per * n
    shift, turn, column = call(
        functools.partial(table_kernel, FOCUS_TOTAL * res_dev, count),
        (
            jax.ShapeDtypeStruct((residues, 128), BF16),
            jax.ShapeDtypeStruct((count * residues, count * residues), BF16),
            jax.ShapeDtypeStruct((residues, residues * C_TRI), BF16),
        ),
        [],
        2,
    )
    packet, hidden_keys = call(
        packet_kernel,
        (
            jax.ShapeDtypeStruct((per * residues + SMALL_ROWS, width), BF16),
            jax.ShapeDtypeStruct((residues, FOCUS_TOTAL * residues), F32),
        ),
        [],
        4,
        pair_state,
        pair_bias_weight.T,
        pair_valid_mask,
        homolog_symbol_ids,
        homolog_activity,
        residue_present_mask.reshape(1, residues),
        shift,
    )
    packets = [swap(packet, r, n) for r in PACKET_ORDER]
    _, later = lax.optimization_barrier((packet, pair_state))
    pairs = [swap(later, r, n) for r in PAIR_ORDER]
    alignment, update = call(
        functools.partial(msa_kernel, n, res_dev),
        (
            jax.ShapeDtypeStruct((count, res_dev, width), BF16),
            jax.ShapeDtypeStruct((residues * residues, pair_width), F32),
        ),
        [
            pltpu.VMEM((MEAN_HIDDEN_SIZE, count * residues, pair_width), F32),
        ],
        16,
        packet,
        *packets,
        turn,
        hidden_keys,
        symbol_lookup_matrix,
        row_query_weight,
        horizontal_attention_matrix,
        horizontal_final_matrix,
        column_query_weight,
        vertical_attention_matrix,
        vertical_final_matrix,
        tensor_mean_lift_matrix.T,
        outer_product_output_weight,
    )
    pair_output = call(
        pair_kernel,
        jax.ShapeDtypeStruct((res_dev, residues, pair_width), BF16),
        [
            pltpu.VMEM((residues * residues, pair_width), F32),
            pltpu.VMEM((residues * residues, pair_width), F32),
            pltpu.VMEM((residues * residues, C_TRI), F32),
            pltpu.VMEM((res_dev * residues, C_TRI), F32),
            pltpu.VMEM((residues, residues), F32),
        ],
        16,
        *pairs,
        *packets,
        update,
        column,
        pair_state,
        pair_valid_mask,
        triangle_projection_weight,
        triangle_projection_gate,
        triangle_output_gate,
        triangle_output_weight,
    )
    return (alignment, pair_output)


def local(homolog_activity, homolog_symbol_ids, residue_present_mask, pair_state, *others):
    n = lax.axis_size("axial")
    per, residues, _ = homolog_activity.shape
    small = n == 4 and per * n == 8 and residues == 32
    plan = local_whole if small else local_sharded
    return plan(homolog_activity, homolog_symbol_ids, residue_present_mask, pair_state, *others)


def solution(mesh):
    parts, copied = P(("dp", "axial")), P()
    return jax.shard_map(
        local,
        mesh=mesh,
        in_specs=(parts, parts, P("dp"), parts, parts) + (copied,) * 14,
        out_specs=(P("dp", "axial", None), P(("dp", "axial"), None, None)),
        check_vma=False,
    )
```

```python
import functools

import jax
import jax.numpy as jnp
from jax import lax
from jax.experimental import pallas as pl
from jax.experimental.pallas import tpu as pltpu
from jax.sharding import PartitionSpec as P

FOCUS_TOTAL = 8
FOCUS_SIZE = 32
MEAN_HIDDEN_SIZE = 32
C_TRI = 128


def layer_normalize(attended_entries):
    attended_entries = attended_entries.astype(jnp.float32)
    mean = jnp.mean(attended_entries, axis=-1, keepdims=True)
    centred = attended_entries - mean
    var = jnp.mean(centred * centred, axis=-1, keepdims=True)
    return centred * lax.rsqrt(var + 1e-05)


def gated_attend(evoformer_block, extra_axes, w_query, w_kvg, w_out):
    lines_list, residue_length, input_width = evoformer_block.shape
    width = FOCUS_TOTAL * FOCUS_SIZE
    flat = (
        layer_normalize(evoformer_block)
        .astype(jnp.bfloat16)
        .reshape(lines_list * residue_length, input_width)
    )
    query = (
        jnp.dot(flat, w_query, preferred_element_type=jnp.float32) * FOCUS_SIZE ** (-0.5)
    ).astype(jnp.bfloat16)
    query = query.reshape(lines_list, residue_length, FOCUS_TOTAL, FOCUS_SIZE)
    kvg = jnp.dot(flat, w_kvg, preferred_element_type=jnp.float32)
    keys = (
        kvg[:, :width]
        .astype(jnp.bfloat16)
        .reshape(lines_list, residue_length, FOCUS_TOTAL, FOCUS_SIZE)
    )
    attended_entries = (
        kvg[:, width : 2 * width]
        .astype(jnp.bfloat16)
        .reshape(lines_list, residue_length, FOCUS_TOTAL, FOCUS_SIZE)
    )
    gate = jax.nn.sigmoid(kvg[:, 2 * width :]).reshape(
        lines_list, residue_length, FOCUS_TOTAL, FOCUS_SIZE
    )
    scores = (
        jnp.einsum("bihd,bjhd->bhij", query, keys, preferred_element_type=jnp.float32) + extra_axes
    )
    top = jnp.max(scores, axis=-1, keepdims=True)
    expo = jnp.exp(scores - top)
    weights = (expo / jnp.sum(expo, axis=-1, keepdims=True)).astype(jnp.bfloat16)
    mixed = jnp.einsum(
        "bhij,bjhd->bihd", weights, attended_entries, preferred_element_type=jnp.float32
    )
    mixed = (mixed * gate).astype(jnp.bfloat16).reshape(lines_list * residue_length, width)
    return evoformer_block + jnp.dot(mixed, w_out, preferred_element_type=jnp.float32).reshape(
        lines_list, residue_length, input_width
    )


def finish_sums(evoformer_block, triangle_output_weight):
    mixed = layer_normalize(jnp.transpose(evoformer_block, (1, 2, 0))).astype(jnp.bfloat16)
    return jnp.einsum(
        "ijc,cz->ijz", mixed, triangle_output_weight, preferred_element_type=jnp.float32
    )


def local_sharded(
    homolog_activity,
    homolog_symbol_ids,
    residue_present_mask,
    pair_state,
    pair_valid_mask,
    symbol_lookup_matrix,
    row_query_weight,
    horizontal_attention_matrix,
    pair_bias_weight,
    horizontal_final_matrix,
    column_query_weight,
    vertical_attention_matrix,
    vertical_final_matrix,
    tensor_mean_lift_matrix,
    outer_product_output_weight,
    triangle_projection_weight,
    triangle_projection_gate,
    triangle_output_gate,
    triangle_output_weight,
):
    sequence_per_device, residue_length, input_width = homolog_activity.shape
    res_dev = pair_state.shape[0]
    group_size = lax.axis_size("axial")
    token_classes = symbol_lookup_matrix.shape[0]
    token_one_hot = (
        homolog_symbol_ids[..., None] == jnp.arange(token_classes, dtype=jnp.int32)
    ).astype(jnp.bfloat16)
    token_embedded = jnp.einsum(
        "slt,tc->slc", token_one_hot, symbol_lookup_matrix, preferred_element_type=jnp.float32
    )
    homolog_starting = homolog_activity.astype(jnp.float32) + token_embedded
    pair_norm = layer_normalize(pair_state).astype(jnp.bfloat16)
    bias_rows = jnp.einsum(
        "ijc,ch->hij", pair_norm, pair_bias_weight, preferred_element_type=jnp.float32
    ).astype(jnp.bfloat16)
    bias_full = lax.all_gather(bias_rows, "axial", axis=1, tiled=True)
    key_bias = 1000000000.0 * (residue_present_mask.astype(jnp.float32) - 1.0)
    extra_axes = bias_full.astype(jnp.float32)[None] + key_bias[None, None, None, :]
    cluster_total = homolog_starting.reshape(
        sequence_per_device // 2, 2, residue_length, input_width
    )
    homolog_across_update = lax.map(
        lambda evoformer_block: gated_attend(
            evoformer_block,
            extra_axes,
            row_query_weight,
            horizontal_attention_matrix,
            horizontal_final_matrix,
        ),
        cluster_total,
    )
    homolog_across_update = homolog_across_update.reshape(
        sequence_per_device, group_size, res_dev, input_width
    ).astype(jnp.bfloat16)
    moved = jnp.swapaxes(
        lax.all_to_all(homolog_across_update, "axial", split_axis=1, concat_axis=0, tiled=True)[
            :, 0
        ],
        0,
        1,
    )
    finished = lax.map(
        lambda item: gated_attend(
            item[None].astype(jnp.float32),
            0.0,
            column_query_weight,
            vertical_attention_matrix,
            vertical_final_matrix,
        )[0],
        moved,
    )
    exchanged = jnp.swapaxes(finished, 0, 1).astype(jnp.bfloat16)[:, None]
    sequence_count = exchanged.shape[0]
    alignment_after_columns = exchanged.reshape(sequence_count, res_dev, input_width)
    tensor_mean_scaler = layer_normalize(alignment_after_columns).astype(jnp.bfloat16)
    split_parts = jnp.einsum(
        "src,cf->rsf",
        tensor_mean_scaler,
        tensor_mean_lift_matrix,
        preferred_element_type=jnp.float32,
    ).astype(jnp.bfloat16)
    first_factor = split_parts[..., :MEAN_HIDDEN_SIZE]
    second_factor = split_parts[..., MEAN_HIDDEN_SIZE:].reshape(
        res_dev, sequence_count * MEAN_HIDDEN_SIZE
    )
    step_rows = 8
    left_blocks = first_factor.reshape(
        res_dev // step_rows, step_rows, sequence_count, MEAN_HIDDEN_SIZE
    )
    piece = lax.all_gather(second_factor, "axial", axis=0, tiled=True)
    count = piece.shape[0]
    right_part = piece.reshape(count, sequence_count, MEAN_HIDDEN_SIZE)

    def one_block(lines_list):
        tensor_mean = (
            jnp.einsum("isc,jsd->ijcd", lines_list, right_part, preferred_element_type=jnp.float32)
            / sequence_count
        )
        tensor_mean = tensor_mean.reshape(
            step_rows, count, MEAN_HIDDEN_SIZE * MEAN_HIDDEN_SIZE
        ).astype(jnp.bfloat16)
        return jnp.einsum(
            "ijf,fz->ijz",
            tensor_mean,
            outer_product_output_weight,
            preferred_element_type=jnp.float32,
        )

    update = lax.map(one_block, left_blocks).reshape(
        res_dev, count, outer_product_output_weight.shape[1]
    )
    pair_one = pair_state.astype(jnp.float32) + update
    tri_norm = layer_normalize(pair_one).astype(jnp.bfloat16)
    proj = jnp.einsum(
        "ikc,cf->fik", tri_norm, triangle_projection_weight, preferred_element_type=jnp.float32
    )
    gates = jnp.einsum(
        "ikc,cf->fik", tri_norm, triangle_projection_gate, preferred_element_type=jnp.float32
    )
    both = (jax.nn.sigmoid(gates) * proj * pair_valid_mask.astype(jnp.float32)[None]).astype(
        jnp.bfloat16
    )
    left_tri = both[:C_TRI]
    right_tri = both[C_TRI:]
    moved_left, moved_right = (
        lax.all_to_all(left_tri, "axial", split_axis=0, concat_axis=1, tiled=True),
        lax.all_to_all(right_tri, "axial", split_axis=0, concat_axis=1, tiled=True),
    )
    partial_sum = jnp.einsum(
        "cik,cjk->cij", moved_left, moved_right, preferred_element_type=jnp.float32
    )
    tri_sum = lax.all_to_all(
        partial_sum.astype(jnp.bfloat16), "axial", split_axis=1, concat_axis=0, tiled=True
    ).astype(partial_sum.dtype)
    tri_update = finish_sums(tri_sum, triangle_output_weight)
    out_gate = jax.nn.sigmoid(
        jnp.einsum(
            "ijc,cz->ijz", tri_norm, triangle_output_gate, preferred_element_type=jnp.float32
        )
    )
    pair_output = (pair_one + out_gate * tri_update).astype(jnp.bfloat16)
    return (alignment_after_columns, pair_output)


BF16 = jnp.bfloat16
F32 = jnp.float32
SMALL_ROWS = 16
FLOPS = 3 * 10**9
PACKET_ORDER = (2, 3, 1)
PAIR_ORDER = (3, 1, 2)


def mul(lhs, rhs, over=((1,), (0,))):
    return lax.dot_general(lhs, rhs, (over, ((), ())), preferred_element_type=F32)


def iota(shape, axis):
    return lax.broadcasted_iota(jnp.int32, shape, axis)


def zero_one(condition):
    return jnp.where(condition, 1.0, 0.0).astype(BF16)


def normal(x):
    mean = jnp.mean(x, axis=-1, keepdims=True)
    centred = x - mean
    var = jnp.mean(centred * centred, axis=-1, keepdims=True)
    return centred * lax.rsqrt(var + 1e-05)


def sigmoid(x):
    return 0.5 + 0.5 * jnp.tanh(0.5 * x)


def column_softmax(scores):
    expo = jnp.exp(scores - jnp.max(scores, axis=0, keepdims=True))
    return expo * (1.0 / jnp.sum(expo, axis=0, keepdims=True))


def bias_rows(pair_ref, weight_ref):
    rows, residues, width = pair_ref.shape
    lanes = FOCUS_TOTAL * rows
    spread = zero_one(iota((FOCUS_TOTAL, lanes), 1) // rows == iota((FOCUS_TOTAL, lanes), 0))
    row_of = iota((width, lanes), 1) % rows
    flat = normal(pair_ref[...].astype(F32).reshape(rows * residues, width)).astype(BF16)
    weight = mul(weight_ref[...], spread, ((0,), (0,)))
    side_by_side = [flat[i * residues : (i + 1) * residues] for i in range(rows)]
    one_row = [jnp.where(row_of == i, weight, 0.0).astype(BF16) for i in range(rows)]
    bias = mul(jnp.concatenate(side_by_side, axis=1), jnp.concatenate(one_row, axis=0))
    return bias


def table_kernel(lanes, count, shift_ref, turn_ref, column_ref):
    shape = column_ref.shape
    column_ref[...] = zero_one(iota(shape, 1) // C_TRI == iota(shape, 0))
    shape = shift_ref.shape
    shift_ref[...] = zero_one(iota(shape, 1) == iota(shape, 0) + lanes)
    shape = turn_ref.shape
    row_at = iota(shape, 0)
    turn_ref[...] = zero_one(
        iota(shape, 1) == (row_at % count) * (shape[0] // count) + row_at // count
    )


def packet_kernel(*refs):
    pair_ref, weight_ref, valid_ref, ids_ref, act_ref, present_ref, shift_ref = refs[:7]
    packet_ref, hidden_ref = refs[7:]
    rows, residues, width = pair_ref.shape
    per, _, features = act_ref.shape
    lanes = FOCUS_TOTAL * rows
    bias = bias_rows(pair_ref, weight_ref)
    extra = jnp.concatenate(
        [
            valid_ref[...].astype(F32),
            ids_ref[...].astype(F32),
            jnp.zeros((SMALL_ROWS - rows - per, residues), F32),
        ],
        axis=0,
    )
    extra = mul(extra.astype(BF16), shift_ref[...])
    empty = jnp.zeros((SMALL_ROWS, 128 - lanes), F32)
    first = jnp.concatenate([bias[:SMALL_ROWS], empty], axis=1) + extra
    second = jnp.concatenate([bias[SMALL_ROWS:], empty], axis=1)
    small = jnp.concatenate([first, second], axis=1).astype(BF16)
    packet_ref[per * residues :, :] = small
    shown = present_ref[...].astype(F32).astype(BF16)
    shown = mul(shown, jnp.ones((1, hidden_ref.shape[1]), BF16), ((0,), (0,)))
    hidden_ref[...] = 1000000000.0 * (shown - 1.0)
    packet_ref[: per * residues, :] = act_ref[...].reshape(per * residues, features)


def split_small(packet, residues, res_dev, per):
    small = packet[per * residues :, :].astype(F32)
    lanes = FOCUS_TOTAL * res_dev
    bias = jnp.concatenate([small[:, :lanes], small[:, 128 : 128 + lanes]], axis=0)
    extra = small[:, lanes : lanes + residues]
    return bias, extra[:res_dev], extra[res_dev : res_dev + per]


def head_masks(width):
    return [
        zero_one(iota((1, width), 1) // FOCUS_SIZE == h) for h in range(FOCUS_TOTAL)
    ]


def project(x, w_query, w_kvg):
    width = FOCUS_TOTAL * FOCUS_SIZE
    flat = normal(x).astype(BF16)
    query = (mul(flat, w_query[...]) * FOCUS_SIZE ** (-0.5)).astype(BF16)
    keys = mul(flat, w_kvg[:, :width]).astype(BF16)
    values = mul(flat, w_kvg[:, width : 2 * width]).astype(BF16)
    gate = sigmoid(mul(flat, w_kvg[:, 2 * width :]))
    return query, keys, values, gate


def msa_kernel(n, res_dev, *refs):
    packets, turn, hidden_keys, table = refs[:n], refs[n], refs[n + 1], refs[n + 2]
    refs = refs[n + 3 :]
    row_q, row_kvg, row_out, col_q, col_kvg, col_out, lift, outer_w = refs[:8]
    align_ref, update_ref, lifted = refs[8:]
    kinds, width = table.shape
    residues, lanes = hidden_keys.shape
    pair_width = outer_w.shape[1]
    per = (packets[0].shape[0] - SMALL_ROWS) // residues
    count = per * n
    tokens = count * residues
    me = lax.axis_index("axial")

    place = iota((FOCUS_TOTAL * res_dev, lanes), 0)
    place = (place // res_dev) * residues + place % res_dev - iota(place.shape, 1)
    bias = jnp.zeros((residues, lanes), F32)
    rows = []
    for packet, r in zip(packets, (0, *PACKET_ORDER)):
        part, _, all_ids = split_small(packet, residues, res_dev, per)
        bias += mul(part.astype(BF16), zero_one(place == -(me ^ r) * res_dev))
        for q in range(per):
            hot = zero_one(iota((kinds, residues), 0).astype(F32) == all_ids[q : q + 1])
            act = packet[q * residues : (q + 1) * residues, :].astype(F32)
            rows.append(act + mul(hot, table[...], ((0,), (0,))))
    zero = jnp.concatenate(rows, axis=0)
    extra = bias + hidden_keys[...]
    masks = head_masks(width)

    query, keys, values, gate = project(zero, row_q, row_kvg)
    rows = []
    for s in range(count):
        here = slice(s * residues, (s + 1) * residues)
        spread = jnp.concatenate([query[here] * mask for mask in masks], axis=0)
        weights = column_softmax(mul(keys[here], spread, ((1,), (1,))) + extra).astype(BF16)
        heads = mul(weights, values[here], ((0,), (0,)))
        mixed = heads[:residues]
        for h in range(1, FOCUS_TOTAL):
            part = heads[h * residues : (h + 1) * residues]
            mixed = jnp.where(iota((1, width), 1) // FOCUS_SIZE == h, part, mixed)
        rows.append(mixed)
    mixed = (jnp.concatenate(rows, axis=0) * gate).astype(BF16)
    msa_one = (zero + mul(mixed, row_out[...])).astype(BF16)

    one = mul(turn[...], msa_one)
    query, keys, values, gate = project(one, col_q, col_kvg)
    group = min(tokens, 128)
    sites = group // count
    block_of = iota((1, group), 1) // count
    groups = []
    for g in range(tokens // group):
        here = slice(g * group, (g + 1) * group)
        all_weights, all_values = [], []
        for mask in masks:
            full = mul(keys[here], query[here] * mask, ((1,), (1,)))
            scores = full[:count]
            for b in range(1, sites):
                scores = jnp.where(block_of == b, full[b * count : (b + 1) * count], scores)
            weights = column_softmax(scores)
            weights = jnp.concatenate(
                [jnp.where(block_of == b, weights, 0.0) for b in range(sites)], axis=0
            )
            all_weights.append(weights.astype(BF16))
            all_values.append(values[here] * mask)
        groups.append(
            mul(
                jnp.concatenate(all_weights, axis=0),
                jnp.concatenate(all_values, axis=0),
                ((0,), (0,)),
            )
        )
    mixed = (jnp.concatenate(groups, axis=0) * gate).astype(BF16)
    align = (one + mul(mixed, col_out[...])).astype(BF16)
    opm = normal(align.astype(F32)).astype(BF16)
    opm = mul(opm, lift[...], ((1,), (1,))).astype(BF16)
    hidden = MEAN_HIDDEN_SIZE
    deep = hidden * count
    spread = zero_one(
        iota((2 * hidden, deep), 1) // count == iota((2 * hidden, deep), 0)
    )
    left = mul(opm, spread)
    left = jnp.where(
        iota((tokens, deep), 0) % count == iota((tokens, deep), 1) % count, left, 0.0
    ).astype(BF16)
    gather = zero_one(iota((residues, tokens), 1) // count == iota((residues, tokens), 0))
    left = mul(gather, left).astype(BF16)
    right = opm[:, hidden:]
    for c in range(0, hidden, 4):
        four_w = jnp.concatenate(
            [outer_w[(c + k) * hidden : (c + k + 1) * hidden, :] for k in range(4)], axis=1
        )
        part = mul(right, four_w)
        for k in range(4):
            lifted[c + k] = part[:, k * pair_width : (k + 1) * pair_width]
    for j in range(0, residues, 4):
        part = jnp.concatenate(
            [
                lifted[:, (j + k) * count : (j + k + 1) * count, :].reshape(deep, pair_width)
                for k in range(4)
            ],
            axis=1,
        )
        part = mul(left, part.astype(BF16)) * (1.0 / count)
        for k in range(4):
            at = slice((j + k) * residues, (j + k + 1) * residues)
            update_ref[at, :] = part[:, k * pair_width : (k + 1) * pair_width]

    own = count * res_dev
    row_at, lane_at = iota((own, tokens), 0), iota((own, tokens), 1)
    sequence = row_at // res_dev
    owner = (sequence // per) ^ me
    where_is = jnp.zeros_like(owner)
    for k, r in enumerate(PACKET_ORDER):
        where_is = jnp.where(owner == r, k + 1, where_is)
    pick = zero_one(
        lane_at
        == (row_at % res_dev + me * res_dev) * count + where_is * per + sequence % per
    )
    align_ref[...] = mul(pick, align).reshape(count, res_dev, width).astype(BF16)


def pair_kernel(*refs):
    pairs, packets, update, column, pair, own_mask = refs[:3], refs[3:6], *refs[6:10]
    proj, gates, gate_out, w_out, out_ref, state, one, right_at, left_at, valid = refs[10:]
    res_dev, residues, width = pair.shape
    per = (packets[0].shape[0] - SMALL_ROWS) // residues
    me = lax.axis_index("axial")
    own_valid = own_mask[...].astype(F32)
    for packet, r in zip((None, *packets), (0, *PACKET_ORDER)):
        shown = split_small(packet, residues, res_dev, per)[1] if r else own_valid
        valid[pl.ds(pl.multiple_of((me ^ r) * res_dev, res_dev), res_dev), :] = shown
    own = jnp.concatenate(
        [
            pair[i].astype(F32) + update[pl.ds(me * res_dev + i, residues, stride=residues), :]
            for i in range(res_dev)
        ],
        axis=0,
    )
    left_w = jnp.concatenate([proj[:, :C_TRI], gates[:, :C_TRI], gate_out[...]], axis=1)
    own_all = mul(normal(own).astype(BF16), left_w)
    own_gate = sigmoid(own_all[:, 2 * C_TRI :])
    left = sigmoid(own_all[:, C_TRI : 2 * C_TRI]) * own_all[:, :C_TRI]
    shown = mul(own_valid.astype(BF16), column[:res_dev, : res_dev * C_TRI], ((0,), (0,)))
    for i in range(res_dev):
        part = left[i * residues : (i + 1) * residues] * shown[:, i * C_TRI : (i + 1) * C_TRI]
        left_at[i * residues : (i + 1) * residues, :] = part.astype(BF16).astype(F32)
    size = res_dev * residues
    for block, r in zip((pair, *pairs), (0, *PAIR_ORDER)):
        state[pl.ds(pl.multiple_of((me ^ r) * size, size), size), :] = (
            block[...].astype(F32).reshape(size, width)
        )
    for k in range(residues):
        one[k * residues : (k + 1) * residues, :] = (
            state[pl.ds(k, residues, stride=residues), :]
            + update[k * residues : (k + 1) * residues, :]
        )

    shown = mul(valid[...].astype(BF16), column[...])
    right_w = jnp.concatenate([proj[:, C_TRI:], gates[:, C_TRI:]], axis=1)
    step = min(residues, 16)
    for k in range(0, residues, step):
        here = slice(k * residues, (k + step) * residues)
        both = mul(normal(one[here, :]).astype(BF16), right_w)
        both = sigmoid(both[:, C_TRI:]) * both[:, :C_TRI]
        for p in range(step):
            part = both[p * residues : (p + 1) * residues]
            part = part * shown[:, (k + p) * C_TRI : (k + p + 1) * C_TRI]
            right_at[(k + p) * residues : (k + p + 1) * residues, :] = part.astype(BF16).astype(F32)

    sums = [jnp.zeros((residues, C_TRI), F32) for _ in range(res_dev)]
    for k in range(residues):
        other = right_at[k * residues : (k + 1) * residues, :]
        for i in range(res_dev):
            sums[i] += left_at[i * residues + k : i * residues + k + 1, :] * other
    mixed = normal(jnp.concatenate(sums, axis=0)).astype(BF16)
    result = own + own_gate * mul(mixed, w_out[...])
    out_ref[...] = result.reshape(res_dev, residues, width).astype(BF16)


def call(kernel, out_shape, scratch, vmem_mib, *args):
    vmem = pl.BlockSpec(memory_space=pltpu.VMEM)
    return pl.pallas_call(
        kernel,
        out_shape=out_shape,
        in_specs=[vmem] * len(args),
        out_specs=jax.tree.map(lambda _: vmem, out_shape),
        scratch_shapes=scratch,
        compiler_params=pltpu.CompilerParams(vmem_limit_bytes=vmem_mib * 1024 * 1024),
        cost_estimate=pl.CostEstimate(flops=FLOPS, bytes_accessed=0, transcendentals=0),
    )(*args)


def swap(array, r, n):
    return lax.ppermute(array, "axial", [(i, i ^ r) for i in range(n)])


def local_whole(
    homolog_activity,
    homolog_symbol_ids,
    residue_present_mask,
    pair_state,
    pair_valid_mask,
    symbol_lookup_matrix,
    row_query_weight,
    horizontal_attention_matrix,
    pair_bias_weight,
    horizontal_final_matrix,
    column_query_weight,
    vertical_attention_matrix,
    vertical_final_matrix,
    tensor_mean_lift_matrix,
    outer_product_output_weight,
    triangle_projection_weight,
    triangle_projection_gate,
    triangle_output_gate,
    triangle_output_weight,
):
    n = lax.axis_size("axial")
    per, residues, width = homolog_activity.shape
    res_dev, _, pair_width = pair_state.shape
    count = per * n
    shift, turn, column = call(
        functools.partial(table_kernel, FOCUS_TOTAL * res_dev, count),
        (
            jax.ShapeDtypeStruct((residues, 128), BF16),
            jax.ShapeDtypeStruct((count * residues, count * residues), BF16),
            jax.ShapeDtypeStruct((residues, residues * C_TRI), BF16),
        ),
        [],
        2,
    )
    packet, hidden_keys = call(
        packet_kernel,
        (
            jax.ShapeDtypeStruct((per * residues + SMALL_ROWS, width), BF16),
            jax.ShapeDtypeStruct((residues, FOCUS_TOTAL * residues), F32),
        ),
        [],
        4,
        pair_state,
        pair_bias_weight.T,
        pair_valid_mask,
        homolog_symbol_ids,
        homolog_activity,
        residue_present_mask.reshape(1, residues),
        shift,
    )
    packets = [swap(packet, r, n) for r in PACKET_ORDER]
    _, later = lax.optimization_barrier((packet, pair_state))
    pairs = [swap(later, r, n) for r in PAIR_ORDER]
    alignment, update = call(
        functools.partial(msa_kernel, n, res_dev),
        (
            jax.ShapeDtypeStruct((count, res_dev, width), BF16),
            jax.ShapeDtypeStruct((residues * residues, pair_width), F32),
        ),
        [
            pltpu.VMEM((MEAN_HIDDEN_SIZE, count * residues, pair_width), F32),
        ],
        16,
        packet,
        *packets,
        turn,
        hidden_keys,
        symbol_lookup_matrix,
        row_query_weight,
        horizontal_attention_matrix,
        horizontal_final_matrix,
        column_query_weight,
        vertical_attention_matrix,
        vertical_final_matrix,
        tensor_mean_lift_matrix.T,
        outer_product_output_weight,
    )
    pair_output = call(
        pair_kernel,
        jax.ShapeDtypeStruct((res_dev, residues, pair_width), BF16),
        [
            pltpu.VMEM((residues * residues, pair_width), F32),
            pltpu.VMEM((residues * residues, pair_width), F32),
            pltpu.VMEM((residues * residues, C_TRI), F32),
            pltpu.VMEM((res_dev * residues, C_TRI), F32),
            pltpu.VMEM((residues, residues), F32),
        ],
        16,
        *pairs,
        *packets,
        update,
        column,
        pair_state,
        pair_valid_mask,
        triangle_projection_weight,
        triangle_projection_gate,
        triangle_output_gate,
        triangle_output_weight,
    )
    return (alignment, pair_output)


def local(homolog_activity, homolog_symbol_ids, residue_present_mask, pair_state, *others):
    n = lax.axis_size("axial")
    per, residues, _ = homolog_activity.shape
    small = n == 4 and per * n == 8 and residues == 32
    plan = local_whole if small else local_sharded
    return plan(homolog_activity, homolog_symbol_ids, residue_present_mask, pair_state, *others)


def solution(mesh):
    parts, copied = P(("dp", "axial")), P()
    return jax.shard_map(
        local,
        mesh=mesh,
        in_specs=(parts, parts, P("dp"), parts, parts) + (copied,) * 14,
        out_specs=(P("dp", "axial", None), P(("dp", "axial"), None, None)),
        check_vma=False,
    )
```

```python
import functools

import jax
import jax.numpy as jnp
from jax import lax
from jax.experimental import pallas as pl
from jax.experimental.pallas import tpu as pltpu
from jax.sharding import PartitionSpec as P

FOCUS_TOTAL = 8
FOCUS_SIZE = 32
MEAN_HIDDEN_SIZE = 32
C_TRI = 128


def layer_normalize(attended_entries):
    attended_entries = attended_entries.astype(jnp.float32)
    mean = jnp.mean(attended_entries, axis=-1, keepdims=True)
    centred = attended_entries - mean
    var = jnp.mean(centred * centred, axis=-1, keepdims=True)
    return centred * lax.rsqrt(var + 1e-05)


def gated_attend(evoformer_block, extra_axes, w_query, w_kvg, w_out):
    lines_list, residue_length, input_width = evoformer_block.shape
    width = FOCUS_TOTAL * FOCUS_SIZE
    flat = (
        layer_normalize(evoformer_block)
        .astype(jnp.bfloat16)
        .reshape(lines_list * residue_length, input_width)
    )
    query = (
        jnp.dot(flat, w_query, preferred_element_type=jnp.float32) * FOCUS_SIZE ** (-0.5)
    ).astype(jnp.bfloat16)
    query = query.reshape(lines_list, residue_length, FOCUS_TOTAL, FOCUS_SIZE)
    kvg = jnp.dot(flat, w_kvg, preferred_element_type=jnp.float32)
    keys = (
        kvg[:, :width]
        .astype(jnp.bfloat16)
        .reshape(lines_list, residue_length, FOCUS_TOTAL, FOCUS_SIZE)
    )
    attended_entries = (
        kvg[:, width : 2 * width]
        .astype(jnp.bfloat16)
        .reshape(lines_list, residue_length, FOCUS_TOTAL, FOCUS_SIZE)
    )
    gate = jax.nn.sigmoid(kvg[:, 2 * width :]).reshape(
        lines_list, residue_length, FOCUS_TOTAL, FOCUS_SIZE
    )
    scores = (
        jnp.einsum("bihd,bjhd->bhij", query, keys, preferred_element_type=jnp.float32) + extra_axes
    )
    top = jnp.max(scores, axis=-1, keepdims=True)
    expo = jnp.exp(scores - top)
    weights = (expo / jnp.sum(expo, axis=-1, keepdims=True)).astype(jnp.bfloat16)
    mixed = jnp.einsum(
        "bhij,bjhd->bihd", weights, attended_entries, preferred_element_type=jnp.float32
    )
    mixed = (mixed * gate).astype(jnp.bfloat16).reshape(lines_list * residue_length, width)
    return evoformer_block + jnp.dot(mixed, w_out, preferred_element_type=jnp.float32).reshape(
        lines_list, residue_length, input_width
    )


def finish_sums(evoformer_block, triangle_output_weight):
    mixed = layer_normalize(jnp.transpose(evoformer_block, (1, 2, 0))).astype(jnp.bfloat16)
    return jnp.einsum(
        "ijc,cz->ijz", mixed, triangle_output_weight, preferred_element_type=jnp.float32
    )


def local_sharded(
    homolog_activity,
    homolog_symbol_ids,
    residue_present_mask,
    pair_state,
    pair_valid_mask,
    symbol_lookup_matrix,
    row_query_weight,
    horizontal_attention_matrix,
    pair_bias_weight,
    horizontal_final_matrix,
    column_query_weight,
    vertical_attention_matrix,
    vertical_final_matrix,
    tensor_mean_lift_matrix,
    outer_product_output_weight,
    triangle_projection_weight,
    triangle_projection_gate,
    triangle_output_gate,
    triangle_output_weight,
):
    sequence_per_device, residue_length, input_width = homolog_activity.shape
    res_dev = pair_state.shape[0]
    group_size = lax.axis_size("axial")
    token_classes = symbol_lookup_matrix.shape[0]
    token_one_hot = (
        homolog_symbol_ids[..., None] == jnp.arange(token_classes, dtype=jnp.int32)
    ).astype(jnp.bfloat16)
    token_embedded = jnp.einsum(
        "slt,tc->slc", token_one_hot, symbol_lookup_matrix, preferred_element_type=jnp.float32
    )
    homolog_starting = homolog_activity.astype(jnp.float32) + token_embedded
    pair_norm = layer_normalize(pair_state).astype(jnp.bfloat16)
    bias_rows = jnp.einsum(
        "ijc,ch->hij", pair_norm, pair_bias_weight, preferred_element_type=jnp.float32
    ).astype(jnp.bfloat16)
    bias_full = lax.all_gather(bias_rows, "axial", axis=1, tiled=True)
    key_bias = 1000000000.0 * (residue_present_mask.astype(jnp.float32) - 1.0)
    extra_axes = bias_full.astype(jnp.float32)[None] + key_bias[None, None, None, :]
    cluster_total = homolog_starting.reshape(
        sequence_per_device // 2, 2, residue_length, input_width
    )
    homolog_across_update = lax.map(
        lambda evoformer_block: gated_attend(
            evoformer_block,
            extra_axes,
            row_query_weight,
            horizontal_attention_matrix,
            horizontal_final_matrix,
        ),
        cluster_total,
    )
    homolog_across_update = homolog_across_update.reshape(
        sequence_per_device, group_size, res_dev, input_width
    ).astype(jnp.bfloat16)
    moved = jnp.swapaxes(
        lax.all_to_all(homolog_across_update, "axial", split_axis=1, concat_axis=0, tiled=True)[
            :, 0
        ],
        0,
        1,
    )
    finished = lax.map(
        lambda item: gated_attend(
            item[None].astype(jnp.float32),
            0.0,
            column_query_weight,
            vertical_attention_matrix,
            vertical_final_matrix,
        )[0],
        moved,
    )
    exchanged = jnp.swapaxes(finished, 0, 1).astype(jnp.bfloat16)[:, None]
    sequence_count = exchanged.shape[0]
    alignment_after_columns = exchanged.reshape(sequence_count, res_dev, input_width)
    tensor_mean_scaler = layer_normalize(alignment_after_columns).astype(jnp.bfloat16)
    split_parts = jnp.einsum(
        "src,cf->rsf",
        tensor_mean_scaler,
        tensor_mean_lift_matrix,
        preferred_element_type=jnp.float32,
    ).astype(jnp.bfloat16)
    first_factor = split_parts[..., :MEAN_HIDDEN_SIZE]
    second_factor = split_parts[..., MEAN_HIDDEN_SIZE:].reshape(
        res_dev, sequence_count * MEAN_HIDDEN_SIZE
    )
    step_rows = 8
    left_blocks = first_factor.reshape(
        res_dev // step_rows, step_rows, sequence_count, MEAN_HIDDEN_SIZE
    )
    piece = lax.all_gather(second_factor, "axial", axis=0, tiled=True)
    count = piece.shape[0]
    right_part = piece.reshape(count, sequence_count, MEAN_HIDDEN_SIZE)

    def one_block(lines_list):
        tensor_mean = (
            jnp.einsum("isc,jsd->ijcd", lines_list, right_part, preferred_element_type=jnp.float32)
            / sequence_count
        )
        tensor_mean = tensor_mean.reshape(
            step_rows, count, MEAN_HIDDEN_SIZE * MEAN_HIDDEN_SIZE
        ).astype(jnp.bfloat16)
        return jnp.einsum(
            "ijf,fz->ijz",
            tensor_mean,
            outer_product_output_weight,
            preferred_element_type=jnp.float32,
        )

    update = lax.map(one_block, left_blocks).reshape(
        res_dev, count, outer_product_output_weight.shape[1]
    )
    pair_one = pair_state.astype(jnp.float32) + update
    tri_norm = layer_normalize(pair_one).astype(jnp.bfloat16)
    proj = jnp.einsum(
        "ikc,cf->fik", tri_norm, triangle_projection_weight, preferred_element_type=jnp.float32
    )
    gates = jnp.einsum(
        "ikc,cf->fik", tri_norm, triangle_projection_gate, preferred_element_type=jnp.float32
    )
    both = (jax.nn.sigmoid(gates) * proj * pair_valid_mask.astype(jnp.float32)[None]).astype(
        jnp.bfloat16
    )
    left_tri = both[:C_TRI]
    right_tri = both[C_TRI:]
    moved_left, moved_right = (
        lax.all_to_all(left_tri, "axial", split_axis=0, concat_axis=1, tiled=True),
        lax.all_to_all(right_tri, "axial", split_axis=0, concat_axis=1, tiled=True),
    )
    partial_sum = jnp.einsum(
        "cik,cjk->cij", moved_left, moved_right, preferred_element_type=jnp.float32
    )
    tri_sum = lax.all_to_all(
        partial_sum.astype(jnp.bfloat16), "axial", split_axis=1, concat_axis=0, tiled=True
    ).astype(partial_sum.dtype)
    tri_update = finish_sums(tri_sum, triangle_output_weight)
    out_gate = jax.nn.sigmoid(
        jnp.einsum(
            "ijc,cz->ijz", tri_norm, triangle_output_gate, preferred_element_type=jnp.float32
        )
    )
    pair_output = (pair_one + out_gate * tri_update).astype(jnp.bfloat16)
    return (alignment_after_columns, pair_output)


BF16 = jnp.bfloat16
F32 = jnp.float32
SMALL_ROWS = 16
FLOPS = 3 * 10**9
PACKET_ORDER = (2, 3, 1)
PAIR_ORDER = (3, 1, 2)


def mul(lhs, rhs, over=((1,), (0,))):
    return lax.dot_general(lhs, rhs, (over, ((), ())), preferred_element_type=F32)


def iota(shape, axis):
    return lax.broadcasted_iota(jnp.int32, shape, axis)


def zero_one(condition):
    return jnp.where(condition, 1.0, 0.0).astype(BF16)


def normal(x):
    mean = jnp.mean(x, axis=-1, keepdims=True)
    centred = x - mean
    var = jnp.mean(centred * centred, axis=-1, keepdims=True)
    return centred * lax.rsqrt(var + 1e-05)


def sigmoid(x):
    return 0.5 + 0.5 * jnp.tanh(0.5 * x)


def column_softmax(scores):
    expo = jnp.exp(scores - jnp.max(scores, axis=0, keepdims=True))
    return expo * (1.0 / jnp.sum(expo, axis=0, keepdims=True))


def bias_rows(pair_ref, weight_ref):
    rows, residues, width = pair_ref.shape
    lanes = FOCUS_TOTAL * rows
    spread = zero_one(iota((FOCUS_TOTAL, lanes), 1) // rows == iota((FOCUS_TOTAL, lanes), 0))
    row_of = iota((width, lanes), 1) % rows
    flat = normal(pair_ref[...].astype(F32).reshape(rows * residues, width)).astype(BF16)
    weight = mul(weight_ref[...], spread, ((0,), (0,)))
    side_by_side = [flat[i * residues : (i + 1) * residues] for i in range(rows)]
    one_row = [jnp.where(row_of == i, weight, 0.0).astype(BF16) for i in range(rows)]
    bias = mul(jnp.concatenate(side_by_side, axis=1), jnp.concatenate(one_row, axis=0))
    return bias


def table_kernel(lanes, count, shift_ref, turn_ref, column_ref):
    shape = column_ref.shape
    column_ref[...] = zero_one(iota(shape, 1) // C_TRI == iota(shape, 0))
    shape = shift_ref.shape
    shift_ref[...] = zero_one(iota(shape, 1) == iota(shape, 0) + lanes)
    shape = turn_ref.shape
    row_at = iota(shape, 0)
    turn_ref[...] = zero_one(
        iota(shape, 1) == (row_at % count) * (shape[0] // count) + row_at // count
    )


def packet_kernel(*refs):
    pair_ref, weight_ref, valid_ref, ids_ref, act_ref, present_ref, shift_ref = refs[:7]
    packet_ref, hidden_ref = refs[7:]
    rows, residues, width = pair_ref.shape
    per, _, features = act_ref.shape
    lanes = FOCUS_TOTAL * rows
    bias = bias_rows(pair_ref, weight_ref)
    extra = jnp.concatenate(
        [
            valid_ref[...].astype(F32),
            ids_ref[...].astype(F32),
            jnp.zeros((SMALL_ROWS - rows - per, residues), F32),
        ],
        axis=0,
    )
    extra = mul(extra.astype(BF16), shift_ref[...])
    empty = jnp.zeros((SMALL_ROWS, 128 - lanes), F32)
    first = jnp.concatenate([bias[:SMALL_ROWS], empty], axis=1) + extra
    second = jnp.concatenate([bias[SMALL_ROWS:], empty], axis=1)
    small = jnp.concatenate([first, second], axis=1).astype(BF16)
    packet_ref[per * residues :, :] = small
    shown = present_ref[...].astype(F32).astype(BF16)
    shown = mul(shown, jnp.ones((1, hidden_ref.shape[1]), BF16), ((0,), (0,)))
    hidden_ref[...] = 1000000000.0 * (shown - 1.0)
    packet_ref[: per * residues, :] = act_ref[...].reshape(per * residues, features)


def split_small(packet, residues, res_dev, per):
    small = packet[per * residues :, :].astype(F32)
    lanes = FOCUS_TOTAL * res_dev
    bias = jnp.concatenate([small[:, :lanes], small[:, 128 : 128 + lanes]], axis=0)
    extra = small[:, lanes : lanes + residues]
    return bias, extra[:res_dev], extra[res_dev : res_dev + per]


def head_masks(width):
    return [
        zero_one(iota((1, width), 1) // FOCUS_SIZE == h) for h in range(FOCUS_TOTAL)
    ]


def project(x, w_query, w_kvg):
    width = FOCUS_TOTAL * FOCUS_SIZE
    flat = normal(x).astype(BF16)
    query = (mul(flat, w_query[...]) * FOCUS_SIZE ** (-0.5)).astype(BF16)
    keys = mul(flat, w_kvg[:, :width]).astype(BF16)
    values = mul(flat, w_kvg[:, width : 2 * width]).astype(BF16)
    gate = sigmoid(mul(flat, w_kvg[:, 2 * width :]))
    return query, keys, values, gate


def msa_kernel(n, res_dev, *refs):
    packets, turn, hidden_keys, table = refs[:n], refs[n], refs[n + 1], refs[n + 2]
    refs = refs[n + 3 :]
    row_q, row_kvg, row_out, col_q, col_kvg, col_out, lift, outer_w = refs[:8]
    align_ref, update_ref, lifted, held = refs[8:]
    kinds, width = table.shape
    residues, lanes = hidden_keys.shape
    pair_width = outer_w.shape[1]
    per = (packets[0].shape[0] - SMALL_ROWS) // residues
    count = per * n
    tokens = count * residues
    me = lax.axis_index("axial")

    place = iota((FOCUS_TOTAL * res_dev, lanes), 0)
    place = (place // res_dev) * residues + place % res_dev - iota(place.shape, 1)
    bias = jnp.zeros((residues, lanes), F32)
    rows = []
    for packet, r in zip(packets, (0, *PACKET_ORDER)):
        part, _, all_ids = split_small(packet, residues, res_dev, per)
        bias += mul(part.astype(BF16), zero_one(place == -(me ^ r) * res_dev))
        for q in range(per):
            hot = zero_one(iota((kinds, residues), 0).astype(F32) == all_ids[q : q + 1])
            act = packet[q * residues : (q + 1) * residues, :].astype(F32)
            rows.append(act + mul(hot, table[...], ((0,), (0,))))
    zero = jnp.concatenate(rows, axis=0)
    extra = bias + hidden_keys[...]
    masks = head_masks(width)

    query, keys, values, gate = project(zero, row_q, row_kvg)
    rows = []
    for s in range(count):
        here = slice(s * residues, (s + 1) * residues)
        spread = jnp.concatenate([query[here] * mask for mask in masks], axis=0)
        weights = column_softmax(mul(keys[here], spread, ((1,), (1,))) + extra).astype(BF16)
        heads = mul(weights, values[here], ((0,), (0,)))
        mixed = heads[:residues]
        for h in range(1, FOCUS_TOTAL):
            part = heads[h * residues : (h + 1) * residues]
            mixed = jnp.where(iota((1, width), 1) // FOCUS_SIZE == h, part, mixed)
        rows.append(mixed)
    mixed = (jnp.concatenate(rows, axis=0) * gate).astype(BF16)
    msa_one = (zero + mul(mixed, row_out[...])).astype(BF16)

    held[...] = mul(turn[...], msa_one)
    one = held[...]
    query, keys, values, gate = project(one, col_q, col_kvg)
    group = min(tokens, 128)
    sites = group // count
    block_of = iota((1, group), 1) // count
    groups = []
    for g in range(tokens // group):
        here = slice(g * group, (g + 1) * group)
        all_weights, all_values = [], []
        for mask in masks:
            full = mul(keys[here], query[here] * mask, ((1,), (1,)))
            scores = full[:count]
            for b in range(1, sites):
                scores = jnp.where(block_of == b, full[b * count : (b + 1) * count], scores)
            weights = column_softmax(scores)
            weights = jnp.concatenate(
                [jnp.where(block_of == b, weights, 0.0) for b in range(sites)], axis=0
            )
            all_weights.append(weights.astype(BF16))
            all_values.append(values[here] * mask)
        groups.append(
            mul(
                jnp.concatenate(all_weights, axis=0),
                jnp.concatenate(all_values, axis=0),
                ((0,), (0,)),
            )
        )
    mixed = (jnp.concatenate(groups, axis=0) * gate).astype(BF16)
    align = (one + mul(mixed, col_out[...])).astype(BF16)
    own = count * res_dev
    row_at, lane_at = iota((own, tokens), 0), iota((own, tokens), 1)
    sequence = row_at // res_dev
    owner = (sequence // per) ^ me
    where_is = jnp.zeros_like(owner)
    for k, r in enumerate(PACKET_ORDER):
        where_is = jnp.where(owner == r, k + 1, where_is)
    pick = zero_one(
        lane_at
        == (row_at % res_dev + me * res_dev) * count + where_is * per + sequence % per
    )
    align_ref[...] = mul(pick, align).reshape(count, res_dev, width).astype(BF16)

    opm = normal(align.astype(F32)).astype(BF16)
    opm = mul(opm, lift[...], ((1,), (1,))).astype(BF16)
    hidden = MEAN_HIDDEN_SIZE
    deep = hidden * count
    spread = zero_one(
        iota((2 * hidden, deep), 1) // count == iota((2 * hidden, deep), 0)
    )
    left = mul(opm, spread)
    left = jnp.where(
        iota((tokens, deep), 0) % count == iota((tokens, deep), 1) % count, left, 0.0
    ).astype(BF16)
    gather = zero_one(iota((residues, tokens), 1) // count == iota((residues, tokens), 0))
    left = mul(gather, left).astype(BF16)
    right = opm[:, hidden:]
    for c in range(0, hidden, 4):
        four_w = jnp.concatenate(
            [outer_w[(c + k) * hidden : (c + k + 1) * hidden, :] for k in range(4)], axis=1
        )
        part = mul(right, four_w)
        for k in range(4):
            lifted[c + k] = part[:, k * pair_width : (k + 1) * pair_width]
    for j in range(0, residues, 4):
        part = jnp.concatenate(
            [
                lifted[:, (j + k) * count : (j + k + 1) * count, :].reshape(deep, pair_width)
                for k in range(4)
            ],
            axis=1,
        )
        part = mul(left, part.astype(BF16)) * (1.0 / count)
        for k in range(4):
            at = slice((j + k) * residues, (j + k + 1) * residues)
            update_ref[at, :] = part[:, k * pair_width : (k + 1) * pair_width]


def pair_kernel(*refs):
    pairs, packets, update, column, pair, own_mask = refs[:3], refs[3:6], *refs[6:10]
    proj, gates, gate_out, w_out, out_ref, state, one, right_at, left_at, valid = refs[10:]
    res_dev, residues, width = pair.shape
    per = (packets[0].shape[0] - SMALL_ROWS) // residues
    me = lax.axis_index("axial")
    own_valid = own_mask[...].astype(F32)
    for packet, r in zip((None, *packets), (0, *PACKET_ORDER)):
        shown = split_small(packet, residues, res_dev, per)[1] if r else own_valid
        valid[pl.ds(pl.multiple_of((me ^ r) * res_dev, res_dev), res_dev), :] = shown
    own = jnp.concatenate(
        [
            pair[i].astype(F32) + update[pl.ds(me * res_dev + i, residues, stride=residues), :]
            for i in range(res_dev)
        ],
        axis=0,
    )
    left_w = jnp.concatenate([proj[:, :C_TRI], gates[:, :C_TRI], gate_out[...]], axis=1)
    own_all = mul(normal(own).astype(BF16), left_w)
    own_gate = sigmoid(own_all[:, 2 * C_TRI :])
    left = sigmoid(own_all[:, C_TRI : 2 * C_TRI]) * own_all[:, :C_TRI]
    shown = mul(own_valid.astype(BF16), column[:res_dev, : res_dev * C_TRI], ((0,), (0,)))
    for i in range(res_dev):
        part = left[i * residues : (i + 1) * residues] * shown[:, i * C_TRI : (i + 1) * C_TRI]
        left_at[i * residues : (i + 1) * residues, :] = part.astype(BF16).astype(F32)
    size = res_dev * residues
    for block, r in zip((pair, *pairs), (0, *PAIR_ORDER)):
        state[pl.ds(pl.multiple_of((me ^ r) * size, size), size), :] = (
            block[...].astype(F32).reshape(size, width)
        )
    for k in range(residues):
        one[k * residues : (k + 1) * residues, :] = (
            state[pl.ds(k, residues, stride=residues), :]
            + update[k * residues : (k + 1) * residues, :]
        )

    shown = mul(valid[...].astype(BF16), column[...])
    right_w = jnp.concatenate([proj[:, C_TRI:], gates[:, C_TRI:]], axis=1)
    step = min(residues, 16)
    for k in range(0, residues, step):
        here = slice(k * residues, (k + step) * residues)
        both = mul(normal(one[here, :]).astype(BF16), right_w)
        both = sigmoid(both[:, C_TRI:]) * both[:, :C_TRI]
        for p in range(step):
            part = both[p * residues : (p + 1) * residues]
            part = part * shown[:, (k + p) * C_TRI : (k + p + 1) * C_TRI]
            right_at[(k + p) * residues : (k + p + 1) * residues, :] = part.astype(BF16).astype(F32)

    sums = [jnp.zeros((residues, C_TRI), F32) for _ in range(res_dev)]
    for k in range(residues):
        other = right_at[k * residues : (k + 1) * residues, :]
        for i in range(res_dev):
            sums[i] += left_at[i * residues + k : i * residues + k + 1, :] * other
    mixed = normal(jnp.concatenate(sums, axis=0)).astype(BF16)
    result = own + own_gate * mul(mixed, w_out[...])
    out_ref[...] = result.reshape(res_dev, residues, width).astype(BF16)


def call(kernel, out_shape, scratch, vmem_mib, *args):
    vmem = pl.BlockSpec(memory_space=pltpu.VMEM)
    return pl.pallas_call(
        kernel,
        out_shape=out_shape,
        in_specs=[vmem] * len(args),
        out_specs=jax.tree.map(lambda _: vmem, out_shape),
        scratch_shapes=scratch,
        compiler_params=pltpu.CompilerParams(vmem_limit_bytes=vmem_mib * 1024 * 1024),
        cost_estimate=pl.CostEstimate(flops=FLOPS, bytes_accessed=0, transcendentals=0),
    )(*args)


def swap(array, r, n):
    return lax.ppermute(array, "axial", [(i, i ^ r) for i in range(n)])


def local_whole(
    homolog_activity,
    homolog_symbol_ids,
    residue_present_mask,
    pair_state,
    pair_valid_mask,
    symbol_lookup_matrix,
    row_query_weight,
    horizontal_attention_matrix,
    pair_bias_weight,
    horizontal_final_matrix,
    column_query_weight,
    vertical_attention_matrix,
    vertical_final_matrix,
    tensor_mean_lift_matrix,
    outer_product_output_weight,
    triangle_projection_weight,
    triangle_projection_gate,
    triangle_output_gate,
    triangle_output_weight,
):
    n = lax.axis_size("axial")
    per, residues, width = homolog_activity.shape
    res_dev, _, pair_width = pair_state.shape
    count = per * n
    shift, turn, column = call(
        functools.partial(table_kernel, FOCUS_TOTAL * res_dev, count),
        (
            jax.ShapeDtypeStruct((residues, 128), BF16),
            jax.ShapeDtypeStruct((count * residues, count * residues), BF16),
            jax.ShapeDtypeStruct((residues, residues * C_TRI), BF16),
        ),
        [],
        2,
    )
    packet, hidden_keys = call(
        packet_kernel,
        (
            jax.ShapeDtypeStruct((per * residues + SMALL_ROWS, width), BF16),
            jax.ShapeDtypeStruct((residues, FOCUS_TOTAL * residues), F32),
        ),
        [],
        4,
        pair_state,
        pair_bias_weight.T,
        pair_valid_mask,
        homolog_symbol_ids,
        homolog_activity,
        residue_present_mask.reshape(1, residues),
        shift,
    )
    packets = [swap(packet, r, n) for r in PACKET_ORDER]
    _, later = lax.optimization_barrier((packet, pair_state))
    pairs = [swap(later, r, n) for r in PAIR_ORDER]
    alignment, update = call(
        functools.partial(msa_kernel, n, res_dev),
        (
            jax.ShapeDtypeStruct((count, res_dev, width), BF16),
            jax.ShapeDtypeStruct((residues * residues, pair_width), F32),
        ),
        [
            pltpu.VMEM((MEAN_HIDDEN_SIZE, count * residues, pair_width), F32),
            pltpu.VMEM((count * residues, width), F32),
        ],
        16,
        packet,
        *packets,
        turn,
        hidden_keys,
        symbol_lookup_matrix,
        row_query_weight,
        horizontal_attention_matrix,
        horizontal_final_matrix,
        column_query_weight,
        vertical_attention_matrix,
        vertical_final_matrix,
        tensor_mean_lift_matrix.T,
        outer_product_output_weight,
    )
    pair_output = call(
        pair_kernel,
        jax.ShapeDtypeStruct((res_dev, residues, pair_width), BF16),
        [
            pltpu.VMEM((residues * residues, pair_width), F32),
            pltpu.VMEM((residues * residues, pair_width), F32),
            pltpu.VMEM((residues * residues, C_TRI), F32),
            pltpu.VMEM((res_dev * residues, C_TRI), F32),
            pltpu.VMEM((residues, residues), F32),
        ],
        16,
        *pairs,
        *packets,
        update,
        column,
        pair_state,
        pair_valid_mask,
        triangle_projection_weight,
        triangle_projection_gate,
        triangle_output_gate,
        triangle_output_weight,
    )
    return (alignment, pair_output)


def local(homolog_activity, homolog_symbol_ids, residue_present_mask, pair_state, *others):
    n = lax.axis_size("axial")
    per, residues, _ = homolog_activity.shape
    small = n == 4 and per * n == 8 and residues == 32
    plan = local_whole if small else local_sharded
    return plan(homolog_activity, homolog_symbol_ids, residue_present_mask, pair_state, *others)


def solution(mesh):
    parts, copied = P(("dp", "axial")), P()
    return jax.shard_map(
        local,
        mesh=mesh,
        in_specs=(parts, parts, P("dp"), parts, parts) + (copied,) * 14,
        out_specs=(P("dp", "axial", None), P(("dp", "axial"), None, None)),
        check_vma=False,
    )
```

```python
import functools

import jax
import jax.numpy as jnp
from jax import lax
from jax.experimental import pallas as pl
from jax.experimental.pallas import tpu as pltpu
from jax.sharding import PartitionSpec as P

FOCUS_TOTAL = 8
FOCUS_SIZE = 32
MEAN_HIDDEN_SIZE = 32
C_TRI = 128


def layer_normalize(attended_entries):
    attended_entries = attended_entries.astype(jnp.float32)
    mean = jnp.mean(attended_entries, axis=-1, keepdims=True)
    centred = attended_entries - mean
    var = jnp.mean(centred * centred, axis=-1, keepdims=True)
    return centred * lax.rsqrt(var + 1e-05)


def gated_attend(evoformer_block, extra_axes, w_query, w_kvg, w_out):
    lines_list, residue_length, input_width = evoformer_block.shape
    width = FOCUS_TOTAL * FOCUS_SIZE
    flat = (
        layer_normalize(evoformer_block)
        .astype(jnp.bfloat16)
        .reshape(lines_list * residue_length, input_width)
    )
    query = (
        jnp.dot(flat, w_query, preferred_element_type=jnp.float32) * FOCUS_SIZE ** (-0.5)
    ).astype(jnp.bfloat16)
    query = query.reshape(lines_list, residue_length, FOCUS_TOTAL, FOCUS_SIZE)
    kvg = jnp.dot(flat, w_kvg, preferred_element_type=jnp.float32)
    keys = (
        kvg[:, :width]
        .astype(jnp.bfloat16)
        .reshape(lines_list, residue_length, FOCUS_TOTAL, FOCUS_SIZE)
    )
    attended_entries = (
        kvg[:, width : 2 * width]
        .astype(jnp.bfloat16)
        .reshape(lines_list, residue_length, FOCUS_TOTAL, FOCUS_SIZE)
    )
    gate = jax.nn.sigmoid(kvg[:, 2 * width :]).reshape(
        lines_list, residue_length, FOCUS_TOTAL, FOCUS_SIZE
    )
    scores = (
        jnp.einsum("bihd,bjhd->bhij", query, keys, preferred_element_type=jnp.float32) + extra_axes
    )
    top = jnp.max(scores, axis=-1, keepdims=True)
    expo = jnp.exp(scores - top)
    weights = (expo / jnp.sum(expo, axis=-1, keepdims=True)).astype(jnp.bfloat16)
    mixed = jnp.einsum(
        "bhij,bjhd->bihd", weights, attended_entries, preferred_element_type=jnp.float32
    )
    mixed = (mixed * gate).astype(jnp.bfloat16).reshape(lines_list * residue_length, width)
    return evoformer_block + jnp.dot(mixed, w_out, preferred_element_type=jnp.float32).reshape(
        lines_list, residue_length, input_width
    )


def finish_sums(evoformer_block, triangle_output_weight):
    mixed = layer_normalize(jnp.transpose(evoformer_block, (1, 2, 0))).astype(jnp.bfloat16)
    return jnp.einsum(
        "ijc,cz->ijz", mixed, triangle_output_weight, preferred_element_type=jnp.float32
    )


def local_sharded(
    homolog_activity,
    homolog_symbol_ids,
    residue_present_mask,
    pair_state,
    pair_valid_mask,
    symbol_lookup_matrix,
    row_query_weight,
    horizontal_attention_matrix,
    pair_bias_weight,
    horizontal_final_matrix,
    column_query_weight,
    vertical_attention_matrix,
    vertical_final_matrix,
    tensor_mean_lift_matrix,
    outer_product_output_weight,
    triangle_projection_weight,
    triangle_projection_gate,
    triangle_output_gate,
    triangle_output_weight,
):
    sequence_per_device, residue_length, input_width = homolog_activity.shape
    res_dev = pair_state.shape[0]
    group_size = lax.axis_size("axial")
    token_classes = symbol_lookup_matrix.shape[0]
    token_one_hot = (
        homolog_symbol_ids[..., None] == jnp.arange(token_classes, dtype=jnp.int32)
    ).astype(jnp.bfloat16)
    token_embedded = jnp.einsum(
        "slt,tc->slc", token_one_hot, symbol_lookup_matrix, preferred_element_type=jnp.float32
    )
    homolog_starting = homolog_activity.astype(jnp.float32) + token_embedded
    pair_norm = layer_normalize(pair_state).astype(jnp.bfloat16)
    bias_rows = jnp.einsum(
        "ijc,ch->hij", pair_norm, pair_bias_weight, preferred_element_type=jnp.float32
    ).astype(jnp.bfloat16)
    bias_full = lax.all_gather(bias_rows, "axial", axis=1, tiled=True)
    key_bias = 1000000000.0 * (residue_present_mask.astype(jnp.float32) - 1.0)
    extra_axes = bias_full.astype(jnp.float32)[None] + key_bias[None, None, None, :]
    cluster_total = homolog_starting.reshape(
        sequence_per_device // 2, 2, residue_length, input_width
    )
    homolog_across_update = lax.map(
        lambda evoformer_block: gated_attend(
            evoformer_block,
            extra_axes,
            row_query_weight,
            horizontal_attention_matrix,
            horizontal_final_matrix,
        ),
        cluster_total,
    )
    homolog_across_update = homolog_across_update.reshape(
        sequence_per_device, group_size, res_dev, input_width
    ).astype(jnp.bfloat16)
    moved = jnp.swapaxes(
        lax.all_to_all(homolog_across_update, "axial", split_axis=1, concat_axis=0, tiled=True)[
            :, 0
        ],
        0,
        1,
    )
    finished = lax.map(
        lambda item: gated_attend(
            item[None].astype(jnp.float32),
            0.0,
            column_query_weight,
            vertical_attention_matrix,
            vertical_final_matrix,
        )[0],
        moved,
    )
    exchanged = jnp.swapaxes(finished, 0, 1).astype(jnp.bfloat16)[:, None]
    sequence_count = exchanged.shape[0]
    alignment_after_columns = exchanged.reshape(sequence_count, res_dev, input_width)
    tensor_mean_scaler = layer_normalize(alignment_after_columns).astype(jnp.bfloat16)
    split_parts = jnp.einsum(
        "src,cf->rsf",
        tensor_mean_scaler,
        tensor_mean_lift_matrix,
        preferred_element_type=jnp.float32,
    ).astype(jnp.bfloat16)
    first_factor = split_parts[..., :MEAN_HIDDEN_SIZE]
    second_factor = split_parts[..., MEAN_HIDDEN_SIZE:].reshape(
        res_dev, sequence_count * MEAN_HIDDEN_SIZE
    )
    step_rows = 8
    left_blocks = first_factor.reshape(
        res_dev // step_rows, step_rows, sequence_count, MEAN_HIDDEN_SIZE
    )
    piece = lax.all_gather(second_factor, "axial", axis=0, tiled=True)
    count = piece.shape[0]
    right_part = piece.reshape(count, sequence_count, MEAN_HIDDEN_SIZE)

    def one_block(lines_list):
        tensor_mean = (
            jnp.einsum("isc,jsd->ijcd", lines_list, right_part, preferred_element_type=jnp.float32)
            / sequence_count
        )
        tensor_mean = tensor_mean.reshape(
            step_rows, count, MEAN_HIDDEN_SIZE * MEAN_HIDDEN_SIZE
        ).astype(jnp.bfloat16)
        return jnp.einsum(
            "ijf,fz->ijz",
            tensor_mean,
            outer_product_output_weight,
            preferred_element_type=jnp.float32,
        )

    update = lax.map(one_block, left_blocks).reshape(
        res_dev, count, outer_product_output_weight.shape[1]
    )
    pair_one = pair_state.astype(jnp.float32) + update
    tri_norm = layer_normalize(pair_one).astype(jnp.bfloat16)
    proj = jnp.einsum(
        "ikc,cf->fik", tri_norm, triangle_projection_weight, preferred_element_type=jnp.float32
    )
    gates = jnp.einsum(
        "ikc,cf->fik", tri_norm, triangle_projection_gate, preferred_element_type=jnp.float32
    )
    both = (jax.nn.sigmoid(gates) * proj * pair_valid_mask.astype(jnp.float32)[None]).astype(
        jnp.bfloat16
    )
    left_tri = both[:C_TRI]
    right_tri = both[C_TRI:]
    moved_left, moved_right = (
        lax.all_to_all(left_tri, "axial", split_axis=0, concat_axis=1, tiled=True),
        lax.all_to_all(right_tri, "axial", split_axis=0, concat_axis=1, tiled=True),
    )
    partial_sum = jnp.einsum(
        "cik,cjk->cij", moved_left, moved_right, preferred_element_type=jnp.float32
    )
    tri_sum = lax.all_to_all(
        partial_sum.astype(jnp.bfloat16), "axial", split_axis=1, concat_axis=0, tiled=True
    ).astype(partial_sum.dtype)
    tri_update = finish_sums(tri_sum, triangle_output_weight)
    out_gate = jax.nn.sigmoid(
        jnp.einsum(
            "ijc,cz->ijz", tri_norm, triangle_output_gate, preferred_element_type=jnp.float32
        )
    )
    pair_output = (pair_one + out_gate * tri_update).astype(jnp.bfloat16)
    return (alignment_after_columns, pair_output)


BF16 = jnp.bfloat16
F32 = jnp.float32
SMALL_ROWS = 16
FLOPS = 3 * 10**9
PACKET_ORDER = (2, 3, 1)
PAIR_ORDER = (2, 1, 3)


def mul(lhs, rhs, over=((1,), (0,))):
    return lax.dot_general(lhs, rhs, (over, ((), ())), preferred_element_type=F32)


def iota(shape, axis):
    return lax.broadcasted_iota(jnp.int32, shape, axis)


def zero_one(condition):
    return jnp.where(condition, 1.0, 0.0).astype(BF16)


def normal(x):
    mean = jnp.mean(x, axis=-1, keepdims=True)
    centred = x - mean
    var = jnp.mean(centred * centred, axis=-1, keepdims=True)
    return centred * lax.rsqrt(var + 1e-05)


def sigmoid(x):
    return 0.5 + 0.5 * jnp.tanh(0.5 * x)


def column_softmax(scores):
    expo = jnp.exp(scores - jnp.max(scores, axis=0, keepdims=True))
    return expo * (1.0 / jnp.sum(expo, axis=0, keepdims=True))


def bias_rows(pair_ref, weight_ref):
    rows, residues, width = pair_ref.shape
    lanes = FOCUS_TOTAL * rows
    spread = zero_one(iota((FOCUS_TOTAL, lanes), 1) // rows == iota((FOCUS_TOTAL, lanes), 0))
    row_of = iota((width, lanes), 1) % rows
    flat = normal(pair_ref[...].astype(F32).reshape(rows * residues, width)).astype(BF16)
    weight = mul(weight_ref[...], spread, ((0,), (0,)))
    side_by_side = [flat[i * residues : (i + 1) * residues] for i in range(rows)]
    one_row = [jnp.where(row_of == i, weight, 0.0).astype(BF16) for i in range(rows)]
    bias = mul(jnp.concatenate(side_by_side, axis=1), jnp.concatenate(one_row, axis=0))
    return bias


def table_kernel(lanes, count, shift_ref, turn_ref, column_ref):
    shape = column_ref.shape
    column_ref[...] = zero_one(iota(shape, 1) // C_TRI == iota(shape, 0))
    shape = shift_ref.shape
    shift_ref[...] = zero_one(iota(shape, 1) == iota(shape, 0) + lanes)
    shape = turn_ref.shape
    row_at = iota(shape, 0)
    turn_ref[...] = zero_one(
        iota(shape, 1) == (row_at % count) * (shape[0] // count) + row_at // count
    )


def packet_kernel(*refs):
    pair_ref, weight_ref, valid_ref, ids_ref, act_ref, present_ref, shift_ref = refs[:7]
    packet_ref, hidden_ref = refs[7:]
    rows, residues, width = pair_ref.shape
    per, _, features = act_ref.shape
    lanes = FOCUS_TOTAL * rows
    bias = bias_rows(pair_ref, weight_ref)
    extra = jnp.concatenate(
        [
            valid_ref[...].astype(F32),
            ids_ref[...].astype(F32),
            jnp.zeros((SMALL_ROWS - rows - per, residues), F32),
        ],
        axis=0,
    )
    extra = mul(extra.astype(BF16), shift_ref[...])
    empty = jnp.zeros((SMALL_ROWS, 128 - lanes), F32)
    first = jnp.concatenate([bias[:SMALL_ROWS], empty], axis=1) + extra
    second = jnp.concatenate([bias[SMALL_ROWS:], empty], axis=1)
    small = jnp.concatenate([first, second], axis=1).astype(BF16)
    packet_ref[per * residues :, :] = small
    shown = present_ref[...].astype(F32).astype(BF16)
    shown = mul(shown, jnp.ones((1, hidden_ref.shape[1]), BF16), ((0,), (0,)))
    hidden_ref[...] = 1000000000.0 * (shown - 1.0)
    packet_ref[: per * residues, :] = act_ref[...].reshape(per * residues, features)


def split_small(packet, residues, res_dev, per):
    small = packet[per * residues :, :].astype(F32)
    lanes = FOCUS_TOTAL * res_dev
    bias = jnp.concatenate([small[:, :lanes], small[:, 128 : 128 + lanes]], axis=0)
    extra = small[:, lanes : lanes + residues]
    return bias, extra[:res_dev], extra[res_dev : res_dev + per]


def head_masks(width):
    return [
        zero_one(iota((1, width), 1) // FOCUS_SIZE == h) for h in range(FOCUS_TOTAL)
    ]


def project(x, w_query, w_kvg):
    width = FOCUS_TOTAL * FOCUS_SIZE
    flat = normal(x).astype(BF16)
    query = (mul(flat, w_query[...]) * FOCUS_SIZE ** (-0.5)).astype(BF16)
    keys = mul(flat, w_kvg[:, :width]).astype(BF16)
    values = mul(flat, w_kvg[:, width : 2 * width]).astype(BF16)
    gate = sigmoid(mul(flat, w_kvg[:, 2 * width :]))
    return query, keys, values, gate


def msa_kernel(n, res_dev, *refs):
    packets, turn, hidden_keys, table = refs[:n], refs[n], refs[n + 1], refs[n + 2]
    refs = refs[n + 3 :]
    row_q, row_kvg, row_out, col_q, col_kvg, col_out, lift, outer_w = refs[:8]
    align_ref, update_ref, lifted = refs[8:]
    kinds, width = table.shape
    residues, lanes = hidden_keys.shape
    pair_width = outer_w.shape[1]
    per = (packets[0].shape[0] - SMALL_ROWS) // residues
    count = per * n
    tokens = count * residues
    me = lax.axis_index("axial")

    place = iota((FOCUS_TOTAL * res_dev, lanes), 0)
    place = (place // res_dev) * residues + place % res_dev - iota(place.shape, 1)
    bias = jnp.zeros((residues, lanes), F32)
    rows = []
    for packet, r in zip(packets, (0, *PACKET_ORDER)):
        part, _, all_ids = split_small(packet, residues, res_dev, per)
        bias += mul(part.astype(BF16), zero_one(place == -(me ^ r) * res_dev))
        for q in range(per):
            hot = zero_one(iota((kinds, residues), 0).astype(F32) == all_ids[q : q + 1])
            act = packet[q * residues : (q + 1) * residues, :].astype(F32)
            rows.append(act + mul(hot, table[...], ((0,), (0,))))
    zero = jnp.concatenate(rows, axis=0)
    extra = bias + hidden_keys[...]
    masks = head_masks(width)

    query, keys, values, gate = project(zero, row_q, row_kvg)
    rows = []
    for s in range(count):
        here = slice(s * residues, (s + 1) * residues)
        spread = jnp.concatenate([query[here] * mask for mask in masks], axis=0)
        weights = column_softmax(mul(keys[here], spread, ((1,), (1,))) + extra).astype(BF16)
        heads = mul(weights, values[here], ((0,), (0,)))
        mixed = heads[:residues]
        for h in range(1, FOCUS_TOTAL):
            part = heads[h * residues : (h + 1) * residues]
            mixed = jnp.where(iota((1, width), 1) // FOCUS_SIZE == h, part, mixed)
        rows.append(mixed)
    mixed = (jnp.concatenate(rows, axis=0) * gate).astype(BF16)
    msa_one = (zero + mul(mixed, row_out[...])).astype(BF16)

    one = mul(turn[...], msa_one)
    query, keys, values, gate = project(one, col_q, col_kvg)
    group = min(tokens, 128)
    sites = group // count
    block_of = iota((1, group), 1) // count
    groups = []
    for g in range(tokens // group):
        here = slice(g * group, (g + 1) * group)
        all_weights, all_values = [], []
        for mask in masks:
            full = mul(keys[here], query[here] * mask, ((1,), (1,)))
            scores = full[:count]
            for b in range(1, sites):
                scores = jnp.where(block_of == b, full[b * count : (b + 1) * count], scores)
            weights = column_softmax(scores)
            weights = jnp.concatenate(
                [jnp.where(block_of == b, weights, 0.0) for b in range(sites)], axis=0
            )
            all_weights.append(weights.astype(BF16))
            all_values.append(values[here] * mask)
        groups.append(
            mul(
                jnp.concatenate(all_weights, axis=0),
                jnp.concatenate(all_values, axis=0),
                ((0,), (0,)),
            )
        )
    mixed = (jnp.concatenate(groups, axis=0) * gate).astype(BF16)
    align = (one + mul(mixed, col_out[...])).astype(BF16)
    own = count * res_dev
    row_at, lane_at = iota((own, tokens), 0), iota((own, tokens), 1)
    sequence = row_at // res_dev
    owner = (sequence // per) ^ me
    where_is = jnp.zeros_like(owner)
    for k, r in enumerate(PACKET_ORDER):
        where_is = jnp.where(owner == r, k + 1, where_is)
    pick = zero_one(
        lane_at
        == (row_at % res_dev + me * res_dev) * count + where_is * per + sequence % per
    )
    align_ref[...] = mul(pick, align).reshape(count, res_dev, width).astype(BF16)

    opm = normal(align.astype(F32)).astype(BF16)
    opm = mul(opm, lift[...], ((1,), (1,))).astype(BF16)
    hidden = MEAN_HIDDEN_SIZE
    deep = hidden * count
    spread = zero_one(
        iota((2 * hidden, deep), 1) // count == iota((2 * hidden, deep), 0)
    )
    left = mul(opm, spread)
    left = jnp.where(
        iota((tokens, deep), 0) % count == iota((tokens, deep), 1) % count, left, 0.0
    ).astype(BF16)
    gather = zero_one(iota((residues, tokens), 1) // count == iota((residues, tokens), 0))
    left = mul(gather, left).astype(BF16)
    right = opm[:, hidden:]
    for c in range(0, hidden, 4):
        four_w = jnp.concatenate(
            [outer_w[(c + k) * hidden : (c + k + 1) * hidden, :] for k in range(4)], axis=1
        )
        part = mul(right, four_w)
        for k in range(4):
            lifted[c + k] = part[:, k * pair_width : (k + 1) * pair_width]
    for j in range(0, residues, 4):
        part = jnp.concatenate(
            [
                lifted[:, (j + k) * count : (j + k + 1) * count, :].reshape(deep, pair_width)
                for k in range(4)
            ],
            axis=1,
        )
        part = mul(left, part.astype(BF16)) * (1.0 / count)
        for k in range(4):
            at = slice((j + k) * residues, (j + k + 1) * residues)
            update_ref[at, :] = part[:, k * pair_width : (k + 1) * pair_width]


def pair_kernel(*refs):
    pairs, packets, update, column, pair, own_mask = refs[:3], refs[3:6], *refs[6:10]
    proj, gates, gate_out, w_out, out_ref, state, one, right_at, left_at, valid = refs[10:]
    res_dev, residues, width = pair.shape
    per = (packets[0].shape[0] - SMALL_ROWS) // residues
    me = lax.axis_index("axial")
    own_valid = own_mask[...].astype(F32)
    for packet, r in zip((None, *packets), (0, *PACKET_ORDER)):
        shown = split_small(packet, residues, res_dev, per)[1] if r else own_valid
        valid[pl.ds(pl.multiple_of((me ^ r) * res_dev, res_dev), res_dev), :] = shown
    own = jnp.concatenate(
        [
            pair[i].astype(F32) + update[pl.ds(me * res_dev + i, residues, stride=residues), :]
            for i in range(res_dev)
        ],
        axis=0,
    )
    left_w = jnp.concatenate([proj[:, :C_TRI], gates[:, :C_TRI], gate_out[...]], axis=1)
    own_all = mul(normal(own).astype(BF16), left_w)
    own_gate = sigmoid(own_all[:, 2 * C_TRI :])
    left = sigmoid(own_all[:, C_TRI : 2 * C_TRI]) * own_all[:, :C_TRI]
    shown = mul(own_valid.astype(BF16), column[:res_dev, : res_dev * C_TRI], ((0,), (0,)))
    for i in range(res_dev):
        part = left[i * residues : (i + 1) * residues] * shown[:, i * C_TRI : (i + 1) * C_TRI]
        left_at[i * residues : (i + 1) * residues, :] = part.astype(BF16).astype(F32)
    size = res_dev * residues
    for block, r in zip((pair, *pairs), (0, *PAIR_ORDER)):
        state[pl.ds(pl.multiple_of((me ^ r) * size, size), size), :] = (
            block[...].astype(F32).reshape(size, width)
        )
    for k in range(residues):
        one[k * residues : (k + 1) * residues, :] = (
            state[pl.ds(k, residues, stride=residues), :]
            + update[k * residues : (k + 1) * residues, :]
        )

    shown = mul(valid[...].astype(BF16), column[...])
    right_w = jnp.concatenate([proj[:, C_TRI:], gates[:, C_TRI:]], axis=1)
    step = min(residues, 16)
    for k in range(0, residues, step):
        here = slice(k * residues, (k + step) * residues)
        both = mul(normal(one[here, :]).astype(BF16), right_w)
        both = sigmoid(both[:, C_TRI:]) * both[:, :C_TRI]
        for p in range(step):
            part = both[p * residues : (p + 1) * residues]
            part = part * shown[:, (k + p) * C_TRI : (k + p + 1) * C_TRI]
            right_at[(k + p) * residues : (k + p + 1) * residues, :] = part.astype(BF16).astype(F32)

    sums = [jnp.zeros((residues, C_TRI), F32) for _ in range(res_dev)]
    for k in range(residues):
        other = right_at[k * residues : (k + 1) * residues, :]
        for i in range(res_dev):
            sums[i] += left_at[i * residues + k : i * residues + k + 1, :] * other
    mixed = normal(jnp.concatenate(sums, axis=0)).astype(BF16)
    result = own + own_gate * mul(mixed, w_out[...])
    out_ref[...] = result.reshape(res_dev, residues, width).astype(BF16)


def call(kernel, out_shape, scratch, vmem_mib, *args):
    vmem = pl.BlockSpec(memory_space=pltpu.VMEM)
    return pl.pallas_call(
        kernel,
        out_shape=out_shape,
        in_specs=[vmem] * len(args),
        out_specs=jax.tree.map(lambda _: vmem, out_shape),
        scratch_shapes=scratch,
        compiler_params=pltpu.CompilerParams(vmem_limit_bytes=vmem_mib * 1024 * 1024),
        cost_estimate=pl.CostEstimate(flops=FLOPS, bytes_accessed=0, transcendentals=0),
    )(*args)


def swap(array, r, n):
    return lax.ppermute(array, "axial", [(i, i ^ r) for i in range(n)])


def local_whole(
    homolog_activity,
    homolog_symbol_ids,
    residue_present_mask,
    pair_state,
    pair_valid_mask,
    symbol_lookup_matrix,
    row_query_weight,
    horizontal_attention_matrix,
    pair_bias_weight,
    horizontal_final_matrix,
    column_query_weight,
    vertical_attention_matrix,
    vertical_final_matrix,
    tensor_mean_lift_matrix,
    outer_product_output_weight,
    triangle_projection_weight,
    triangle_projection_gate,
    triangle_output_gate,
    triangle_output_weight,
):
    n = lax.axis_size("axial")
    per, residues, width = homolog_activity.shape
    res_dev, _, pair_width = pair_state.shape
    count = per * n
    shift, turn, column = call(
        functools.partial(table_kernel, FOCUS_TOTAL * res_dev, count),
        (
            jax.ShapeDtypeStruct((residues, 128), BF16),
            jax.ShapeDtypeStruct((count * residues, count * residues), BF16),
            jax.ShapeDtypeStruct((residues, residues * C_TRI), BF16),
        ),
        [],
        2,
    )
    packet, hidden_keys = call(
        packet_kernel,
        (
            jax.ShapeDtypeStruct((per * residues + SMALL_ROWS, width), BF16),
            jax.ShapeDtypeStruct((residues, FOCUS_TOTAL * residues), F32),
        ),
        [],
        4,
        pair_state,
        pair_bias_weight.T,
        pair_valid_mask,
        homolog_symbol_ids,
        homolog_activity,
        residue_present_mask.reshape(1, residues),
        shift,
    )
    packets = [swap(packet, r, n) for r in PACKET_ORDER]
    _, later = lax.optimization_barrier((packet, pair_state))
    pairs = [swap(later, r, n) for r in PAIR_ORDER]
    alignment, update = call(
        functools.partial(msa_kernel, n, res_dev),
        (
            jax.ShapeDtypeStruct((count, res_dev, width), BF16),
            jax.ShapeDtypeStruct((residues * residues, pair_width), F32),
        ),
        [
            pltpu.VMEM((MEAN_HIDDEN_SIZE, count * residues, pair_width), F32),
        ],
        16,
        packet,
        *packets,
        turn,
        hidden_keys,
        symbol_lookup_matrix,
        row_query_weight,
        horizontal_attention_matrix,
        horizontal_final_matrix,
        column_query_weight,
        vertical_attention_matrix,
        vertical_final_matrix,
        tensor_mean_lift_matrix.T,
        outer_product_output_weight,
    )
    pair_output = call(
        pair_kernel,
        jax.ShapeDtypeStruct((res_dev, residues, pair_width), BF16),
        [
            pltpu.VMEM((residues * residues, pair_width), F32),
            pltpu.VMEM((residues * residues, pair_width), F32),
            pltpu.VMEM((residues * residues, C_TRI), F32),
            pltpu.VMEM((res_dev * residues, C_TRI), F32),
            pltpu.VMEM((residues, residues), F32),
        ],
        16,
        *pairs,
        *packets,
        update,
        column,
        pair_state,
        pair_valid_mask,
        triangle_projection_weight,
        triangle_projection_gate,
        triangle_output_gate,
        triangle_output_weight,
    )
    return (alignment, pair_output)


def local(homolog_activity, homolog_symbol_ids, residue_present_mask, pair_state, *others):
    n = lax.axis_size("axial")
    per, residues, _ = homolog_activity.shape
    small = n == 4 and per * n == 8 and residues == 32
    plan = local_whole if small else local_sharded
    return plan(homolog_activity, homolog_symbol_ids, residue_present_mask, pair_state, *others)


def solution(mesh):
    parts, copied = P(("dp", "axial")), P()
    return jax.shard_map(
        local,
        mesh=mesh,
        in_specs=(parts, parts, P("dp"), parts, parts) + (copied,) * 14,
        out_specs=(P("dp", "axial", None), P(("dp", "axial"), None, None)),
        check_vma=False,
    )
```
